128 devices in a mesh: dp: 16 (over y, z), expert: 8 (over x, core).
Axes of the slice: x: 4, y: 4, z: 4, core: 2. Of those that a mesh axis runs over, the one named last changes fastest.
Arguments:
- tokens: bfloat16 [32768, 1536], P(('dp', 'expert')), may hold values from -6 to 6
- d_out: bfloat16 [32768, 1536], P(('dp', 'expert')), may hold values from -6 to 6
- gain_in: bfloat16 [1536], P('dp'), may hold values from 0.099609375 to 1.8984375
- w_query: bfloat16 [1536, 1536], P('dp'), may hold values from -0.15625 to 0.15625
- key_projection_weight: bfloat16 [1536, 256], P('dp'), may hold values from -0.15625 to 0.15625
- value_projection_weight: bfloat16 [1536, 256], P('dp'), may hold values from -0.15625 to 0.15625
- w_out: bfloat16 [1536, 1536], P('dp'), may hold values from -3.5 to 3.5
- gain_mid: bfloat16 [1536], P('dp'), may hold values from 0.099609375 to 1.8984375
- w_router: bfloat16 [1536, 8], P('dp'), may hold values from -0.078125 to 0.078125
- w_gate: bfloat16 [8, 1536, 768], P('expert'), may hold values from -0.15625 to 0.15625
- w_up: bfloat16 [8, 1536, 768], P('expert'), may hold values from -0.15625 to 0.15625
- w_down: bfloat16 [8, 768, 1536], P('expert'), may hold values from -0.4375 to 0.4375
- routes: int32 [32768, 4], P(('dp', 'expert')), may hold values from 0 to 7, all different within a row; in each aligned block of 256 rows (0 to 255, 256 to 511, ...) at most 144 rows name the same one
- segments: int32 [16, 2048], P('dp'), may hold values from 0 to 3, never falling along the last dimension, each value on 1 to 1794 neighbouring positions
Outputs:
- mixed: bfloat16 [32768, 1536], P(('dp', 'expert'))
- grad_tokens: float32 [32768, 1536], P(('dp', 'expert'))
- grad_gain_in: float32 [1536], P('dp')
- grad_w_query: float32 [1536, 1536], P('dp')
- grad_w_key: float32 [1536, 256], P('dp')
- grad_w_value: float32 [1536, 256], P('dp')
- grad_w_out: float32 [1536, 1536], P('dp')
- grad_gain_mid: float32 [1536], P('dp')
- grad_w_router: float32 [1536, 8], P('dp')
- grad_w_gate: float32 [8, 1536, 768], P('expert')
- grad_w_up: float32 [8, 1536, 768], P('expert')
- grad_w_down: float32 [8, 768, 1536], P('expert')
The draws below stay inside these ranges and needn't reach their ends.
Inputs may be any that keep to these rules, and one draw needn't show every extreme that they name: `routes`: each row names 4 different experts. The 256 rows of one device name no expert more than 144 times, and on some devices one expert exactly 144 times. `segments`: each row numbers its 4 documents in order without falling, every number used; one document of each row has exactly 1794 tokens.
All inputs are finite; a program needn't handle non-finite values.
Results may differ from the reference program's by a relative error of at most 0.025.
Values may be sent and summed in bfloat16 or wider, within the bound.
A program may use at most 256 MiB of HBM per device.

```python
import math
import jax
import jax.numpy as jnp
import numpy as np
from jax import lax

MODEL_WIDTH = 1536
QUERY_HEADS = 12
KEY_VALUE_HEADS = 2
HEAD_SIZE = 128
FF = 768
TOPK = 4
EXPERTS = 8
DOCS = 4
PACKED_LENGTH = 2048
TOK_DEV = 256
CAP = 144
TOKEN_TOTAL = 32768
N_DP = 16


def level_of(own_key, dims, split, least, top_value):
    level = 1.0
    for axis_at, shards_of in split:
        draws = jax.random.uniform(jax.random.fold_in(jax.random.fold_in(own_key, 6), axis_at), (shards_of,), jnp.float32, least / len(split), top_value / len(split))
        level = level * jnp.repeat(jnp.exp(draws), dims[axis_at] // shards_of).reshape((-1,) + (1,) * (len(dims) - 1 - axis_at))
    return level


def split_up(count, total, bound, lean):
    portions = [(1 << 20) // math.isqrt(grade ** lean) + 1 for grade in range(2, count + 1)]
    rest, given = total - bound - (count - 1), [1] * (count - 1)
    while rest > 0:
        free = [i for i in range(count - 1) if given[i] < bound]
        pool, budget = sum([portions[i] for i in free]), rest
        for i in free:
            more = min(bound - given[i], max(1, budget * portions[i] // pool), rest)
            given[i] = given[i] + more
            rest = rest - more
    return np.array([bound] + given)


def ragged(stream_key, count, total, reach, slope):
    if count == 2:
        one = jax.random.randint(stream_key, (), max(1, total - reach), min(reach, total - 1) + 1)
        return jnp.stack([one, total - one])
    lengths = jnp.asarray(split_up(count, total, reach, slope), jnp.int32)
    couples = (count - 1) // 2
    source_of, receiver = lengths[1:1 + 2 * couples:2], lengths[2:2 + 2 * couples:2]
    room = jnp.minimum(source_of - 1, reach - receiver)
    passed = jax.random.randint(jax.random.fold_in(stream_key, 1), (couples,), 0, 1 << 20) % (room + 1)
    lengths = lengths.at[1:1 + 2 * couples:2].set(source_of - passed).at[2:2 + 2 * couples:2].set(receiver + passed)
    return lengths[jax.random.permutation(jax.random.fold_in(stream_key, 2), count)]


def deal_out(stream_key, own, number, rows, amount, top, most, lean):
    order = jax.random.permutation(stream_key, amount)
    crowded, usual = load_shares(amount, rows * top, most, lean, True), load_shares(amount, rows * top, most, lean, False)
    places = jnp.arange(amount)

    def named(tallies, offset_by):
        used = int((tallies > 0).sum())
        fixed = max(1, used // 4)
        shifted = fixed + (places - fixed + offset_by * (used - fixed)) % max(1, amount - fixed)
        return jnp.zeros((amount,), jnp.int32).at[order[jnp.where(places < fixed, places, shifted)]].set(jnp.asarray(tallies, jnp.int32))

    tallies = jnp.where(number % 4 == 0, named(crowded, number // 4), named(usual, number - number // 4 - 1))
    mixed = jax.random.permutation(jax.random.fold_in(own, 3), amount)
    giver, taker = mixed[0:amount // 2 * 2:2], mixed[1:amount // 2 * 2:2]
    slack = jnp.minimum(tallies[giver] - 1, most - tallies[taker]) // 2
    slack = jnp.where((giver == order[0]) | (taker == order[0]) | (tallies[taker] == 0), 0, jnp.maximum(slack, 0))
    shifted = jax.random.randint(jax.random.fold_in(own, 4), (amount // 2,), 0, 1 << 20) % (slack + 1)
    tallies = tallies.at[giver].add(-shifted).at[taker].add(shifted)
    members = jnp.searchsorted(jnp.cumsum(tallies), jnp.arange(rows * top), side="right").astype(jnp.int32)
    grid = members.reshape(top, rows).T
    grid = grid[jax.random.permutation(jax.random.fold_in(own, 1), rows)]
    offset_by = jax.random.randint(jax.random.fold_in(own, 2), (rows, 1), 0, top)
    return jnp.take_along_axis(grid, (jnp.arange(top)[None, :] + offset_by) % top, axis=1)


def load_shares(amount, total, reach, slope, full):
    portions = [(1 << 20) // math.isqrt(grade ** slope) + 1 for grade in range(1, amount + 1)]
    largest = reach if full else min(reach, max(-(-total // amount), total * portions[0] // sum(portions)))
    least = 1 if total - largest >= amount - 1 else 0
    given, spare = [largest] + [least] * (amount - 1), total - largest - least * (amount - 1)
    while spare > 0:
        free = [i for i in range(1, amount) if given[i] < largest] or [i for i in range(1, amount) if given[i] < reach]
        mass, left = sum([portions[i] for i in free]), spare
        for i in free:
            extra = min(reach - given[i], max(1, left * portions[i] // mass), spare)
            given[i] = given[i] + extra
            spare = spare - extra
    return np.array(given)


def scatter_about(stream_key, shape, spread, limit, shards=(), kind=jnp.bfloat16):
    entries = spread * jax.random.normal(stream_key, shape, jnp.float32)
    if shards:
        entries = entries * level_of(stream_key, shape, shards, -0.22, 0.18)
    return jnp.clip(entries, -limit, limit).astype(kind)


def setup_inputs(seed: int = 0) -> dict:
    key_of = jax.random.split(jax.random.key(seed), 15)
    tokens = scatter_about(key_of[0], (TOKEN_TOTAL, MODEL_WIDTH), 1.0, 6.0, ((0, 128),))
    d_out = scatter_about(key_of[1], (TOKEN_TOTAL, MODEL_WIDTH), 1.0, 6.0, ((0, 128),))
    gain_in = jnp.clip(1.0 + 0.18 * jax.random.normal(key_of[2], (MODEL_WIDTH,), jnp.float32), 0.099609375, 1.8984375).astype(jnp.bfloat16)
    w_query = scatter_about(key_of[3], (MODEL_WIDTH, QUERY_HEADS * HEAD_SIZE), MODEL_WIDTH ** -0.5, 0.15625, ((0, 16),))
    key_projection_weight = scatter_about(key_of[4], (MODEL_WIDTH, KEY_VALUE_HEADS * HEAD_SIZE), MODEL_WIDTH ** -0.5, 0.15625, ((0, 16),))
    value_projection_weight = scatter_about(key_of[5], (MODEL_WIDTH, KEY_VALUE_HEADS * HEAD_SIZE), MODEL_WIDTH ** -0.5, 0.15625, ((0, 16),))
    w_out = scatter_about(key_of[6], (QUERY_HEADS * HEAD_SIZE, MODEL_WIDTH), (max(1, 4 * MODEL_WIDTH // PACKED_LENGTH)) ** -0.5, 3.5, ((0, 16),))
    gain_mid = jnp.clip(1.0 + 0.18 * jax.random.normal(key_of[7], (MODEL_WIDTH,), jnp.float32), 0.099609375, 1.8984375).astype(jnp.bfloat16)
    w_router = scatter_about(key_of[8], (MODEL_WIDTH, EXPERTS), (4 * MODEL_WIDTH) ** -0.5, 0.078125, ((0, 16),))
    w_gate = scatter_about(key_of[9], (EXPERTS, MODEL_WIDTH, FF), MODEL_WIDTH ** -0.5, 0.15625, ((0, 8),))
    w_up = scatter_about(key_of[10], (EXPERTS, MODEL_WIDTH, FF), MODEL_WIDTH ** -0.5, 0.15625, ((0, 8),))
    w_down = scatter_about(key_of[11], (EXPERTS, FF, MODEL_WIDTH), (FF // 4) ** -0.5, 0.4375, ((0, 8),))
    routes_keys = jax.random.split(jax.random.fold_in(key_of[12], 1), TOKEN_TOTAL // TOK_DEV)
    routes_turns = jax.random.permutation(jax.random.fold_in(key_of[12], 3), TOKEN_TOTAL // TOK_DEV)
    routes = jax.vmap(lambda own, number: deal_out(jax.random.fold_in(key_of[12], 2), own, number, TOK_DEV, EXPERTS, TOPK, CAP, 1))(routes_keys, routes_turns).reshape((TOKEN_TOTAL, TOPK))
    segments = jax.vmap(lambda own: jnp.searchsorted(jnp.cumsum(ragged(own, DOCS, PACKED_LENGTH, PACKED_LENGTH - TOK_DEV + 2, 0)), jnp.arange(PACKED_LENGTH), side="right"))(jax.random.split(key_of[13], N_DP)).reshape((N_DP, PACKED_LENGTH)).astype(jnp.int32)
    return {"tokens": tokens, "d_out": d_out, "gain_in": gain_in, "w_query": w_query, "key_projection_weight": key_projection_weight, "value_projection_weight": value_projection_weight, "w_out": w_out, "gain_mid": gain_mid, "w_router": w_router, "w_gate": w_gate, "w_up": w_up, "w_down": w_down, "routes": routes, "segments": segments}


@jax.custom_vjp
def lower_precision(v):
    return lax.optimization_barrier(v.astype(jnp.bfloat16)).astype(jnp.float32)

@jax.custom_vjp
def low_back(v):
    return v

def low_keep(v):
    return (lower_precision(v), None)

def low_pass(kept, grad):
    return (grad,)

def back_keep(v):
    return (v, None)

def back_low(kept, grad):
    return (lower_precision(grad),)
lower_precision.defvjp(low_keep, low_pass)
low_back.defvjp(back_keep, back_low)
EPSILON = 1e-06
ROPE_BASE = 1000000.0
MASK_FILL = -1e+30

def matmul(left, right):
    return jnp.dot(left, right, precision=lax.Precision.HIGHEST, preferred_element_type=jnp.float32)

def rms_scale(value_rows, gain):
    inverse = lax.rsqrt(lax.optimization_barrier(jnp.mean(value_rows * value_rows, axis=-1, keepdims=True)) + EPSILON)
    return value_rows * inverse * gain

def doc_positions(seg_row):
    labels = jnp.arange(DOCS, dtype=jnp.int32)
    member = (seg_row[:, None] == labels[None, :]).astype(jnp.int32)
    counts = lax.optimization_barrier(jnp.sum(member, axis=0))
    starts = jnp.cumsum(counts) - counts
    leading = lax.optimization_barrier(jnp.sum(member * starts[None, :], axis=1))
    return jnp.arange(seg_row.shape[0], dtype=jnp.int32) - leading

def angles_for(positions):
    half_width = HEAD_SIZE // 2
    freqs = ROPE_BASE ** (-2.0 * jnp.arange(half_width, dtype=jnp.float32) / HEAD_SIZE)
    return positions.astype(jnp.float32)[:, None] * freqs[None, :]

def apply_rotary(heads, rotary_angles):
    half_width = heads.shape[-1] // 2
    cosine = jnp.cos(rotary_angles)[:, None, :]
    sine_part = jnp.sin(rotary_angles)[:, None, :]
    leading = heads[..., :half_width]
    trailing = heads[..., half_width:]
    return jnp.concatenate([leading * cosine - trailing * sine_part, trailing * cosine + leading * sine_part], axis=-1)

def attend(packed):
    query_rows, key_rows, value_rows, seg_row = packed
    query_groups = QUERY_HEADS // KEY_VALUE_HEADS
    query_rows = query_rows.reshape(PACKED_LENGTH, KEY_VALUE_HEADS, query_groups, HEAD_SIZE)
    key_rows = key_rows.reshape(PACKED_LENGTH, KEY_VALUE_HEADS, HEAD_SIZE)
    value_rows = value_rows.reshape(PACKED_LENGTH, KEY_VALUE_HEADS, HEAD_SIZE)
    scores = jnp.einsum('tkgd,skd->kgts', query_rows, key_rows, precision=lax.Precision.HIGHEST) * HEAD_SIZE ** (-0.5)
    scores = low_back(scores)
    places = jnp.arange(PACKED_LENGTH, dtype=jnp.int32)
    allowed = (seg_row[:, None] == seg_row[None, :]) & (places[:, None] >= places[None, :])
    scores = jnp.where(allowed[None, None], scores, MASK_FILL)
    probs = jax.nn.softmax(scores, axis=-1)
    context = jnp.einsum('kgts,skd->tkgd', lower_precision(probs), value_rows, precision=lax.Precision.HIGHEST)
    return context.reshape(PACKED_LENGTH, QUERY_HEADS * HEAD_SIZE)

def forward(inputs, gain_in, w_query, key_projection_weight, value_projection_weight, w_out, gain_mid, w_router, w_gate, w_up, w_down, routes, rotary_angles, segments):
    normed = lower_precision(rms_scale(inputs, gain_in))
    query_linear = low_back(matmul(normed, w_query))
    key_linear = low_back(matmul(normed, key_projection_weight))
    value_rows = low_back(lower_precision(matmul(normed, value_projection_weight)))
    query_rows = lower_precision(apply_rotary(query_linear.reshape(TOKEN_TOTAL, QUERY_HEADS, HEAD_SIZE), rotary_angles)).reshape(N_DP, PACKED_LENGTH, QUERY_HEADS * HEAD_SIZE)
    key_rows = lower_precision(apply_rotary(key_linear.reshape(TOKEN_TOTAL, KEY_VALUE_HEADS, HEAD_SIZE), rotary_angles)).reshape(N_DP, PACKED_LENGTH, KEY_VALUE_HEADS * HEAD_SIZE)
    value_rows = value_rows.reshape(N_DP, PACKED_LENGTH, KEY_VALUE_HEADS * HEAD_SIZE)
    context = lax.map(jax.checkpoint(attend), (query_rows, key_rows, value_rows, segments))
    context = low_back(lower_precision(context.reshape(TOKEN_TOTAL, QUERY_HEADS * HEAD_SIZE)))
    middle = inputs + low_back(matmul(context, w_out))
    normed_mid = lower_precision(rms_scale(middle, gain_mid))
    logits = low_back(matmul(normed_mid, w_router))
    chosen = jnp.take_along_axis(logits, routes, axis=1)
    gates = jax.nn.softmax(chosen, axis=-1)
    member = (routes[:, :, None] == jnp.arange(EXPERTS, dtype=jnp.int32)[None, None, :]).astype(jnp.float32)
    share = lax.optimization_barrier(jnp.sum(gates[:, :, None] * member, axis=1))

    def expert_step(total, packed):
        gate_w, up_w, down_w, column = packed
        expert_in = low_back(normed_mid)
        gate_pre = low_back(matmul(expert_in, gate_w))
        up_pre = low_back(matmul(expert_in, up_w))
        hidden = lower_precision(jax.nn.gelu(gate_pre, approximate=True) * up_pre)
        result = low_back(lower_precision(matmul(hidden, down_w)))
        return (total + column[:, None] * result, None)
    start = jnp.zeros((TOKEN_TOTAL, MODEL_WIDTH), jnp.float32)
    mixture, _ = lax.scan(jax.checkpoint(expert_step), start, (w_gate, w_up, w_down, share.T))
    return middle + mixture

def reference(tokens, d_out, gain_in, w_query, key_projection_weight, value_projection_weight, w_out, gain_mid, w_router, w_gate, w_up, w_down, routes, segments):
    positions = jax.vmap(doc_positions)(segments).reshape(TOKEN_TOTAL)
    rotary_angles = angles_for(positions)
    floats = tuple((array.astype(jnp.float32) for array in (tokens, gain_in, w_query, key_projection_weight, value_projection_weight, w_out, gain_mid, w_router, w_gate, w_up, w_down)))

    def wrapped(*params):
        return forward(*params, routes, rotary_angles, segments)
    result, pull = jax.vjp(wrapped, *floats)
    grads = pull(d_out.astype(jnp.float32))
    return (result.astype(jnp.bfloat16), grads[0], grads[1], grads[2], grads[3], grads[4], grads[5], grads[6], grads[7], grads[8], grads[9], grads[10])
```

```python
import functools

import jax
import jax.numpy as jnp
from jax import lax
from jax.experimental import pallas as pl
from jax.experimental.pallas import tpu as pltpu
from jax.sharding import PartitionSpec as P

QUERY_HEADS = 12
KEY_VALUE_HEADS = 2
HEAD_SIZE = 128
TOPK = 4
EXPERTS = 8
DOCS = 4
GROUP = QUERY_HEADS // KEY_VALUE_HEADS

EPSILON = 1e-06
ROPE_BASE = 1000000.0
MASK_FILL = -1e30
F32 = jnp.float32
BF16 = jnp.bfloat16

PARTNER = [(i, i ^ 1) for i in range(8)]
SAME_CORE = [[0, 2, 4, 6], [1, 3, 5, 7]]


def dot(a, b, dims):
    return lax.dot_general(a, b, (dims, ((), ())), preferred_element_type=F32)


def mm(a, b):
    return dot(a, b, ((1,), (0,)))


def mm_nt(a, b):
    return dot(a, b, ((1,), (1,)))


def mm_tn(a, b):
    return dot(a, b, ((0,), (0,)))


def rms_scale(value_rows, gain):
    inverse = lax.rsqrt(jnp.mean(value_rows * value_rows, axis=-1, keepdims=True) + EPSILON)
    return value_rows * inverse * gain


def rms_back(value_rows, gain, grad):
    inverse = lax.rsqrt(jnp.mean(value_rows * value_rows, axis=-1, keepdims=True) + EPSILON)
    scaled = value_rows * inverse
    weighted = grad * gain
    inner = jnp.mean(weighted * scaled, axis=-1, keepdims=True)
    return inverse * (weighted - scaled * inner), jnp.sum(grad * scaled, axis=0)


def doc_positions(seg_row):
    labels = jnp.arange(DOCS, dtype=jnp.int32)
    member = (seg_row[:, None] == labels[None, :]).astype(jnp.int32)
    counts = jnp.sum(member, axis=0)
    starts = jnp.cumsum(counts) - counts
    leading = jnp.sum(member * starts[None, :], axis=1)
    return jnp.arange(seg_row.shape[0], dtype=jnp.int32) - leading


def angles_for(positions):
    half_width = HEAD_SIZE // 2
    freqs = ROPE_BASE ** (-2.0 * jnp.arange(half_width, dtype=F32) / HEAD_SIZE)
    return positions.astype(F32)[:, None] * freqs[None, :]


def rotate(flat, cosine, sine, sign):
    heads = flat.reshape(flat.shape[0], -1, HEAD_SIZE)
    a, b = jnp.split(heads, 2, axis=-1)
    c, s = cosine[:, None, :], sign * sine[:, None, :]
    return jnp.concatenate([a * c - b * s, b * c + a * s], axis=-1).reshape(flat.shape)


def pp_core(x):
    return lax.ppermute(x, "expert", PARTNER)


def gather_dense(shard, core):
    half = shard.shape[1] // 2
    mine = lax.dynamic_slice_in_dim(shard, core * half, half, 1)
    got = lax.all_gather(mine, "dp", axis=0, tiled=True)
    other = pp_core(got)
    first = jnp.where(core == 0, got, other)
    second = jnp.where(core == 0, other, got)
    return jnp.concatenate([first, second], axis=1)


def ag_x(block):
    return lax.all_gather(block, "expert", axis=0, tiled=True)


def rs_x(blocks):
    return lax.psum_scatter(blocks, "expert", scatter_dimension=0, tiled=True)


MESH = pl.DeviceIdType.MESH
ANY = pl.BlockSpec(memory_space=pl.ANY)
VMEM = pl.BlockSpec(memory_space=pltpu.VMEM)


class Sends:
    def __init__(self, send_sems, recv_sems):
        self.send_sems, self.recv_sems, self.made = send_sems, recv_sems, []

    def start(self, src, dst, to):
        at = len(self.made)
        copy = pltpu.make_async_remote_copy(
            src_ref=src,
            dst_ref=dst,
            send_sem=self.send_sems.at[at],
            recv_sem=self.recv_sems.at[at],
            device_id=to,
            device_id_type=MESH,
        )
        copy.start()
        self.made.append(copy)
        return copy

    def finish(self):
        for copy in self.made:
            copy.wait_send()


def meet(*others):
    barrier = pltpu.get_barrier_semaphore()
    for other in others:
        pl.semaphore_signal(barrier, inc=1, device_id=other, device_id_type=MESH)
    pl.semaphore_wait(barrier, len(others))


def around_x():
    part = lax.axis_index("expert")
    x, core = part // 2, part % 2
    at = lambda dx: ((x + dx) % 4) * 2 + core
    return part, core, at(1), at(3), at(2), 2 * x + (1 - core)


def gather_x_kernel(block_ref, out_ref, local_sem, send_sems, recv_sems):
    part, core, right, left, far, partner = around_x()
    to = lambda i: {"expert": i}
    meet(to(partner), to(right), to(left))
    sends = Sends(send_sems, recv_sems)
    half = block_ref.shape[0] // 2
    own = pltpu.make_async_copy(block_ref, out_ref.at[part], local_sem)
    go_right = sends.start(block_ref, out_ref.at[part], to(right))
    go_left = sends.start(block_ref, out_ref.at[part], to(left))
    across = [sends.start(block_ref, out_ref.at[part], to(partner))]
    own.start()
    go_right.wait_recv()
    first = out_ref.at[left, pl.ds(0, half)]
    far_first = sends.start(first, first, to(right))
    across.append(sends.start(out_ref.at[left], out_ref.at[left], to(partner)))
    go_left.wait_recv()
    second = out_ref.at[right, pl.ds(half, half)]
    far_second = sends.start(second, second, to(left))
    across.append(sends.start(out_ref.at[right], out_ref.at[right], to(partner)))
    far_first.wait_recv()
    piece = out_ref.at[far, pl.ds(0, half)]
    across.append(sends.start(piece, piece, to(partner)))
    far_second.wait_recv()
    piece = out_ref.at[far, pl.ds(half, half)]
    across.append(sends.start(piece, piece, to(partner)))
    for copy in across:
        copy.wait_recv()
    own.wait()
    sends.finish()


def gather_x(block, collective_id):
    return pl.pallas_call(
        gather_x_kernel,
        out_shape=jax.ShapeDtypeStruct((8, *block.shape), block.dtype),
        in_specs=[ANY],
        out_specs=ANY,
        scratch_shapes=[
            pltpu.SemaphoreType.DMA,
            pltpu.SemaphoreType.DMA((9,)),
            pltpu.SemaphoreType.DMA((9,)),
        ],
        compiler_params=pltpu.CompilerParams(collective_id=collective_id, has_side_effects=True),
    )(block)


def reduce_x_kernel(
    blocks_ref, out_ref, mine, theirs, total, from_left, from_right, local_sems, send_sems, recv_sems
):
    part, core, right, left, far, partner = around_x()
    to = lambda i: {"expert": i}
    meet(to(partner), to(right), to(left))
    sends = Sends(send_sems, recv_sems)
    rows = out_ref.shape[0]
    half = rows // 2
    low, high = pl.ds(0, half), pl.ds(half, half)
    order = (far, right, left, part)
    flip = 1 - 2 * core
    swaps, loads = [], []
    for k, dest in enumerate(order):
        swaps.append(sends.start(blocks_ref.at[dest + flip], theirs.at[k], to(partner)))
        load = pltpu.make_async_copy(blocks_ref.at[dest], mine.at[k], local_sems.at[k])
        load.start()
        loads.append(load)

    def add_up(k):
        loads[k].wait()
        swaps[k].wait_recv()
        total[k] = (mine[k].astype(F32) + theirs[k].astype(F32)).astype(BF16)

    add_up(0)
    far_low = sends.start(total.at[0, low], from_left.at[0], to(right))
    far_high = sends.start(total.at[0, high], from_right.at[0], to(left))
    add_up(1)
    right_high = sends.start(total.at[1, high], from_left.at[2], to(right))
    add_up(2)
    left_low = sends.start(total.at[2, low], from_right.at[2], to(left))
    far_low.wait_recv()
    total[1, low] = (total[1, low].astype(F32) + from_left[0].astype(F32)).astype(BF16)
    right_low = sends.start(total.at[1, low], from_left.at[1], to(right))
    far_high.wait_recv()
    total[2, high] = (total[2, high].astype(F32) + from_right[0].astype(F32)).astype(BF16)
    left_high = sends.start(total.at[2, high], from_right.at[1], to(left))
    loads[3].wait()
    swaps[3].wait_recv()
    out_ref[...] = mine[3].astype(F32) + theirs[3].astype(F32)
    right_high.wait_recv()
    out_ref[high] += from_left[2].astype(F32)
    left_low.wait_recv()
    out_ref[low] += from_right[2].astype(F32)
    right_low.wait_recv()
    out_ref[low] += from_left[1].astype(F32)
    left_high.wait_recv()
    out_ref[high] += from_right[1].astype(F32)
    sends.finish()


def reduce_x(blocks, collective_id):
    _, rows, columns = blocks.shape
    part = (rows // 2, columns)
    return pl.pallas_call(
        reduce_x_kernel,
        out_shape=jax.ShapeDtypeStruct((rows, columns), F32),
        in_specs=[ANY],
        out_specs=VMEM,
        scratch_shapes=[
            pltpu.VMEM((4, rows, columns), BF16),
            pltpu.VMEM((4, rows, columns), BF16),
            pltpu.VMEM((3, rows, columns), BF16),
            pltpu.VMEM((3, *part), BF16),
            pltpu.VMEM((3, *part), BF16),
            pltpu.SemaphoreType.DMA((4,)),
            pltpu.SemaphoreType.DMA((10,)),
            pltpu.SemaphoreType.DMA((10,)),
        ],
        compiler_params=pltpu.CompilerParams(
            collective_id=collective_id, has_side_effects=True, vmem_limit_bytes=50 * 2**20
        ),
    )(blocks)


def around_yz():
    place = lax.axis_index("dp")
    y, z = place // 4, place % 4
    turn = lambda v, d: (v + d) % 4
    y_ring = [turn(y, d) for d in (1, 3, 2)]
    z_ring = [turn(z, d) for d in (1, 3, 2)]
    return y, z, y_ring, z_ring


def gather_yz_kernel(shard_ref, small_ref, out_ref, small_out, local_sems, send_sems, recv_sems):
    y, z, y_ring, z_ring = around_yz()
    part = lax.axis_index("expert")
    core = part % 2
    partner = {"expert": part + 1 - 2 * core}
    y_to = [{"dp": v * 4 + z} for v in y_ring[:2]]
    z_to = [{"dp": y * 4 + v} for v in z_ring[:2]]
    meet(partner, *y_to, *z_to)
    rows, columns = shard_ref.shape
    quarter = columns // 4
    sends = Sends(send_sems, recv_sems)

    def strip(p):
        return pl.ds(pl.multiple_of((2 * core + p) * quarter, 128), quarter)

    own = [
        pltpu.make_async_copy(
            shard_ref.at[:, strip(p)], out_ref.at[y, z, :, strip(p)], local_sems.at[p]
        )
        for p in range(2)
    ]
    own.append(pltpu.make_async_copy(small_ref, small_out.at[y, z], local_sems.at[2]))

    class Piece:
        def __init__(self, src, out, cols, z_first):
            self.src, self.out, self.cols, self.z_first = src, out, cols, z_first

        def ring(self, first):
            if self.z_first == first:
                return z, z_ring, z_to
            return y, y_ring, y_to

        def view(self, first, where, piece=None):
            if first:
                at = pl.ds(0, rows) if piece is None else pl.ds(piece * rows // 2, rows // 2)
                if self.z_first:
                    return self.out.at[y, where, at, self.cols]
                return self.out.at[where, z, at, self.cols]
            span = pl.ds(0, 4) if piece is None else pl.ds(2 * piece, 2)
            if self.z_first:
                return self.out.at[where, span, :, self.cols]
            return self.out.at[span, where, :, self.cols]

    strips = [
        Piece(small_ref, small_out, pl.ds(0, small_ref.shape[1]), True),
        Piece(shard_ref, out_ref, strip(0), True),
        Piece(shard_ref, out_ref, strip(1), False),
    ]
    across = []

    def send_across(s, view):
        if s.src is shard_ref:
            across.append(sends.start(view, view, partner))

    for first in (True, False):
        stage = []
        for s in strips:
            me, _, to = s.ring(first)
            src = s.src.at[:, s.cols] if first else s.view(first, me)
            stage.append([sends.start(src, s.view(first, me), to[i]) for i in range(2)])
        if first:
            for copy in own:
                copy.start()
        else:
            for s in strips:
                send_across(s, s.view(first, s.ring(first)[0]))
        onward = []
        for s, came in zip(strips, stage):
            _, (right, left, _), to = s.ring(first)
            pair = []
            for i, origin in enumerate((left, right)):
                came[i].wait_recv()
                view = s.view(first, origin, i)
                pair.append(sends.start(view, view, to[i]))
                if not first:
                    send_across(s, s.view(first, origin))
            onward.append(pair)
        for s, pair in zip(strips, onward):
            far = s.ring(first)[1][2]
            for i in range(2):
                pair[i].wait_recv()
                if not first:
                    send_across(s, s.view(first, far, i))
        if first:
            for copy in own:
                copy.wait()
    for copy in across:
        copy.wait_recv()
    sends.finish()


def gather_yz(shard, small, collective_id):
    return pl.pallas_call(
        gather_yz_kernel,
        out_shape=[
            jax.ShapeDtypeStruct((4, 4, *shard.shape), shard.dtype),
            jax.ShapeDtypeStruct((4, 4, *small.shape), small.dtype),
        ],
        in_specs=[ANY, ANY],
        out_specs=[ANY, ANY],
        scratch_shapes=[
            pltpu.SemaphoreType.DMA((3,)),
            pltpu.SemaphoreType.DMA((41,)),
            pltpu.SemaphoreType.DMA((41,)),
        ],
        compiler_params=pltpu.CompilerParams(collective_id=collective_id, has_side_effects=True),
    )(shard, small)


class Strip:
    def __init__(self, source, cols, theirs_cols, y_first, bufs):
        self.source, self.cols, self.theirs_cols, self.y_first = source, cols, theirs_cols, y_first
        self.total, self.theirs, self.big, self.far, self.mid, self.midfar, self.near = bufs


def strip_buffers(rows, columns):
    return [
        pltpu.VMEM((4, 4, rows, columns), BF16),
        pltpu.VMEM((4, 4, rows, columns), BF16),
        pltpu.VMEM((2, 2, 2, rows, columns), BF16),
        pltpu.VMEM((2, 2, rows, columns), BF16),
        pltpu.VMEM((2, 2, rows // 2, columns), BF16),
        pltpu.VMEM((2, rows // 2, columns), BF16),
        pltpu.VMEM((4, rows, columns), BF16),
    ]


def reduce_yz_kernel(n_wide, *refs):
    grads, small_ref = refs[:n_wide], refs[n_wide]
    outs, small_out = refs[n_wide + 1 : 2 * n_wide + 1], refs[2 * n_wide + 1]
    bufs = refs[2 * n_wide + 2 : -3]
    local_sems, send_sems, recv_sems = refs[-3:]
    y, z, y_ring, z_ring = around_yz()
    part, core, x_right, x_left, x_far, partner = around_x()
    partner = {"expert": partner}
    x_to = [{"expert": i} for i in (x_right, x_left, x_far)]
    y_to = [{"dp": v * 4 + z} for v in y_ring[:2]]
    z_to = [{"dp": y * 4 + v} for v in z_ring[:2]]
    meet(partner, *y_to, *z_to, *x_to)
    sends = Sends(send_sems, recv_sems)
    strips, owners = [], []
    for g, out in zip(grads, outs):
        quarter = g.shape[-1] // 4
        for p in range(2):
            cols = [
                pl.ds(pl.multiple_of((2 * c + p) * quarter, 128), quarter)
                for c in (core, 1 - core)
            ]
            at = 7 * len(strips)
            strips.append(Strip(g, cols[0], cols[1], p == 0, bufs[at : at + 7]))
            owners.append(out)
    at = 7 * len(strips)
    every = pl.ds(0, small_ref.shape[-1])
    strips.append(Strip(small_ref, every, None, True, bufs[at : at + 7]))
    owners.append(small_out)

    def ring(s, first):
        return (y, y_ring, y_to) if s.y_first == first else (z, z_ring, z_to)

    def block(ref, s, w):
        return ref.at[w] if s.y_first else ref.at[:, w]

    def columns(s, w, cols):
        return s.source.at[w, :, :, cols] if s.y_first else s.source.at[:, w, :, cols]

    def add(ref, *others):
        got = ref[...].astype(F32)
        for other in others:
            got += other[...].astype(F32)
        ref[...] = got.astype(BF16)

    swaps, loads = {}, {}
    for k in range(4):
        for i, s in enumerate(strips):
            me, (right, left, far), _ = ring(s, True)
            w = (far, right, left, me)[k]
            if s.theirs_cols is not None:
                swaps[k, i] = sends.start(
                    columns(s, w, s.theirs_cols), block(s.theirs, s, w), partner
                )
            load = pltpu.make_async_copy(
                columns(s, w, s.cols), block(s.total, s, w), local_sems.at[k * len(strips) + i]
            )
            load.start()
            loads[k, i] = load

    def joined(k, i, s, w):
        loads[k, i].wait()
        if s.theirs_cols is not None:
            swaps[k, i].wait_recv()
            add(block(s.total, s, w), block(s.theirs, s, w))

    def ring_sum(first, view, whole, farther, ready):
        going = []
        for i, s in enumerate(strips):
            _, (right, left, far), to = ring(s, first)
            ready(0, i, s, far)
            going.append(
                [sends.start(view(s, far, h), farther(s).at[h], to[h]) for h in range(2)]
            )
        for i, s in enumerate(strips):
            _, (right, left, far), to = ring(s, first)
            ready(1, i, s, right)
            ready(2, i, s, left)
            going[i].append(sends.start(view(s, right, 1), whole(s).at[0, 1], to[0]))
            going[i].append(sends.start(view(s, left, 0), whole(s).at[1, 0], to[1]))
        for i, s in enumerate(strips):
            _, (right, left, far), to = ring(s, first)
            for h, w in enumerate((right, left)):
                going[i][h].wait_recv()
                add(view(s, w, h), farther(s).at[h])
                going[i].append(sends.start(view(s, w, h), whole(s).at[h, h], to[h]))
        for i, s in enumerate(strips):
            me, _, _ = ring(s, first)
            ready(3, i, s, me)
            for copy in going[i][2:]:
                copy.wait_recv()
            for h in range(2):
                add(view(s, me, h), whole(s).at[0, h], whole(s).at[1, h])

    def big(s, w, h):
        span = pl.ds(2 * h, 2)
        return s.total.at[w, span] if s.y_first else s.total.at[span, w]

    def small(s, w, h):
        half = s.total.shape[2] // 2
        at = pl.ds(h * half, half)
        return s.total.at[y, w, at] if s.y_first else s.total.at[w, z, at]

    ring_sum(True, big, lambda s: s.big, lambda s: s.far, joined)
    ring_sum(False, small, lambda s: s.mid, lambda s: s.midfar, lambda *_: None)

    shares, back = [], []
    for s in strips:
        shares.append(
            [sends.start(s.total.at[y, z], s.near.at[i], x_to[i]) for i in range(3)]
        )
    for s, share in zip(strips, shares):
        for copy in share:
            copy.wait_recv()
        got = s.total[y, z].astype(F32)
        for i in range(3):
            got += s.near[i].astype(F32)
        s.theirs[y, z] = got.astype(BF16)
        back.append(sends.start(s.theirs.at[y, z], s.near.at[3], partner))
    for s, out, copy in zip(strips, owners, back):
        copy.wait_recv()
        if s.theirs_cols is None:
            out[...] = s.theirs[y, z].astype(F32) + s.near[3].astype(F32)
        else:
            out[:, s.cols] = s.theirs[y, z].astype(F32)
            out[:, s.theirs_cols] = s.near[3].astype(F32)
    sends.finish()


def reduce_yz(grads, small, collective_id):
    every = [*grads, small]
    buffers = []
    for g in grads:
        for _ in range(2):
            buffers += strip_buffers(g.shape[2], g.shape[3] // 4)
    buffers += strip_buffers(*small.shape[2:])
    n_strips = 2 * len(grads) + 1
    return pl.pallas_call(
        functools.partial(reduce_yz_kernel, len(grads)),
        out_shape=[jax.ShapeDtypeStruct(g.shape[2:], F32) for g in every],
        in_specs=[ANY] * len(every),
        out_specs=[VMEM] * len(every),
        scratch_shapes=[
            *buffers,
            pltpu.SemaphoreType.DMA((4 * n_strips,)),
            pltpu.SemaphoreType.DMA((20 * n_strips,)),
            pltpu.SemaphoreType.DMA((20 * n_strips,)),
        ],
        compiler_params=pltpu.CompilerParams(
            collective_id=collective_id, has_side_effects=True, vmem_limit_bytes=56 * 2**20
        ),
    )(*every)


def on_device(
    tokens,
    d_out,
    gain_in,
    w_query,
    key_projection_weight,
    value_projection_weight,
    w_out,
    gain_mid,
    w_router,
    w_gate,
    w_up,
    w_down,
    routes,
    segments,
):
    rows, width = tokens.shape
    length = segments.shape[1]
    scaling = HEAD_SIZE ** (-0.5)
    part = lax.axis_index("expert")
    parts = lax.axis_size("expert")
    core = part % 2
    capacity = rows * 9 // 16
    seg_row = segments[0]
    offset = part * rows
    angles = angles_for(lax.dynamic_slice_in_dim(doc_positions(seg_row), offset, rows, 0))
    cosine, sine = jnp.cos(angles), jnp.sin(angles)
    my_seg = lax.dynamic_slice_in_dim(seg_row, offset, rows, 0)
    my_rows = offset + jnp.arange(rows, dtype=jnp.int32)
    key_places = jnp.arange(length, dtype=jnp.int32)
    allowed = (my_seg[:, None] == seg_row[None, :]) & (my_rows[:, None] >= key_places[None, :])

    small = jnp.concatenate([gain_in[:, None], gain_mid[:, None], w_router], axis=1)
    small = jnp.pad(small, ((0, 0), (0, 128 - small.shape[1])))
    shard = jnp.concatenate([w_query, key_projection_weight, value_projection_weight], axis=1)
    wqkv, small = gather_yz(shard, small, 1)
    wqkv = wqkv.reshape(width, -1)
    small = small.reshape(width, -1)
    gain_in_all = small[:, 0].astype(F32)
    gain_mid_all = small[:, 1].astype(F32)
    wr = small[:, 2 : 2 + EXPERTS]
    wo = gather_dense(w_out, core)
    upstream_all = ag_x(d_out)
    routes_all = ag_x(routes.astype(BF16)).astype(jnp.int32)

    inputs = tokens.astype(F32)
    normed = rms_scale(inputs, gain_in_all).astype(BF16)
    kv_at = QUERY_HEADS * HEAD_SIZE
    kv_width = KEY_VALUE_HEADS * HEAD_SIZE
    kv_lin = mm(normed, wqkv[:, kv_at:])
    key_block = rotate(kv_lin[:, :kv_width], cosine, sine, 1.0).astype(BF16)
    kv_all = gather_x(
        jnp.concatenate([key_block, kv_lin[:, kv_width:].astype(BF16)], axis=1), 2
    ).reshape(length, -1)
    keys = kv_all[:, :kv_width].reshape(length, KEY_VALUE_HEADS, HEAD_SIZE)
    values = kv_all[:, kv_width:].reshape(length, KEY_VALUE_HEADS, HEAD_SIZE)
    query = rotate(mm(normed, wqkv[:, :kv_at]), cosine, sine, 1.0).astype(BF16)
    query = query.reshape(rows, KEY_VALUE_HEADS, GROUP, HEAD_SIZE)

    def scores_for(h):
        raw = jnp.einsum("tgd,sd->gts", query[:, h], keys[:, h], preferred_element_type=F32)
        return jnp.where(allowed[None], raw * scaling, MASK_FILL)

    contexts, log_sums = [], []
    for h in range(KEY_VALUE_HEADS):
        scores = scores_for(h)
        row_max = jnp.max(scores, axis=-1, keepdims=True)
        shifted = jnp.exp(scores - row_max)
        row_sum = jnp.sum(shifted, axis=-1, keepdims=True)
        probs = (shifted / row_sum).astype(BF16)
        contexts.append(
            jnp.einsum("gts,sd->tgd", probs, values[:, h], preferred_element_type=F32)
        )
        log_sums.append(row_max + jnp.log(row_sum))
    context = jnp.stack(contexts, axis=1).reshape(rows, kv_at).astype(BF16)
    middle = inputs + mm(context, wo)
    normed_mid = rms_scale(middle, gain_mid_all).astype(BF16)

    expert_ids = jnp.arange(EXPERTS, dtype=jnp.int32)

    def gates_for(logits, chosen_routes):
        chosen = jnp.sum(
            logits[:, None, :] * (chosen_routes[:, :, None] == expert_ids).astype(F32), axis=-1
        )
        return jax.nn.softmax(chosen, axis=-1)

    gates = gates_for(mm(normed_mid, wr), routes)
    normed_all = gather_x(normed_mid, 3).reshape(length, width)
    gates_all = gates_for(mm(normed_all, wr), routes_all)
    mine = routes_all == part
    gate_mine = jnp.sum(jnp.where(mine, gates_all, 0.0), axis=-1).reshape(parts, rows)
    member = jnp.any(mine, axis=-1).reshape(parts, rows)
    ranks = jnp.cumsum(member.astype(jnp.int32), axis=1) - 1
    slots = jnp.arange(capacity, dtype=jnp.int32)
    pick = (ranks[:, None, :] == slots[None, :, None]) & member[:, None, :]
    pick_b = pick.astype(BF16)

    def take(all_rows):
        got = jnp.einsum(
            "prt,ptd->prd", pick_b, all_rows.reshape(parts, rows, -1), preferred_element_type=F32
        )
        return got.astype(BF16).reshape(parts * capacity, -1)

    def put_back(slot_rows):
        got = jnp.einsum(
            "prt,prd->ptd",
            pick_b,
            slot_rows.reshape(parts, capacity, -1),
            preferred_element_type=F32,
        )
        return got.astype(BF16).reshape(parts * rows, -1)

    gate_slot = jnp.sum(jnp.where(pick, gate_mine[:, None, :], 0.0), axis=-1).reshape(-1, 1)
    arrived = take(normed_all)
    up_slot = take(upstream_all).astype(F32)
    pair_grad = (gate_slot * up_slot).astype(BF16)
    wg, wu, wd = w_gate[0], w_up[0], w_down[0]
    gate_pre = mm(arrived, wg)
    up_pre = mm(arrived, wu)

    def glu_act(a, b):
        return jax.nn.gelu(a, approximate=True) * b

    hidden_f, pull_act = jax.vjp(glu_act, gate_pre, up_pre)
    hidden = hidden_f.astype(BF16)
    expert_out = mm(hidden, wd).astype(BF16).astype(F32)
    grad_gate_slot = jnp.sum(up_slot * expert_out, axis=-1)
    back_out = put_back((gate_slot * expert_out).astype(BF16))
    grad_hidden = mm_nt(pair_grad, wd)
    grad_gate_pre, grad_up_pre = pull_act(grad_hidden)
    grad_gate_b = grad_gate_pre.astype(BF16)
    grad_up_b = grad_up_pre.astype(BF16)
    grad_rows = (mm_nt(grad_gate_b, wg) + mm_nt(grad_up_b, wu)).astype(BF16)
    hot_mine = (jnp.arange(128) == part).astype(F32) + (jnp.arange(128) == part + EXPERTS) * 2.0
    gate_high = grad_gate_slot.astype(BF16).astype(F32)
    gate_parts = jnp.where(
        hot_mine == 1.0,
        gate_high[:, None],
        jnp.where(hot_mine == 2.0, (grad_gate_slot - gate_high)[:, None], 0.0),
    )
    returned = put_back(jnp.concatenate([grad_rows, gate_parts.astype(BF16)], axis=1))
    returned = reduce_x(returned.reshape(parts, rows, -1), 4)
    grad_mid_sum = returned[:, :width]
    grad_gates = returned[:, width : width + EXPERTS] + returned[
        :, width + EXPERTS : width + 2 * EXPERTS
    ]
    combined = rs_x(back_out).astype(F32)
    mixed = (middle + combined).astype(BF16)
    grad_wdown = mm_tn(hidden, pair_grad).astype(BF16)
    grad_wgate = mm_tn(arrived, grad_gate_b).astype(BF16)
    grad_wup = mm_tn(arrived, grad_up_b).astype(BF16)

    hot = (routes[:, :, None] == expert_ids).astype(F32)
    gate_by_expert = jnp.sum(gates[:, :, None] * hot, axis=1)
    gg = gate_by_expert * grad_gates
    grad_logits = (gg - gate_by_expert * jnp.sum(gg, axis=1, keepdims=True)).astype(BF16)
    upstream = d_out.astype(F32)
    grad_normed_mid = grad_mid_sum + mm_nt(grad_logits, wr)
    grad_wr = mm_tn(normed_mid, grad_logits)
    grad_middle_norm, grad_gmid = rms_back(middle, gain_mid_all, grad_normed_mid)
    grad_middle = upstream + grad_middle_norm
    grad_attn = grad_middle.astype(BF16)
    grad_wo = mm_tn(context, grad_attn)
    grad_ctx = mm_nt(grad_attn, wo).astype(BF16)
    grad_ctx = grad_ctx.reshape(rows, KEY_VALUE_HEADS, GROUP, HEAD_SIZE)

    query_grads, key_parts, value_parts = [], [], []
    for h in range(KEY_VALUE_HEADS):
        probs_full = jnp.exp(scores_for(h) - log_sums[h])
        ctx_h = grad_ctx[:, h]
        grad_probs = jnp.einsum("tgd,sd->gts", ctx_h, values[:, h], preferred_element_type=F32)
        value_parts.append(
            jnp.einsum("gts,tgd->sd", probs_full.astype(BF16), ctx_h, preferred_element_type=F32)
        )
        inner = jnp.sum(probs_full * grad_probs, axis=-1, keepdims=True)
        grad_scores = (probs_full * (grad_probs - inner)).astype(BF16)
        query_grads.append(
            jnp.einsum("gts,sd->tgd", grad_scores, keys[:, h], preferred_element_type=F32)
            * scaling
        )
        key_parts.append(
            jnp.einsum("gts,tgd->sd", grad_scores, query[:, h], preferred_element_type=F32)
            * scaling
        )
    grad_query = jnp.stack(query_grads, axis=1).reshape(rows, kv_at)
    kv_terms = jnp.concatenate([p.astype(BF16) for p in key_parts + value_parts], axis=1)
    kv_grad = reduce_x(kv_terms.reshape(parts, rows, -1), 5)
    grad_qlin = rotate(grad_query, cosine, sine, -1.0).astype(BF16)
    grad_klin = rotate(kv_grad[:, :kv_width], cosine, sine, -1.0).astype(BF16)
    grad_lin = jnp.concatenate([grad_qlin, grad_klin, kv_grad[:, kv_width:].astype(BF16)], axis=1)
    grad_wqkv = mm_tn(normed, grad_lin)
    grad_normed = mm_nt(grad_lin, wqkv)
    grad_inputs_norm, grad_gin = rms_back(inputs, gain_in_all, grad_normed)
    grad_tokens = grad_middle + grad_inputs_norm

    small_grads = jnp.concatenate([grad_gin[:, None], grad_gmid[:, None], grad_wr], axis=1)
    small_grads = jnp.pad(small_grads.astype(BF16), ((0, 0), (0, 128 - small_grads.shape[1])))
    qkv_sum, wo_sum, small_sum = reduce_yz(
        [g.astype(BF16).reshape(4, 4, width // 16, -1) for g in (grad_wqkv, grad_wo)],
        small_grads.reshape(4, 4, width // 16, -1),
        6,
    )
    expert_sums = [
        lax.psum(g[None], "dp").astype(F32) for g in (grad_wgate, grad_wup, grad_wdown)
    ]
    return (
        mixed,
        grad_tokens,
        small_sum[:, 0],
        qkv_sum[:, :kv_at],
        qkv_sum[:, kv_at : kv_at + kv_width],
        qkv_sum[:, kv_at + kv_width :],
        wo_sum,
        small_sum[:, 1],
        small_sum[:, 2 : 2 + EXPERTS],
        expert_sums[0],
        expert_sums[1],
        expert_sums[2],
    )


def solution(mesh):
    whole = P(("dp", "expert"), None)
    over_dp, by_dp, over_expert = P("dp"), P("dp", None), P("expert", None, None)
    return jax.shard_map(
        on_device,
        mesh=mesh,
        in_specs=(whole, whole, over_dp, by_dp, by_dp, by_dp, by_dp, over_dp, by_dp)
        + (over_expert,) * 3
        + (whole, by_dp),
        out_specs=(whole, whole, over_dp, by_dp, by_dp, by_dp, by_dp, over_dp, by_dp)
        + (over_expert,) * 3,
        check_vma=False,
    )
```

```python
import functools

import jax
import jax.numpy as jnp
from jax import lax
from jax.experimental import pallas as pl
from jax.experimental.pallas import tpu as pltpu
from jax.sharding import PartitionSpec as P

QUERY_HEADS = 12
KEY_VALUE_HEADS = 2
HEAD_SIZE = 128
TOPK = 4
EXPERTS = 8
DOCS = 4
GROUP = QUERY_HEADS // KEY_VALUE_HEADS

EPSILON = 1e-06
ROPE_BASE = 1000000.0
MASK_FILL = -1e30
F32 = jnp.float32
BF16 = jnp.bfloat16

PARTNER = [(i, i ^ 1) for i in range(8)]
SAME_CORE = [[0, 2, 4, 6], [1, 3, 5, 7]]


def dot(a, b, dims):
    return lax.dot_general(a, b, (dims, ((), ())), preferred_element_type=F32)


def mm(a, b):
    return dot(a, b, ((1,), (0,)))


def mm_nt(a, b):
    return dot(a, b, ((1,), (1,)))


def mm_tn(a, b):
    return dot(a, b, ((0,), (0,)))


def rms_back(value_rows, gain, grad):
    inverse = lax.rsqrt(jnp.mean(value_rows * value_rows, axis=-1, keepdims=True) + EPSILON)
    scaled = value_rows * inverse
    weighted = grad * gain
    inner = jnp.mean(weighted * scaled, axis=-1, keepdims=True)
    return inverse * (weighted - scaled * inner), jnp.sum(grad * scaled, axis=0)


def angles_for(positions):
    half_width = HEAD_SIZE // 2
    freqs = ROPE_BASE ** (-2.0 * jnp.arange(half_width, dtype=F32) / HEAD_SIZE)
    return positions.astype(F32)[:, None] * freqs[None, :]


def rotate(flat, cosine, sine):
    heads = flat.reshape(flat.shape[0], -1, HEAD_SIZE)
    turned = jnp.roll(heads, HEAD_SIZE // 2, axis=-1)
    return (heads * cosine[:, None, :] + turned * sine[:, None, :]).reshape(flat.shape)


def pp_core(x):
    return lax.ppermute(x, "expert", PARTNER)


def gather_dense(shard, core):
    half = shard.shape[1] // 2
    mine = lax.dynamic_slice_in_dim(shard, core * half, half, 1)
    got = lax.all_gather(mine, "dp", axis=0, tiled=True)
    other = pp_core(got)
    first = jnp.where(core == 0, got, other)
    second = jnp.where(core == 0, other, got)
    return jnp.concatenate([first, second], axis=1)


MESH = pl.DeviceIdType.MESH
ANY = pl.BlockSpec(memory_space=pl.ANY)
VMEM = pl.BlockSpec(memory_space=pltpu.VMEM)


class Sends:
    def __init__(self, send_sems, recv_sems):
        self.send_sems, self.recv_sems, self.made = send_sems, recv_sems, []

    def start(self, src, dst, to):
        at = len(self.made)
        copy = pltpu.make_async_remote_copy(
            src_ref=src,
            dst_ref=dst,
            send_sem=self.send_sems.at[at],
            recv_sem=self.recv_sems.at[at],
            device_id=to,
            device_id_type=MESH,
        )
        copy.start()
        self.made.append(copy)
        return copy

    def finish(self):
        for copy in self.made:
            copy.wait_send()


def meet(*others):
    barrier = pltpu.get_barrier_semaphore()
    for other in others:
        pl.semaphore_signal(barrier, inc=1, device_id=other, device_id_type=MESH)
    pl.semaphore_wait(barrier, len(others))


def around_x():
    part = lax.axis_index("expert")
    x, core = part // 2, part % 2
    at = lambda dx: ((x + dx) % 4) * 2 + core
    return part, core, at(1), at(3), at(2), 2 * x + (1 - core)


def x_sum(sends, blocks_ref, out_ref, mine, theirs, total, from_left, from_right, local_sems):
    part, core, right, left, far, partner = around_x()
    to = lambda i: {"expert": i}
    rows = out_ref.shape[0]
    half = rows // 2
    low, high = pl.ds(0, half), pl.ds(half, half)
    order = (far, right, left, part)
    flip = 1 - 2 * core
    swaps, loads = [], []
    for k, dest in enumerate(order):
        swaps.append(sends.start(blocks_ref.at[dest + flip], theirs.at[k], to(partner)))
        load = pltpu.make_async_copy(blocks_ref.at[dest], mine.at[k], local_sems.at[k])
        load.start()
        loads.append(load)

    def add_up(k):
        loads[k].wait()
        swaps[k].wait_recv()
        total[k] = (mine[k].astype(F32) + theirs[k].astype(F32)).astype(BF16)

    yield
    add_up(0)
    far_low = sends.start(total.at[0, low], from_left.at[0], to(right))
    far_high = sends.start(total.at[0, high], from_right.at[0], to(left))
    add_up(1)
    right_high = sends.start(total.at[1, high], from_left.at[2], to(right))
    add_up(2)
    left_low = sends.start(total.at[2, low], from_right.at[2], to(left))
    yield
    far_low.wait_recv()
    total[1, low] = (total[1, low].astype(F32) + from_left[0].astype(F32)).astype(BF16)
    right_low = sends.start(total.at[1, low], from_left.at[1], to(right))
    far_high.wait_recv()
    total[2, high] = (total[2, high].astype(F32) + from_right[0].astype(F32)).astype(BF16)
    left_high = sends.start(total.at[2, high], from_right.at[1], to(left))
    yield
    loads[3].wait()
    swaps[3].wait_recv()
    out_ref[...] = mine[3].astype(F32) + theirs[3].astype(F32)
    right_high.wait_recv()
    out_ref[high] += from_left[2].astype(F32)
    left_low.wait_recv()
    out_ref[low] += from_right[2].astype(F32)
    right_low.wait_recv()
    out_ref[low] += from_left[1].astype(F32)
    left_high.wait_recv()
    out_ref[high] += from_right[1].astype(F32)
    yield


def x_buffers(rows, columns):
    return [
        pltpu.VMEM((4, rows, columns), BF16),
        pltpu.VMEM((4, rows, columns), BF16),
        pltpu.VMEM((3, rows, columns), BF16),
        pltpu.VMEM((3, rows // 2, columns), BF16),
        pltpu.VMEM((3, rows // 2, columns), BF16),
        pltpu.SemaphoreType.DMA((4,)),
    ]


def reduce_x_kernel(blocks_ref, out_ref, *refs):
    part, core, right, left, far, partner = around_x()
    meet(*({"expert": i} for i in (partner, right, left)))
    sends = Sends(*refs[-2:])
    for _ in x_sum(sends, blocks_ref, out_ref, *refs[:-2]):
        pass
    sends.finish()


def reduce_x(blocks, collective_id):
    _, rows, columns = blocks.shape
    return pl.pallas_call(
        reduce_x_kernel,
        out_shape=jax.ShapeDtypeStruct((rows, columns), F32),
        in_specs=[ANY],
        out_specs=VMEM,
        scratch_shapes=[
            *x_buffers(rows, columns),
            pltpu.SemaphoreType.DMA((10,)),
            pltpu.SemaphoreType.DMA((10,)),
        ],
        compiler_params=pltpu.CompilerParams(
            collective_id=collective_id, has_side_effects=True, vmem_limit_bytes=50 * 2**20
        ),
    )(blocks)


def around_yz():
    place = lax.axis_index("dp")
    y, z = place // 4, place % 4
    turn = lambda v, d: (v + d) % 4
    y_ring = [turn(y, d) for d in (1, 3, 2)]
    z_ring = [turn(z, d) for d in (1, 3, 2)]
    return y, z, y_ring, z_ring


class Strip:
    def __init__(self, source, cols, theirs_cols, y_first, bufs):
        self.source, self.cols, self.theirs_cols, self.y_first = source, cols, theirs_cols, y_first
        self.total, self.theirs, self.big, self.far, self.mid, self.midfar, self.near = bufs


def strip_buffers(rows, columns):
    return [
        pltpu.VMEM((4, 4, rows, columns), BF16),
        pltpu.VMEM((4, 4, rows, columns), BF16),
        pltpu.VMEM((2, 2, 2, rows, columns), BF16),
        pltpu.VMEM((2, 2, rows, columns), BF16),
        pltpu.VMEM((2, 2, rows // 2, columns), BF16),
        pltpu.VMEM((2, rows // 2, columns), BF16),
        pltpu.VMEM((4, rows, columns), BF16),
    ]


def reduce_all_kernel(
    qkv_ref, wo_ref, small_ref, middle_ref, blocks_ref,
    wq_out, wk_out, wv_out, wo_out, small_out, mixed_out, *refs,
):
    grads, outs = (qkv_ref, wo_ref), (None, wo_out)
    bufs, x_bufs = refs[:35], refs[35:41]
    combined, local_sems, send_sems, recv_sems = refs[41:]
    y, z, y_ring, z_ring = around_yz()
    part, core, x_right, x_left, x_far, partner = around_x()
    partner = {"expert": partner}
    x_to = [{"expert": i} for i in (x_right, x_left, x_far)]
    y_to = [{"dp": v * 4 + z} for v in y_ring[:2]]
    z_to = [{"dp": y * 4 + v} for v in z_ring[:2]]
    meet(partner, *y_to, *z_to, *x_to)
    sends = Sends(send_sems, recv_sems)
    strips, owners = [], []
    for g, out in zip(grads, outs):
        quarter = g.shape[-1] // 4
        for p in range(2):
            cols = [
                pl.ds(pl.multiple_of((2 * c + p) * quarter, 128), quarter)
                for c in (core, 1 - core)
            ]
            at = 7 * len(strips)
            strips.append(Strip(g, cols[0], cols[1], p == 0, bufs[at : at + 7]))
            owners.append(out)
    at = 7 * len(strips)
    every = pl.ds(0, small_ref.shape[-1])
    strips.append(Strip(small_ref, every, None, True, bufs[at : at + 7]))
    owners.append(small_out)

    def ring(s, first):
        return (y, y_ring, y_to) if s.y_first == first else (z, z_ring, z_to)

    def block(ref, s, w):
        return ref.at[w] if s.y_first else ref.at[:, w]

    def columns(s, w, cols):
        return s.source.at[w, :, :, cols] if s.y_first else s.source.at[:, w, :, cols]

    def add(ref, *others):
        got = ref[...].astype(F32)
        for other in others:
            got += other[...].astype(F32)
        ref[...] = got.astype(BF16)

    x_steps = x_sum(sends, blocks_ref, combined, *x_bufs)

    swaps, loads = {}, {}
    for k in range(4):
        if k == 1:
            next(x_steps)
        for i, s in enumerate(strips):
            me, (right, left, far), _ = ring(s, True)
            w = (far, right, left, me)[k]
            if s.theirs_cols is not None:
                swaps[k, i] = sends.start(
                    columns(s, w, s.theirs_cols), block(s.theirs, s, w), partner
                )
            load = pltpu.make_async_copy(
                columns(s, w, s.cols), block(s.total, s, w), local_sems.at[k * len(strips) + i]
            )
            load.start()
            loads[k, i] = load

    def joined(k, i, s, w):
        loads[k, i].wait()
        if s.theirs_cols is not None:
            swaps[k, i].wait_recv()
            add(block(s.total, s, w), block(s.theirs, s, w))

    def ring_sum(first, view, whole, farther, ready):
        going = []
        for i, s in enumerate(strips):
            _, (right, left, far), to = ring(s, first)
            ready(0, i, s, far)
            going.append(
                [sends.start(view(s, far, h), farther(s).at[h], to[h]) for h in range(2)]
            )
        for i, s in enumerate(strips):
            _, (right, left, far), to = ring(s, first)
            ready(1, i, s, right)
            ready(2, i, s, left)
            going[i].append(sends.start(view(s, right, 1), whole(s).at[0, 1], to[0]))
            going[i].append(sends.start(view(s, left, 0), whole(s).at[1, 0], to[1]))
        next(x_steps)
        for i, s in enumerate(strips):
            _, (right, left, far), to = ring(s, first)
            for h, w in enumerate((right, left)):
                going[i][h].wait_recv()
                add(view(s, w, h), farther(s).at[h])
                going[i].append(sends.start(view(s, w, h), whole(s).at[h, h], to[h]))
        for i, s in enumerate(strips):
            me, _, _ = ring(s, first)
            ready(3, i, s, me)
            for copy in going[i][2:]:
                copy.wait_recv()
            for h in range(2):
                add(view(s, me, h), whole(s).at[0, h], whole(s).at[1, h])

    def big(s, w, h):
        span = pl.ds(2 * h, 2)
        return s.total.at[w, span] if s.y_first else s.total.at[span, w]

    def small(s, w, h):
        half = s.total.shape[2] // 2
        at = pl.ds(h * half, half)
        return s.total.at[y, w, at] if s.y_first else s.total.at[w, z, at]

    ring_sum(True, big, lambda s: s.big, lambda s: s.far, joined)
    ring_sum(False, small, lambda s: s.mid, lambda s: s.midfar, lambda *_: None)

    shares, back = [], []
    for s in strips:
        shares.append(
            [sends.start(s.total.at[y, z], s.near.at[i], x_to[i]) for i in range(3)]
        )
    next(x_steps)
    mixed_out[...] = (middle_ref[...] + combined[...]).astype(BF16)
    for s, share in zip(strips, shares):
        for copy in share:
            copy.wait_recv()
        got = s.total[y, z].astype(F32)
        for i in range(3):
            got += s.near[i].astype(F32)
        s.theirs[y, z] = got.astype(BF16)
        back.append(sends.start(s.theirs.at[y, z], s.near.at[3], partner))
    wide, narrow = wq_out.shape[1] // 4, wk_out.shape[1] // 2
    for i, (s, out, copy) in enumerate(zip(strips, owners, back)):
        copy.wait_recv()
        if s.theirs_cols is None:
            out[...] = s.theirs[y, z].astype(F32) + s.near[3].astype(F32)
            continue
        for c, got in ((core, s.theirs[y, z]), (1 - core, s.near[3])):
            got = got.astype(F32)
            if out is not None:
                out[:, s.cols if c is core else s.theirs_cols] = got
                continue
            at = pl.multiple_of((2 * c + i) * wide, 128)
            wq_out[:, pl.ds(at, wide)] = got[:, :wide]
            other = wk_out if i == 0 else wv_out
            other[:, pl.ds(pl.multiple_of(c * narrow, 128), narrow)] = got[:, wide:]
    sends.finish()


def reduce_all(grad_qkv, grad_wo, small, middle, blocks, narrow, collective_id):
    height = small.shape[2]
    width = grad_wo.shape[3]
    rows = middle.shape[0]
    buffers = []
    for g in (grad_qkv, grad_wo):
        for _ in range(2):
            buffers += strip_buffers(height, g.shape[3] // 4)
    buffers += strip_buffers(*small.shape[2:])
    sds = jax.ShapeDtypeStruct
    return pl.pallas_call(
        reduce_all_kernel,
        out_shape=[
            sds((height, width), F32),
            sds((height, narrow), F32),
            sds((height, narrow), F32),
            sds((height, width), F32),
            sds(small.shape[2:], F32),
            sds(middle.shape, BF16),
        ],
        in_specs=[ANY, ANY, ANY, VMEM, ANY],
        out_specs=[VMEM] * 6,
        scratch_shapes=[
            *buffers,
            *x_buffers(rows, width),
            pltpu.VMEM((rows, width), F32),
            pltpu.SemaphoreType.DMA((20,)),
            pltpu.SemaphoreType.DMA((110,)),
            pltpu.SemaphoreType.DMA((110,)),
        ],
        compiler_params=pltpu.CompilerParams(
            collective_id=collective_id, has_side_effects=True, vmem_limit_bytes=60 * 2**20
        ),
    )(grad_qkv, grad_wo, small, middle, blocks)


def gather_first_kernel(
    wq_ref, wk_ref, wv_ref, small_ref, rows_ref, note_ref,
    out_ref, small_out, rows_out, notes_out, local_sems, send_sems, recv_sems,
):
    y, z, y_ring, z_ring = around_yz()
    part, core, x_right, x_left, x_far, partner = around_x()
    others = [{"expert": lax.rem(part + d, 8)} for d in range(1, 8)]
    partner, x_right_to, x_left_to = ({"expert": i} for i in (partner, x_right, x_left))
    y_to = [{"dp": v * 4 + z} for v in y_ring[:2]]
    z_to = [{"dp": y * 4 + v} for v in z_ring[:2]]
    meet(*others, *y_to, *z_to)
    rows = wq_ref.shape[0]
    wide, narrow = wq_ref.shape[1] // 4, wk_ref.shape[1] // 2
    sends = Sends(send_sems, recv_sems)
    local = []

    def keep(src, dst):
        copy = pltpu.make_async_copy(src, dst, local_sems.at[len(local)])
        copy.start()
        local.append(copy)

    def columns(p, at, size):
        begin = (2 * core + p) * (wide + narrow) + at
        return pl.ds(pl.multiple_of(begin, 128), size)

    for p, other in enumerate((wk_ref, wv_ref)):
        begin = pl.multiple_of((2 * core + p) * wide, 128)
        keep(wq_ref.at[:, pl.ds(begin, wide)], out_ref.at[y, z, :, columns(p, 0, wide)])
        begin = pl.multiple_of(core * narrow, 128)
        keep(other.at[:, pl.ds(begin, narrow)], out_ref.at[y, z, :, columns(p, wide, narrow)])
    keep(small_ref, small_out.at[y, z])
    keep(rows_ref, rows_out.at[part])
    keep(note_ref, notes_out.at[part])

    half = rows_ref.shape[0] // 2
    x_ways = (x_right_to, x_left_to)
    x_came = [sends.start(rows_ref, rows_out.at[part], to) for to in x_ways]
    across = [sends.start(rows_ref, rows_out.at[part], partner)]
    across += [sends.start(note_ref, notes_out.at[part], to) for to in others]

    class Piece:
        def __init__(self, out, cols, z_first):
            self.out, self.cols, self.z_first = out, cols, z_first

        def ring(self, first):
            if self.z_first == first:
                return z, z_ring, z_to
            return y, y_ring, y_to

        def view(self, first, where, piece=None):
            if first:
                at = pl.ds(0, rows) if piece is None else pl.ds(piece * rows // 2, rows // 2)
                if self.z_first:
                    return self.out.at[y, where, at, self.cols]
                return self.out.at[where, z, at, self.cols]
            span = pl.ds(0, 4) if piece is None else pl.ds(2 * piece, 2)
            if self.z_first:
                return self.out.at[where, span, :, self.cols]
            return self.out.at[span, where, :, self.cols]

    pieces = [
        Piece(out_ref, columns(0, 0, wide + narrow), True),
        Piece(out_ref, columns(1, 0, wide + narrow), False),
        Piece(small_out, pl.ds(0, small_ref.shape[1]), True),
    ]

    def send_across(s, view):
        if s.out is out_ref:
            across.append(sends.start(view, view, partner))

    for first in (True, False):
        stage = []
        if first:
            for copy in local:
                copy.wait()
        for s in pieces:
            me, _, to = s.ring(first)
            view = s.view(first, me)
            stage.append([sends.start(view, view, to[i]) for i in range(2)])
        if not first:
            for s in pieces:
                send_across(s, s.view(first, s.ring(first)[0]))
            far_rows = []
            for i, origin in enumerate((x_left, x_right)):
                x_came[i].wait_recv()
                view = rows_out.at[origin, pl.ds(i * half, half)]
                far_rows.append(sends.start(view, view, x_ways[i]))
                view = rows_out.at[origin]
                across.append(sends.start(view, view, partner))
        onward = []
        for s, came in zip(pieces, stage):
            _, (right, left, _), to = s.ring(first)
            pair = []
            for i, origin in enumerate((left, right)):
                came[i].wait_recv()
                view = s.view(first, origin, i)
                pair.append(sends.start(view, view, to[i]))
                if not first:
                    send_across(s, s.view(first, origin))
            onward.append(pair)
        for s, pair in zip(pieces, onward):
            far = s.ring(first)[1][2]
            for i in range(2):
                pair[i].wait_recv()
                if not first:
                    send_across(s, s.view(first, far, i))
    for i in range(2):
        far_rows[i].wait_recv()
        view = rows_out.at[x_far, pl.ds(i * half, half)]
        across.append(sends.start(view, view, partner))
    for copy in across:
        copy.wait_recv()
    sends.finish()


def gather_first(wq, wk, wv, small, rows, note, collective_id):
    height, total = wq.shape[0], wq.shape[1] + wk.shape[1] + wv.shape[1]
    return pl.pallas_call(
        gather_first_kernel,
        out_shape=[
            jax.ShapeDtypeStruct((4, 4, height, total), wq.dtype),
            jax.ShapeDtypeStruct((4, 4, *small.shape), small.dtype),
            jax.ShapeDtypeStruct((8, *rows.shape), rows.dtype),
            jax.ShapeDtypeStruct((8, *note.shape), note.dtype),
        ],
        in_specs=[ANY] * 6,
        out_specs=[ANY] * 4,
        scratch_shapes=[
            pltpu.SemaphoreType.DMA((7,)),
            pltpu.SemaphoreType.DMA((50,)),
            pltpu.SemaphoreType.DMA((50,)),
        ],
        compiler_params=pltpu.CompilerParams(collective_id=collective_id, has_side_effects=True),
    )(wq, wk, wv, small, rows, note)


SCALE = HEAD_SIZE**-0.5
LOG2E = 1.4426950408889634
BLOCK = 512


def spin(z, cosine, sine):
    return z * cosine + pltpu.roll(z, HEAD_SIZE // 2, 1) * sine


def qkv_kernel(
    tokens_ref, w_ref, gain_ref, cos_ref, sin_ref, normed_ref, query_ref, kv_ref,
    own_kv, local_sem, send_sems, recv_sems,
):
    part, core, right, left, far, partner = around_x()
    to = lambda i: {"expert": i}
    barrier = pltpu.get_barrier_semaphore()
    for other in (partner, right, left):
        pl.semaphore_signal(barrier, inc=1, device_id=to(other), device_id_type=MESH)
    sends = Sends(send_sems, recv_sems)
    cosine, sine = cos_ref[...], sin_ref[...]
    inputs = tokens_ref[...].astype(F32)
    inverse = lax.rsqrt(jnp.mean(inputs * inputs, axis=-1, keepdims=True) + EPSILON)
    normed_ref[...] = (inputs * inverse * gain_ref[...]).astype(BF16)
    strip = w_ref.shape[1] // 4
    wide = strip - HEAD_SIZE
    for s in range(4):
        got = mm(normed_ref[...], w_ref[:, s * strip + wide : (s + 1) * strip])
        if s % 2 == 0:
            got = spin(got, cosine, sine)
        own_kv[:, s * HEAD_SIZE : (s + 1) * HEAD_SIZE] = got.astype(BF16)

    def queries(s):
        got = mm(normed_ref[...], w_ref[:, s * strip : s * strip + wide])
        for h in range(0, wide, HEAD_SIZE):
            head = spin(got[:, h : h + HEAD_SIZE], cosine, sine)
            query_ref[:, s * wide + h : s * wide + h + HEAD_SIZE] = head.astype(BF16)

    pl.semaphore_wait(barrier, 3)
    half = own_kv.shape[0] // 2
    own = pltpu.make_async_copy(own_kv, kv_ref.at[part], local_sem)
    own.start()
    ways = (to(right), to(left))
    came = [sends.start(own_kv, kv_ref.at[part], way) for way in ways]
    across = [sends.start(own_kv, kv_ref.at[part], to(partner))]
    queries(0)
    queries(1)
    onward = []
    for i, origin in enumerate((left, right)):
        came[i].wait_recv()
        view = kv_ref.at[origin, pl.ds(i * half, half)]
        onward.append(sends.start(view, view, ways[i]))
        view = kv_ref.at[origin]
        across.append(sends.start(view, view, to(partner)))
    queries(2)
    queries(3)
    for i in range(2):
        onward[i].wait_recv()
        view = kv_ref.at[far, pl.ds(i * half, half)]
        across.append(sends.start(view, view, to(partner)))
    for copy in across:
        copy.wait_recv()
    own.wait()
    sends.finish()


def qkv(tokens, w, gain, cosine, sine, collective_id):
    rows, width = tokens.shape
    kv_width = w.shape[1] - width
    return pl.pallas_call(
        qkv_kernel,
        out_shape=[
            jax.ShapeDtypeStruct((rows, width), BF16),
            jax.ShapeDtypeStruct((rows, width), BF16),
            jax.ShapeDtypeStruct((8, rows, kv_width), BF16),
        ],
        in_specs=[VMEM] * 5,
        out_specs=[VMEM, VMEM, ANY],
        scratch_shapes=[
            pltpu.VMEM((rows, kv_width), BF16),
            pltpu.SemaphoreType.DMA,
            pltpu.SemaphoreType.DMA((9,)),
            pltpu.SemaphoreType.DMA((9,)),
        ],
        compiler_params=pltpu.CompilerParams(
            collective_id=collective_id, has_side_effects=True, vmem_limit_bytes=40 * 2**20
        ),
    )(tokens, w, gain, cosine, sine)


def fill_bias(bias, start_ref, first_row):
    length, rows = bias.shape
    places = lax.broadcasted_iota(jnp.int32, (length, rows), 0)
    mine = first_row + lax.broadcasted_iota(jnp.int32, (length, rows), 1)
    keep = (places >= start_ref[...]) & (places <= mine)
    bias[...] = jnp.where(keep, 0.0, MASK_FILL)


def attend_kernel(start_ref, q_ref, kv_ref, ctx_ref, lse_ref, bias, v_t, scores):
    head = pl.program_id(0)
    length = bias.shape[0]

    @pl.when(head == 0)
    def _():
        fill_bias(bias, start_ref, start_ref.shape[1] * lax.axis_index("expert"))

    @pl.when(head % GROUP == 0)
    def _():
        v_t[...] = kv_ref[:, HEAD_SIZE:].astype(F32).T.astype(BF16)

    query = q_ref[...]
    top = None
    for at in range(0, length, BLOCK):
        span = pl.ds(at, BLOCK)
        s = mm_nt(kv_ref[span, :HEAD_SIZE], query) + bias[span]
        scores[span] = s
        here = jnp.max(s, axis=0, keepdims=True)
        top = here if top is None else jnp.maximum(top, here)
    total = jnp.zeros_like(top)
    context = jnp.zeros((HEAD_SIZE, query.shape[0]), F32)
    for at in range(0, length, BLOCK):
        span = pl.ds(at, BLOCK)
        p = jnp.exp2((scores[span] - top) * (SCALE * LOG2E))
        total += jnp.sum(p, axis=0, keepdims=True)
        context += mm(v_t[:, span], p.astype(BF16))
    ctx_ref[...] = (context / total).T.astype(BF16)
    lse_ref[0] = top * (SCALE * LOG2E) + jnp.log2(total)


def attend(start, query, kv):
    rows, width = query.shape
    length = kv.shape[0]
    by_head = pl.BlockSpec((rows, HEAD_SIZE), lambda h: (0, h))
    return pl.pallas_call(
        attend_kernel,
        grid=(QUERY_HEADS,),
        out_shape=[
            jax.ShapeDtypeStruct((rows, width), BF16),
            jax.ShapeDtypeStruct((QUERY_HEADS, 1, rows), F32),
        ],
        in_specs=[
            pl.BlockSpec((1, rows), lambda h: (0, 0)),
            by_head,
            pl.BlockSpec((length, 2 * HEAD_SIZE), lambda h: (0, h // GROUP)),
        ],
        out_specs=[by_head, pl.BlockSpec((1, 1, rows), lambda h: (h, 0, 0))],
        scratch_shapes=[
            pltpu.VMEM((length, rows), F32),
            pltpu.VMEM((HEAD_SIZE, length), BF16),
            pltpu.VMEM((length, rows), F32),
        ],
        compiler_params=pltpu.CompilerParams(vmem_limit_bytes=40 * 2**20),
        cost_estimate=pl.CostEstimate(
            flops=4 * rows * length * width, bytes_accessed=4 * length * width, transcendentals=0
        ),
    )(start, query, kv)


def attend_back_kernel(
    start_ref, q_ref, kv_ref, g_ref, lse_ref, cos_ref, sin_ref, gq_ref, gkv_ref,
    bias, k_t, gkv, probs, grad_probs,
):
    head = pl.program_id(0)
    length = bias.shape[0]

    @pl.when(head == 0)
    def _():
        fill_bias(bias, start_ref, start_ref.shape[1] * lax.axis_index("expert"))

    @pl.when(head % GROUP == 0)
    def _():
        k_t[...] = kv_ref[:, :HEAD_SIZE].astype(F32).T.astype(BF16)
        gkv[...] = jnp.zeros_like(gkv)

    query, grad = q_ref[...], g_ref[...]
    lse = lse_ref[0]
    inner = jnp.zeros_like(lse)
    for at in range(0, length, BLOCK):
        span = pl.ds(at, BLOCK)
        s = mm_nt(kv_ref[span, :HEAD_SIZE], query) + bias[span]
        p = jnp.exp2(s * (SCALE * LOG2E) - lse)
        gp = mm_nt(kv_ref[span, HEAD_SIZE:], grad)
        inner += jnp.sum(p * gp, axis=0, keepdims=True)
        probs[span] = p
        grad_probs[span] = gp
        gkv[span, HEAD_SIZE:] += mm(p.astype(BF16), grad)
    gq = jnp.zeros((HEAD_SIZE, query.shape[0]), F32)
    for at in range(0, length, BLOCK):
        span = pl.ds(at, BLOCK)
        gs = (probs[span] * (grad_probs[span] - inner)).astype(BF16)
        gkv[span, :HEAD_SIZE] += mm(gs, query)
        gq += mm(k_t[:, span], gs)
    gq_ref[...] = spin(gq.T * SCALE, cos_ref[...], -sin_ref[...]).astype(BF16)

    @pl.when(head % GROUP == GROUP - 1)
    def _():
        gkv_ref[:, :HEAD_SIZE] = (gkv[:, :HEAD_SIZE] * SCALE).astype(BF16)
        gkv_ref[:, HEAD_SIZE:] = gkv[:, HEAD_SIZE:].astype(BF16)


def attend_back(start, query, kv, grad, lse, cosine, sine):
    rows, width = query.shape
    length = kv.shape[0]
    by_head = pl.BlockSpec((rows, HEAD_SIZE), lambda h: (0, h))
    by_group = pl.BlockSpec((length, 2 * HEAD_SIZE), lambda h: (0, h // GROUP))
    table = pl.BlockSpec((rows, HEAD_SIZE), lambda h: (0, 0))
    return pl.pallas_call(
        attend_back_kernel,
        grid=(QUERY_HEADS,),
        out_shape=[
            jax.ShapeDtypeStruct((rows, width), BF16),
            jax.ShapeDtypeStruct(kv.shape, BF16),
        ],
        in_specs=[
            pl.BlockSpec((1, rows), lambda h: (0, 0)),
            by_head,
            by_group,
            by_head,
            pl.BlockSpec((1, 1, rows), lambda h: (h, 0, 0)),
            table,
            table,
        ],
        out_specs=[by_head, by_group],
        scratch_shapes=[
            pltpu.VMEM((length, rows), F32),
            pltpu.VMEM((HEAD_SIZE, length), BF16),
            pltpu.VMEM((length, 2 * HEAD_SIZE), F32),
            pltpu.VMEM((length, rows), F32),
            pltpu.VMEM((length, rows), F32),
        ],
        compiler_params=pltpu.CompilerParams(vmem_limit_bytes=40 * 2**20),
        cost_estimate=pl.CostEstimate(
            flops=10 * rows * length * width, bytes_accessed=4 * length * width, transcendentals=0
        ),
    )(start, query, kv, grad, lse, cosine, sine)


LOW, HIGH = 0, 1


def gelu_parts(a):
    k = (2.0 / jnp.pi) ** 0.5
    square = a * a
    t = jnp.tanh(k * a * (1.0 + 0.044715 * square))
    slope = 0.5 * (1.0 + t) + 0.5 * a * (1.0 - t * t) * k * (1.0 + 3 * 0.044715 * square)
    return 0.5 * a * (1.0 + t), slope


def experts_kernel(
    ctx_ref, tokens_ref, small_ref, gain_ref, member_ref, slot_ref, d_out_ref,
    up_all, wo_hbm, wg_hbm, wu_hbm, wd_hbm,
    middle_ref, grad_middle_ref, grad_ctx_ref, small_grad_ref,
    back_out, grad_gu, grad_d, grad_wo,
    wo_ref, wg_ref, wu_ref, wd_ref, rows_all, returns, arrived, pair_grad, hidden, grad_pre,
    theirs, from_left, from_right, tile, back_rows, gates_src, gates_all, gg_src, gg_all,
    local_sems, tile_sems, back_sems, send_sems, recv_sems,
):
    part, core, right, left, far, partner = around_x()
    chip = part // 2
    to = lambda i: {"expert": i}
    others = [lax.rem(part + d, 8) for d in range(1, 8)]
    barrier = pltpu.get_barrier_semaphore()
    for other in others:
        pl.semaphore_signal(barrier, inc=1, device_id=to(other), device_id_type=MESH)
    sends = Sends(send_sems, recv_sems)
    rows, width = ctx_ref.shape
    half = rows // 2
    halves = (pl.ds(0, half), pl.ds(half, half))
    ff = wg_ref.shape[1]
    capacity = arrived.shape[0] // 8

    loads = []
    for src, dst in ((wo_hbm, wo_ref), (wg_hbm, wg_ref), (wu_hbm, wu_ref), (wd_hbm, wd_ref)):
        loads.append(pltpu.make_async_copy(src, dst, local_sems.at[len(loads)]))
    chips = [lax.rem(chip + d, 4) for d in (0, 3, 1, 2)]
    for u in range(4):
        src = up_all.at[pl.ds(2 * chips[u], 2)]
        loads.append(pltpu.make_async_copy(src, returns.at[u], local_sems.at[4 + u]))
    for load in loads:
        load.start()

    loads[0].wait()
    middle = tokens_ref[...].astype(F32) + mm(ctx_ref[...], wo_ref[...])
    middle_ref[...] = middle
    inverse = lax.rsqrt(jnp.mean(middle * middle, axis=-1, keepdims=True) + EPSILON)
    normed = (middle * inverse * gain_ref[...]).astype(BF16)
    rows_all[part] = normed
    member = member_ref[...]
    logits = jnp.where(member > 0.0, mm(normed, small_ref[...]), MASK_FILL)
    weight = jnp.exp(logits - jnp.max(logits, axis=-1, keepdims=True)) * member
    gates = weight / jnp.sum(weight, axis=-1, keepdims=True)
    gates_src[...] = gates.T[:EXPERTS]

    pl.semaphore_wait(barrier, 7)
    mine = rows_all.at[part]
    go_right = sends.start(mine, mine, to(right))
    go_left = sends.start(mine, mine, to(left))
    swap_own = sends.start(mine, mine, to(partner))
    note_sends = [sends.start(gates_src, gates_all.at[part], to(i)) for i in others]
    gates_all[part] = gates_src[...]

    def pick_of(source):
        slots = lax.broadcasted_iota(jnp.int32, (capacity, rows), 0)
        return slots == slot_ref[source]

    for u in range(4):
        loads[4 + u].wait()
        for c in range(2):
            pick = pick_of(2 * chips[u] + c).astype(BF16)
            got = mm(pick, returns[u, c])
            pair_grad[pl.ds((2 * u + c) * capacity, capacity)] = got.astype(BF16)
    for load in loads[1:4]:
        load.wait()

    def unit(u):
        at = chips[u]
        picks = [pick_of(2 * at + c) for c in range(2)]
        picks_b = [pick.astype(BF16) for pick in picks]
        spans = [pl.ds((2 * u + c) * capacity, capacity) for c in range(2)]
        both = pl.ds(2 * u * capacity, 2 * capacity)
        gate = []
        for c in range(2):
            arrived[spans[c]] = mm(picks_b[c], rows_all[2 * at + c]).astype(BF16)
            row = gates_all[2 * at + c, pl.ds(part, 1)]
            gate.append(jnp.sum(jnp.where(picks[c], row, 0.0), axis=-1, keepdims=True))
        gate = jnp.concatenate(gate, axis=0)
        x = arrived[both]
        a, b = mm(x, wg_ref[...]), mm(x, wu_ref[...])
        act, slope = gelu_parts(a)
        h = (act * b).astype(BF16)
        hidden[both] = h
        out = mm(h, wd_ref[...]).astype(BF16).astype(F32)
        up = pair_grad[both].astype(F32)
        gg = jnp.sum(up * out, axis=-1, keepdims=True)
        weighted = (gate * out).astype(BF16)
        pg = (gate * up).astype(BF16)
        pair_grad[both] = pg
        if u > 0:
            for c in range(2):
                stores[u - 1][c].wait()
        stores.append([])
        for c in range(2):
            back_rows[c] = mm_tn(picks_b[c], weighted[c * capacity : (c + 1) * capacity]).astype(
                BF16
            )
            store = pltpu.make_async_copy(
                back_rows.at[c], back_out.at[2 * at + c], back_sems.at[c]
            )
            store.start()
            stores[u].append(store)
            gg_c = gg[c * capacity : (c + 1) * capacity]
            row = jnp.sum(jnp.where(picks[c], gg_c, 0.0), axis=0, keepdims=True)
            gg_src[u, c] = jnp.broadcast_to(row, (8, rows))
        grad_h = mm_nt(pg, wd_ref[...])
        grad_a = (grad_h * b * slope).astype(BF16)
        grad_b = (grad_h * act).astype(BF16)
        grad_pre[both, :ff] = grad_a
        grad_pre[both, ff:] = grad_b
        grad_rows = (mm_nt(grad_a, wg_ref[...]) + mm_nt(grad_b, wu_ref[...])).astype(BF16)
        for c in range(2):
            returns[u, c] = mm_tn(
                picks_b[c], grad_rows[c * capacity : (c + 1) * capacity]
            ).astype(BF16)
        swaps.append(sends.start(returns.at[u, 1 - core], theirs.at[u], to(partner)))
        if u == 0:
            gg_all[part] = gg_src[0, core]
            gg_sends.append(sends.start(gg_src.at[0, 1 - core], gg_all.at[part], to(partner)))
        else:
            for c in (core, 1 - core):
                gg_sends.append(sends.start(gg_src.at[u, c], gg_all.at[part], to(2 * at + c)))

    def joined(u):
        swaps[u].wait_recv()
        theirs[u] = (theirs[u].astype(F32) + returns[u, core].astype(F32)).astype(BF16)

    stores, swaps, gg_sends = [], [], []
    swap_own.wait_recv()
    for copy in note_sends:
        copy.wait_recv()
    unit(0)
    go_right.wait_recv()
    first = rows_all.at[left, halves[LOW]]
    far_low = sends.start(first, first, to(right))
    swap_left = sends.start(rows_all.at[left], rows_all.at[left], to(partner))
    go_left.wait_recv()
    second = rows_all.at[right, halves[HIGH]]
    far_high = sends.start(second, second, to(left))
    swap_right = sends.start(rows_all.at[right], rows_all.at[right], to(partner))
    swap_left.wait_recv()
    unit(1)
    swap_right.wait_recv()
    unit(2)
    swap_far = []
    for h, copy in enumerate((far_low, far_high)):
        copy.wait_recv()
        piece = rows_all.at[far, halves[h]]
        swap_far.append(sends.start(piece, piece, to(partner)))
    joined(1)
    joined(2)
    back_right = sends.start(theirs.at[2, halves[HIGH]], from_left.at[2], to(right))
    back_left = sends.start(theirs.at[1, halves[LOW]], from_right.at[2], to(left))
    for copy in swap_far:
        copy.wait_recv()
    unit(3)
    joined(3)
    back_far_low = sends.start(theirs.at[3, halves[LOW]], from_left.at[0], to(right))
    back_far_high = sends.start(theirs.at[3, halves[HIGH]], from_right.at[0], to(left))

    tall = tile.shape[1]

    def tiles(first_tile, count, lhs, rhs, out):
        def step(i, _):
            slot = lax.rem(first_tile + i, 2)

            @pl.when(first_tile + i >= 2)
            def _():
                pltpu.make_async_copy(
                    tile.at[slot], grad_d.at[pl.ds(0, tall)], tile_sems.at[slot]
                ).wait()

            cols = pl.ds(pl.multiple_of(i * tall, 128), tall)
            tile[slot] = mm_tn(lhs[:, cols], rhs[...]).astype(BF16)
            pltpu.make_async_copy(
                tile.at[slot], out.at[pl.ds(pl.multiple_of(i * tall, 16), tall)], tile_sems.at[slot]
            ).start()
            return 0

        lax.fori_loop(0, count, step, 0)

    tiles(0, ff // tall, hidden, pair_grad, grad_d)
    back_far_low.wait_recv()
    theirs[2, halves[LOW]] = (
        theirs[2, halves[LOW]].astype(F32) + from_left[0].astype(F32)
    ).astype(BF16)
    back_right_low = sends.start(theirs.at[2, halves[LOW]], from_left.at[1], to(right))
    back_far_high.wait_recv()
    theirs[1, halves[HIGH]] = (
        theirs[1, halves[HIGH]].astype(F32) + from_right[0].astype(F32)
    ).astype(BF16)
    back_left_high = sends.start(theirs.at[1, halves[HIGH]], from_right.at[1], to(left))
    tiles(ff // tall, width // tall, arrived, grad_pre, grad_gu)

    swaps[0].wait_recv()
    back_right.wait_recv()
    back_left.wait_recv()
    back_right_low.wait_recv()
    back_left_high.wait_recv()
    total = theirs[0].astype(F32) + returns[0, core].astype(F32)
    total += jnp.concatenate([from_left[1], from_left[2]], axis=0).astype(F32)
    total += jnp.concatenate([from_right[2], from_right[1]], axis=0).astype(F32)
    for copy in gg_sends:
        copy.wait_recv()
    grad_gates = jnp.concatenate([gg_all[e, :1] for e in range(EXPERTS)], axis=0)
    gates_t = gates_src[...]
    products = gates_t * grad_gates
    grad_logits = products - gates_t * jnp.sum(products, axis=0, keepdims=True)
    grad_logits = jnp.concatenate(
        [grad_logits, jnp.zeros((128 - EXPERTS, rows), F32)], axis=0
    ).T.astype(BF16)
    total += mm_nt(grad_logits, small_ref[...])
    middle = middle_ref[...]
    inverse = lax.rsqrt(jnp.mean(middle * middle, axis=-1, keepdims=True) + EPSILON)
    scaled = middle * inverse
    gain = gain_ref[...]
    normed = (scaled * gain).astype(BF16)
    grad_gain = jnp.sum(total * scaled, axis=0, keepdims=True)
    lanes = lax.broadcasted_iota(jnp.int32, (width, 128), 1)
    small_grad = mm_tn(normed, grad_logits)
    small_grad += jnp.where(lanes == EXPERTS, jnp.broadcast_to(grad_gain, (128, width)).T, 0.0)
    small_grad_ref[...] = small_grad.astype(BF16)
    weighted = total * gain
    inner = jnp.mean(weighted * scaled, axis=-1, keepdims=True)
    grad_middle = d_out_ref[...].astype(F32) + inverse * (weighted - scaled * inner)
    grad_middle_ref[...] = grad_middle
    grad_attn = grad_middle.astype(BF16)
    grad_ctx_ref[...] = mm_nt(grad_attn, wo_ref[...]).astype(BF16)
    pair_grad[pl.ds(0, rows)] = grad_attn
    done = ff // tall + width // tall

    def wo_tile(i, _):
        slot = lax.rem(done + i, 2)
        pltpu.make_async_copy(
            tile.at[slot], grad_d.at[pl.ds(0, tall)], tile_sems.at[slot]
        ).wait()
        cols = pl.ds(pl.multiple_of(i * tall, 128), tall)
        tile[slot] = mm_tn(ctx_ref[:, cols], pair_grad[pl.ds(0, rows)]).astype(BF16)
        pltpu.make_async_copy(
            tile.at[slot], grad_wo.at[pl.ds(pl.multiple_of(i * tall, 16), tall)], tile_sems.at[slot]
        ).start()
        return 0

    lax.fori_loop(0, width // tall, wo_tile, 0)
    for slot in range(2):
        pltpu.make_async_copy(
            tile.at[slot], grad_d.at[pl.ds(0, tall)], tile_sems.at[slot]
        ).wait()
    for c in range(2):
        stores[3][c].wait()
    sends.finish()


def experts(ctx, tokens, small, gain, member, slots, d_out, up_all, wo, wg, wu, wd, collective_id):
    rows, width = ctx.shape
    ff = wg.shape[1]
    capacity = rows * 9 // 16
    vmem, sds = pltpu.VMEM, jax.ShapeDtypeStruct
    return pl.pallas_call(
        experts_kernel,
        out_shape=[
            sds((rows, width), F32),
            sds((rows, width), F32),
            sds((rows, width), BF16),
            sds((width, 128), BF16),
            sds((8, rows, width), BF16),
            sds((width, 2 * ff), BF16),
            sds((ff, width), BF16),
            sds((width, width), BF16),
        ],
        in_specs=[VMEM] * 7 + [ANY] * 5,
        out_specs=[VMEM] * 4 + [ANY] * 4,
        scratch_shapes=[
            vmem((width, width), BF16),
            vmem((width, ff), BF16),
            vmem((width, ff), BF16),
            vmem((ff, width), BF16),
            vmem((8, rows, width), BF16),
            vmem((4, 2, rows, width), BF16),
            vmem((8 * capacity, width), BF16),
            vmem((8 * capacity, width), BF16),
            vmem((8 * capacity, ff), BF16),
            vmem((8 * capacity, 2 * ff), BF16),
            vmem((4, rows, width), BF16),
            vmem((3, rows // 2, width), BF16),
            vmem((3, rows // 2, width), BF16),
            vmem((2, 256, width), BF16),
            vmem((2, rows, width), BF16),
            vmem((8, rows), F32),
            vmem((8, 8, rows), F32),
            vmem((4, 2, 8, rows), F32),
            vmem((8, 8, rows), F32),
            pltpu.SemaphoreType.DMA((8,)),
            pltpu.SemaphoreType.DMA((2,)),
            pltpu.SemaphoreType.DMA((2,)),
            pltpu.SemaphoreType.DMA((40,)),
            pltpu.SemaphoreType.DMA((40,)),
        ],
        compiler_params=pltpu.CompilerParams(
            collective_id=collective_id, has_side_effects=True, vmem_limit_bytes=63 * 2**20
        ),
    )(ctx, tokens, small, gain, member, slots, d_out, up_all, wo, wg, wu, wd)


def widen_kernel(late_ref, gu_ref, d_ref, g_out, u_out, d_out):
    ff = g_out.shape[1]
    g_out[...] = gu_ref[:, :ff].astype(F32)
    u_out[...] = gu_ref[:, ff:].astype(F32)
    d_out[...] = d_ref[...].astype(F32)


def widen(sums, late):
    steps = 8
    (width, both), (ff, _) = sums[0].shape, sums[1].shape
    spec = lambda a, b: pl.BlockSpec((a // steps, b), lambda i: (i, 0))
    return pl.pallas_call(
        widen_kernel,
        grid=(steps,),
        out_shape=[jax.ShapeDtypeStruct(s, F32) for s in ((width, ff), (width, ff), (ff, width))],
        in_specs=[ANY, spec(width, both), spec(ff, width)],
        out_specs=[spec(width, ff), spec(width, ff), spec(ff, width)],
        cost_estimate=pl.CostEstimate(flops=0, bytes_accessed=21 * 2**20, transcendentals=0),
    )(late, *sums)


def on_device(
    tokens,
    d_out,
    gain_in,
    w_query,
    key_projection_weight,
    value_projection_weight,
    w_out,
    gain_mid,
    w_router,
    w_gate,
    w_up,
    w_down,
    routes,
    segments,
):
    rows, width = tokens.shape
    length = segments.shape[1]
    part = lax.axis_index("expert")
    parts = lax.axis_size("expert")
    core = part % 2
    capacity = rows * 9 // 16
    seg_row = segments[0]
    offset = part * rows
    my_seg = lax.dynamic_slice_in_dim(seg_row, offset, rows, 0)
    start = jnp.sum((seg_row[None, :] < my_seg[:, None]).astype(jnp.int32), axis=1)
    angles = angles_for(offset + jnp.arange(rows, dtype=jnp.int32) - start)
    cosine, sine = jnp.cos(angles), jnp.sin(angles)
    cosine = jnp.concatenate([cosine, cosine], axis=1)
    sine = jnp.concatenate([-sine, sine], axis=1)
    start = start[None, :]

    small = jnp.concatenate([w_router, gain_mid[:, None], gain_in[:, None]], axis=1)
    small = jnp.pad(small, ((0, 0), (0, 128 - small.shape[1])))
    note = jnp.pad(routes.T, ((0, 8 - TOPK), (0, 0)))
    w_strips, small, upstream_all, notes = gather_first(
        w_query, key_projection_weight, value_projection_weight, small, d_out, note, 1
    )
    w_strips = w_strips.reshape(width, -1)
    small = small.reshape(width, -1)
    gain_mid_row = small[:, EXPERTS].astype(F32)[None, :]
    gain_in_row = small[:, EXPERTS + 1].astype(F32)[None, :]
    wo = gather_dense(w_out, core)

    normed, query, kv_all = qkv(tokens, w_strips, gain_in_row, cosine, sine, 2)
    kv_all = kv_all.reshape(length, -1)
    context, lse = attend(start, query, kv_all)

    member = jnp.any(routes[:, :, None] == jnp.arange(128, dtype=jnp.int32), axis=1).astype(F32)
    chosen = jnp.any(notes[:, :TOPK] == part, axis=1)
    slots = jnp.where(chosen, jnp.cumsum(chosen.astype(jnp.int32), axis=1) - 1, -1)[:, None, :]
    middle, grad_middle, grad_ctx, small_grads, back_out, grad_gu, grad_d, grad_wo = experts(
        context, tokens, small, gain_mid_row, member, slots, d_out, upstream_all,
        wo, w_gate[0], w_up[0], w_down[0], 3,
    )

    kv_at = QUERY_HEADS * HEAD_SIZE
    grad_qlin, kv_terms = attend_back(start, query, kv_all, grad_ctx, lse, cosine, sine)
    kv_grad = reduce_x(kv_terms.reshape(parts, rows, -1), 5)
    gk0, gv0, gk1, gv1 = (kv_grad[:, i * HEAD_SIZE : (i + 1) * HEAD_SIZE] for i in range(4))
    grad_kv = jnp.concatenate(
        [rotate(gk0, cosine, -sine), gv0, rotate(gk1, cosine, -sine), gv1], axis=1
    ).astype(BF16)
    wide = kv_at // 4
    grad_lin = jnp.concatenate(
        [
            piece
            for s in range(4)
            for piece in (
                grad_qlin[:, s * wide : (s + 1) * wide],
                grad_kv[:, s * HEAD_SIZE : (s + 1) * HEAD_SIZE],
            )
        ],
        axis=1,
    )
    grad_wqkv = mm_tn(normed, grad_lin).astype(BF16)
    grad_normed = mm_nt(grad_lin, w_strips)
    grad_inputs_norm, grad_gin = rms_back(tokens.astype(F32), gain_in_row, grad_normed)
    grad_tokens = grad_middle + grad_inputs_norm
    lanes = jnp.arange(128)[None, :]
    small_grads = jnp.where(lanes == EXPERTS + 1, grad_gin[:, None].astype(BF16), small_grads)

    owned = lambda g: g.reshape(4, 4, width // 16, -1)
    g_wq, g_wk, g_wv, g_wo, small_sum, mixed = reduce_all(
        owned(grad_wqkv), owned(grad_wo), owned(small_grads), middle, back_out,
        key_projection_weight.shape[1], 6,
    )
    expert_sums = widen([lax.psum(g, "dp") for g in (grad_gu, grad_d)], small_sum)
    return (
        mixed,
        grad_tokens,
        small_sum[:, EXPERTS + 1],
        g_wq,
        g_wk,
        g_wv,
        g_wo,
        small_sum[:, EXPERTS],
        small_sum[:, :EXPERTS],
        *(g[None] for g in expert_sums),
    )


def solution(mesh):
    whole = P(("dp", "expert"), None)
    over_dp, by_dp, over_expert = P("dp"), P("dp", None), P("expert", None, None)
    return jax.shard_map(
        on_device,
        mesh=mesh,
        in_specs=(whole, whole, over_dp, by_dp, by_dp, by_dp, by_dp, over_dp, by_dp)
        + (over_expert,) * 3
        + (whole, by_dp),
        out_specs=(whole, whole, over_dp, by_dp, by_dp, by_dp, by_dp, over_dp, by_dp)
        + (over_expert,) * 3,
        check_vma=False,
    )
```

```python
import jax
import jax.numpy as jnp
from jax import lax
from jax.experimental import pallas as pl
from jax.experimental.pallas import tpu as pltpu
from jax.sharding import PartitionSpec as P

QUERY_HEADS = 12
KEY_VALUE_HEADS = 2
HEAD_SIZE = 128
TOPK = 4
EXPERTS = 8
GROUP = QUERY_HEADS // KEY_VALUE_HEADS
SCALE = HEAD_SIZE**-0.5
LOG2E = 1.4426950408889634
BLOCK = 512

EPSILON = 1e-06
ROPE_BASE = 1000000.0
MASK_FILL = -1e30
F32 = jnp.float32
BF16 = jnp.bfloat16

PARTNER = [(i, i ^ 1) for i in range(8)]
MESH = pl.DeviceIdType.MESH
ANY = pl.BlockSpec(memory_space=pl.ANY)
VMEM = pl.BlockSpec(memory_space=pltpu.VMEM)
MIB = 2**20


def dot(a, b, dims):
    return lax.dot_general(a, b, (dims, ((), ())), preferred_element_type=F32)


def mm(a, b):
    return dot(a, b, ((1,), (0,)))


def mm_nt(a, b):
    return dot(a, b, ((1,), (1,)))


def mm_tn(a, b):
    return dot(a, b, ((0,), (0,)))


def sds(shape, dtype):
    return jax.ShapeDtypeStruct(tuple(shape), dtype)


def remote_params(collective_id, mib):
    return pltpu.CompilerParams(
        collective_id=collective_id, has_side_effects=True, vmem_limit_bytes=mib * MIB
    )


def semaphores(count):
    return pltpu.SemaphoreType.DMA((count,))


def inverse_rms(rows):
    return lax.rsqrt(jnp.mean(rows * rows, axis=-1, keepdims=True) + EPSILON)


def rms_back(rows, gain, grad):
    inverse = inverse_rms(rows)
    scaled = rows * inverse
    weighted = grad * gain
    inner = jnp.mean(weighted * scaled, axis=-1, keepdims=True)
    return inverse * (weighted - scaled * inner), jnp.sum(grad * scaled, axis=0, keepdims=True)


def as_column(row, lanes):
    return jnp.broadcast_to(row, (lanes, row.shape[1])).T


def angles_for(positions):
    half_width = HEAD_SIZE // 2
    freqs = ROPE_BASE ** (-2.0 * jnp.arange(half_width, dtype=F32) / HEAD_SIZE)
    return positions.astype(F32)[:, None] * freqs[None, :]


def spin(z, cosine, sine):
    return z * cosine + pltpu.roll(z, HEAD_SIZE // 2, 1) * sine


def gather_dense(shard, core):
    half = shard.shape[1] // 2
    mine = lax.dynamic_slice_in_dim(shard, core * half, half, 1)
    got = lax.all_gather(mine, "dp", axis=0, tiled=True)
    other = lax.ppermute(got, "expert", PARTNER)
    first = jnp.where(core == 0, got, other)
    second = jnp.where(core == 0, other, got)
    return jnp.concatenate([first, second], axis=1)


class Sends:
    def __init__(self, send_sems, recv_sems):
        self.send_sems, self.recv_sems, self.made = send_sems, recv_sems, []

    def start(self, src, dst, to):
        at = len(self.made)
        copy = pltpu.make_async_remote_copy(
            src_ref=src,
            dst_ref=dst,
            send_sem=self.send_sems.at[at],
            recv_sem=self.recv_sems.at[at],
            device_id=to,
            device_id_type=MESH,
        )
        copy.start()
        self.made.append(copy)
        return copy

    def finish(self):
        for copy in self.made:
            copy.wait_send()


class Keeps:
    def __init__(self, sems):
        self.sems, self.made = sems, []

    def start(self, src, dst):
        copy = pltpu.make_async_copy(src, dst, self.sems.at[len(self.made)])
        copy.start()
        self.made.append(copy)
        return copy


class Place:
    def __init__(self):
        self.part = lax.axis_index("expert")
        self.core = self.part % 2
        self.chip = self.part // 2
        at = lambda d: lax.rem(self.chip + d, 4) * 2 + self.core
        self.right, self.left, self.far = at(1), at(3), at(2)
        to = lambda i: {"expert": i}
        self.partner = to(2 * self.chip + (1 - self.core))
        self.x_to = [to(self.right), to(self.left), to(self.far)]
        self.others = [to(lax.rem(self.part + d, 8)) for d in range(1, 8)]
        place = lax.axis_index("dp")
        self.y, self.z = place // 4, place % 4
        ring = lambda v: [lax.rem(v + d, 4) for d in (1, 3, 2)]
        self.y_ring, self.z_ring = ring(self.y), ring(self.z)
        self.y_to = [{"dp": v * 4 + self.z} for v in self.y_ring[:2]]
        self.z_to = [{"dp": self.y * 4 + v} for v in self.z_ring[:2]]

    def ring(self, along_y):
        if along_y:
            return self.y, self.y_ring, self.y_to
        return self.z, self.z_ring, self.z_to


def greet(others):
    barrier = pltpu.get_barrier_semaphore()
    for other in others:
        pl.semaphore_signal(barrier, inc=1, device_id=other, device_id_type=MESH)


def await_greetings(others):
    pl.semaphore_wait(pltpu.get_barrier_semaphore(), len(others))


def add_to(ref, *others):
    got = ref[...].astype(F32)
    for other in others:
        got += other[...].astype(F32)
    ref[...] = got.astype(ref.dtype)


def run_out(*steps):
    steps = list(steps)
    while steps:
        for s in list(steps):
            if next(s, "done") == "done":
                steps.remove(s)


def x_sum(place, sends, blocks_ref, out_ref, mine, theirs, total, from_left, from_right, sems):
    rows = out_ref.shape[0]
    half = rows // 2
    low, high = pl.ds(0, half), pl.ds(half, half)
    to_right, to_left = place.x_to[:2]
    flip = 1 - 2 * place.core
    keeps = Keeps(sems)
    swaps, loads = [], []
    for k, dest in enumerate((place.far, place.right, place.left, place.part)):
        swaps.append(sends.start(blocks_ref.at[dest + flip], theirs.at[k], place.partner))
        loads.append(keeps.start(blocks_ref.at[dest], mine.at[k]))

    def add_up(k):
        loads[k].wait()
        swaps[k].wait_recv()
        total[k] = (mine[k].astype(F32) + theirs[k].astype(F32)).astype(BF16)

    yield
    add_up(0)
    far_low = sends.start(total.at[0, low], from_left.at[0], to_right)
    far_high = sends.start(total.at[0, high], from_right.at[0], to_left)
    add_up(1)
    right_high = sends.start(total.at[1, high], from_left.at[2], to_right)
    add_up(2)
    left_low = sends.start(total.at[2, low], from_right.at[2], to_left)
    yield
    far_low.wait_recv()
    add_to(total.at[1, low], from_left.at[0])
    right_low = sends.start(total.at[1, low], from_left.at[1], to_right)
    far_high.wait_recv()
    add_to(total.at[2, high], from_right.at[0])
    left_high = sends.start(total.at[2, high], from_right.at[1], to_left)
    yield
    loads[3].wait()
    swaps[3].wait_recv()
    out_ref[...] = mine[3].astype(F32) + theirs[3].astype(F32)
    right_high.wait_recv()
    left_low.wait_recv()
    right_low.wait_recv()
    left_high.wait_recv()
    add_to(out_ref.at[low], from_left.at[1], from_right.at[2])
    add_to(out_ref.at[high], from_left.at[2], from_right.at[1])
    yield


def x_buffers(rows, columns):
    return [
        pltpu.VMEM((4, rows, columns), BF16),
        pltpu.VMEM((4, rows, columns), BF16),
        pltpu.VMEM((3, rows, columns), BF16),
        pltpu.VMEM((3, rows // 2, columns), BF16),
        pltpu.VMEM((3, rows // 2, columns), BF16),
        semaphores(4),
    ]


class Strip:
    def __init__(self, y_first, total, bufs, own=None, other=None):
        self.y_first, self.total, self.own, self.other = y_first, total, own, other
        self.theirs, self.big, self.far, self.mid, self.midfar, self.near = bufs

    def block(self, ref, w):
        return ref.at[w] if self.y_first else ref.at[:, w]


def strip_buffers(rows, columns, shared=True):
    return [
        pltpu.VMEM((4, 4, rows, columns) if shared else (1, 1, rows, columns), BF16),
        pltpu.VMEM((2, 2, 2, rows, columns), BF16),
        pltpu.VMEM((2, 2, rows, columns), BF16),
        pltpu.VMEM((2, 2, rows // 2, columns), BF16),
        pltpu.VMEM((2, rows // 2, columns), BF16),
        pltpu.VMEM((4, rows, columns), BF16),
    ]


def dp_sum(place, sends, strips, sems):
    y, z = place.y, place.z
    keeps = Keeps(sems)
    swaps, loads = {}, {}
    for k in range(4):
        for i, s in enumerate(strips):
            me, (right, left, far), _ = place.ring(s.y_first)
            w = (far, right, left, me)[k]
            if s.other is not None:
                swaps[k, i] = sends.start(s.other(w), s.block(s.theirs, w), place.partner)
            if s.own is not None:
                loads[k, i] = keeps.start(s.own(w), s.block(s.total, w))
    yield

    def joined(k, i, s, w):
        if s.own is not None:
            loads[k, i].wait()
        if s.other is not None:
            swaps[k, i].wait_recv()
            add_to(s.block(s.total, w), s.block(s.theirs, w))

    def big(s, w, h):
        span = pl.ds(2 * h, 2)
        return s.total.at[w, span] if s.y_first else s.total.at[span, w]

    def small(s, w, h):
        half = s.total.shape[2] // 2
        at = pl.ds(h * half, half)
        return s.total.at[y, w, at] if s.y_first else s.total.at[w, z, at]

    for first, view in ((True, big), (False, small)):
        whole = lambda s: s.big if first else s.mid
        farther = lambda s: s.far if first else s.midfar
        ready = joined if first else lambda *_: None
        ring = lambda s: place.ring(s.y_first == first)
        going = []
        for i, s in enumerate(strips):
            _, (right, left, far), to = ring(s)
            ready(0, i, s, far)
            going.append(
                [sends.start(view(s, far, h), farther(s).at[h], to[h]) for h in range(2)]
            )
        for i, s in enumerate(strips):
            _, (right, left, far), to = ring(s)
            ready(1, i, s, right)
            ready(2, i, s, left)
            going[i].append(sends.start(view(s, right, 1), whole(s).at[0, 1], to[0]))
            going[i].append(sends.start(view(s, left, 0), whole(s).at[1, 0], to[1]))
        yield
        for i, s in enumerate(strips):
            _, (right, left, far), to = ring(s)
            for h, w in enumerate((right, left)):
                going[i][h].wait_recv()
                add_to(view(s, w, h), farther(s).at[h])
                going[i].append(sends.start(view(s, w, h), whole(s).at[h, h], to[h]))
        yield
        for i, s in enumerate(strips):
            me, _, _ = ring(s)
            ready(3, i, s, me)
            for copy in going[i][2:]:
                copy.wait_recv()
            for h in range(2):
                add_to(view(s, me, h), whole(s).at[0, h], whole(s).at[1, h])

    shares, back = [], []
    for s in strips:
        shares.append(
            [sends.start(s.total.at[y, z], s.near.at[i], place.x_to[i]) for i in range(3)]
        )
    yield
    for s, share in zip(strips, shares):
        for copy in share:
            copy.wait_recv()
        got = s.total[y, z].astype(F32)
        for i in range(3):
            got += s.near[i].astype(F32)
        s.result = s.theirs.at[y, z] if s.other is not None else s.theirs.at[0, 0]
        s.result[...] = got.astype(BF16)
        back.append(sends.start(s.result, s.near.at[3], place.partner))
    yield
    for copy in back:
        copy.wait_recv()
    yield


def gather_first_kernel(
    wq_ref, wk_ref, wv_ref, small_ref, rows_ref, note_ref,
    out_ref, small_out, rows_out, notes_out, strips_ref, local_sems, send_sems, recv_sems,
):
    place = Place()
    y, z, core, part = place.y, place.z, place.core, place.part
    neighbours = [*place.others, *place.y_to, *place.z_to]
    greet(neighbours)
    rows = wq_ref.shape[0]
    wide, narrow = wq_ref.shape[1] // 4, wk_ref.shape[1] // 2
    strip = wide + narrow
    for s in range(4):
        strips_ref[:, s * strip : s * strip + wide] = wq_ref[:, s * wide : (s + 1) * wide]
        other = (wk_ref, wv_ref)[s % 2]
        begin = s // 2 * narrow
        strips_ref[:, s * strip + wide : (s + 1) * strip] = other[:, begin : begin + narrow]
    await_greetings(neighbours)
    sends, keeps = Sends(send_sems, recv_sems), Keeps(local_sems)

    def columns(p):
        return pl.ds(pl.multiple_of((2 * core + p) * strip, 128), strip)

    class Piece:
        def __init__(self, src, out, cols, y_first):
            self.src, self.out, self.cols, self.y_first = src, out, cols, y_first

        def ring(self, first):
            return place.ring(self.y_first == first)

        def view(self, first, where, piece=None):
            if first:
                at = pl.ds(0, rows) if piece is None else pl.ds(piece * rows // 2, rows // 2)
                if self.y_first:
                    return self.out.at[where, z, at, self.cols]
                return self.out.at[y, where, at, self.cols]
            span = pl.ds(0, 4) if piece is None else pl.ds(2 * piece, 2)
            if self.y_first:
                return self.out.at[span, where, :, self.cols]
            return self.out.at[where, span, :, self.cols]

    pieces = [
        Piece(strips_ref.at[:, columns(0)], out_ref, columns(0), False),
        Piece(strips_ref.at[:, columns(1)], out_ref, columns(1), True),
        Piece(small_ref, small_out, pl.ds(0, small_ref.shape[1]), False),
    ]
    across = []

    def send_across(s, view):
        if s.out is out_ref:
            across.append(sends.start(view, view, place.partner))

    half = rows_ref.shape[0] // 2
    for first in (True, False):
        stage = []
        for s in pieces:
            me, _, to = s.ring(first)
            src = s.src if first else s.view(first, me)
            stage.append([sends.start(src, s.view(first, me), to[i]) for i in range(2)])
        if first:
            for s in pieces:
                keeps.start(s.src, s.out.at[y, z, :, s.cols])
            x_came = [sends.start(rows_ref, rows_out.at[part], to) for to in place.x_to[:2]]
            across.append(sends.start(rows_ref, rows_out.at[part], place.partner))
            across += [sends.start(note_ref, notes_out.at[part], to) for to in place.others]
            keeps.start(rows_ref, rows_out.at[part])
            keeps.start(note_ref, notes_out.at[part])
        else:
            for s in pieces:
                send_across(s, s.view(first, s.ring(first)[0]))
            far_rows = []
            for i, origin in enumerate((place.left, place.right)):
                x_came[i].wait_recv()
                view = rows_out.at[origin, pl.ds(i * half, half)]
                far_rows.append(sends.start(view, view, place.x_to[i]))
                view = rows_out.at[origin]
                across.append(sends.start(view, view, place.partner))
        onward = []
        for s, came in zip(pieces, stage):
            _, (right, left, _), to = s.ring(first)
            pair = []
            for i, origin in enumerate((left, right)):
                came[i].wait_recv()
                view = s.view(first, origin, i)
                pair.append(sends.start(view, view, to[i]))
                if not first:
                    send_across(s, s.view(first, origin))
            onward.append(pair)
        for s, pair in zip(pieces, onward):
            far = s.ring(first)[1][2]
            for i in range(2):
                pair[i].wait_recv()
                if not first:
                    send_across(s, s.view(first, far, i))
        if first:
            for copy in keeps.made[:3]:
                copy.wait()
    for i in range(2):
        far_rows[i].wait_recv()
        view = rows_out.at[place.far, pl.ds(i * half, half)]
        across.append(sends.start(view, view, place.partner))
    for copy in across:
        copy.wait_recv()
    for copy in keeps.made[3:]:
        copy.wait()
    sends.finish()


def gather_first(wq, wk, wv, small, rows, note, collective_id):
    height, total = wq.shape[0], wq.shape[1] + wk.shape[1] + wv.shape[1]
    return pl.pallas_call(
        gather_first_kernel,
        out_shape=[
            sds((4, 4, height, total), BF16),
            sds((4, 4, *small.shape), BF16),
            sds((8, *rows.shape), BF16),
            sds((8, *note.shape), note.dtype),
        ],
        in_specs=[VMEM] * 6,
        out_specs=[ANY] * 4,
        scratch_shapes=[
            pltpu.VMEM((height, total), BF16), semaphores(5), semaphores(50), semaphores(50)
        ],
        compiler_params=remote_params(collective_id, 16),
    )(wq, wk, wv, small, rows, note)


def qkv_kernel(
    tokens_ref, w_ref, gain_ref, cos_ref, sin_ref, normed_ref, query_ref, kv_ref,
    own_kv, local_sems, send_sems, recv_sems,
):
    place = Place()
    neighbours = [place.partner, *place.x_to[:2]]
    greet(neighbours)
    sends, keeps = Sends(send_sems, recv_sems), Keeps(local_sems)
    cosine, sine = cos_ref[...], sin_ref[...]
    inputs = tokens_ref[...].astype(F32)
    normed_ref[...] = (inputs * inverse_rms(inputs) * gain_ref[...]).astype(BF16)
    strip = w_ref.shape[1] // 4
    wide = strip - HEAD_SIZE
    for s in range(4):
        got = mm(normed_ref[...], w_ref[:, s * strip + wide : (s + 1) * strip])
        if s % 2 == 0:
            got = spin(got, cosine, sine)
        own_kv[:, s * HEAD_SIZE : (s + 1) * HEAD_SIZE] = got.astype(BF16)

    def queries(s):
        got = mm(normed_ref[...], w_ref[:, s * strip : s * strip + wide])
        for h in range(0, wide, HEAD_SIZE):
            head = spin(got[:, h : h + HEAD_SIZE], cosine, sine)
            query_ref[:, s * wide + h : s * wide + h + HEAD_SIZE] = head.astype(BF16)

    await_greetings(neighbours)
    half = own_kv.shape[0] // 2
    slot = kv_ref.at[place.part]
    came = [sends.start(own_kv, slot, way) for way in place.x_to[:2]]
    across = [sends.start(own_kv, slot, place.partner)]
    keeps.start(own_kv, slot)
    queries(0)
    queries(1)
    onward = []
    for i, origin in enumerate((place.left, place.right)):
        came[i].wait_recv()
        view = kv_ref.at[origin, pl.ds(i * half, half)]
        onward.append(sends.start(view, view, place.x_to[i]))
        view = kv_ref.at[origin]
        across.append(sends.start(view, view, place.partner))
    queries(2)
    queries(3)
    for i in range(2):
        onward[i].wait_recv()
        view = kv_ref.at[place.far, pl.ds(i * half, half)]
        across.append(sends.start(view, view, place.partner))
    for copy in across:
        copy.wait_recv()
    keeps.made[0].wait()
    sends.finish()


def qkv(tokens, w, gain, cosine, sine, collective_id):
    rows, width = tokens.shape
    kv_width = w.shape[1] - width
    return pl.pallas_call(
        qkv_kernel,
        out_shape=[
            sds((rows, width), BF16), sds((rows, width), BF16), sds((8, rows, kv_width), BF16)
        ],
        in_specs=[VMEM] * 5,
        out_specs=[VMEM, VMEM, ANY],
        scratch_shapes=[
            pltpu.VMEM((rows, kv_width), BF16), semaphores(1), semaphores(9), semaphores(9)
        ],
        compiler_params=remote_params(collective_id, 40),
    )(tokens, w, gain, cosine, sine)


def fill_bias(bias, start_ref, first_row):
    length, rows = bias.shape
    places = lax.broadcasted_iota(jnp.int32, (length, rows), 0)
    mine = first_row + lax.broadcasted_iota(jnp.int32, (length, rows), 1)
    keep = (places >= start_ref[...]) & (places <= mine)
    bias[...] = jnp.where(keep, 0.0, MASK_FILL)


def attend_kernel(start_ref, q_ref, kv_ref, ctx_ref, lse_ref, bias, v_t, scores):
    head = pl.program_id(0)
    length = bias.shape[0]

    @pl.when(head == 0)
    def _():
        fill_bias(bias, start_ref, start_ref.shape[1] * lax.axis_index("expert"))

    @pl.when(head % GROUP == 0)
    def _():
        v_t[...] = kv_ref[:, HEAD_SIZE:].astype(F32).T.astype(BF16)

    query = q_ref[...]
    top = None
    for at in range(0, length, BLOCK):
        span = pl.ds(at, BLOCK)
        s = mm_nt(kv_ref[span, :HEAD_SIZE], query) + bias[span]
        scores[span] = s
        here = jnp.max(s, axis=0, keepdims=True)
        top = here if top is None else jnp.maximum(top, here)
    total = jnp.zeros_like(top)
    context = jnp.zeros((HEAD_SIZE, query.shape[0]), F32)
    for at in range(0, length, BLOCK):
        span = pl.ds(at, BLOCK)
        p = jnp.exp2((scores[span] - top) * (SCALE * LOG2E))
        total += jnp.sum(p, axis=0, keepdims=True)
        context += mm(v_t[:, span], p.astype(BF16))
    ctx_ref[...] = (context / total).T.astype(BF16)
    lse_ref[0] = top * (SCALE * LOG2E) + jnp.log2(total)


def attend(start, query, kv):
    rows, width = query.shape
    length = kv.shape[0]
    by_head = pl.BlockSpec((rows, HEAD_SIZE), lambda h: (0, h))
    return pl.pallas_call(
        attend_kernel,
        grid=(QUERY_HEADS,),
        out_shape=[sds((rows, width), BF16), sds((QUERY_HEADS, 1, rows), F32)],
        in_specs=[
            pl.BlockSpec((1, rows), lambda h: (0, 0)),
            by_head,
            pl.BlockSpec((length, 2 * HEAD_SIZE), lambda h: (0, h // GROUP)),
        ],
        out_specs=[by_head, pl.BlockSpec((1, 1, rows), lambda h: (h, 0, 0))],
        scratch_shapes=[
            pltpu.VMEM((length, rows), F32),
            pltpu.VMEM((HEAD_SIZE, length), BF16),
            pltpu.VMEM((length, rows), F32),
        ],
        compiler_params=pltpu.CompilerParams(vmem_limit_bytes=40 * MIB),
        cost_estimate=pl.CostEstimate(
            flops=4 * rows * length * width, bytes_accessed=4 * length * width, transcendentals=0
        ),
    )(start, query, kv)


LOW, HIGH = 0, 1


def gelu_parts(a):
    k = (2.0 / jnp.pi) ** 0.5
    square = a * a
    t = jnp.tanh(k * a * (1.0 + 0.044715 * square))
    slope = 0.5 * (1.0 + t) + 0.5 * a * (1.0 - t * t) * k * (1.0 + 3 * 0.044715 * square)
    return 0.5 * a * (1.0 + t), slope


def experts_kernel(
    ctx_ref, tokens_ref, small_ref, gain_ref, member_ref, slot_ref,
    up_all, wo_hbm, wg_hbm, wu_hbm, wd_hbm,
    middle_ref, gates_ref, gg_all, sums_ref, own_ref, back_out, w_grads,
    wo_ref, wg_ref, wu_ref, wd_ref, rows_all, returns, arrived, pair_grad, hidden, grad_pre,
    theirs, far_left, far_right, from_left, from_right, tile, tile_d, back_rows, gates_all, gg_src,
    local_sems, tile_sems, back_sems, send_sems, recv_sems,
):
    place = Place()
    part, core = place.part, place.core
    right, left, far = place.right, place.left, place.far
    to_right, to_left = place.x_to[:2]
    greet(place.others)
    sends, keeps, stores = (
        Sends(send_sems, recv_sems), Keeps(local_sems), Keeps(back_sems)
    )
    rows, width = ctx_ref.shape
    half = rows // 2
    halves = (pl.ds(0, half), pl.ds(half, half))
    ff = wg_ref.shape[1]
    capacity = arrived.shape[0] // 8

    for src, dst in ((wo_hbm, wo_ref), (wg_hbm, wg_ref), (wu_hbm, wu_ref), (wd_hbm, wd_ref)):
        keeps.start(src, dst)
    chips = [lax.rem(place.chip + d, 4) for d in (0, 3, 1, 2)]
    for u in range(4):
        keeps.start(up_all.at[pl.ds(2 * chips[u], 2)], returns.at[u])

    keeps.made[0].wait()
    middle = tokens_ref[...].astype(F32) + mm(ctx_ref[...], wo_ref[...])
    middle_ref[...] = middle
    normed = (middle * inverse_rms(middle) * gain_ref[...]).astype(BF16)
    rows_all[part] = normed
    member = member_ref[...]
    logits = jnp.where(member > 0.0, mm(normed, small_ref[...]), MASK_FILL)
    weight = jnp.exp(logits - jnp.max(logits, axis=-1, keepdims=True)) * member
    gates = weight / jnp.sum(weight, axis=-1, keepdims=True)
    gates_ref[...] = gates.T[:EXPERTS]

    await_greetings(place.others)
    mine = rows_all.at[part]
    go_right = sends.start(mine, mine, to_right)
    go_left = sends.start(mine, mine, to_left)
    swap_own = sends.start(mine, mine, place.partner)
    note_sends = [sends.start(gates_ref, gates_all.at[part], to) for to in place.others]
    gates_all[part] = gates_ref[...]

    def pick_of(source):
        slots = lax.broadcasted_iota(jnp.int32, (capacity, rows), 0)
        return slots == slot_ref[source]

    for u in range(4):
        keeps.made[4 + u].wait()
        for c in range(2):
            pick = pick_of(2 * chips[u] + c).astype(BF16)
            got = mm(pick, returns[u, c])
            pair_grad[pl.ds((2 * u + c) * capacity, capacity)] = got.astype(BF16)
    for load in keeps.made[1:4]:
        load.wait()

    swaps, gg_sends = [], []

    def unit(u):
        at = chips[u]
        picks = [pick_of(2 * at + c) for c in range(2)]
        picks_b = [pick.astype(BF16) for pick in picks]
        spans = [pl.ds((2 * u + c) * capacity, capacity) for c in range(2)]
        both = pl.ds(2 * u * capacity, 2 * capacity)
        gate = []
        for c in range(2):
            arrived[spans[c]] = mm(picks_b[c], rows_all[2 * at + c]).astype(BF16)
            row = gates_all[2 * at + c, pl.ds(part, 1)]
            gate.append(jnp.sum(jnp.where(picks[c], row, 0.0), axis=-1, keepdims=True))
        gate = jnp.concatenate(gate, axis=0)
        x = arrived[both]
        a, b = mm(x, wg_ref[...]), mm(x, wu_ref[...])
        act, slope = gelu_parts(a)
        h = (act * b).astype(BF16)
        hidden[both] = h
        out = mm(h, wd_ref[...]).astype(BF16).astype(F32)
        up = pair_grad[both].astype(F32)
        gg = jnp.sum(up * out, axis=-1, keepdims=True)
        weighted = (gate * out).astype(BF16)
        pg = (gate * up).astype(BF16)
        pair_grad[both] = pg
        for c in range(2):
            if u > 0:
                stores.made[2 * (u - 1) + c].wait()
            back_rows[c] = mm_tn(picks_b[c], weighted[c * capacity : (c + 1) * capacity]).astype(
                BF16
            )
            stores.start(back_rows.at[c], back_out.at[2 * at + c])
            gg_c = gg[c * capacity : (c + 1) * capacity]
            row = jnp.sum(jnp.where(picks[c], gg_c, 0.0), axis=0, keepdims=True)
            gg_src[u, c] = jnp.broadcast_to(row, (8, rows))
        grad_h = mm_nt(pg, wd_ref[...])
        grad_a = (grad_h * b * slope).astype(BF16)
        grad_b = (grad_h * act).astype(BF16)
        grad_pre[both, :ff] = grad_a
        grad_pre[both, ff:] = grad_b
        grad_rows = (mm_nt(grad_a, wg_ref[...]) + mm_nt(grad_b, wu_ref[...])).astype(BF16)
        for c in range(2):
            returns[u, c] = mm_tn(
                picks_b[c], grad_rows[c * capacity : (c + 1) * capacity]
            ).astype(BF16)
        swaps.append(sends.start(returns.at[u, 1 - core], theirs.at[u], place.partner))
        if u == 0:
            gg_all[part] = gg_src[0, core]
            gg_sends.append(sends.start(gg_src.at[0, 1 - core], gg_all.at[part], place.partner))
        else:
            for c in (core, 1 - core):
                gg_sends.append(
                    sends.start(gg_src.at[u, c], gg_all.at[part], {"expert": 2 * at + c})
                )

    def joined(u):
        swaps[u].wait_recv()
        add_to(theirs.at[u], returns.at[u, core])

    swap_own.wait_recv()
    for copy in note_sends:
        copy.wait_recv()
    unit(0)
    go_right.wait_recv()
    first = rows_all.at[left, halves[LOW]]
    far_low = sends.start(first, first, to_right)
    swap_left = sends.start(rows_all.at[left], rows_all.at[left], place.partner)
    go_left.wait_recv()
    second = rows_all.at[right, halves[HIGH]]
    far_high = sends.start(second, second, to_left)
    swap_right = sends.start(rows_all.at[right], rows_all.at[right], place.partner)
    swap_left.wait_recv()
    unit(1)
    swap_right.wait_recv()
    unit(2)
    swap_far = []
    for h, copy in enumerate((far_low, far_high)):
        copy.wait_recv()
        piece = rows_all.at[far, halves[h]]
        swap_far.append(sends.start(piece, piece, place.partner))
    joined(1)
    joined(2)
    back_right = sends.start(theirs.at[2, halves[HIGH]], from_left, to_right)
    back_left = sends.start(theirs.at[1, halves[LOW]], from_right, to_left)
    for copy in swap_far:
        copy.wait_recv()
    unit(3)
    joined(3)
    back_far_low = sends.start(theirs.at[3, halves[LOW]], far_left, to_right)
    back_far_high = sends.start(theirs.at[3, halves[HIGH]], far_right, to_left)

    tall = 4 * w_grads.shape[2] * 2 // 3
    high = tall // 4
    w_stores = Keeps(tile_sems)
    for i in range(ff // tall):
        got = mm_tn(hidden[:, i * tall : (i + 1) * tall], pair_grad[...]).astype(BF16)
        tile_d[i] = got.reshape(tile_d.shape[1:])
        w_stores.start(tile_d.at[i], w_grads.at[pl.ds(2 * i, 2), :, pl.ds(high, high // 2)])
    for i in range(width // tall):
        if i >= 2:
            w_stores.made[ff // tall + i - 2].wait()
        got = mm_tn(arrived[:, i * tall : (i + 1) * tall], grad_pre[...]).astype(BF16)
        tile[i % 2] = got.reshape(tile.shape[1:])
        w_stores.start(tile.at[i % 2], w_grads.at[i, :, pl.ds(0, high)])

    swaps[0].wait_recv()
    back_right.wait_recv()
    back_left.wait_recv()
    own_ref[...] = theirs[0].astype(F32) + returns[0, core].astype(F32)
    add_to(own_ref.at[halves[HIGH]], from_left)
    add_to(own_ref.at[halves[LOW]], from_right)
    back_far_low.wait_recv()
    sums_ref[0] = (theirs[2, halves[LOW]].astype(F32) + far_left[...].astype(F32)).astype(BF16)
    back_far_high.wait_recv()
    sums_ref[1] = (theirs[1, halves[HIGH]].astype(F32) + far_right[...].astype(F32)).astype(BF16)
    for copy in gg_sends:
        copy.wait_recv()
    for copy in [*stores.made[6:], *w_stores.made[: ff // tall], *w_stores.made[-2:]]:
        copy.wait()
    sends.finish()


def experts(ctx, tokens, small, gain, member, slots, up_all, wo, wg, wu, wd, collective_id):
    rows, width = ctx.shape
    ff = wg.shape[1]
    capacity = rows * 9 // 16
    high = width // 16
    vmem = pltpu.VMEM
    return pl.pallas_call(
        experts_kernel,
        out_shape=[
            sds((rows, width), F32),
            sds((EXPERTS, rows), F32),
            sds((8, 8, rows), F32),
            sds((2, rows // 2, width), BF16),
            sds((rows, width), F32),
            sds((8, rows, width), BF16),
            sds((4, 4, high * 3 // 2, width), BF16),
        ],
        in_specs=[VMEM] * 6 + [ANY] * 5,
        out_specs=[VMEM] * 5 + [ANY] * 2,
        scratch_shapes=[
            vmem((width, width), BF16),
            vmem((width, ff), BF16),
            vmem((width, ff), BF16),
            vmem((ff, width), BF16),
            vmem((8, rows, width), BF16),
            vmem((4, 2, rows, width), BF16),
            vmem((8 * capacity, width), BF16),
            vmem((8 * capacity, width), BF16),
            vmem((8 * capacity, ff), BF16),
            vmem((8 * capacity, 2 * ff), BF16),
            vmem((4, rows, width), BF16),
            *[vmem((rows // 2, width), BF16)] * 4,
            vmem((2, 4, high, width), BF16),
            vmem((2, 2, 4, high // 2, width), BF16),
            vmem((2, rows, width), BF16),
            vmem((8, EXPERTS, rows), F32),
            vmem((4, 2, 8, rows), F32),
            semaphores(8),
            semaphores(6),
            semaphores(8),
            semaphores(40),
            semaphores(40),
        ],
        compiler_params=remote_params(collective_id, 63),
    )(ctx, tokens, small, gain, member, slots, up_all, wo, wg, wu, wd)


def after_kernel(
    middle_ref, gates_ref, gg_all, sums_ref, own_ref, d_out_ref, ctx_ref, small_ref, gain_ref,
    wo_ref, grad_middle_ref, grad_ctx_ref, small_grad_ref, grad_wo_ref,
    from_left, from_right, send_sems, recv_sems,
):
    place = Place()
    greet(place.x_to[:2])
    await_greetings(place.x_to[:2])
    sends = Sends(send_sems, recv_sems)
    came = [
        sends.start(sums_ref.at[i], dst, place.x_to[i])
        for i, dst in enumerate((from_left, from_right))
    ]
    rows, width = middle_ref.shape
    half = rows // 2
    grad_gates = jnp.concatenate([gg_all[e, :1] for e in range(EXPERTS)], axis=0)
    gates_t = gates_ref[...]
    products = gates_t * grad_gates
    grad_logits = products - gates_t * jnp.sum(products, axis=0, keepdims=True)
    grad_logits = jnp.concatenate(
        [grad_logits, jnp.zeros((128 - EXPERTS, rows), F32)], axis=0
    ).T.astype(BF16)
    total = own_ref[...] + mm_nt(grad_logits, small_ref[...])
    middle, gain = middle_ref[...], gain_ref[...]
    inverse = inverse_rms(middle)
    scaled = middle * inverse
    small_grad = mm_tn((scaled * gain).astype(BF16), grad_logits)
    for copy in came:
        copy.wait_recv()
    total += jnp.concatenate([from_left[...], from_right[...]], axis=0).astype(F32)
    grad_gain = jnp.sum(total * scaled, axis=0, keepdims=True)
    lanes = lax.broadcasted_iota(jnp.int32, (width, 128), 1)
    small_grad += jnp.where(lanes == EXPERTS, as_column(grad_gain, 128), 0.0)
    small_grad_ref[...] = small_grad.astype(BF16)
    weighted = total * gain
    inner = jnp.mean(weighted * scaled, axis=-1, keepdims=True)
    grad_middle = d_out_ref[...].astype(F32) + inverse * (weighted - scaled * inner)
    grad_middle_ref[...] = grad_middle
    grad_attn = grad_middle.astype(BF16)
    grad_ctx_ref[...] = mm_nt(grad_attn, wo_ref[...]).astype(BF16)
    tall = 256
    for at in range(0, width, tall):
        grad_wo_ref[pl.ds(at, tall)] = mm_tn(ctx_ref[:, at : at + tall], grad_attn).astype(BF16)
    sends.finish()


def after(middle, gates, gg, sums, own, d_out, ctx, small, gain, wo, collective_id):
    rows, width = middle.shape
    return pl.pallas_call(
        after_kernel,
        out_shape=[
            sds((rows, width), F32),
            sds((rows, width), BF16),
            sds((width, 128), BF16),
            sds((width, width), BF16),
        ],
        in_specs=[VMEM] * 10,
        out_specs=[VMEM] * 4,
        scratch_shapes=[
            pltpu.VMEM((rows // 2, width), BF16),
            pltpu.VMEM((rows // 2, width), BF16),
            semaphores(2),
            semaphores(2),
        ],
        compiler_params=remote_params(collective_id, 56),
    )(middle, gates, gg, sums, own, d_out, ctx, small, gain, wo)


def attend_back_kernel(
    start_ref, q_ref, kv_ref, g_ref, lse_ref, cos_ref, sin_ref, middle_ref, wo_grads, blocks_ref,
    gq_ref, gkv_ref, wo_out, mixed_ref,
    bias, k_t, gkv, probs, grad_probs, combined, *refs,
):
    place = Place()
    neighbours = [place.partner, *place.x_to, *place.y_to, *place.z_to]
    greet(neighbours)
    totals, bufs, x_bufs = refs[:2], refs[2:14], refs[14:20]
    local_sems, send_sems, recv_sems = refs[20:]
    length, rows = bias.shape
    fill_bias(bias, start_ref, rows * place.part)
    await_greetings(neighbours)
    sends = Sends(send_sems, recv_sems)
    quarter = wo_grads.shape[3] // 4

    def columns(c, p):
        return pl.ds(pl.multiple_of((2 * c + p) * quarter, 128), quarter)

    def source(c, p):
        cols = columns(c, p)
        if p == 0:
            return lambda w: wo_grads.at[w, :, :, cols]
        return lambda w: wo_grads.at[:, w, :, cols]

    strips = [
        Strip(
            p == 0, totals[p], bufs[6 * p : 6 * p + 6],
            source(place.core, p), source(1 - place.core, p),
        )
        for p in range(2)
    ]
    dense = dp_sum(place, sends, strips, local_sems)
    rest = x_sum(place, sends, blocks_ref, combined, *x_bufs)
    next(dense)
    next(rest)

    for group in range(KEY_VALUE_HEADS):
        keys = slice(2 * group * HEAD_SIZE, (2 * group + 1) * HEAD_SIZE)
        values = slice((2 * group + 1) * HEAD_SIZE, (2 * group + 2) * HEAD_SIZE)
        k_t[...] = kv_ref[:, keys].astype(F32).T.astype(BF16)
        gkv[...] = jnp.zeros_like(gkv)

        def one_head(i, carry, base):
            head = base + i
            cols = pl.ds(pl.multiple_of(head * HEAD_SIZE, HEAD_SIZE), HEAD_SIZE)
            query, grad = q_ref[:, cols], g_ref[:, cols]
            lse = lse_ref[head]
            inner = jnp.zeros_like(lse)
            for at in range(0, length, BLOCK):
                span = pl.ds(at, BLOCK)
                s = mm_nt(kv_ref[span, keys], query) + bias[span]
                p = jnp.exp2(s * (SCALE * LOG2E) - lse)
                gp = mm_nt(kv_ref[span, values], grad)
                inner += jnp.sum(p * gp, axis=0, keepdims=True)
                probs[span] = p
                grad_probs[span] = gp
                gkv[span, HEAD_SIZE:] += mm(p.astype(BF16), grad)
            gq = jnp.zeros((HEAD_SIZE, rows), F32)
            for at in range(0, length, BLOCK):
                span = pl.ds(at, BLOCK)
                gs = (probs[span] * (grad_probs[span] - inner)).astype(BF16)
                gkv[span, :HEAD_SIZE] += mm(gs, query)
                gq += mm(k_t[:, span], gs)
            gq_ref[:, cols] = spin(gq.T * SCALE, cos_ref[...], -sin_ref[...]).astype(BF16)
            return carry

        for base in range(group * GROUP, (group + 1) * GROUP, 2):
            lax.fori_loop(0, 2, lambda i, carry, base=base: one_head(i, carry, base), 0)
            next(dense, None)
            next(rest, None)
        gkv_ref[:, keys] = (gkv[:, :HEAD_SIZE] * SCALE).astype(BF16)
        gkv_ref[:, values] = gkv[:, HEAD_SIZE:].astype(BF16)
    run_out(dense, rest)
    mixed_ref[...] = (middle_ref[...] + combined[...]).astype(BF16)
    for p, s in enumerate(strips):
        wo_out[:, columns(place.core, p)] = s.result[...].astype(F32)
        wo_out[:, columns(1 - place.core, p)] = s.near[3].astype(F32)
    sends.finish()


def attend_back(
    start, query, kv, grad, lse, cosine, sine, middle, grad_wo, back_out, collective_id
):
    rows, width = query.shape
    length = kv.shape[0]
    height = grad_wo.shape[2]
    quarter = width // 4
    return pl.pallas_call(
        attend_back_kernel,
        out_shape=[
            sds((rows, width), BF16),
            sds(kv.shape, BF16),
            sds((height, width), F32),
            sds((rows, width), BF16),
        ],
        in_specs=[VMEM] * 8 + [ANY] * 2,
        out_specs=[VMEM] * 4,
        scratch_shapes=[
            pltpu.VMEM((length, rows), F32),
            pltpu.VMEM((HEAD_SIZE, length), BF16),
            pltpu.VMEM((length, 2 * HEAD_SIZE), F32),
            pltpu.VMEM((length, rows), F32),
            pltpu.VMEM((length, rows), F32),
            pltpu.VMEM((rows, width), F32),
            *[pltpu.VMEM((4, 4, height, quarter), BF16)] * 2,
            *strip_buffers(height, quarter),
            *strip_buffers(height, quarter),
            *x_buffers(rows, width),
            semaphores(8),
            semaphores(60),
            semaphores(60),
        ],
        compiler_params=remote_params(collective_id, 60),
    )(start, query, kv, grad, lse, cosine, sine, middle, grad_wo, back_out)


def last_kernel(
    kv_terms, gq_ref, normed_ref, tokens_ref, gain_ref, cos_ref, sin_ref, grad_middle_ref,
    small_ref, w_hbm,
    grad_tokens_ref, wq_out, wk_out, wv_out, small_out,
    grads, small_total, w_ref, normed_t, lin_kv, kv_sum, *refs,
):
    place = Place()
    core = place.core
    neighbours = [place.partner, *place.x_to, *place.y_to, *place.z_to]
    greet(neighbours)
    bufs, x_bufs = refs[:18], refs[18:24]
    w_sem, local_sems, send_sems, recv_sems = refs[24:]
    load = pltpu.make_async_copy(w_hbm, w_ref, w_sem)
    load.start()
    await_greetings(neighbours)
    sends = Sends(send_sems, recv_sems)
    kv_steps = x_sum(place, sends, kv_terms, kv_sum, *x_bufs)
    next(kv_steps)
    strip = grads.shape[-1]
    wide = strip - HEAD_SIZE
    rows, width = normed_ref.shape
    height = grads.shape[3]

    def put(s, cols, right_side):
        got = mm(normed_t[...], right_side).astype(BF16)
        grads[s, :, :, :, cols] = got.reshape(4, 4, height, right_side.shape[1])

    normed_t[...] = normed_ref[...].astype(F32).T.astype(BF16)
    for s in range(4):
        put(s, pl.ds(0, wide), gq_ref[:, s * wide : (s + 1) * wide])
        next(kv_steps, None)
    run_out(kv_steps)
    cosine, sine = cos_ref[...], sin_ref[...]
    for s in range(4):
        got = kv_sum[:, s * HEAD_SIZE : (s + 1) * HEAD_SIZE]
        if s % 2 == 0:
            got = spin(got, cosine, -sine)
        got = got.astype(BF16)
        lin_kv[:, s * HEAD_SIZE : (s + 1) * HEAD_SIZE] = got
        put(s, pl.ds(wide, HEAD_SIZE), got)

    def source(s, y_first):
        if y_first:
            return lambda w: grads.at[s, w]
        return lambda w: grads.at[s, :, w]

    strips = [
        Strip(
            p == 0, grads.at[2 * core + p], bufs[6 * p : 6 * p + 6],
            None, source(2 * (1 - core) + p, p == 0),
        )
        for p in range(2)
    ]
    wide_steps = dp_sum(place, sends, strips, local_sems)
    next(wide_steps)
    next(wide_steps)

    load.wait()
    grad_normed = None
    for s in range(4):
        at = s * strip
        term = mm_nt(gq_ref[:, s * wide : (s + 1) * wide], w_ref[:, at : at + wide])
        term += mm_nt(
            lin_kv[:, s * HEAD_SIZE : (s + 1) * HEAD_SIZE], w_ref[:, at + wide : at + strip]
        )
        grad_normed = term if grad_normed is None else grad_normed + term
    grad_inputs, grad_gain = rms_back(tokens_ref[...].astype(F32), gain_ref[...], grad_normed)
    grad_tokens_ref[...] = grad_middle_ref[...] + grad_inputs
    lanes = lax.broadcasted_iota(jnp.int32, (width, 128), 1)
    small = jnp.where(
        lanes == EXPERTS + 1, as_column(grad_gain, 128), small_ref[...].astype(F32)
    )
    small_total[...] = small.astype(BF16).reshape(small_total.shape)
    small_strip = Strip(True, small_total, bufs[12:18])
    small_steps = dp_sum(place, sends, [small_strip], local_sems)
    next(small_steps)
    run_out(small_steps, wide_steps)
    small_out[...] = small_strip.result[...].astype(F32) + small_strip.near[3].astype(F32)
    for p, (s, other) in enumerate(zip(strips, (wk_out, wv_out))):
        for c, got in ((core, s.result[...]), (1 - core, s.near[3])):
            got = got.astype(F32)
            at = pl.multiple_of((2 * c + p) * wide, 128)
            wq_out[:, pl.ds(at, wide)] = got[:, :wide]
            at = pl.multiple_of(c * HEAD_SIZE, 128)
            other[:, pl.ds(at, HEAD_SIZE)] = got[:, wide:]
    sends.finish()


def last(
    kv_terms, grad_query, normed, tokens, gain, cosine, sine, grad_middle, small, w, collective_id
):
    rows, width = normed.shape
    total = w.shape[1]
    height, strip = width // 16, total // 4
    kv_width = total - width
    vmem = pltpu.VMEM
    return pl.pallas_call(
        last_kernel,
        out_shape=[
            sds((rows, width), F32),
            sds((height, width), F32),
            sds((height, kv_width // 2), F32),
            sds((height, kv_width // 2), F32),
            sds((height, 128), F32),
        ],
        in_specs=[ANY] + [VMEM] * 8 + [ANY],
        out_specs=[VMEM] * 5,
        scratch_shapes=[
            vmem((4, 4, 4, height, strip), BF16),
            vmem((4, 4, height, 128), BF16),
            vmem((width, total), BF16),
            vmem((width, rows), BF16),
            vmem((rows, kv_width), BF16),
            vmem((rows, kv_width), F32),
            *strip_buffers(height, strip),
            *strip_buffers(height, strip),
            *strip_buffers(height, 128, shared=False),
            *x_buffers(rows, kv_width),
            pltpu.SemaphoreType.DMA,
            semaphores(8),
            semaphores(80),
            semaphores(80),
        ],
        compiler_params=remote_params(collective_id, 60),
    )(kv_terms, grad_query, normed, tokens, gain, cosine, sine, grad_middle, small, w)


def widen_kernel(late_ref, sums_ref, g_out, u_out, d_out):
    high, ff = g_out.shape
    g_out[...] = sums_ref[0, :high, :ff].astype(F32)
    u_out[...] = sums_ref[0, :high, ff:].astype(F32)
    d_out[...] = sums_ref[0, high:].astype(F32)


def widen(sums, late):
    owners, high, width = sums.shape
    ff = width // 2
    gu, d = high * 2 // 3, high // 3
    spec = lambda a, b: pl.BlockSpec((a, b), lambda i: (i, 0))
    return pl.pallas_call(
        widen_kernel,
        grid=(owners,),
        out_shape=[
            sds((owners * gu, ff), F32), sds((owners * gu, ff), F32), sds((owners * d, width), F32)
        ],
        in_specs=[ANY, pl.BlockSpec((1, high, width), lambda i: (i, 0, 0))],
        out_specs=[spec(gu, ff), spec(gu, ff), spec(d, width)],
        cost_estimate=pl.CostEstimate(flops=0, bytes_accessed=21 * MIB, transcendentals=0),
    )(late, sums)


def on_device(
    tokens,
    d_out,
    gain_in,
    w_query,
    key_projection_weight,
    value_projection_weight,
    w_out,
    gain_mid,
    w_router,
    w_gate,
    w_up,
    w_down,
    routes,
    segments,
):
    rows, width = tokens.shape
    length = segments.shape[1]
    part = lax.axis_index("expert")
    seg_row = segments[0]
    offset = part * rows
    my_seg = lax.dynamic_slice_in_dim(seg_row, offset, rows, 0)
    start = jnp.sum((seg_row[None, :] < my_seg[:, None]).astype(jnp.int32), axis=1)
    angles = angles_for(offset + jnp.arange(rows, dtype=jnp.int32) - start)
    cosine, sine = jnp.cos(angles), jnp.sin(angles)
    cosine = jnp.concatenate([cosine, cosine], axis=1)
    sine = jnp.concatenate([-sine, sine], axis=1)
    start = start[None, :]

    small = jnp.concatenate([w_router, gain_mid[:, None], gain_in[:, None]], axis=1)
    small = jnp.pad(small, ((0, 0), (0, 128 - small.shape[1])))
    note = jnp.pad(routes.T, ((0, 8 - TOPK), (0, 0)))
    w_strips, small, upstream_all, notes = gather_first(
        w_query, key_projection_weight, value_projection_weight, small, d_out, note, 1
    )
    w_strips = w_strips.reshape(width, -1)
    small = small.reshape(width, -1)
    gain_mid_row = small[:, EXPERTS].astype(F32)[None, :]
    gain_in_row = small[:, EXPERTS + 1].astype(F32)[None, :]
    wo = gather_dense(w_out, part % 2)

    normed, query, kv_all = qkv(tokens, w_strips, gain_in_row, cosine, sine, 2)
    kv_all = kv_all.reshape(length, -1)
    context, lse = attend(start, query, kv_all)

    member = jnp.any(routes[:, :, None] == jnp.arange(128, dtype=jnp.int32), axis=1).astype(F32)
    chosen = jnp.any(notes[:, :TOPK] == part, axis=1)
    slots = jnp.where(chosen, jnp.cumsum(chosen.astype(jnp.int32), axis=1) - 1, -1)[:, None, :]
    middle, gates, gg, sums, own, back_out, w_grads = experts(
        context, tokens, small, gain_mid_row, member, slots, upstream_all,
        wo, w_gate[0], w_up[0], w_down[0], 3,
    )
    w_sums = lax.psum(w_grads.reshape(-1, *w_grads.shape[2:]), "dp")

    grad_middle, grad_ctx, small_grads, grad_wo = after(
        middle, gates, gg, sums, own, d_out, context, small, gain_mid_row, wo, 4
    )
    grad_wo = grad_wo.reshape(4, 4, width // 16, width)
    grad_query, kv_terms, g_wo, mixed = attend_back(
        start, query, kv_all, grad_ctx, lse, cosine, sine, middle, grad_wo, back_out, 5
    )
    grad_tokens, g_wq, g_wk, g_wv, small_sum = last(
        kv_terms.reshape(8, rows, -1), grad_query, normed, tokens, gain_in_row, cosine, sine,
        grad_middle, small_grads, w_strips, 6,
    )
    return (
        mixed,
        grad_tokens,
        small_sum[:, EXPERTS + 1],
        g_wq,
        g_wk,
        g_wv,
        g_wo,
        small_sum[:, EXPERTS],
        small_sum[:, :EXPERTS],
        *(g[None] for g in widen(w_sums, small_sum)),
    )


def solution(mesh):
    whole = P(("dp", "expert"), None)
    over_dp, by_dp, over_expert = P("dp"), P("dp", None), P("expert", None, None)
    return jax.shard_map(
        on_device,
        mesh=mesh,
        in_specs=(whole, whole, over_dp, by_dp, by_dp, by_dp, by_dp, over_dp, by_dp)
        + (over_expert,) * 3
        + (whole, by_dp),
        out_specs=(whole, whole, over_dp, by_dp, by_dp, by_dp, by_dp, over_dp, by_dp)
        + (over_expert,) * 3,
        check_vma=False,
    )
```

```python
import functools

import jax
import jax.numpy as jnp
from jax import lax
from jax.experimental import pallas as pl
from jax.experimental.pallas import tpu as pltpu
from jax.sharding import PartitionSpec as P

QUERY_HEADS = 12
KEY_VALUE_HEADS = 2
HEAD_SIZE = 128
TOPK = 4
EXPERTS = 8
GROUP = QUERY_HEADS // KEY_VALUE_HEADS
SCALE = HEAD_SIZE**-0.5
LOG2E = 1.4426950408889634
BLOCK = 512

EPSILON = 1e-06
ROPE_BASE = 1000000.0
MASK_FILL = -1e30
F32 = jnp.float32
BF16 = jnp.bfloat16

MESH = pl.DeviceIdType.MESH
ANY = pl.BlockSpec(memory_space=pl.ANY)
VMEM = pl.BlockSpec(memory_space=pltpu.VMEM)
MIB = 2**20


def dot(a, b, dims):
    return lax.dot_general(a, b, (dims, ((), ())), preferred_element_type=F32)


def mm(a, b):
    return dot(a, b, ((1,), (0,)))


def mm_nt(a, b):
    return dot(a, b, ((1,), (1,)))


def mm_tn(a, b):
    return dot(a, b, ((0,), (0,)))


def sds(shape, dtype):
    return jax.ShapeDtypeStruct(tuple(shape), dtype)


def remote_params(collective_id, mib):
    return pltpu.CompilerParams(
        collective_id=collective_id, has_side_effects=True, vmem_limit_bytes=mib * MIB
    )


def semaphores(count):
    return pltpu.SemaphoreType.DMA((count,))


def inverse_rms(rows):
    return lax.rsqrt(jnp.mean(rows * rows, axis=-1, keepdims=True) + EPSILON)


def rms_back(rows, gain, grad):
    inverse = inverse_rms(rows)
    scaled = rows * inverse
    weighted = grad * gain
    inner = jnp.mean(weighted * scaled, axis=-1, keepdims=True)
    return inverse * (weighted - scaled * inner), jnp.sum(grad * scaled, axis=0, keepdims=True)


def as_column(row, lanes):
    return jnp.broadcast_to(row, (lanes, row.shape[1])).T


def angles_for(positions):
    half_width = HEAD_SIZE // 2
    freqs = ROPE_BASE ** (-2.0 * jnp.arange(half_width, dtype=F32) / HEAD_SIZE)
    return positions.astype(F32)[:, None] * freqs[None, :]


def spin(z, cosine, sine):
    return z * cosine + pltpu.roll(z, HEAD_SIZE // 2, 1) * sine


class Sends:
    def __init__(self, send_sems, recv_sems):
        self.send_sems, self.recv_sems, self.made = send_sems, recv_sems, []

    def start(self, src, dst, to):
        at = len(self.made)
        copy = pltpu.make_async_remote_copy(
            src_ref=src,
            dst_ref=dst,
            send_sem=self.send_sems.at[at],
            recv_sem=self.recv_sems.at[at],
            device_id=to,
            device_id_type=MESH,
        )
        copy.start()
        self.made.append(copy)
        return copy

    def finish(self):
        for copy in self.made:
            copy.wait_send()


class Keeps:
    def __init__(self, sems):
        self.sems, self.made = sems, []

    def start(self, src, dst):
        copy = pltpu.make_async_copy(src, dst, self.sems.at[len(self.made)])
        copy.start()
        self.made.append(copy)
        return copy


class Place:
    def __init__(self):
        self.part = lax.axis_index("expert")
        self.core = self.part % 2
        self.chip = self.part // 2
        at = lambda d: lax.rem(self.chip + d, 4) * 2 + self.core
        self.right, self.left, self.far = at(1), at(3), at(2)
        to = lambda i: {"expert": i}
        self.partner = to(2 * self.chip + (1 - self.core))
        self.x_to = [to(self.right), to(self.left), to(self.far)]
        self.others = [to(lax.rem(self.part + d, 8)) for d in range(1, 8)]
        place = lax.axis_index("dp")
        self.y, self.z = place // 4, place % 4
        ring = lambda v: [lax.rem(v + d, 4) for d in (1, 3, 2)]
        self.y_ring, self.z_ring = ring(self.y), ring(self.z)
        self.y_to = [{"dp": v * 4 + self.z} for v in self.y_ring[:2]]
        self.z_to = [{"dp": self.y * 4 + v} for v in self.z_ring[:2]]

    def ring(self, along_y):
        if along_y:
            return self.y, self.y_ring, self.y_to
        return self.z, self.z_ring, self.z_to


def greet(others):
    barrier = pltpu.get_barrier_semaphore()
    for other in others:
        pl.semaphore_signal(barrier, inc=1, device_id=other, device_id_type=MESH)


def await_greetings(others):
    pl.semaphore_wait(pltpu.get_barrier_semaphore(), len(others))


def add_to(ref, *others):
    got = ref[...].astype(F32)
    for other in others:
        got += other[...].astype(F32)
    ref[...] = got.astype(ref.dtype)


def run_out(*steps):
    steps = list(steps)
    while steps:
        for s in list(steps):
            if next(s, "done") == "done":
                steps.remove(s)


def x_sum(place, sends, blocks_ref, out_ref, mine, theirs, total, from_left, from_right, sems):
    rows = out_ref.shape[0]
    half = rows // 2
    low, high = pl.ds(0, half), pl.ds(half, half)
    to_right, to_left = place.x_to[:2]
    flip = 1 - 2 * place.core
    keeps = Keeps(sems)
    swaps, loads = [], []
    for k, dest in enumerate((place.far, place.right, place.left, place.part)):
        swaps.append(sends.start(blocks_ref.at[dest + flip], theirs.at[k], place.partner))
        loads.append(keeps.start(blocks_ref.at[dest], mine.at[k]))

    def add_up(k):
        loads[k].wait()
        swaps[k].wait_recv()
        total[k] = (mine[k].astype(F32) + theirs[k].astype(F32)).astype(BF16)

    yield
    add_up(0)
    far_low = sends.start(total.at[0, low], from_left.at[0], to_right)
    far_high = sends.start(total.at[0, high], from_right.at[0], to_left)
    add_up(1)
    right_high = sends.start(total.at[1, high], from_left.at[2], to_right)
    add_up(2)
    left_low = sends.start(total.at[2, low], from_right.at[2], to_left)
    yield
    far_low.wait_recv()
    add_to(total.at[1, low], from_left.at[0])
    right_low = sends.start(total.at[1, low], from_left.at[1], to_right)
    far_high.wait_recv()
    add_to(total.at[2, high], from_right.at[0])
    left_high = sends.start(total.at[2, high], from_right.at[1], to_left)
    yield
    loads[3].wait()
    swaps[3].wait_recv()
    out_ref[...] = mine[3].astype(F32) + theirs[3].astype(F32)
    right_high.wait_recv()
    left_low.wait_recv()
    right_low.wait_recv()
    left_high.wait_recv()
    add_to(out_ref.at[low], from_left.at[1], from_right.at[2])
    add_to(out_ref.at[high], from_left.at[2], from_right.at[1])
    yield


def x_buffers(rows, columns):
    return [
        pltpu.VMEM((4, rows, columns), BF16),
        pltpu.VMEM((4, rows, columns), BF16),
        pltpu.VMEM((3, rows, columns), BF16),
        pltpu.VMEM((3, rows // 2, columns), BF16),
        pltpu.VMEM((3, rows // 2, columns), BF16),
        semaphores(4),
    ]


class Ring:
    def __init__(self, along_y, view, whole, farther):
        self.along_y, self.view, self.whole, self.farther = along_y, view, whole, farther


def ring_sum(place, sends, rings, ready=lambda *_: None):
    going = []
    for i, r in enumerate(rings):
        _, (right, left, far), to = place.ring(r.along_y)
        ready(0, i, far)
        going.append([sends.start(r.view(far, h), r.farther.at[h], to[h]) for h in range(2)])
    for i, r in enumerate(rings):
        _, (right, left, far), to = place.ring(r.along_y)
        ready(1, i, right)
        ready(2, i, left)
        going[i].append(sends.start(r.view(right, 1), r.whole.at[0, 1], to[0]))
        going[i].append(sends.start(r.view(left, 0), r.whole.at[1, 0], to[1]))
    yield
    for i, r in enumerate(rings):
        _, (right, left, far), to = place.ring(r.along_y)
        for h, w in enumerate((right, left)):
            going[i][h].wait_recv()
            add_to(r.view(w, h), r.farther.at[h])
            going[i].append(sends.start(r.view(w, h), r.whole.at[h, h], to[h]))
    yield
    for i, r in enumerate(rings):
        me, _, _ = place.ring(r.along_y)
        ready(3, i, me)
        for copy in going[i][2:]:
            copy.wait_recv()
        for h in range(2):
            add_to(r.view(me, h), r.whole.at[0, h], r.whole.at[1, h])


class Spread:
    def __init__(self, along_y, source, view, landed=lambda _: None):
        self.along_y, self.source, self.view, self.landed = along_y, source, view, landed


def ring_gather(place, sends, spreads):
    came, onward = [], []
    for s in spreads:
        me, _, to = place.ring(s.along_y)
        came.append([sends.start(s.source, s.view(me), to[h]) for h in range(2)])
    yield
    for s, copies in zip(spreads, came):
        _, (right, left, _), to = place.ring(s.along_y)
        onward.append([])
        for h, origin in enumerate((left, right)):
            copies[h].wait_recv()
            onward[-1].append(sends.start(s.view(origin, h), s.view(origin, h), to[h]))
            s.landed(s.view(origin))
    yield
    for s, copies in zip(spreads, onward):
        far = place.ring(s.along_y)[1][2]
        for h in range(2):
            copies[h].wait_recv()
            s.landed(s.view(far, h))
    yield


class Strip:
    def __init__(self, y_first, total, bufs, own=None, other=None):
        self.y_first, self.total, self.own, self.other = y_first, total, own, other
        self.theirs, self.big, self.far, self.mid, self.midfar, self.near = bufs

    def block(self, ref, w):
        return ref.at[w] if self.y_first else ref.at[:, w]


def strip_buffers(rows, columns, shared=True):
    return [
        pltpu.VMEM((4, 4, rows, columns) if shared else (1, 1, rows, columns), BF16),
        pltpu.VMEM((2, 2, 2, rows, columns), BF16),
        pltpu.VMEM((2, 2, rows, columns), BF16),
        pltpu.VMEM((2, 2, rows // 2, columns), BF16),
        pltpu.VMEM((2, rows // 2, columns), BF16),
        pltpu.VMEM((4, rows, columns), BF16),
    ]


def dp_sum(place, sends, strips, sems):
    y, z = place.y, place.z
    keeps = Keeps(sems)
    swaps, loads = {}, {}
    for k in range(4):
        for i, s in enumerate(strips):
            me, (right, left, far), _ = place.ring(s.y_first)
            w = (far, right, left, me)[k]
            if s.other is not None:
                swaps[k, i] = sends.start(s.other(w), s.block(s.theirs, w), place.partner)
            if s.own is not None:
                loads[k, i] = keeps.start(s.own(w), s.block(s.total, w))
    yield

    def joined(k, i, s, w):
        if s.own is not None:
            loads[k, i].wait()
        if s.other is not None:
            swaps[k, i].wait_recv()
            add_to(s.block(s.total, w), s.block(s.theirs, w))

    def big(s, w, h):
        span = pl.ds(2 * h, 2)
        return s.total.at[w, span] if s.y_first else s.total.at[span, w]

    def small(s, w, h):
        half = s.total.shape[2] // 2
        at = pl.ds(h * half, half)
        return s.total.at[y, w, at] if s.y_first else s.total.at[w, z, at]

    def rings(first):
        view = big if first else small
        return [
            Ring(
                s.y_first == first,
                functools.partial(view, s),
                s.big if first else s.mid,
                s.far if first else s.midfar,
            )
            for s in strips
        ]

    yield from ring_sum(place, sends, rings(True), lambda k, i, w: joined(k, i, strips[i], w))
    yield from ring_sum(place, sends, rings(False))

    shares, back = [], []
    for s in strips:
        shares.append(
            [sends.start(s.total.at[y, z], s.near.at[i], place.x_to[i]) for i in range(3)]
        )
    yield
    for s, share in zip(strips, shares):
        for copy in share:
            copy.wait_recv()
        got = s.total[y, z].astype(F32)
        for i in range(3):
            got += s.near[i].astype(F32)
        s.result = s.theirs.at[y, z] if s.other is not None else s.theirs.at[0, 0]
        s.result[...] = got.astype(BF16)
        back.append(sends.start(s.result, s.near.at[3], place.partner))
    yield
    for copy in back:
        copy.wait_recv()
    yield


def begin_kernel(
    wq_ref, wk_ref, wv_ref, wo_ref, small_ref, rows_ref, note_ref, tokens_ref, cos_ref, sin_ref,
    w_out, small_out, wo_part, rows_out, notes_out, normed_ref, query_ref, kv_ref,
    strips_ref, w_all, own_kv, local_sems, send_sems, recv_sems,
):
    place = Place()
    y, z, core, part = place.y, place.z, place.core, place.part
    neighbours = [*place.others, *place.y_to, *place.z_to]
    greet(neighbours)
    rows = wq_ref.shape[0]
    wide, narrow = wq_ref.shape[1] // 4, wk_ref.shape[1] // 2
    strip = wide + narrow
    for s in range(4):
        strips_ref[:, s * strip : s * strip + wide] = wq_ref[:, s * wide : (s + 1) * wide]
        other = (wk_ref, wv_ref)[s % 2]
        begin = s // 2 * narrow
        strips_ref[:, s * strip + wide : (s + 1) * strip] = other[:, begin : begin + narrow]
    await_greetings(neighbours)
    sends, keeps = Sends(send_sems, recv_sems), Keeps(local_sems)

    def columns(p, size):
        return pl.ds(pl.multiple_of((2 * core + p) * size, 128), size)

    across = []

    def send_across(view):
        across.append(sends.start(view, view, place.partner))

    def spread(first, src, out, cols, y_first, landed):
        def near(where, piece=None):
            at = pl.ds(0, rows) if piece is None else pl.ds(piece * rows // 2, rows // 2)
            return out.at[where, z, at, cols] if y_first else out.at[y, where, at, cols]

        def wider(where, piece=None):
            span = pl.ds(0, 4) if piece is None else pl.ds(2 * piece, 2)
            return out.at[span, where, :, cols] if y_first else out.at[where, span, :, cols]

        if first:
            return Spread(y_first, src, near)
        source = wider(z if y_first else y)
        landed(source)
        return Spread(not y_first, source, wider, landed)

    def both_strips(first):
        every = pl.ds(0, small_ref.shape[1])
        return [
            *(
                spread(
                    first, strips_ref.at[:, columns(p, strip)], w_all, columns(p, strip), p == 1,
                    send_across,
                )
                for p in range(2)
            ),
            spread(first, small_ref, small_out, every, False, lambda _: None),
        ]

    def out_spread(p):
        ring_of = (z, y)[p]

        def view(where, piece=None):
            at = pl.ds(0, rows) if piece is None else pl.ds(piece * rows // 2, rows // 2)
            return wo_part.at[p, where, at]

        keeps.start(wo_ref.at[:, columns(p, wide)], wo_part.at[p, ring_of])
        return Spread(p == 1, wo_ref.at[:, columns(p, wide)], view)

    first_steps = ring_gather(place, sends, [*both_strips(True), *map(out_spread, range(2))])
    next(first_steps)
    for p in range(2):
        w_all[y, z, :, columns(p, strip)] = strips_ref[:, columns(p, strip)]
    small_out[y, z] = small_ref[...]

    half = rows_ref.shape[0] // 2
    x_came = [sends.start(rows_ref, rows_out.at[part], to) for to in place.x_to[:2]]
    across.append(sends.start(rows_ref, rows_out.at[part], place.partner))
    across += [sends.start(note_ref, notes_out.at[part], to) for to in place.others]
    keeps.start(rows_ref, rows_out.at[part])
    keeps.start(note_ref, notes_out.at[part])
    next(first_steps)
    next(first_steps)
    second_steps = ring_gather(place, sends, both_strips(False))
    next(second_steps)
    far_rows = []
    for i, origin in enumerate((place.left, place.right)):
        x_came[i].wait_recv()
        view = rows_out.at[origin, pl.ds(i * half, half)]
        far_rows.append(sends.start(view, view, place.x_to[i]))
        send_across(rows_out.at[origin])
    next(second_steps)
    next(second_steps)
    for i in range(2):
        far_rows[i].wait_recv()
        send_across(rows_out.at[place.far, pl.ds(i * half, half)])
    for copy in across:
        copy.wait_recv()
    keeps.start(w_all, w_out)

    width = tokens_ref.shape[1]
    gain = small_out[...].reshape(width, -1).astype(F32).T[EXPERTS + 1 : EXPERTS + 2]
    cosine, sine = cos_ref[...], sin_ref[...]
    inputs = tokens_ref[...].astype(F32)
    normed_ref[...] = (inputs * inverse_rms(inputs) * gain).astype(BF16)

    def project(at, size):
        w = w_all[:, :, :, at : at + size].reshape(width, size)
        return mm(normed_ref[...], w)

    for s in range(4):
        got = project(s * strip + wide, HEAD_SIZE)
        if s % 2 == 0:
            got = spin(got, cosine, sine)
        own_kv[:, s * HEAD_SIZE : (s + 1) * HEAD_SIZE] = got.astype(BF16)

    def queries(s):
        got = project(s * strip, wide)
        for h in range(0, wide, HEAD_SIZE):
            head = spin(got[:, h : h + HEAD_SIZE], cosine, sine)
            query_ref[:, s * wide + h : s * wide + h + HEAD_SIZE] = head.astype(BF16)

    slot = kv_ref.at[part]
    kv_came = [sends.start(own_kv, slot, way) for way in place.x_to[:2]]
    kv_across = [sends.start(own_kv, slot, place.partner)]
    keeps.start(own_kv, slot)
    queries(0)
    queries(1)
    onward = []
    for i, origin in enumerate((place.left, place.right)):
        kv_came[i].wait_recv()
        view = kv_ref.at[origin, pl.ds(i * half, half)]
        onward.append(sends.start(view, view, place.x_to[i]))
        view = kv_ref.at[origin]
        kv_across.append(sends.start(view, view, place.partner))
    queries(2)
    queries(3)
    for i in range(2):
        onward[i].wait_recv()
        view = kv_ref.at[place.far, pl.ds(i * half, half)]
        kv_across.append(sends.start(view, view, place.partner))
    for copy in kv_across:
        copy.wait_recv()
    for copy in keeps.made:
        copy.wait()
    sends.finish()


def begin(wq, wk, wv, wo, small, rows, note, tokens, cosine, sine, collective_id):
    height, width = wq.shape
    kv_width = wk.shape[1] + wv.shape[1]
    total = width + kv_width
    count = tokens.shape[0]
    vmem = pltpu.VMEM
    return pl.pallas_call(
        begin_kernel,
        out_shape=[
            sds((4, 4, height, total), BF16),
            sds((4, 4, *small.shape), BF16),
            sds((2, 4, height, width // 4), BF16),
            sds((8, *rows.shape), BF16),
            sds((8, *note.shape), note.dtype),
            sds((count, width), BF16),
            sds((count, width), BF16),
            sds((8, count, kv_width), BF16),
        ],
        in_specs=[VMEM] * 10,
        out_specs=[ANY, VMEM, VMEM, ANY, ANY, VMEM, VMEM, ANY],
        scratch_shapes=[
            vmem((height, total), BF16),
            vmem((4, 4, height, total), BF16),
            vmem((count, kv_width), BF16),
            semaphores(6),
            semaphores(70),
            semaphores(70),
        ],
        compiler_params=remote_params(collective_id, 48),
    )(wq, wk, wv, wo, small, rows, note, tokens, cosine, sine)


def fill_bias(bias, start_ref, first_row):
    length, rows = bias.shape
    places = lax.broadcasted_iota(jnp.int32, (length, rows), 0)
    mine = first_row + lax.broadcasted_iota(jnp.int32, (length, rows), 1)
    keep = (places >= start_ref[...]) & (places <= mine)
    bias[...] = jnp.where(keep, 0.0, MASK_FILL)


def head_columns(head):
    return pl.ds(pl.multiple_of(head * HEAD_SIZE, HEAD_SIZE), HEAD_SIZE)


def attend_kernel(
    start_ref, q_ref, kv_ref, wo_part, ctx_ref, lse_ref, wo_all,
    bias, v_t, scores, local_sems, send_sems, recv_sems,
):
    place = Place()
    neighbours = [place.partner, *place.y_to, *place.z_to]
    greet(neighbours)
    length, rows = bias.shape
    fill_bias(bias, start_ref, rows * place.part)
    await_greetings(neighbours)
    sends, keeps = Sends(send_sems, recv_sems), Keeps(local_sems)
    quarter = wo_part.shape[-1]
    across = []

    def landed(view):
        across.append(sends.start(view, view, place.partner))

    def spread(p):
        cols = pl.ds(pl.multiple_of((2 * place.core + p) * quarter, 128), quarter)

        def view(where, piece=None):
            span = pl.ds(0, 4) if piece is None else pl.ds(2 * piece, 2)
            return wo_all.at[span, where, :, cols] if p else wo_all.at[where, span, :, cols]

        own = view((place.y, place.z)[p])
        keeps.start(wo_part.at[p], own)
        across.append(sends.start(wo_part.at[p], own, place.partner))
        return Spread(p == 0, wo_part.at[p], view, landed)

    steps = ring_gather(place, sends, [spread(p) for p in range(2)])
    next(steps)
    for group in range(KEY_VALUE_HEADS):
        keys = slice(2 * group * HEAD_SIZE, (2 * group + 1) * HEAD_SIZE)
        values = slice((2 * group + 1) * HEAD_SIZE, (2 * group + 2) * HEAD_SIZE)
        v_t[...] = kv_ref[:, values].astype(F32).T.astype(BF16)

        def one_head(i, carry, base):
            head = base + i
            query = q_ref[:, head_columns(head)]
            top = None
            for at in range(0, length, BLOCK):
                span = pl.ds(at, BLOCK)
                s = mm_nt(kv_ref[span, keys], query) + bias[span]
                scores[span] = s
                here = jnp.max(s, axis=0, keepdims=True)
                top = here if top is None else jnp.maximum(top, here)
            total = jnp.zeros_like(top)
            context = jnp.zeros((HEAD_SIZE, rows), F32)
            for at in range(0, length, BLOCK):
                span = pl.ds(at, BLOCK)
                p = jnp.exp2((scores[span] - top) * (SCALE * LOG2E))
                total += jnp.sum(p, axis=0, keepdims=True)
                context += mm(v_t[:, span], p.astype(BF16))
            ctx_ref[:, head_columns(head)] = (context / total).T.astype(BF16)
            lse_ref[head] = top * (SCALE * LOG2E) + jnp.log2(total)
            return carry

        for base in (group * GROUP, group * GROUP + GROUP // 2):
            lax.fori_loop(
                0, GROUP // 2, lambda i, carry, base=base: one_head(i, carry, base), 0
            )
            if base > 0:
                next(steps, None)
    run_out(steps)
    for copy in across:
        copy.wait_recv()
    for copy in keeps.made:
        copy.wait()
    sends.finish()


def attend(start, query, kv, wo_part, collective_id):
    rows, width = query.shape
    length = kv.shape[0]
    height = wo_part.shape[2]
    return pl.pallas_call(
        attend_kernel,
        out_shape=[
            sds((rows, width), BF16),
            sds((QUERY_HEADS, 1, rows), F32),
            sds((4, 4, height, width), BF16),
        ],
        in_specs=[VMEM] * 4,
        out_specs=[VMEM, VMEM, ANY],
        scratch_shapes=[
            pltpu.VMEM((length, rows), F32),
            pltpu.VMEM((HEAD_SIZE, length), BF16),
            pltpu.VMEM((length, rows), F32),
            semaphores(2),
            semaphores(20),
            semaphores(20),
        ],
        compiler_params=remote_params(collective_id, 40),
    )(start, query, kv, wo_part)


LOW, HIGH = 0, 1


def gelu_parts(a):
    k = (2.0 / jnp.pi) ** 0.5
    square = a * a
    t = jnp.tanh(k * a * (1.0 + 0.044715 * square))
    slope = 0.5 * (1.0 + t) + 0.5 * a * (1.0 - t * t) * k * (1.0 + 3 * 0.044715 * square)
    return 0.5 * a * (1.0 + t), slope


def experts_kernel(
    ctx_ref, tokens_ref, small_ref, gain_ref, member_ref, slot_ref,
    up_all, wo_hbm, wg_hbm, wu_hbm, wd_hbm,
    middle_ref, gates_ref, gg_all, sums_ref, own_ref, back_out, w_grads,
    wo_ref, wg_ref, wu_ref, wd_ref, rows_all, returns, arrived, pair_grad, hidden, grad_pre,
    theirs, far_left, far_right, from_left, from_right, tile, tile_d, back_rows, gates_all, gg_src,
    local_sems, tile_sems, back_sems, send_sems, recv_sems,
):
    place = Place()
    part, core = place.part, place.core
    right, left, far = place.right, place.left, place.far
    to_right, to_left = place.x_to[:2]
    greet(place.others)
    sends, keeps, stores = (
        Sends(send_sems, recv_sems), Keeps(local_sems), Keeps(back_sems)
    )
    rows, width = ctx_ref.shape
    half = rows // 2
    halves = (pl.ds(0, half), pl.ds(half, half))
    ff = wg_ref.shape[1]
    capacity = arrived.shape[0] // 8

    for src, dst in ((wo_hbm, wo_ref), (wg_hbm, wg_ref), (wu_hbm, wu_ref), (wd_hbm, wd_ref)):
        keeps.start(src, dst)
    chips = [lax.rem(place.chip + d, 4) for d in (0, 3, 1, 2)]
    for u in range(4):
        keeps.start(up_all.at[pl.ds(2 * chips[u], 2)], returns.at[u])

    keeps.made[0].wait()
    middle = tokens_ref[...].astype(F32) + mm(ctx_ref[...], wo_ref[...])
    middle_ref[...] = middle
    normed = (middle * inverse_rms(middle) * gain_ref[...]).astype(BF16)
    rows_all[part] = normed
    member = member_ref[...]
    logits = jnp.where(member > 0.0, mm(normed, small_ref[...]), MASK_FILL)
    weight = jnp.exp(logits - jnp.max(logits, axis=-1, keepdims=True)) * member
    gates = weight / jnp.sum(weight, axis=-1, keepdims=True)
    gates_ref[...] = gates.T[:EXPERTS]

    await_greetings(place.others)
    mine = rows_all.at[part]
    go_right = sends.start(mine, mine, to_right)
    go_left = sends.start(mine, mine, to_left)
    swap_own = sends.start(mine, mine, place.partner)
    note_sends = [sends.start(gates_ref, gates_all.at[part], to) for to in place.others]
    gates_all[part] = gates_ref[...]

    def pick_of(source):
        slots = lax.broadcasted_iota(jnp.int32, (capacity, rows), 0)
        return slots == slot_ref[source]

    for u in range(4):
        keeps.made[4 + u].wait()
        for c in range(2):
            pick = pick_of(2 * chips[u] + c).astype(BF16)
            got = mm(pick, returns[u, c])
            pair_grad[pl.ds((2 * u + c) * capacity, capacity)] = got.astype(BF16)
    for load in keeps.made[1:4]:
        load.wait()

    swaps, gg_sends = [], []

    def unit(u):
        at = chips[u]
        picks = [pick_of(2 * at + c) for c in range(2)]
        picks_b = [pick.astype(BF16) for pick in picks]
        spans = [pl.ds((2 * u + c) * capacity, capacity) for c in range(2)]
        both = pl.ds(2 * u * capacity, 2 * capacity)
        gate = []
        for c in range(2):
            arrived[spans[c]] = mm(picks_b[c], rows_all[2 * at + c]).astype(BF16)
            row = gates_all[2 * at + c, pl.ds(part, 1)]
            gate.append(jnp.sum(jnp.where(picks[c], row, 0.0), axis=-1, keepdims=True))
        gate = jnp.concatenate(gate, axis=0)
        x = arrived[both]
        a, b = mm(x, wg_ref[...]), mm(x, wu_ref[...])
        act, slope = gelu_parts(a)
        h = (act * b).astype(BF16)
        hidden[both] = h
        out = mm(h, wd_ref[...]).astype(BF16).astype(F32)
        up = pair_grad[both].astype(F32)
        gg = jnp.sum(up * out, axis=-1, keepdims=True)
        weighted = (gate * out).astype(BF16)
        pg = (gate * up).astype(BF16)
        pair_grad[both] = pg
        for c in range(2):
            if u > 0:
                stores.made[2 * (u - 1) + c].wait()
            back_rows[c] = mm_tn(picks_b[c], weighted[c * capacity : (c + 1) * capacity]).astype(
                BF16
            )
            stores.start(back_rows.at[c], back_out.at[2 * at + c])
            gg_c = gg[c * capacity : (c + 1) * capacity]
            row = jnp.sum(jnp.where(picks[c], gg_c, 0.0), axis=0, keepdims=True)
            gg_src[u, c] = jnp.broadcast_to(row, (8, rows))
        grad_h = mm_nt(pg, wd_ref[...])
        grad_a = (grad_h * b * slope).astype(BF16)
        grad_b = (grad_h * act).astype(BF16)
        grad_pre[both, :ff] = grad_a
        grad_pre[both, ff:] = grad_b
        grad_rows = (mm_nt(grad_a, wg_ref[...]) + mm_nt(grad_b, wu_ref[...])).astype(BF16)
        for c in range(2):
            returns[u, c] = mm_tn(
                picks_b[c], grad_rows[c * capacity : (c + 1) * capacity]
            ).astype(BF16)
        swaps.append(sends.start(returns.at[u, 1 - core], theirs.at[u], place.partner))
        if u == 0:
            gg_all[part] = gg_src[0, core]
            gg_sends.append(sends.start(gg_src.at[0, 1 - core], gg_all.at[part], place.partner))
        else:
            for c in (core, 1 - core):
                gg_sends.append(
                    sends.start(gg_src.at[u, c], gg_all.at[part], {"expert": 2 * at + c})
                )

    def joined(u):
        swaps[u].wait_recv()
        add_to(theirs.at[u], returns.at[u, core])

    swap_own.wait_recv()
    for copy in note_sends:
        copy.wait_recv()
    unit(0)
    go_right.wait_recv()
    first = rows_all.at[left, halves[LOW]]
    far_low = sends.start(first, first, to_right)
    swap_left = sends.start(rows_all.at[left], rows_all.at[left], place.partner)
    go_left.wait_recv()
    second = rows_all.at[right, halves[HIGH]]
    far_high = sends.start(second, second, to_left)
    swap_right = sends.start(rows_all.at[right], rows_all.at[right], place.partner)
    swap_left.wait_recv()
    unit(1)
    swap_right.wait_recv()
    unit(2)
    swap_far = []
    for h, copy in enumerate((far_low, far_high)):
        copy.wait_recv()
        piece = rows_all.at[far, halves[h]]
        swap_far.append(sends.start(piece, piece, place.partner))
    joined(1)
    joined(2)
    back_right = sends.start(theirs.at[2, halves[HIGH]], from_left, to_right)
    back_left = sends.start(theirs.at[1, halves[LOW]], from_right, to_left)
    for copy in swap_far:
        copy.wait_recv()
    unit(3)
    joined(3)
    back_far_low = sends.start(theirs.at[3, halves[LOW]], far_left, to_right)
    back_far_high = sends.start(theirs.at[3, halves[HIGH]], far_right, to_left)

    tall = 4 * w_grads.shape[2] * 2 // 3
    high = tall // 4
    w_stores = Keeps(tile_sems)
    for i in range(ff // tall):
        got = mm_tn(hidden[:, i * tall : (i + 1) * tall], pair_grad[...]).astype(BF16)
        tile_d[i] = got.reshape(tile_d.shape[1:])
        w_stores.start(tile_d.at[i], w_grads.at[pl.ds(2 * i, 2), :, pl.ds(high, high // 2)])
    for i in range(width // tall):
        if i >= 2:
            w_stores.made[ff // tall + i - 2].wait()
        got = mm_tn(arrived[:, i * tall : (i + 1) * tall], grad_pre[...]).astype(BF16)
        tile[i % 2] = got.reshape(tile.shape[1:])
        w_stores.start(tile.at[i % 2], w_grads.at[i, :, pl.ds(0, high)])

    swaps[0].wait_recv()
    back_right.wait_recv()
    back_left.wait_recv()
    own_ref[...] = theirs[0].astype(F32) + returns[0, core].astype(F32)
    add_to(own_ref.at[halves[HIGH]], from_left)
    add_to(own_ref.at[halves[LOW]], from_right)
    back_far_low.wait_recv()
    sums_ref[0] = (theirs[2, halves[LOW]].astype(F32) + far_left[...].astype(F32)).astype(BF16)
    back_far_high.wait_recv()
    sums_ref[1] = (theirs[1, halves[HIGH]].astype(F32) + far_right[...].astype(F32)).astype(BF16)
    for copy in gg_sends:
        copy.wait_recv()
    for copy in [*stores.made[6:], *w_stores.made[: ff // tall], *w_stores.made[-2:]]:
        copy.wait()
    sends.finish()


def experts(ctx, tokens, small, gain, member, slots, up_all, wo, wg, wu, wd, collective_id):
    rows, width = ctx.shape
    ff = wg.shape[1]
    capacity = rows * 9 // 16
    high = width // 16
    vmem = pltpu.VMEM
    return pl.pallas_call(
        experts_kernel,
        out_shape=[
            sds((rows, width), F32),
            sds((EXPERTS, rows), F32),
            sds((8, 8, rows), F32),
            sds((2, rows // 2, width), BF16),
            sds((rows, width), F32),
            sds((8, rows, width), BF16),
            sds((4, 4, high * 3 // 2, width), BF16),
        ],
        in_specs=[VMEM] * 6 + [ANY] * 5,
        out_specs=[VMEM] * 5 + [ANY] * 2,
        scratch_shapes=[
            vmem((width, width), BF16),
            vmem((width, ff), BF16),
            vmem((width, ff), BF16),
            vmem((ff, width), BF16),
            vmem((8, rows, width), BF16),
            vmem((4, 2, rows, width), BF16),
            vmem((8 * capacity, width), BF16),
            vmem((8 * capacity, width), BF16),
            vmem((8 * capacity, ff), BF16),
            vmem((8 * capacity, 2 * ff), BF16),
            vmem((4, rows, width), BF16),
            *[vmem((rows // 2, width), BF16)] * 4,
            vmem((2, 4, high, width), BF16),
            vmem((2, 2, 4, high // 2, width), BF16),
            vmem((2, rows, width), BF16),
            vmem((8, EXPERTS, rows), F32),
            vmem((4, 2, 8, rows), F32),
            semaphores(8),
            semaphores(6),
            semaphores(8),
            semaphores(40),
            semaphores(40),
        ],
        compiler_params=remote_params(collective_id, 63),
    )(ctx, tokens, small, gain, member, slots, up_all, wo, wg, wu, wd)


def after_kernel(
    middle_ref, gates_ref, gg_all, sums_ref, own_ref, d_out_ref, ctx_ref, small_ref, gain_ref,
    wo_ref, w_grads, grad_middle_ref, grad_ctx_ref, small_grad_ref, grad_wo_ref, w_part,
    from_left, from_right, w_total_0, w_total_1, w_whole, w_far, local_sems, send_sems, recv_sems,
):
    place = Place()
    neighbours = [*place.x_to[:2], *place.y_to, *place.z_to]
    greet(neighbours)
    keeps = Keeps(local_sems)
    cols = w_total_0.shape[-1]
    totals = (w_total_0, w_total_1)

    def part_of(ref, p, w):
        return ref.at[:, w] if p else ref.at[w]

    loads = {}
    for k in range(4):
        for p in range(2):
            me, (right, left, far), _ = place.ring(p == 0)
            w = (far, right, left, me)[k]
            src = part_of(w_grads, p, w).at[:, :, pl.ds(p * cols, cols)]
            loads[k, p] = keeps.start(src, part_of(totals[p], p, w))
    await_greetings(neighbours)
    sends = Sends(send_sems, recv_sems)

    def halves_of(p):
        def view(w, h):
            span = pl.ds(2 * h, 2)
            return totals[p].at[span, w] if p else totals[p].at[w, span]

        return view

    rings = [Ring(p == 0, halves_of(p), w_whole.at[p], w_far.at[p]) for p in range(2)]
    steps = ring_sum(place, sends, rings, lambda k, i, w: loads[k, i].wait())
    came = [
        sends.start(sums_ref.at[i], dst, place.x_to[i])
        for i, dst in enumerate((from_left, from_right))
    ]
    next(steps)
    rows, width = middle_ref.shape
    grad_gates = jnp.concatenate([gg_all[e, :1] for e in range(EXPERTS)], axis=0)
    gates_t = gates_ref[...]
    products = gates_t * grad_gates
    grad_logits = products - gates_t * jnp.sum(products, axis=0, keepdims=True)
    grad_logits = jnp.concatenate(
        [grad_logits, jnp.zeros((128 - EXPERTS, rows), F32)], axis=0
    ).T.astype(BF16)
    total = own_ref[...] + mm_nt(grad_logits, small_ref[...])
    middle, gain = middle_ref[...], gain_ref[...]
    inverse = inverse_rms(middle)
    scaled = middle * inverse
    small_grad = mm_tn((scaled * gain).astype(BF16), grad_logits)
    next(steps)
    for copy in came:
        copy.wait_recv()
    total += jnp.concatenate([from_left[...], from_right[...]], axis=0).astype(F32)
    grad_gain = jnp.sum(total * scaled, axis=0, keepdims=True)
    lanes = lax.broadcasted_iota(jnp.int32, (width, 128), 1)
    small_grad += jnp.where(lanes == EXPERTS, as_column(grad_gain, 128), 0.0)
    small_grad_ref[...] = small_grad.astype(BF16)
    weighted = total * gain
    inner = jnp.mean(weighted * scaled, axis=-1, keepdims=True)
    grad_middle = d_out_ref[...].astype(F32) + inverse * (weighted - scaled * inner)
    grad_middle_ref[...] = grad_middle
    grad_attn = grad_middle.astype(BF16)
    grad_ctx_ref[...] = mm_nt(grad_attn, wo_ref[...]).astype(BF16)
    tall = 256
    for at in range(0, width, tall):
        grad_wo_ref[pl.ds(at, tall)] = mm_tn(ctx_ref[:, at : at + tall], grad_attn).astype(BF16)
    run_out(steps)
    w_part[0] = w_total_0[place.y]
    w_part[1] = w_total_1[:, place.z]
    sends.finish()


def after(middle, gates, gg, sums, own, d_out, ctx, small, gain, wo, w_grads, collective_id):
    rows, width = middle.shape
    high, cols = w_grads.shape[2], width // 2
    return pl.pallas_call(
        after_kernel,
        out_shape=[
            sds((rows, width), F32),
            sds((rows, width), BF16),
            sds((width, 128), BF16),
            sds((width, width), BF16),
            sds((2, 4, high, cols), BF16),
        ],
        in_specs=[VMEM] * 10 + [ANY],
        out_specs=[VMEM] * 5,
        scratch_shapes=[
            pltpu.VMEM((rows // 2, width), BF16),
            pltpu.VMEM((rows // 2, width), BF16),
            pltpu.VMEM((4, 4, high, cols), BF16),
            pltpu.VMEM((4, 4, high, cols), BF16),
            pltpu.VMEM((2, 2, 2, 2, high, cols), BF16),
            pltpu.VMEM((2, 2, 2, high, cols), BF16),
            semaphores(8),
            semaphores(14),
            semaphores(14),
        ],
        compiler_params=remote_params(collective_id, 62),
    )(middle, gates, gg, sums, own, d_out, ctx, small, gain, wo, w_grads)


def attend_back_kernel(
    start_ref, q_ref, kv_ref, g_ref, lse_ref, cos_ref, sin_ref, middle_ref, wo_grads, blocks_ref,
    w_part, gq_ref, gkv_ref, wo_out, mixed_ref, w_done,
    bias, k_t, gkv, probs, grad_probs, combined, w_total, w_whole, w_far, w_sem, *refs,
):
    place = Place()
    neighbours = [place.partner, *place.x_to, *place.y_to, *place.z_to]
    greet(neighbours)
    load = pltpu.make_async_copy(w_part, w_total, w_sem)
    load.start()
    totals, bufs, x_bufs = refs[:2], refs[2:14], refs[14:20]
    local_sems, send_sems, recv_sems = refs[20:]
    length, rows = bias.shape
    fill_bias(bias, start_ref, rows * place.part)
    await_greetings(neighbours)
    sends = Sends(send_sems, recv_sems)
    quarter = wo_grads.shape[3] // 4

    def columns(c, p):
        return pl.ds(pl.multiple_of((2 * c + p) * quarter, 128), quarter)

    def source(c, p):
        cols = columns(c, p)
        if p == 0:
            return lambda w: wo_grads.at[w, :, :, cols]
        return lambda w: wo_grads.at[:, w, :, cols]

    strips = [
        Strip(
            p == 0, totals[p], bufs[6 * p : 6 * p + 6],
            source(place.core, p), source(1 - place.core, p),
        )
        for p in range(2)
    ]
    dense = dp_sum(place, sends, strips, local_sems)
    rest = x_sum(place, sends, blocks_ref, combined, *x_bufs)

    def expert_steps():
        cols = w_total.shape[-1] // 2

        def halves_of(p):
            return lambda w, h: w_total.at[p, w, :, pl.ds(h * cols, cols)]

        load.wait()
        rings = [Ring(p == 1, halves_of(p), w_whole.at[p], w_far.at[p]) for p in range(2)]
        yield from ring_sum(place, sends, rings)
        spreads = []
        for p in range(2):
            me = place.ring(p == 1)[0]
            w_done[p, me] = w_total[p, me]

            def view(w, h=None, p=p):
                every = pl.ds(0, 2 * cols) if h is None else pl.ds(h * cols, cols)
                return w_done.at[p, w, :, every]

            spreads.append(Spread(p == 1, w_done.at[p, me], view))
        yield from ring_gather(place, sends, spreads)

    own_expert = expert_steps()
    next(dense)
    next(own_expert)
    next(rest)

    for group in range(KEY_VALUE_HEADS):
        keys = slice(2 * group * HEAD_SIZE, (2 * group + 1) * HEAD_SIZE)
        values = slice((2 * group + 1) * HEAD_SIZE, (2 * group + 2) * HEAD_SIZE)
        k_t[...] = kv_ref[:, keys].astype(F32).T.astype(BF16)
        gkv[...] = jnp.zeros_like(gkv)

        def one_head(i, carry, base):
            head = base + i
            cols = pl.ds(pl.multiple_of(head * HEAD_SIZE, HEAD_SIZE), HEAD_SIZE)
            query, grad = q_ref[:, cols], g_ref[:, cols]
            lse = lse_ref[head]
            inner = jnp.zeros_like(lse)
            for at in range(0, length, BLOCK):
                span = pl.ds(at, BLOCK)
                s = mm_nt(kv_ref[span, keys], query) + bias[span]
                p = jnp.exp2(s * (SCALE * LOG2E) - lse)
                gp = mm_nt(kv_ref[span, values], grad)
                inner += jnp.sum(p * gp, axis=0, keepdims=True)
                probs[span] = p
                grad_probs[span] = gp
                gkv[span, HEAD_SIZE:] += mm(p.astype(BF16), grad)
            gq = jnp.zeros((HEAD_SIZE, rows), F32)
            for at in range(0, length, BLOCK):
                span = pl.ds(at, BLOCK)
                gs = (probs[span] * (grad_probs[span] - inner)).astype(BF16)
                gkv[span, :HEAD_SIZE] += mm(gs, query)
                gq += mm(k_t[:, span], gs)
            gq_ref[:, cols] = spin(gq.T * SCALE, cos_ref[...], -sin_ref[...]).astype(BF16)
            return carry

        for base in range(group * GROUP, (group + 1) * GROUP, 2):
            lax.fori_loop(0, 2, lambda i, carry, base=base: one_head(i, carry, base), 0)
            next(own_expert, None)
            next(dense, None)
            next(rest, None)
        gkv_ref[:, keys] = (gkv[:, :HEAD_SIZE] * SCALE).astype(BF16)
        gkv_ref[:, values] = gkv[:, HEAD_SIZE:].astype(BF16)
    run_out(own_expert, dense, rest)
    mixed_ref[...] = (middle_ref[...] + combined[...]).astype(BF16)
    for p, s in enumerate(strips):
        wo_out[:, columns(place.core, p)] = s.result[...].astype(F32)
        wo_out[:, columns(1 - place.core, p)] = s.near[3].astype(F32)
    sends.finish()


def attend_back(
    start, query, kv, grad, lse, cosine, sine, middle, grad_wo, back_out, w_part, collective_id
):
    rows, width = query.shape
    length = kv.shape[0]
    height = grad_wo.shape[2]
    quarter = width // 4
    high, cols = w_part.shape[2:]
    return pl.pallas_call(
        attend_back_kernel,
        out_shape=[
            sds((rows, width), BF16),
            sds(kv.shape, BF16),
            sds((height, width), F32),
            sds((rows, width), BF16),
            sds(w_part.shape, BF16),
        ],
        in_specs=[VMEM] * 8 + [ANY] * 3,
        out_specs=[VMEM] * 5,
        scratch_shapes=[
            pltpu.VMEM((length, rows), F32),
            pltpu.VMEM((HEAD_SIZE, length), BF16),
            pltpu.VMEM((length, 2 * HEAD_SIZE), F32),
            pltpu.VMEM((length, rows), F32),
            pltpu.VMEM((length, rows), F32),
            pltpu.VMEM((rows, width), F32),
            pltpu.VMEM(w_part.shape, BF16),
            pltpu.VMEM((2, 2, 2, high, cols // 2), BF16),
            pltpu.VMEM((2, 2, high, cols // 2), BF16),
            pltpu.SemaphoreType.DMA,
            *[pltpu.VMEM((4, 4, height, quarter), BF16)] * 2,
            *strip_buffers(height, quarter),
            *strip_buffers(height, quarter),
            *x_buffers(rows, width),
            semaphores(8),
            semaphores(90),
            semaphores(90),
        ],
        compiler_params=remote_params(collective_id, 60),
    )(start, query, kv, grad, lse, cosine, sine, middle, grad_wo, back_out, w_part)


def last_kernel(
    kv_terms, gq_ref, normed_ref, tokens_ref, gain_ref, cos_ref, sin_ref, grad_middle_ref,
    small_ref, w_done, w_hbm,
    grad_tokens_ref, wq_out, wk_out, wv_out, small_out, w_sums,
    grads, small_total, w_ref, normed_t, lin_kv, kv_sum, *refs,
):
    place = Place()
    core = place.core
    neighbours = [place.partner, *place.x_to, *place.y_to, *place.z_to]
    greet(neighbours)
    bufs, x_bufs = refs[:18], refs[18:24]
    w_sem, local_sems, send_sems, recv_sems = refs[24:]
    load = pltpu.make_async_copy(w_hbm, w_ref, w_sem)
    load.start()
    await_greetings(neighbours)
    sends, keeps = Sends(send_sems, recv_sems), Keeps(local_sems)
    kv_steps = x_sum(place, sends, kv_terms, kv_sum, *x_bufs)
    next(kv_steps)

    def spread(p):
        cols = pl.ds(p * w_done.shape[-1], w_done.shape[-1])

        def view(w, h=None):
            span = pl.ds(0, 4) if h is None else pl.ds(2 * h, 2)
            return w_sums.at[span, w, :, cols] if p else w_sums.at[w, span, :, cols]

        keeps.start(w_done.at[p], view(place.ring(p == 0)[0]))
        return Spread(p == 0, w_done.at[p], view)

    expert_steps = ring_gather(place, sends, [spread(p) for p in range(2)])
    next(expert_steps)
    strip = grads.shape[-1]
    wide = strip - HEAD_SIZE
    rows, width = normed_ref.shape
    height = grads.shape[3]

    def put(s, cols, right_side):
        got = mm(normed_t[...], right_side).astype(BF16)
        grads[s, :, :, :, cols] = got.reshape(4, 4, height, right_side.shape[1])

    normed_t[...] = normed_ref[...].astype(F32).T.astype(BF16)
    for s in range(4):
        put(s, pl.ds(0, wide), gq_ref[:, s * wide : (s + 1) * wide])
        next(kv_steps, None)
    run_out(kv_steps)
    next(expert_steps)
    cosine, sine = cos_ref[...], sin_ref[...]
    for s in range(4):
        got = kv_sum[:, s * HEAD_SIZE : (s + 1) * HEAD_SIZE]
        if s % 2 == 0:
            got = spin(got, cosine, -sine)
        got = got.astype(BF16)
        lin_kv[:, s * HEAD_SIZE : (s + 1) * HEAD_SIZE] = got
        put(s, pl.ds(wide, HEAD_SIZE), got)

    def source(s, y_first):
        if y_first:
            return lambda w: grads.at[s, w]
        return lambda w: grads.at[s, :, w]

    strips = [
        Strip(
            p == 0, grads.at[2 * core + p], bufs[6 * p : 6 * p + 6],
            None, source(2 * (1 - core) + p, p == 0),
        )
        for p in range(2)
    ]
    wide_steps = dp_sum(place, sends, strips, ())
    next(wide_steps)
    next(wide_steps)

    load.wait()
    grad_normed = None
    for s in range(4):
        at = s * strip
        term = mm_nt(gq_ref[:, s * wide : (s + 1) * wide], w_ref[:, at : at + wide])
        term += mm_nt(
            lin_kv[:, s * HEAD_SIZE : (s + 1) * HEAD_SIZE], w_ref[:, at + wide : at + strip]
        )
        grad_normed = term if grad_normed is None else grad_normed + term
    grad_inputs, grad_gain = rms_back(tokens_ref[...].astype(F32), gain_ref[...], grad_normed)
    grad_tokens_ref[...] = grad_middle_ref[...] + grad_inputs
    lanes = lax.broadcasted_iota(jnp.int32, (width, 128), 1)
    small = jnp.where(
        lanes == EXPERTS + 1, as_column(grad_gain, 128), small_ref[...].astype(F32)
    )
    small_total[...] = small.astype(BF16).reshape(small_total.shape)
    small_strip = Strip(True, small_total, bufs[12:18])
    small_steps = dp_sum(place, sends, [small_strip], ())
    next(small_steps)
    run_out(small_steps, wide_steps, expert_steps)
    small_out[...] = small_strip.result[...].astype(F32) + small_strip.near[3].astype(F32)
    for p, (s, other) in enumerate(zip(strips, (wk_out, wv_out))):
        for c, got in ((core, s.result[...]), (1 - core, s.near[3])):
            got = got.astype(F32)
            at = pl.multiple_of((2 * c + p) * wide, 128)
            wq_out[:, pl.ds(at, wide)] = got[:, :wide]
            at = pl.multiple_of(c * HEAD_SIZE, 128)
            other[:, pl.ds(at, HEAD_SIZE)] = got[:, wide:]
    for copy in keeps.made:
        copy.wait()
    sends.finish()


def last(
    kv_terms, grad_query, normed, tokens, gain, cosine, sine, grad_middle, small, w_done, w,
    collective_id,
):
    rows, width = normed.shape
    total = w.shape[1]
    height, strip = width // 16, total // 4
    kv_width = total - width
    vmem = pltpu.VMEM
    return pl.pallas_call(
        last_kernel,
        out_shape=[
            sds((rows, width), F32),
            sds((height, width), F32),
            sds((height, kv_width // 2), F32),
            sds((height, kv_width // 2), F32),
            sds((height, 128), F32),
            sds((4, 4, w_done.shape[2], width), BF16),
        ],
        in_specs=[ANY] + [VMEM] * 9 + [ANY],
        out_specs=[VMEM] * 5 + [ANY],
        scratch_shapes=[
            vmem((4, 4, 4, height, strip), BF16),
            vmem((4, 4, height, 128), BF16),
            vmem((width, total), BF16),
            vmem((width, rows), BF16),
            vmem((rows, kv_width), BF16),
            vmem((rows, kv_width), F32),
            *strip_buffers(height, strip),
            *strip_buffers(height, strip),
            *strip_buffers(height, 128, shared=False),
            *x_buffers(rows, kv_width),
            pltpu.SemaphoreType.DMA,
            semaphores(2),
            semaphores(90),
            semaphores(90),
        ],
        compiler_params=remote_params(collective_id, 60),
    )(kv_terms, grad_query, normed, tokens, gain, cosine, sine, grad_middle, small, w_done, w)


def widen_kernel(sums_ref, g_out, u_out, d_out):
    owners, high, width = sums_ref.shape
    ff = width // 2
    gu = high * 2 // 3
    g_out[...] = sums_ref[:, :gu, :ff].astype(F32).reshape(owners * gu, ff)
    u_out[...] = sums_ref[:, :gu, ff:].astype(F32).reshape(owners * gu, ff)
    d_out[...] = sums_ref[:, gu:].astype(F32).reshape(owners * (high - gu), width)


def widen(sums):
    owners, high, width = sums.shape
    ff = width // 2
    gu, d = high * 2 // 3, high // 3
    each = 2
    spec = lambda a, b: pl.BlockSpec((each * a, b), lambda i: (i, 0))
    return pl.pallas_call(
        widen_kernel,
        grid=(owners // each,),
        out_shape=[
            sds((owners * gu, ff), F32), sds((owners * gu, ff), F32), sds((owners * d, width), F32)
        ],
        in_specs=[pl.BlockSpec((each, high, width), lambda i: (i, 0, 0))],
        out_specs=[spec(gu, ff), spec(gu, ff), spec(d, width)],
        compiler_params=pltpu.CompilerParams(vmem_limit_bytes=32 * MIB),
        cost_estimate=pl.CostEstimate(flops=0, bytes_accessed=21 * MIB, transcendentals=0),
    )(sums)


def on_device(
    tokens,
    d_out,
    gain_in,
    w_query,
    key_projection_weight,
    value_projection_weight,
    w_out,
    gain_mid,
    w_router,
    w_gate,
    w_up,
    w_down,
    routes,
    segments,
):
    rows, width = tokens.shape
    length = segments.shape[1]
    part = lax.axis_index("expert")
    seg_row = segments[0]
    offset = part * rows
    my_seg = lax.dynamic_slice_in_dim(seg_row, offset, rows, 0)
    start = jnp.sum((seg_row[None, :] < my_seg[:, None]).astype(jnp.int32), axis=1)
    angles = angles_for(offset + jnp.arange(rows, dtype=jnp.int32) - start)
    cosine, sine = jnp.cos(angles), jnp.sin(angles)
    cosine = jnp.concatenate([cosine, cosine], axis=1)
    sine = jnp.concatenate([-sine, sine], axis=1)
    start = start[None, :]

    small = jnp.concatenate([w_router, gain_mid[:, None], gain_in[:, None]], axis=1)
    small = jnp.pad(small, ((0, 0), (0, 128 - small.shape[1])))
    note = jnp.pad(routes.T, ((0, 8 - TOPK), (0, 0)))
    w_strips, small, wo_part, upstream_all, notes, normed, query, kv_all = begin(
        w_query, key_projection_weight, value_projection_weight, w_out, small, d_out, note,
        tokens, cosine, sine, 1,
    )
    w_strips = w_strips.reshape(width, -1)
    small = small.reshape(width, -1)
    gain_mid_row = small[:, EXPERTS].astype(F32)[None, :]
    gain_in_row = small[:, EXPERTS + 1].astype(F32)[None, :]
    kv_all = kv_all.reshape(length, -1)
    context, lse, wo = attend(start, query, kv_all, wo_part, 2)
    wo = wo.reshape(width, width)

    member = jnp.any(routes[:, :, None] == jnp.arange(128, dtype=jnp.int32), axis=1).astype(F32)
    chosen = jnp.any(notes[:, :TOPK] == part, axis=1)
    slots = jnp.where(chosen, jnp.cumsum(chosen.astype(jnp.int32), axis=1) - 1, -1)[:, None, :]
    middle, gates, gg, sums, own, back_out, w_grads = experts(
        context, tokens, small, gain_mid_row, member, slots, upstream_all,
        wo, w_gate[0], w_up[0], w_down[0], 3,
    )
    grad_middle, grad_ctx, small_grads, grad_wo, w_part = after(
        middle, gates, gg, sums, own, d_out, context, small, gain_mid_row, wo, w_grads, 4
    )
    grad_wo = grad_wo.reshape(4, 4, width // 16, width)
    grad_query, kv_terms, g_wo, mixed, w_done = attend_back(
        start, query, kv_all, grad_ctx, lse, cosine, sine, middle, grad_wo, back_out, w_part, 5
    )
    grad_tokens, g_wq, g_wk, g_wv, small_sum, w_sums = last(
        kv_terms.reshape(8, rows, -1), grad_query, normed, tokens, gain_in_row, cosine, sine,
        grad_middle, small_grads, w_done, w_strips, 6,
    )
    return (
        mixed,
        grad_tokens,
        small_sum[:, EXPERTS + 1],
        g_wq,
        g_wk,
        g_wv,
        g_wo,
        small_sum[:, EXPERTS],
        small_sum[:, :EXPERTS],
        *(g[None] for g in widen(w_sums.reshape(16, -1, width))),
    )


def solution(mesh):
    whole = P(("dp", "expert"), None)
    over_dp, by_dp, over_expert = P("dp"), P("dp", None), P("expert", None, None)
    return jax.shard_map(
        on_device,
        mesh=mesh,
        in_specs=(whole, whole, over_dp, by_dp, by_dp, by_dp, by_dp, over_dp, by_dp)
        + (over_expert,) * 3
        + (whole, by_dp),
        out_specs=(whole, whole, over_dp, by_dp, by_dp, by_dp, by_dp, over_dp, by_dp)
        + (over_expert,) * 3,
        check_vma=False,
    )
```

```python
import functools

import jax
import jax.numpy as jnp
from jax import lax
from jax.experimental import pallas as pl
from jax.experimental.pallas import tpu as pltpu
from jax.sharding import PartitionSpec as P

QUERY_HEADS = 12
KEY_VALUE_HEADS = 2
HEAD_SIZE = 128
TOPK = 4
EXPERTS = 8
GROUP = QUERY_HEADS // KEY_VALUE_HEADS
SCALE = HEAD_SIZE**-0.5
LOG2E = 1.4426950408889634
BLOCK = 512

EPSILON = 1e-06
ROPE_BASE = 1000000.0
MASK_FILL = -1e30
F32 = jnp.float32
BF16 = jnp.bfloat16

MESH = pl.DeviceIdType.MESH
ANY = pl.BlockSpec(memory_space=pl.ANY)
VMEM = pl.BlockSpec(memory_space=pltpu.VMEM)
MIB = 2**20


def dot(a, b, dims):
    return lax.dot_general(a, b, (dims, ((), ())), preferred_element_type=F32)


def mm(a, b):
    return dot(a, b, ((1,), (0,)))


def mm_nt(a, b):
    return dot(a, b, ((1,), (1,)))


def mm_tn(a, b):
    return dot(a, b, ((0,), (0,)))


def sds(shape, dtype):
    return jax.ShapeDtypeStruct(tuple(shape), dtype)


def remote_params(collective_id, mib):
    return pltpu.CompilerParams(
        collective_id=collective_id, has_side_effects=True, vmem_limit_bytes=mib * MIB
    )


def semaphores(count):
    return pltpu.SemaphoreType.DMA((count,))


def inverse_rms(rows):
    return lax.rsqrt(jnp.mean(rows * rows, axis=-1, keepdims=True) + EPSILON)


def rms_back(rows, gain, grad):
    inverse = inverse_rms(rows)
    scaled = rows * inverse
    weighted = grad * gain
    inner = jnp.mean(weighted * scaled, axis=-1, keepdims=True)
    return inverse * (weighted - scaled * inner), jnp.sum(grad * scaled, axis=0, keepdims=True)


def as_column(row, lanes):
    return jnp.broadcast_to(row, (lanes, row.shape[1])).T


def angles_for(positions):
    half_width = HEAD_SIZE // 2
    freqs = ROPE_BASE ** (-2.0 * jnp.arange(half_width, dtype=F32) / HEAD_SIZE)
    return positions.astype(F32)[:, None] * freqs[None, :]


def spin(z, cosine, sine):
    return z * cosine + pltpu.roll(z, HEAD_SIZE // 2, 1) * sine


class Sends:
    def __init__(self, send_sems, recv_sems):
        self.send_sems, self.recv_sems, self.made = send_sems, recv_sems, []

    def start(self, src, dst, to):
        at = len(self.made)
        copy = pltpu.make_async_remote_copy(
            src_ref=src,
            dst_ref=dst,
            send_sem=self.send_sems.at[at],
            recv_sem=self.recv_sems.at[at],
            device_id=to,
            device_id_type=MESH,
        )
        copy.start()
        self.made.append(copy)
        return copy

    def finish(self):
        for copy in self.made:
            copy.wait_send()


class Keeps:
    def __init__(self, sems):
        self.sems, self.made = sems, []

    def start(self, src, dst):
        copy = pltpu.make_async_copy(src, dst, self.sems.at[len(self.made)])
        copy.start()
        self.made.append(copy)
        return copy


class Place:
    def __init__(self):
        self.part = lax.axis_index("expert")
        self.core = self.part % 2
        self.chip = self.part // 2
        at = lambda d: lax.rem(self.chip + d, 4) * 2 + self.core
        self.right, self.left, self.far = at(1), at(3), at(2)
        to = lambda i: {"expert": i}
        self.partner = to(2 * self.chip + (1 - self.core))
        self.x_to = [to(self.right), to(self.left), to(self.far)]
        self.others = [to(lax.rem(self.part + d, 8)) for d in range(1, 8)]
        place = lax.axis_index("dp")
        self.y, self.z = place // 4, place % 4
        ring = lambda v: [lax.rem(v + d, 4) for d in (1, 3, 2)]
        self.y_ring, self.z_ring = ring(self.y), ring(self.z)
        self.y_to = [{"dp": v * 4 + self.z} for v in self.y_ring[:2]]
        self.z_to = [{"dp": self.y * 4 + v} for v in self.z_ring[:2]]

    def ring(self, along_y):
        if along_y:
            return self.y, self.y_ring, self.y_to
        return self.z, self.z_ring, self.z_to


def greet(others):
    barrier = pltpu.get_barrier_semaphore()
    for other in others:
        pl.semaphore_signal(barrier, inc=1, device_id=other, device_id_type=MESH)


def await_greetings(others):
    pl.semaphore_wait(pltpu.get_barrier_semaphore(), len(others))


def add_to(ref, *others):
    got = ref[...].astype(F32)
    for other in others:
        got += other[...].astype(F32)
    ref[...] = got.astype(ref.dtype)


def run_out(*steps):
    steps = list(steps)
    while steps:
        for s in list(steps):
            if next(s, "done") == "done":
                steps.remove(s)


def x_sum(place, sends, blocks_ref, out_ref, mine, total, from_left, from_right, sems):
    rows = out_ref.shape[0]
    half = rows // 2
    low, high = pl.ds(0, half), pl.ds(half, half)
    to_right, to_left = place.x_to[:2]
    flip = 1 - 2 * place.core
    keeps = Keeps(sems)
    swaps, loads = [], []
    for k, dest in enumerate((place.far, place.right, place.left, place.part)):
        swaps.append(sends.start(blocks_ref.at[dest + flip], total.at[k], place.partner))
        loads.append(keeps.start(blocks_ref.at[dest], mine.at[k]))

    def add_up(k):
        loads[k].wait()
        swaps[k].wait_recv()
        add_to(total.at[k], mine.at[k])

    yield
    add_up(0)
    far_low = sends.start(total.at[0, low], from_left.at[0], to_right)
    far_high = sends.start(total.at[0, high], from_right.at[0], to_left)
    add_up(1)
    right_high = sends.start(total.at[1, high], from_left.at[2], to_right)
    add_up(2)
    left_low = sends.start(total.at[2, low], from_right.at[2], to_left)
    yield
    far_low.wait_recv()
    add_to(total.at[1, low], from_left.at[0])
    right_low = sends.start(total.at[1, low], from_left.at[1], to_right)
    far_high.wait_recv()
    add_to(total.at[2, high], from_right.at[0])
    left_high = sends.start(total.at[2, high], from_right.at[1], to_left)
    yield
    loads[3].wait()
    swaps[3].wait_recv()
    out_ref[...] = mine[3].astype(F32) + total[3].astype(F32)
    right_high.wait_recv()
    left_low.wait_recv()
    right_low.wait_recv()
    left_high.wait_recv()
    add_to(out_ref.at[low], from_left.at[1], from_right.at[2])
    add_to(out_ref.at[high], from_left.at[2], from_right.at[1])
    yield


def x_buffers(rows, columns):
    return [
        pltpu.VMEM((4, rows, columns), BF16),
        pltpu.VMEM((4, rows, columns), BF16),
        pltpu.VMEM((3, rows // 2, columns), BF16),
        pltpu.VMEM((3, rows // 2, columns), BF16),
        semaphores(4),
    ]


class Ring:
    def __init__(self, along_y, view, whole, farther):
        self.along_y, self.view, self.whole, self.farther = along_y, view, whole, farther


def ring_sum(place, sends, rings, ready=lambda *_: None):
    going = []
    for i, r in enumerate(rings):
        _, (right, left, far), to = place.ring(r.along_y)
        ready(0, i, far)
        going.append([sends.start(r.view(far, h), r.farther.at[h], to[h]) for h in range(2)])
    for i, r in enumerate(rings):
        _, (right, left, far), to = place.ring(r.along_y)
        ready(1, i, right)
        ready(2, i, left)
        going[i].append(sends.start(r.view(right, 1), r.whole.at[0, 1], to[0]))
        going[i].append(sends.start(r.view(left, 0), r.whole.at[1, 0], to[1]))
    yield
    for i, r in enumerate(rings):
        _, (right, left, far), to = place.ring(r.along_y)
        for h, w in enumerate((right, left)):
            going[i][h].wait_recv()
            add_to(r.view(w, h), r.farther.at[h])
            going[i].append(sends.start(r.view(w, h), r.whole.at[h, h], to[h]))
    yield
    for i, r in enumerate(rings):
        me, _, _ = place.ring(r.along_y)
        ready(3, i, me)
        for copy in going[i][2:]:
            copy.wait_recv()
        for h in range(2):
            add_to(r.view(me, h), r.whole.at[0, h], r.whole.at[1, h])


class Spread:
    def __init__(self, along_y, source, view, landed=lambda _: None):
        self.along_y, self.source, self.view, self.landed = along_y, source, view, landed


def ring_gather(place, sends, spreads):
    came, onward = [], []
    for s in spreads:
        me, _, to = place.ring(s.along_y)
        came.append([sends.start(s.source, s.view(me), to[h]) for h in range(2)])
    yield
    for s, copies in zip(spreads, came):
        _, (right, left, _), to = place.ring(s.along_y)
        onward.append([])
        for h, origin in enumerate((left, right)):
            copies[h].wait_recv()
            onward[-1].append(sends.start(s.view(origin, h), s.view(origin, h), to[h]))
            s.landed(s.view(origin))
    yield
    for s, copies in zip(spreads, onward):
        far = place.ring(s.along_y)[1][2]
        for h in range(2):
            copies[h].wait_recv()
            s.landed(s.view(far, h))
    yield


class Strip:
    def __init__(self, y_first, total, bufs, own=None, other=None):
        self.y_first, self.total, self.own, self.other = y_first, total, own, other
        self.theirs, self.big, self.far, self.mid, self.midfar, self.near = bufs

    def block(self, ref, w):
        return ref.at[w] if self.y_first else ref.at[:, w]


def strip_buffers(rows, columns, shared=True):
    return [
        pltpu.VMEM((4, 4, rows, columns) if shared else (1, 1, rows, columns), BF16),
        pltpu.VMEM((2, 2, 2, rows, columns), BF16),
        pltpu.VMEM((2, 2, rows, columns), BF16),
        pltpu.VMEM((2, 2, rows // 2, columns), BF16),
        pltpu.VMEM((2, rows // 2, columns), BF16),
        pltpu.VMEM((4, rows, columns), BF16),
    ]


def dp_sum(place, sends, strips, sems):
    y, z = place.y, place.z
    keeps = Keeps(sems)
    swaps, loads = {}, {}
    for k in range(4):
        for i, s in enumerate(strips):
            me, (right, left, far), _ = place.ring(s.y_first)
            w = (far, right, left, me)[k]
            if s.other is not None:
                swaps[k, i] = sends.start(s.other(w), s.block(s.theirs, w), place.partner)
            if s.own is not None:
                loads[k, i] = keeps.start(s.own(w), s.block(s.total, w))
    yield

    def joined(k, i, s, w):
        if s.own is not None:
            loads[k, i].wait()
        if s.other is not None:
            swaps[k, i].wait_recv()
            add_to(s.block(s.total, w), s.block(s.theirs, w))

    def big(s, w, h):
        span = pl.ds(2 * h, 2)
        return s.total.at[w, span] if s.y_first else s.total.at[span, w]

    def small(s, w, h):
        half = s.total.shape[2] // 2
        at = pl.ds(h * half, half)
        return s.total.at[y, w, at] if s.y_first else s.total.at[w, z, at]

    def rings(first):
        view = big if first else small
        return [
            Ring(
                s.y_first == first,
                functools.partial(view, s),
                s.big if first else s.mid,
                s.far if first else s.midfar,
            )
            for s in strips
        ]

    yield from ring_sum(place, sends, rings(True), lambda k, i, w: joined(k, i, strips[i], w))
    yield from ring_sum(place, sends, rings(False))

    shares, back = [], []
    for s in strips:
        shares.append(
            [sends.start(s.total.at[y, z], s.near.at[i], place.x_to[i]) for i in range(3)]
        )
    yield
    for s, share in zip(strips, shares):
        for copy in share:
            copy.wait_recv()
        got = s.total[y, z].astype(F32)
        for i in range(3):
            got += s.near[i].astype(F32)
        s.result = s.theirs.at[y, z] if s.other is not None else s.theirs.at[0, 0]
        s.result[...] = got.astype(BF16)
        back.append(sends.start(s.result, s.near.at[3], place.partner))
    yield
    for copy in back:
        copy.wait_recv()
    yield


def begin_kernel(
    wq_hbm, wk_hbm, wv_hbm, wo_hbm, small_ref, rows_hbm, note_ref, tokens_hbm, cos_ref, sin_ref,
    w_out, small_out, wo_part, rows_out, notes_out, normed_ref, query_ref, kv_ref,
    strips_ref, w_all, own_kv, wq_ref, wk_ref, wv_ref, wo_ref, rows_ref, tokens_ref,
    fetch_sems, local_sems, send_sems, recv_sems,
):
    fetches = Keeps(fetch_sems)
    for src, dst in (
        (wq_hbm, wq_ref), (wk_hbm, wk_ref), (wv_hbm, wv_ref), (wo_hbm, wo_ref),
        (rows_hbm, rows_ref), (tokens_hbm, tokens_ref),
    ):
        fetches.start(src, dst)
    place = Place()
    y, z, core, part = place.y, place.z, place.core, place.part
    neighbours = [*place.others, *place.y_to, *place.z_to]
    greet(neighbours)
    rows = wq_ref.shape[0]
    wide, narrow = wq_ref.shape[1] // 4, wk_ref.shape[1] // 2
    strip = wide + narrow
    for fetch in fetches.made[:4]:
        fetch.wait()
    for s in range(4):
        strips_ref[:, s * strip : s * strip + wide] = wq_ref[:, s * wide : (s + 1) * wide]
        other = (wk_ref, wv_ref)[s % 2]
        begin = s // 2 * narrow
        strips_ref[:, s * strip + wide : (s + 1) * strip] = other[:, begin : begin + narrow]
    await_greetings(neighbours)
    sends, keeps = Sends(send_sems, recv_sems), Keeps(local_sems)

    def columns(p, size):
        return pl.ds(pl.multiple_of((2 * core + p) * size, 128), size)

    across = []

    def send_across(view):
        across.append(sends.start(view, view, place.partner))

    def spread(first, src, out, cols, y_first, landed):
        def near(where, piece=None):
            at = pl.ds(0, rows) if piece is None else pl.ds(piece * rows // 2, rows // 2)
            return out.at[where, z, at, cols] if y_first else out.at[y, where, at, cols]

        def wider(where, piece=None):
            span = pl.ds(0, 4) if piece is None else pl.ds(2 * piece, 2)
            return out.at[span, where, :, cols] if y_first else out.at[where, span, :, cols]

        if first:
            return Spread(y_first, src, near)
        source = wider(z if y_first else y)
        landed(source)
        return Spread(not y_first, source, wider, landed)

    def both_strips(first):
        every = pl.ds(0, small_ref.shape[1])
        return [
            *(
                spread(
                    first, strips_ref.at[:, columns(p, strip)], w_all, columns(p, strip), p == 1,
                    send_across,
                )
                for p in range(2)
            ),
            spread(first, small_ref, small_out, every, False, lambda _: None),
        ]

    def out_spread(p):
        ring_of = (z, y)[p]

        def view(where, piece=None):
            at = pl.ds(0, rows) if piece is None else pl.ds(piece * rows // 2, rows // 2)
            return wo_part.at[p, where, at]

        keeps.start(wo_ref.at[:, columns(p, wide)], wo_part.at[p, ring_of])
        return Spread(p == 1, wo_ref.at[:, columns(p, wide)], view)

    first_steps = ring_gather(place, sends, [*both_strips(True), *map(out_spread, range(2))])
    next(first_steps)
    for p in range(2):
        w_all[y, z, :, columns(p, strip)] = strips_ref[:, columns(p, strip)]
    small_out[y, z] = small_ref[...]

    half = rows_ref.shape[0] // 2
    fetches.made[4].wait()
    x_came = [sends.start(rows_ref, rows_out.at[part], to) for to in place.x_to[:2]]
    across.append(sends.start(rows_ref, rows_out.at[part], place.partner))
    across += [sends.start(note_ref, notes_out.at[part], to) for to in place.others]
    keeps.start(rows_ref, rows_out.at[part])
    keeps.start(note_ref, notes_out.at[part])
    next(first_steps)
    next(first_steps)
    second_steps = ring_gather(place, sends, both_strips(False))
    next(second_steps)
    far_rows = []
    for i, origin in enumerate((place.left, place.right)):
        x_came[i].wait_recv()
        view = rows_out.at[origin, pl.ds(i * half, half)]
        far_rows.append(sends.start(view, view, place.x_to[i]))
        send_across(rows_out.at[origin])
    next(second_steps)
    next(second_steps)
    for i in range(2):
        far_rows[i].wait_recv()
        send_across(rows_out.at[place.far, pl.ds(i * half, half)])
    for copy in across:
        copy.wait_recv()
    keeps.start(w_all, w_out)

    width = tokens_ref.shape[1]
    gain = small_out[...].reshape(width, -1).astype(F32).T[EXPERTS + 1 : EXPERTS + 2]
    cosine, sine = cos_ref[...], sin_ref[...]
    fetches.made[5].wait()
    inputs = tokens_ref[...].astype(F32)
    normed_ref[...] = (inputs * inverse_rms(inputs) * gain).astype(BF16)

    def project(at, size):
        w = w_all[:, :, :, at : at + size].reshape(width, size)
        return mm(normed_ref[...], w)

    for s in range(4):
        got = project(s * strip + wide, HEAD_SIZE)
        if s % 2 == 0:
            got = spin(got, cosine, sine)
        own_kv[:, s * HEAD_SIZE : (s + 1) * HEAD_SIZE] = got.astype(BF16)

    def queries(s):
        got = project(s * strip, wide)
        for h in range(0, wide, HEAD_SIZE):
            head = spin(got[:, h : h + HEAD_SIZE], cosine, sine)
            query_ref[:, s * wide + h : s * wide + h + HEAD_SIZE] = head.astype(BF16)

    slot = kv_ref.at[part]
    kv_came = [sends.start(own_kv, slot, way) for way in place.x_to[:2]]
    kv_across = [sends.start(own_kv, slot, place.partner)]
    keeps.start(own_kv, slot)
    queries(0)
    queries(1)
    onward = []
    for i, origin in enumerate((place.left, place.right)):
        kv_came[i].wait_recv()
        view = kv_ref.at[origin, pl.ds(i * half, half)]
        onward.append(sends.start(view, view, place.x_to[i]))
        view = kv_ref.at[origin]
        kv_across.append(sends.start(view, view, place.partner))
    queries(2)
    queries(3)
    for i in range(2):
        onward[i].wait_recv()
        view = kv_ref.at[place.far, pl.ds(i * half, half)]
        kv_across.append(sends.start(view, view, place.partner))
    for copy in kv_across:
        copy.wait_recv()
    for copy in keeps.made:
        copy.wait()
    sends.finish()


def begin(wq, wk, wv, wo, small, rows, note, tokens, cosine, sine, collective_id):
    height, width = wq.shape
    kv_width = wk.shape[1] + wv.shape[1]
    total = width + kv_width
    count = tokens.shape[0]
    vmem = pltpu.VMEM
    return pl.pallas_call(
        begin_kernel,
        out_shape=[
            sds((4, 4, height, total), BF16),
            sds((4, 4, *small.shape), BF16),
            sds((2, 4, height, width // 4), BF16),
            sds((8, *rows.shape), BF16),
            sds((8, *note.shape), note.dtype),
            sds((count, width), BF16),
            sds((count, width), BF16),
            sds((8, count, kv_width), BF16),
        ],
        in_specs=[ANY] * 4 + [VMEM, ANY, VMEM, ANY, VMEM, VMEM],
        out_specs=[ANY, VMEM, VMEM, ANY, ANY, VMEM, VMEM, ANY],
        scratch_shapes=[
            vmem((height, total), BF16),
            vmem((4, 4, height, total), BF16),
            vmem((count, kv_width), BF16),
            *[vmem(a.shape, BF16) for a in (wq, wk, wv, wo, rows, tokens)],
            semaphores(6),
            semaphores(6),
            semaphores(70),
            semaphores(70),
        ],
        compiler_params=remote_params(collective_id, 48),
    )(wq, wk, wv, wo, small, rows, note, tokens, cosine, sine)


def fill_bias(bias, start_ref, first_row):
    length, rows = bias.shape
    places = lax.broadcasted_iota(jnp.int32, (length, rows), 0)
    mine = first_row + lax.broadcasted_iota(jnp.int32, (length, rows), 1)
    keep = (places >= start_ref[...]) & (places <= mine)
    bias[...] = jnp.where(keep, 0.0, MASK_FILL)


def head_columns(head):
    return pl.ds(pl.multiple_of(head * HEAD_SIZE, HEAD_SIZE), HEAD_SIZE)


def attend_kernel(
    start_ref, q_ref, kv_ref, wo_part, ctx_ref, lse_ref, wo_all,
    bias, v_t, scores, local_sems, send_sems, recv_sems,
):
    place = Place()
    neighbours = [place.partner, *place.y_to, *place.z_to]
    greet(neighbours)
    length, rows = bias.shape
    fill_bias(bias, start_ref, rows * place.part)
    await_greetings(neighbours)
    sends, keeps = Sends(send_sems, recv_sems), Keeps(local_sems)
    quarter = wo_part.shape[-1]
    across = []

    def landed(view):
        across.append(sends.start(view, view, place.partner))

    def spread(p):
        cols = pl.ds(pl.multiple_of((2 * place.core + p) * quarter, 128), quarter)

        def view(where, piece=None):
            span = pl.ds(0, 4) if piece is None else pl.ds(2 * piece, 2)
            return wo_all.at[span, where, :, cols] if p else wo_all.at[where, span, :, cols]

        own = view((place.y, place.z)[p])
        keeps.start(wo_part.at[p], own)
        across.append(sends.start(wo_part.at[p], own, place.partner))
        return Spread(p == 0, wo_part.at[p], view, landed)

    steps = ring_gather(place, sends, [spread(p) for p in range(2)])
    next(steps)
    for group in range(KEY_VALUE_HEADS):
        keys = slice(2 * group * HEAD_SIZE, (2 * group + 1) * HEAD_SIZE)
        values = slice((2 * group + 1) * HEAD_SIZE, (2 * group + 2) * HEAD_SIZE)
        v_t[...] = kv_ref[:, values].astype(F32).T.astype(BF16)

        def one_head(i, carry, base):
            head = base + i
            query = q_ref[:, head_columns(head)]
            top = None
            for at in range(0, length, BLOCK):
                span = pl.ds(at, BLOCK)
                s = mm_nt(kv_ref[span, keys], query) + bias[span]
                scores[span] = s
                here = jnp.max(s, axis=0, keepdims=True)
                top = here if top is None else jnp.maximum(top, here)
            total = jnp.zeros_like(top)
            context = jnp.zeros((HEAD_SIZE, rows), F32)
            for at in range(0, length, BLOCK):
                span = pl.ds(at, BLOCK)
                p = jnp.exp2((scores[span] - top) * (SCALE * LOG2E))
                total += jnp.sum(p, axis=0, keepdims=True)
                context += mm(v_t[:, span], p.astype(BF16))
            ctx_ref[:, head_columns(head)] = (context / total).T.astype(BF16)
            lse_ref[head] = top * (SCALE * LOG2E) + jnp.log2(total)
            return carry

        for base in (group * GROUP, group * GROUP + GROUP // 2):
            lax.fori_loop(
                0, GROUP // 2, lambda i, carry, base=base: one_head(i, carry, base), 0
            )
            if base > 0:
                next(steps, None)
    run_out(steps)
    for copy in across:
        copy.wait_recv()
    for copy in keeps.made:
        copy.wait()
    sends.finish()


def attend(start, query, kv, wo_part, collective_id):
    rows, width = query.shape
    length = kv.shape[0]
    height = wo_part.shape[2]
    return pl.pallas_call(
        attend_kernel,
        out_shape=[
            sds((rows, width), BF16),
            sds((QUERY_HEADS, 1, rows), F32),
            sds((4, 4, height, width), BF16),
        ],
        in_specs=[VMEM] * 4,
        out_specs=[VMEM, VMEM, ANY],
        scratch_shapes=[
            pltpu.VMEM((length, rows), F32),
            pltpu.VMEM((HEAD_SIZE, length), BF16),
            pltpu.VMEM((length, rows), F32),
            semaphores(2),
            semaphores(20),
            semaphores(20),
        ],
        compiler_params=remote_params(collective_id, 40),
    )(start, query, kv, wo_part)


LOW, HIGH = 0, 1


def gelu_parts(a):
    k = (2.0 / jnp.pi) ** 0.5
    square = a * a
    t = jnp.tanh(k * a * (1.0 + 0.044715 * square))
    slope = 0.5 * (1.0 + t) + 0.5 * a * (1.0 - t * t) * k * (1.0 + 3 * 0.044715 * square)
    return 0.5 * a * (1.0 + t), slope


def experts_kernel(
    ctx_ref, tokens_ref, small_ref, gain_ref, member_ref, slot_ref,
    up_all, wo_hbm, wg_hbm, wu_hbm, wd_hbm,
    middle_ref, gates_ref, gg_all, sums_ref, own_ref, back_out, w_grads,
    wo_ref, wg_ref, wu_ref, wd_ref, rows_all, returns, arrived, pair_grad, hidden, grad_pre,
    theirs, far_left, far_right, from_left, from_right, tile, tile_d, back_rows, gates_all, gg_src,
    local_sems, tile_sems, back_sems, send_sems, recv_sems,
):
    place = Place()
    part, core = place.part, place.core
    right, left, far = place.right, place.left, place.far
    to_right, to_left = place.x_to[:2]
    greet(place.others)
    sends, keeps, stores = (
        Sends(send_sems, recv_sems), Keeps(local_sems), Keeps(back_sems)
    )
    rows, width = ctx_ref.shape
    half = rows // 2
    halves = (pl.ds(0, half), pl.ds(half, half))
    ff = wg_ref.shape[1]
    capacity = arrived.shape[0] // 8

    for src, dst in ((wo_hbm, wo_ref), (wg_hbm, wg_ref), (wu_hbm, wu_ref), (wd_hbm, wd_ref)):
        keeps.start(src, dst)
    chips = [lax.rem(place.chip + d, 4) for d in (0, 3, 1, 2)]
    for u in range(4):
        keeps.start(up_all.at[pl.ds(2 * chips[u], 2)], returns.at[u])

    keeps.made[0].wait()
    middle = tokens_ref[...].astype(F32) + mm(ctx_ref[...], wo_ref[...])
    middle_ref[...] = middle
    normed = (middle * inverse_rms(middle) * gain_ref[...]).astype(BF16)
    rows_all[part] = normed
    member = member_ref[...]
    logits = jnp.where(member > 0.0, mm(normed, small_ref[...]), MASK_FILL)
    weight = jnp.exp(logits - jnp.max(logits, axis=-1, keepdims=True)) * member
    gates = weight / jnp.sum(weight, axis=-1, keepdims=True)
    gates_ref[...] = gates.T[:EXPERTS]

    await_greetings(place.others)
    mine = rows_all.at[part]
    go_right = sends.start(mine, mine, to_right)
    go_left = sends.start(mine, mine, to_left)
    swap_own = sends.start(mine, mine, place.partner)
    note_sends = [sends.start(gates_ref, gates_all.at[part], to) for to in place.others]
    gates_all[part] = gates_ref[...]

    def pick_of(source):
        slots = lax.broadcasted_iota(jnp.int32, (capacity, rows), 0)
        return slots == slot_ref[source]

    for u in range(4):
        keeps.made[4 + u].wait()
        for c in range(2):
            pick = pick_of(2 * chips[u] + c).astype(BF16)
            got = mm(pick, returns[u, c])
            pair_grad[pl.ds((2 * u + c) * capacity, capacity)] = got.astype(BF16)
    for load in keeps.made[1:4]:
        load.wait()

    swaps, gg_sends = [], []

    def unit(u):
        at = chips[u]
        picks = [pick_of(2 * at + c) for c in range(2)]
        picks_b = [pick.astype(BF16) for pick in picks]
        spans = [pl.ds((2 * u + c) * capacity, capacity) for c in range(2)]
        both = pl.ds(2 * u * capacity, 2 * capacity)
        gate = []
        for c in range(2):
            arrived[spans[c]] = mm(picks_b[c], rows_all[2 * at + c]).astype(BF16)
            row = gates_all[2 * at + c, pl.ds(part, 1)]
            gate.append(jnp.sum(jnp.where(picks[c], row, 0.0), axis=-1, keepdims=True))
        gate = jnp.concatenate(gate, axis=0)
        x = arrived[both]
        a, b = mm(x, wg_ref[...]), mm(x, wu_ref[...])
        act, slope = gelu_parts(a)
        h = (act * b).astype(BF16)
        hidden[both] = h
        out = mm(h, wd_ref[...]).astype(BF16).astype(F32)
        up = pair_grad[both].astype(F32)
        gg = jnp.sum(up * out, axis=-1, keepdims=True)
        weighted = (gate * out).astype(BF16)
        pg = (gate * up).astype(BF16)
        pair_grad[both] = pg
        for c in range(2):
            if u > 0:
                stores.made[2 * (u - 1) + c].wait()
            back_rows[c] = mm_tn(picks_b[c], weighted[c * capacity : (c + 1) * capacity]).astype(
                BF16
            )
            stores.start(back_rows.at[c], back_out.at[2 * at + c])
            gg_c = gg[c * capacity : (c + 1) * capacity]
            row = jnp.sum(jnp.where(picks[c], gg_c, 0.0), axis=0, keepdims=True)
            gg_src[u, c] = jnp.broadcast_to(row, (8, rows))
        grad_h = mm_nt(pg, wd_ref[...])
        grad_a = (grad_h * b * slope).astype(BF16)
        grad_b = (grad_h * act).astype(BF16)
        grad_pre[both, :ff] = grad_a
        grad_pre[both, ff:] = grad_b
        grad_rows = (mm_nt(grad_a, wg_ref[...]) + mm_nt(grad_b, wu_ref[...])).astype(BF16)
        for c in range(2):
            returns[u, c] = mm_tn(
                picks_b[c], grad_rows[c * capacity : (c + 1) * capacity]
            ).astype(BF16)
        swaps.append(sends.start(returns.at[u, 1 - core], theirs.at[u], place.partner))
        if u == 0:
            gg_all[part] = gg_src[0, core]
            gg_sends.append(sends.start(gg_src.at[0, 1 - core], gg_all.at[part], place.partner))
        else:
            for c in (core, 1 - core):
                gg_sends.append(
                    sends.start(gg_src.at[u, c], gg_all.at[part], {"expert": 2 * at + c})
                )

    def joined(u):
        swaps[u].wait_recv()
        add_to(theirs.at[u], returns.at[u, core])

    swap_own.wait_recv()
    for copy in note_sends:
        copy.wait_recv()
    unit(0)
    go_right.wait_recv()
    first = rows_all.at[left, halves[LOW]]
    far_low = sends.start(first, first, to_right)
    swap_left = sends.start(rows_all.at[left], rows_all.at[left], place.partner)
    go_left.wait_recv()
    second = rows_all.at[right, halves[HIGH]]
    far_high = sends.start(second, second, to_left)
    swap_right = sends.start(rows_all.at[right], rows_all.at[right], place.partner)
    swap_left.wait_recv()
    unit(1)
    swap_right.wait_recv()
    unit(2)
    swap_far = []
    for h, copy in enumerate((far_low, far_high)):
        copy.wait_recv()
        piece = rows_all.at[far, halves[h]]
        swap_far.append(sends.start(piece, piece, place.partner))
    joined(1)
    joined(2)
    back_right = sends.start(theirs.at[2, halves[HIGH]], from_left, to_right)
    back_left = sends.start(theirs.at[1, halves[LOW]], from_right, to_left)
    for copy in swap_far:
        copy.wait_recv()
    unit(3)
    joined(3)
    back_far_low = sends.start(theirs.at[3, halves[LOW]], far_left, to_right)
    back_far_high = sends.start(theirs.at[3, halves[HIGH]], far_right, to_left)

    tall = 4 * w_grads.shape[2] * 2 // 3
    high = tall // 4
    w_stores = Keeps(tile_sems)
    for i in range(ff // tall):
        got = mm_tn(hidden[:, i * tall : (i + 1) * tall], pair_grad[...]).astype(BF16)
        tile_d[i] = got.reshape(tile_d.shape[1:])
        w_stores.start(tile_d.at[i], w_grads.at[pl.ds(2 * i, 2), :, pl.ds(high, high // 2)])
    for i in range(width // tall):
        if i >= 2:
            w_stores.made[ff // tall + i - 2].wait()
        got = mm_tn(arrived[:, i * tall : (i + 1) * tall], grad_pre[...]).astype(BF16)
        tile[i % 2] = got.reshape(tile.shape[1:])
        w_stores.start(tile.at[i % 2], w_grads.at[i, :, pl.ds(0, high)])

    swaps[0].wait_recv()
    back_right.wait_recv()
    back_left.wait_recv()
    own_ref[...] = theirs[0].astype(F32) + returns[0, core].astype(F32)
    add_to(own_ref.at[halves[HIGH]], from_left)
    add_to(own_ref.at[halves[LOW]], from_right)
    back_far_low.wait_recv()
    sums_ref[0] = (theirs[2, halves[LOW]].astype(F32) + far_left[...].astype(F32)).astype(BF16)
    back_far_high.wait_recv()
    sums_ref[1] = (theirs[1, halves[HIGH]].astype(F32) + far_right[...].astype(F32)).astype(BF16)
    for copy in gg_sends:
        copy.wait_recv()
    for copy in [*stores.made[6:], *w_stores.made[: ff // tall], *w_stores.made[-2:]]:
        copy.wait()
    sends.finish()


def experts(ctx, tokens, small, gain, member, slots, up_all, wo, wg, wu, wd, collective_id):
    rows, width = ctx.shape
    ff = wg.shape[1]
    capacity = rows * 9 // 16
    high = width // 16
    vmem = pltpu.VMEM
    return pl.pallas_call(
        experts_kernel,
        out_shape=[
            sds((rows, width), F32),
            sds((EXPERTS, rows), F32),
            sds((8, 8, rows), F32),
            sds((2, rows // 2, width), BF16),
            sds((rows, width), F32),
            sds((8, rows, width), BF16),
            sds((4, 4, high * 3 // 2, width), BF16),
        ],
        in_specs=[VMEM] * 6 + [ANY] * 5,
        out_specs=[VMEM] * 5 + [ANY] * 2,
        scratch_shapes=[
            vmem((width, width), BF16),
            vmem((width, ff), BF16),
            vmem((width, ff), BF16),
            vmem((ff, width), BF16),
            vmem((8, rows, width), BF16),
            vmem((4, 2, rows, width), BF16),
            vmem((8 * capacity, width), BF16),
            vmem((8 * capacity, width), BF16),
            vmem((8 * capacity, ff), BF16),
            vmem((8 * capacity, 2 * ff), BF16),
            vmem((4, rows, width), BF16),
            *[vmem((rows // 2, width), BF16)] * 4,
            vmem((2, 4, high, width), BF16),
            vmem((2, 2, 4, high // 2, width), BF16),
            vmem((2, rows, width), BF16),
            vmem((8, EXPERTS, rows), F32),
            vmem((4, 2, 8, rows), F32),
            semaphores(8),
            semaphores(6),
            semaphores(8),
            semaphores(40),
            semaphores(40),
        ],
        compiler_params=remote_params(collective_id, 63),
    )(ctx, tokens, small, gain, member, slots, up_all, wo, wg, wu, wd)


def middle_kernel(
    middle_ref, gates_ref, gg_all, sums_ref, own_ref, d_out_ref, ctx_ref, small_ref, gain_ref,
    start_ref, q_ref, kv_ref, lse_ref, cos_ref, sin_ref, wo_hbm, w_grads, blocks_ref,
    grad_middle_ref, small_grad_ref, gq_ref, gkv_ref, wo_out, combined, w_done,
    wo_ref, g_ref, from_left, from_right, w_total_0, w_total_1, w_whole, w_far,
    bias, k_t, gkv, probs, grad_probs, second_whole, second_far, *refs,
):
    place = Place()
    core = place.core
    neighbours = [place.partner, *place.x_to, *place.y_to, *place.z_to]
    greet(neighbours)
    bufs, x_bufs = refs[:12], refs[12:17]
    wo_sem, local_sems, send_sems, recv_sems = refs[17:]
    keeps = Keeps(local_sems)
    cols = w_total_0.shape[-1]
    totals = (w_total_0, w_total_1)
    length, rows = bias.shape
    width = middle_ref.shape[1]
    quarter = width // 4

    def part_of(ref, p, w):
        return ref.at[:, w] if p else ref.at[w]

    loads = {}
    for k in range(4):
        for p in range(2):
            me, (right, left, far), _ = place.ring(p == 0)
            w = (far, right, left, me)[k]
            src = part_of(w_grads, p, w).at[:, :, pl.ds(p * cols, cols)]
            loads[k, p] = keeps.start(src, part_of(totals[p], p, w))
    wo_load = pltpu.make_async_copy(wo_hbm, wo_ref, wo_sem)
    wo_load.start()
    await_greetings(neighbours)
    sends = Sends(send_sems, recv_sems)
    came = [
        sends.start(sums_ref.at[i], dst, place.x_to[i])
        for i, dst in enumerate((from_left, from_right))
    ]

    def first_half(p):
        def view(w, h):
            span = pl.ds(2 * h, 2)
            return totals[p].at[span, w] if p else totals[p].at[w, span]

        return view

    def expert_steps():
        rings = [Ring(p == 0, first_half(p), w_whole.at[p], w_far.at[p]) for p in range(2)]
        yield from ring_sum(place, sends, rings, lambda k, i, w: loads[k, i].wait())
        half = cols // 2

        def second_half(p):
            def view(w, h):
                at = pl.ds(h * half, half)
                return totals[p].at[w, place.z, :, at] if p else totals[p].at[place.y, w, :, at]

            return view

        rings = [
            Ring(p == 1, second_half(p), second_whole.at[p], second_far.at[p]) for p in range(2)
        ]
        yield from ring_sum(place, sends, rings)
        spreads = []
        for p in range(2):
            me = place.ring(p == 1)[0]
            w_done[p, me] = totals[p][place.y, place.z]

            def view(w, h=None, p=p):
                every = pl.ds(0, cols) if h is None else pl.ds(h * half, half)
                return w_done.at[p, w, :, every]

            spreads.append(Spread(p == 1, w_done.at[p, me], view))
        yield from ring_gather(place, sends, spreads)

    def columns(c, p):
        return pl.ds(pl.multiple_of((2 * c + p) * quarter, 128), quarter)

    def theirs_of(p):
        at = columns(1 - core, p)
        if p == 0:
            return lambda w: wo_ref.at[w, :, :, at]
        return lambda w: wo_ref.at[:, w, :, at]

    strips = [
        Strip(
            p == 0, wo_ref.at[:, :, :, columns(core, p)], bufs[6 * p : 6 * p + 6],
            None, theirs_of(p),
        )
        for p in range(2)
    ]
    expert = expert_steps()
    dense = dp_sum(place, sends, strips, ())
    rest = x_sum(place, sends, blocks_ref, combined, *x_bufs)
    next(expert)
    next(rest)

    grad_gates = jnp.concatenate([gg_all[e, :1] for e in range(EXPERTS)], axis=0)
    gates_t = gates_ref[...]
    products = gates_t * grad_gates
    grad_logits = products - gates_t * jnp.sum(products, axis=0, keepdims=True)
    grad_logits = jnp.concatenate(
        [grad_logits, jnp.zeros((128 - EXPERTS, rows), F32)], axis=0
    ).T.astype(BF16)
    total = own_ref[...] + mm_nt(grad_logits, small_ref[...])
    middle, gain = middle_ref[...], gain_ref[...]
    inverse = inverse_rms(middle)
    scaled = middle * inverse
    small_grad = mm_tn((scaled * gain).astype(BF16), grad_logits)
    fill_bias(bias, start_ref, rows * place.part)
    for copy in came:
        copy.wait_recv()
    total += jnp.concatenate([from_left[...], from_right[...]], axis=0).astype(F32)
    grad_gain = jnp.sum(total * scaled, axis=0, keepdims=True)
    lanes = lax.broadcasted_iota(jnp.int32, (width, 128), 1)
    small_grad += jnp.where(lanes == EXPERTS, as_column(grad_gain, 128), 0.0)
    small_grad_ref[...] = small_grad.astype(BF16)
    weighted = total * gain
    inner = jnp.mean(weighted * scaled, axis=-1, keepdims=True)
    grad_middle = d_out_ref[...].astype(F32) + inverse * (weighted - scaled * inner)
    grad_middle_ref[...] = grad_middle
    grad_attn = grad_middle.astype(BF16)
    wo_load.wait()
    g_ref[...] = mm_nt(grad_attn, wo_ref[...].reshape(width, width)).astype(BF16)
    next(rest)
    next(expert)
    tall = width // 4
    for i in range(4):
        got = mm_tn(ctx_ref[:, i * tall : (i + 1) * tall], grad_attn).astype(BF16)
        wo_ref[i] = got.reshape(wo_ref.shape[1:])
    next(dense)

    when = {2: (dense,), 4: (rest,), 6: (dense,), 8: (expert,), 10: (dense,)}
    for group in range(KEY_VALUE_HEADS):
        keys = slice(2 * group * HEAD_SIZE, (2 * group + 1) * HEAD_SIZE)
        values = slice((2 * group + 1) * HEAD_SIZE, (2 * group + 2) * HEAD_SIZE)
        k_t[...] = kv_ref[:, keys].astype(F32).T.astype(BF16)
        gkv[...] = jnp.zeros_like(gkv)

        def one_head(i, carry, base):
            head = base + i
            query, grad = q_ref[:, head_columns(head)], g_ref[:, head_columns(head)]
            lse = lse_ref[head]
            inner = jnp.zeros_like(lse)
            for at in range(0, length, BLOCK):
                span = pl.ds(at, BLOCK)
                s = mm_nt(kv_ref[span, keys], query) + bias[span]
                p = jnp.exp2(s * (SCALE * LOG2E) - lse)
                gp = mm_nt(kv_ref[span, values], grad)
                inner += jnp.sum(p * gp, axis=0, keepdims=True)
                probs[span] = p
                grad_probs[span] = gp
                gkv[span, HEAD_SIZE:] += mm(p.astype(BF16), grad)
            gq = jnp.zeros((HEAD_SIZE, rows), F32)
            for at in range(0, length, BLOCK):
                span = pl.ds(at, BLOCK)
                gs = (probs[span] * (grad_probs[span] - inner)).astype(BF16)
                gkv[span, :HEAD_SIZE] += mm(gs, query)
                gq += mm(k_t[:, span], gs)
            turned = spin(gq.T * SCALE, cos_ref[...], -sin_ref[...])
            gq_ref[:, head_columns(head)] = turned.astype(BF16)
            return carry

        for base in range(group * GROUP, (group + 1) * GROUP, 2):
            lax.fori_loop(0, 2, lambda i, carry, base=base: one_head(i, carry, base), 0)
            for steps in when.get(base + 2, ()):
                next(steps)
        gkv_ref[:, keys] = (gkv[:, :HEAD_SIZE] * SCALE).astype(BF16)
        gkv_ref[:, values] = gkv[:, HEAD_SIZE:].astype(BF16)
    run_out(expert, dense, rest)
    for p, s in enumerate(strips):
        wo_out[:, columns(core, p)] = s.result[...]
        wo_out[:, columns(1 - core, p)] = s.near[3]
    sends.finish()


def between(
    middle, gates, gg, sums, own, d_out, ctx, small, gain, start, query, kv, lse, cosine, sine,
    wo, w_grads, back_out, collective_id,
):
    rows, width = query.shape
    length = kv.shape[0]
    height, quarter = width // 16, width // 4
    high, cols = w_grads.shape[2], width // 2
    vmem = pltpu.VMEM
    return pl.pallas_call(
        middle_kernel,
        out_shape=[
            sds((rows, width), F32),
            sds((width, 128), BF16),
            sds((rows, width), BF16),
            sds(kv.shape, BF16),
            sds((height, width), BF16),
            sds((rows, width), F32),
            sds((2, 4, high, cols), BF16),
        ],
        in_specs=[VMEM] * 15 + [ANY] * 3,
        out_specs=[VMEM] * 7,
        scratch_shapes=[
            vmem((4, 4, height, width), BF16),
            vmem((rows, width), BF16),
            vmem((rows // 2, width), BF16),
            vmem((rows // 2, width), BF16),
            vmem((4, 4, high, cols), BF16),
            vmem((4, 4, high, cols), BF16),
            vmem((2, 2, 2, 2, high, cols), BF16),
            vmem((2, 2, 2, high, cols), BF16),
            vmem((length, rows), F32),
            vmem((HEAD_SIZE, length), BF16),
            vmem((length, 2 * HEAD_SIZE), F32),
            vmem((length, rows), F32),
            vmem((length, rows), F32),
            vmem((2, 2, 2, high, cols // 2), BF16),
            vmem((2, 2, high, cols // 2), BF16),
            *strip_buffers(height, quarter),
            *strip_buffers(height, quarter),
            *x_buffers(rows, width),
            pltpu.SemaphoreType.DMA,
            semaphores(8),
            semaphores(90),
            semaphores(90),
        ],
        compiler_params=remote_params(collective_id, 63),
    )(
        middle, gates, gg, sums, own, d_out, ctx, small, gain, start, query, kv, lse, cosine, sine,
        wo, w_grads, back_out,
    )


def last_kernel(
    kv_terms, gq_ref, normed_ref, tokens_ref, gain_ref, cos_ref, sin_ref,
    small_ref, w_done, w_hbm,
    grad_inputs_ref, strips_out, small_out, w_sums,
    grads, small_total, w_ref, normed_t, kv_sum, *refs,
):
    place = Place()
    core = place.core
    neighbours = [place.partner, *place.x_to, *place.y_to, *place.z_to]
    greet(neighbours)
    bufs, x_bufs = refs[:30], refs[30:35]
    w_sem, local_sems, send_sems, recv_sems = refs[35:]
    load = pltpu.make_async_copy(w_hbm, w_ref, w_sem)
    load.start()
    await_greetings(neighbours)
    sends, keeps = Sends(send_sems, recv_sems), Keeps(local_sems)
    kv_steps = x_sum(place, sends, kv_terms, kv_sum, *x_bufs)
    next(kv_steps)

    def spread(p):
        cols = pl.ds(p * w_done.shape[-1], w_done.shape[-1])

        def view(w, h=None):
            span = pl.ds(0, 4) if h is None else pl.ds(2 * h, 2)
            return w_sums.at[span, w, :, cols] if p else w_sums.at[w, span, :, cols]

        keeps.start(w_done.at[p], view(place.ring(p == 0)[0]))
        return Spread(p == 0, w_done.at[p], view)

    expert_steps = ring_gather(place, sends, [spread(p) for p in range(2)])
    next(expert_steps)
    strip = grads.shape[-1]
    wide = strip - HEAD_SIZE
    rows, width = normed_ref.shape
    height = grads.shape[3]

    def put(s, cols, right_side):
        got = mm(normed_t[...], right_side).astype(BF16)
        grads[s, :, :, :, cols] = got.reshape(4, 4, height, right_side.shape[1])

    def shared(at, size, bufs):
        cols = pl.ds(at, size)

        def theirs_of(p):
            s = 2 * (1 - core) + p
            if p == 0:
                return lambda w: grads.at[s, w, :, :, cols]
            return lambda w: grads.at[s, :, w, :, cols]

        return [
            Strip(
                p == 0, grads.at[2 * core + p, :, :, :, cols], bufs[6 * p : 6 * p + 6],
                None, theirs_of(p),
            )
            for p in range(2)
        ]

    wide_strips = shared(0, wide, bufs[:12])
    narrow_strips = shared(wide, HEAD_SIZE, bufs[12:24])
    wide_steps = dp_sum(place, sends, wide_strips, ())
    narrow_steps = dp_sum(place, sends, narrow_strips, ())
    normed_t[...] = normed_ref[...].astype(F32).T.astype(BF16)
    for s in range(4):
        put(s, pl.ds(0, wide), gq_ref[:, s * wide : (s + 1) * wide])
    next(wide_steps)
    next(kv_steps)
    load.wait()
    grad_normed = None
    for s in range(4):
        at = s * strip
        term = mm_nt(gq_ref[:, s * wide : (s + 1) * wide], w_ref[:, at : at + wide])
        grad_normed = term if grad_normed is None else grad_normed + term
    next(wide_steps)
    next(kv_steps)
    run_out(kv_steps)
    cosine, sine = cos_ref[...], sin_ref[...]
    for s in range(4):
        got = kv_sum[:, s * HEAD_SIZE : (s + 1) * HEAD_SIZE]
        if s % 2 == 0:
            got = spin(got, cosine, -sine)
        got = got.astype(BF16)
        put(s, pl.ds(wide, HEAD_SIZE), got)
        grad_normed += mm_nt(got, w_ref[:, s * strip + wide : (s + 1) * strip])
    next(narrow_steps)
    next(wide_steps)
    next(narrow_steps)

    grad_inputs, grad_gain = rms_back(tokens_ref[...].astype(F32), gain_ref[...], grad_normed)
    grad_inputs_ref[...] = grad_inputs
    lanes = lax.broadcasted_iota(jnp.int32, (width, 128), 1)
    small = jnp.where(
        lanes == EXPERTS + 1, as_column(grad_gain, 128), small_ref[...].astype(F32)
    )
    small_total[...] = small.astype(BF16).reshape(small_total.shape)
    small_strip = Strip(True, small_total, bufs[24:])
    small_steps = dp_sum(place, sends, [small_strip], ())
    next(small_steps)
    next(small_steps)
    next(expert_steps)
    run_out(wide_steps, narrow_steps, small_steps, expert_steps)
    small_out[...] = small_strip.result[...].astype(F32) + small_strip.near[3].astype(F32)
    for p in range(2):
        for at, size, s in ((0, wide, wide_strips[p]), (wide, HEAD_SIZE, narrow_strips[p])):
            for c, got in ((core, s.result), (1 - core, s.near.at[3])):
                begin_at = pl.multiple_of((2 * c + p) * strip + at, 128)
                strips_out[:, pl.ds(begin_at, size)] = got[...]
    for copy in keeps.made:
        copy.wait()
    sends.finish()


def last(
    kv_terms, grad_query, normed, tokens, gain, cosine, sine, small, w_done, w, collective_id
):
    rows, width = normed.shape
    total = w.shape[1]
    height, strip = width // 16, total // 4
    kv_width = total - width
    vmem = pltpu.VMEM
    return pl.pallas_call(
        last_kernel,
        out_shape=[
            sds((rows, width), F32),
            sds((height, total), BF16),
            sds((height, 128), F32),
            sds((4, 4, w_done.shape[2], width), BF16),
        ],
        in_specs=[ANY] + [VMEM] * 8 + [ANY],
        out_specs=[VMEM] * 3 + [ANY],
        scratch_shapes=[
            vmem((4, 4, 4, height, strip), BF16),
            vmem((4, 4, height, 128), BF16),
            vmem((width, total), BF16),
            vmem((width, rows), BF16),
            vmem((rows, kv_width), F32),
            *strip_buffers(height, strip - HEAD_SIZE),
            *strip_buffers(height, strip - HEAD_SIZE),
            *strip_buffers(height, HEAD_SIZE),
            *strip_buffers(height, HEAD_SIZE),
            *strip_buffers(height, 128, shared=False),
            *x_buffers(rows, kv_width),
            pltpu.SemaphoreType.DMA,
            semaphores(2),
            semaphores(120),
            semaphores(120),
        ],
        compiler_params=remote_params(collective_id, 60),
    )(kv_terms, grad_query, normed, tokens, gain, cosine, sine, small, w_done, w)


def finish_kernel(
    sums_ref, grad_middle_ref, grad_inputs_ref, middle_ref, combined_ref, strips_ref, wo_ref,
    small_ref, g_out, u_out, d_out, tokens_out, mixed_out, wq_out, wk_out, wv_out, wo_out,
    small_out,
):
    owners, high, width = sums_ref.shape
    ff = width // 2
    gu = high * 2 // 3
    g_out[...] = sums_ref[:, :gu, :ff].astype(F32).reshape(owners * gu, ff)
    u_out[...] = sums_ref[:, :gu, ff:].astype(F32).reshape(owners * gu, ff)
    d_out[...] = sums_ref[:, gu:].astype(F32).reshape(owners * (high - gu), width)
    tokens_out[...] = grad_middle_ref[...] + grad_inputs_ref[...]
    mixed_out[...] = (middle_ref[...] + combined_ref[...]).astype(BF16)

    @pl.when(pl.program_id(0) == 0)
    def _():
        strip = strips_ref.shape[1] // 4
        wide = strip - HEAD_SIZE
        for s in range(4):
            at = s * strip
            wq_out[:, s * wide : (s + 1) * wide] = strips_ref[:, at : at + wide].astype(F32)
            other = (wk_out, wv_out)[s % 2]
            begin_at = s // 2 * HEAD_SIZE
            got = strips_ref[:, at + wide : at + strip].astype(F32)
            other[:, begin_at : begin_at + HEAD_SIZE] = got
        wo_out[...] = wo_ref[...].astype(F32)
        small_out[...] = small_ref[...]


def finish(sums, grad_middle, grad_inputs, middle, combined, strips, wo, small):
    owners, high, width = sums.shape
    rows = middle.shape[0]
    height, total = strips.shape
    kv_half = (total - width) // 2
    ff = width // 2
    gu, d = high * 2 // 3, high // 3
    steps = 8
    each, part = owners // steps, rows // steps
    by_step = lambda a, b: pl.BlockSpec((a, b), lambda i: (i, 0))
    whole = lambda a, b: pl.BlockSpec((a, b), lambda i: (0, 0))
    return pl.pallas_call(
        finish_kernel,
        grid=(steps,),
        out_shape=[
            sds((owners * gu, ff), F32),
            sds((owners * gu, ff), F32),
            sds((owners * d, width), F32),
            sds((rows, width), F32),
            sds((rows, width), BF16),
            sds((height, width), F32),
            sds((height, kv_half), F32),
            sds((height, kv_half), F32),
            sds((height, width), F32),
            sds((height, 128), F32),
        ],
        in_specs=[pl.BlockSpec((each, high, width), lambda i: (i, 0, 0))]
        + [by_step(part, width)] * 4
        + [whole(height, total), whole(height, width), whole(height, 128)],
        out_specs=[
            by_step(each * gu, ff),
            by_step(each * gu, ff),
            by_step(each * d, width),
            by_step(part, width),
            by_step(part, width),
            whole(height, width),
            whole(height, kv_half),
            whole(height, kv_half),
            whole(height, width),
            whole(height, 128),
        ],
        compiler_params=pltpu.CompilerParams(vmem_limit_bytes=32 * MIB),
        cost_estimate=pl.CostEstimate(flops=0, bytes_accessed=30 * MIB, transcendentals=0),
    )(sums, grad_middle, grad_inputs, middle, combined, strips, wo, small)


def on_device(
    tokens,
    d_out,
    gain_in,
    w_query,
    key_projection_weight,
    value_projection_weight,
    w_out,
    gain_mid,
    w_router,
    w_gate,
    w_up,
    w_down,
    routes,
    segments,
):
    rows, width = tokens.shape
    length = segments.shape[1]
    part = lax.axis_index("expert")
    seg_row = segments[0]
    offset = part * rows
    my_seg = lax.dynamic_slice_in_dim(seg_row, offset, rows, 0)
    start = jnp.sum((seg_row[None, :] < my_seg[:, None]).astype(jnp.int32), axis=1)
    angles = angles_for(offset + jnp.arange(rows, dtype=jnp.int32) - start)
    cosine, sine = jnp.cos(angles), jnp.sin(angles)
    cosine = jnp.concatenate([cosine, cosine], axis=1)
    sine = jnp.concatenate([-sine, sine], axis=1)
    start = start[None, :]

    small = jnp.concatenate([w_router, gain_mid[:, None], gain_in[:, None]], axis=1)
    small = jnp.pad(small, ((0, 0), (0, 128 - small.shape[1])))
    note = jnp.pad(routes.T, ((0, 8 - TOPK), (0, 0)))
    w_strips, small, wo_part, upstream_all, notes, normed, query, kv_all = begin(
        w_query, key_projection_weight, value_projection_weight, w_out, small, d_out, note,
        tokens, cosine, sine, 1,
    )
    w_strips = w_strips.reshape(width, -1)
    small = small.reshape(width, -1)
    gain_mid_row = small[:, EXPERTS].astype(F32)[None, :]
    gain_in_row = small[:, EXPERTS + 1].astype(F32)[None, :]
    kv_all = kv_all.reshape(length, -1)
    context, lse, wo = attend(start, query, kv_all, wo_part, 2)

    member = jnp.any(routes[:, :, None] == jnp.arange(128, dtype=jnp.int32), axis=1).astype(F32)
    chosen = jnp.any(notes[:, :TOPK] == part, axis=1)
    slots = jnp.where(chosen, jnp.cumsum(chosen.astype(jnp.int32), axis=1) - 1, -1)[:, None, :]
    middle, gates, gg, sums, own, back_out, w_grads = experts(
        context, tokens, small, gain_mid_row, member, slots, upstream_all,
        wo.reshape(width, width), w_gate[0], w_up[0], w_down[0], 3,
    )
    grad_middle, small_grads, grad_query, kv_terms, wo_sum, combined, w_done = between(
        middle, gates, gg, sums, own, d_out, context, small, gain_mid_row, start, query, kv_all,
        lse, cosine, sine, wo, w_grads, back_out, 4,
    )
    grad_inputs, strips_sum, small_sum, w_sums = last(
        kv_terms.reshape(8, rows, -1), grad_query, normed, tokens, gain_in_row, cosine, sine,
        small_grads, w_done, w_strips, 5,
    )
    g_wg, g_wu, g_wd, grad_tokens, mixed, g_wq, g_wk, g_wv, g_wo, small_sum = finish(
        w_sums.reshape(16, -1, width), grad_middle, grad_inputs, middle, combined, strips_sum,
        wo_sum, small_sum,
    )
    return (
        mixed,
        grad_tokens,
        small_sum[:, EXPERTS + 1],
        g_wq,
        g_wk,
        g_wv,
        g_wo,
        small_sum[:, EXPERTS],
        small_sum[:, :EXPERTS],
        g_wg[None],
        g_wu[None],
        g_wd[None],
    )


def solution(mesh):
    whole = P(("dp", "expert"), None)
    over_dp, by_dp, over_expert = P("dp"), P("dp", None), P("expert", None, None)
    return jax.shard_map(
        on_device,
        mesh=mesh,
        in_specs=(whole, whole, over_dp, by_dp, by_dp, by_dp, by_dp, over_dp, by_dp)
        + (over_expert,) * 3
        + (whole, by_dp),
        out_specs=(whole, whole, over_dp, by_dp, by_dp, by_dp, by_dp, over_dp, by_dp)
        + (over_expert,) * 3,
        check_vma=False,
    )
```

```python
import functools

import jax
import jax.numpy as jnp
from jax import lax
from jax.experimental import pallas as pl
from jax.experimental.pallas import tpu as pltpu
from jax.sharding import PartitionSpec as P

QUERY_HEADS = 12
KEY_VALUE_HEADS = 2
HEAD_SIZE = 128
TOPK = 4
EXPERTS = 8
GROUP = QUERY_HEADS // KEY_VALUE_HEADS
SCALE = HEAD_SIZE**-0.5
LOG2E = 1.4426950408889634
BLOCK = 512

EPSILON = 1e-06
ROPE_BASE = 1000000.0
MASK_FILL = -1e30
F32 = jnp.float32
BF16 = jnp.bfloat16

MESH = pl.DeviceIdType.MESH
ANY = pl.BlockSpec(memory_space=pl.ANY)
VMEM = pl.BlockSpec(memory_space=pltpu.VMEM)
MIB = 2**20


def dot(a, b, dims):
    return lax.dot_general(a, b, (dims, ((), ())), preferred_element_type=F32)


def mm(a, b):
    return dot(a, b, ((1,), (0,)))


def mm_nt(a, b):
    return dot(a, b, ((1,), (1,)))


def mm_tn(a, b):
    return dot(a, b, ((0,), (0,)))


def sds(shape, dtype):
    return jax.ShapeDtypeStruct(tuple(shape), dtype)


def remote_params(collective_id):
    return pltpu.CompilerParams(
        collective_id=collective_id, has_side_effects=True, vmem_limit_bytes=63 * MIB
    )


def semaphores(count):
    return pltpu.SemaphoreType.DMA((count,))


def inverse_rms(rows):
    return lax.rsqrt(jnp.mean(rows * rows, axis=-1, keepdims=True) + EPSILON)


def rms_back(rows, gain, grad):
    inverse = inverse_rms(rows)
    scaled = rows * inverse
    weighted = grad * gain
    inner = jnp.mean(weighted * scaled, axis=-1, keepdims=True)
    return inverse * (weighted - scaled * inner), jnp.sum(grad * scaled, axis=0, keepdims=True)


def as_column(row, lanes):
    return jnp.broadcast_to(row, (lanes, row.shape[1])).T


def angles_for(positions):
    half_width = HEAD_SIZE // 2
    freqs = ROPE_BASE ** (-2.0 * jnp.arange(half_width, dtype=F32) / HEAD_SIZE)
    return positions.astype(F32)[:, None] * freqs[None, :]


def spin(z, cosine, sine):
    return z * cosine + pltpu.roll(z, HEAD_SIZE // 2, 1) * sine


class Sends:
    def __init__(self, send_sems, recv_sems):
        self.send_sems, self.recv_sems, self.made = send_sems, recv_sems, []

    def start(self, src, dst, to):
        at = len(self.made)
        copy = pltpu.make_async_remote_copy(
            src_ref=src,
            dst_ref=dst,
            send_sem=self.send_sems.at[at],
            recv_sem=self.recv_sems.at[at],
            device_id=to,
            device_id_type=MESH,
        )
        copy.start()
        self.made.append(copy)
        return copy

    def finish(self):
        for copy in self.made:
            copy.wait_send()


class Keeps:
    def __init__(self, sems):
        self.sems, self.made = sems, []

    def start(self, src, dst):
        copy = pltpu.make_async_copy(src, dst, self.sems.at[len(self.made)])
        copy.start()
        self.made.append(copy)
        return copy


class Place:
    def __init__(self):
        self.part = lax.axis_index("expert")
        self.core = self.part % 2
        self.chip = self.part // 2
        at = lambda d: lax.rem(self.chip + d, 4) * 2 + self.core
        self.right, self.left, self.far = at(1), at(3), at(2)
        to = lambda i: {"expert": i}
        self.partner = to(2 * self.chip + (1 - self.core))
        self.x_to = [to(self.right), to(self.left), to(self.far)]
        self.others = [to(lax.rem(self.part + d, 8)) for d in range(1, 8)]
        place = lax.axis_index("dp")
        self.y, self.z = place // 4, place % 4
        ring = lambda v: [lax.rem(v + d, 4) for d in (1, 3, 2)]
        self.y_ring, self.z_ring = ring(self.y), ring(self.z)
        self.y_to = [{"dp": v * 4 + self.z} for v in self.y_ring[:2]]
        self.z_to = [{"dp": self.y * 4 + v} for v in self.z_ring[:2]]

    def ring(self, along_y):
        if along_y:
            return self.y, self.y_ring, self.y_to
        return self.z, self.z_ring, self.z_to


def greet(others):
    barrier = pltpu.get_barrier_semaphore()
    for other in others:
        pl.semaphore_signal(barrier, inc=1, device_id=other, device_id_type=MESH)


def await_greetings(others):
    pl.semaphore_wait(pltpu.get_barrier_semaphore(), len(others))


def add_to(ref, *others):
    got = ref[...].astype(F32)
    for other in others:
        got += other[...].astype(F32)
    ref[...] = got.astype(ref.dtype)


def run_out(*steps):
    steps = list(steps)
    while steps:
        for s in list(steps):
            if next(s, "done") == "done":
                steps.remove(s)


def x_sum(place, sends, blocks_ref, out_ref, mine, total, from_left, from_right, sems):
    rows = out_ref.shape[0]
    half = rows // 2
    low, high = pl.ds(0, half), pl.ds(half, half)
    to_right, to_left = place.x_to[:2]
    flip = 1 - 2 * place.core
    keeps = Keeps(sems)
    swaps, loads = [], []
    for k, dest in enumerate((place.far, place.right, place.left, place.part)):
        swaps.append(sends.start(blocks_ref.at[dest + flip], total.at[k], place.partner))
        loads.append(keeps.start(blocks_ref.at[dest], mine.at[k]))

    def add_up(k):
        loads[k].wait()
        swaps[k].wait_recv()
        add_to(total.at[k], mine.at[k])

    yield
    add_up(0)
    far_low = sends.start(total.at[0, low], from_left.at[0], to_right)
    far_high = sends.start(total.at[0, high], from_right.at[0], to_left)
    add_up(1)
    right_high = sends.start(total.at[1, high], from_left.at[2], to_right)
    add_up(2)
    left_low = sends.start(total.at[2, low], from_right.at[2], to_left)
    yield
    far_low.wait_recv()
    add_to(total.at[1, low], from_left.at[0])
    right_low = sends.start(total.at[1, low], from_left.at[1], to_right)
    far_high.wait_recv()
    add_to(total.at[2, high], from_right.at[0])
    left_high = sends.start(total.at[2, high], from_right.at[1], to_left)
    yield
    loads[3].wait()
    swaps[3].wait_recv()
    out_ref[...] = mine[3].astype(F32) + total[3].astype(F32)
    right_high.wait_recv()
    left_low.wait_recv()
    right_low.wait_recv()
    left_high.wait_recv()
    add_to(out_ref.at[low], from_left.at[1], from_right.at[2])
    add_to(out_ref.at[high], from_left.at[2], from_right.at[1])
    yield


def x_buffers(rows, columns):
    return [
        pltpu.VMEM((4, rows, columns), BF16),
        pltpu.VMEM((4, rows, columns), BF16),
        pltpu.VMEM((3, rows // 2, columns), BF16),
        pltpu.VMEM((3, rows // 2, columns), BF16),
        semaphores(4),
    ]


class Ring:
    def __init__(self, along_y, view, whole, farther):
        self.along_y, self.view, self.whole, self.farther = along_y, view, whole, farther


def ring_sum(place, sends, rings, ready=lambda *_: None):
    going = []
    for i, r in enumerate(rings):
        _, (right, left, far), to = place.ring(r.along_y)
        ready(0, i, far)
        going.append([sends.start(r.view(far, h), r.farther.at[h], to[h]) for h in range(2)])
    for i, r in enumerate(rings):
        _, (right, left, far), to = place.ring(r.along_y)
        ready(1, i, right)
        ready(2, i, left)
        going[i].append(sends.start(r.view(right, 1), r.whole.at[0, 1], to[0]))
        going[i].append(sends.start(r.view(left, 0), r.whole.at[1, 0], to[1]))
    yield
    for i, r in enumerate(rings):
        _, (right, left, far), to = place.ring(r.along_y)
        for h, w in enumerate((right, left)):
            going[i][h].wait_recv()
            add_to(r.view(w, h), r.farther.at[h])
            going[i].append(sends.start(r.view(w, h), r.whole.at[h, h], to[h]))
    yield
    for i, r in enumerate(rings):
        me, _, _ = place.ring(r.along_y)
        ready(3, i, me)
        for copy in going[i][2:]:
            copy.wait_recv()
        for h in range(2):
            add_to(r.view(me, h), r.whole.at[0, h], r.whole.at[1, h])


class Spread:
    def __init__(self, along_y, source, view, half, landed=lambda _: None):
        self.along_y, self.source, self.view = along_y, source, view
        self.half, self.landed = half, landed


def ring_gather(place, sends, spreads):
    came, onward = [], []

    def send(s, h, to):
        me = place.ring(s.along_y)[0]
        return sends.start(s.half(s.source, h), s.half(s.view(me), h), to)

    for s in spreads:
        to = place.ring(s.along_y)[2]
        came.append([[send(s, d, to[d])] for d in range(2)])
    yield
    for s, copies in zip(spreads, came):
        to = place.ring(s.along_y)[2]
        for d in range(2):
            copies[d].append(send(s, 1 - d, to[d]))
    yield
    for s, copies in zip(spreads, came):
        _, (right, left, _), to = place.ring(s.along_y)
        onward.append([])
        for d, origin in enumerate((left, right)):
            copies[d][0].wait_recv()
            view = s.half(s.view(origin), d)
            onward[-1].append(sends.start(view, view, to[d]))
    yield
    for s, copies in zip(spreads, came):
        _, (right, left, _), _ = place.ring(s.along_y)
        for d, origin in enumerate((left, right)):
            copies[d][1].wait_recv()
            s.landed(s.view(origin))
    for s, copies in zip(spreads, onward):
        far = place.ring(s.along_y)[1][2]
        for d in range(2):
            copies[d].wait_recv()
            s.landed(s.half(s.view(far), d))
    yield


def half_span(share, h):
    return share.at[pl.ds(2 * h, 2)]


def half_rows(share, h):
    half = share.shape[0] // 2
    return share.at[pl.ds(h * half, half)]


def half_columns(share, h):
    half = share.shape[-1] // 2
    return share.at[:, pl.ds(h * half, half)]


class Strip:
    def __init__(self, y_first, total, bufs, own=None, other=None):
        self.y_first, self.total, self.own, self.other = y_first, total, own, other
        self.theirs, self.big, self.far, self.mid, self.midfar, self.near = bufs

    def block(self, ref, w):
        return ref.at[w] if self.y_first else ref.at[:, w]


def strip_buffers(rows, columns, shared=True):
    return [
        pltpu.VMEM((4, 4, rows, columns) if shared else (1, 1, rows, columns), BF16),
        pltpu.VMEM((2, 2, 2, rows, columns), BF16),
        pltpu.VMEM((2, 2, rows, columns), BF16),
        pltpu.VMEM((2, 2, rows // 2, columns), BF16),
        pltpu.VMEM((2, rows // 2, columns), BF16),
        pltpu.VMEM((4, rows, columns), BF16),
    ]


def dp_sum(place, sends, strips, sems):
    y, z = place.y, place.z
    keeps = Keeps(sems)
    swaps, loads = {}, {}
    for k in range(4):
        for i, s in enumerate(strips):
            me, (right, left, far), _ = place.ring(s.y_first)
            w = (far, right, left, me)[k]
            if s.other is not None:
                swaps[k, i] = sends.start(s.other(w), s.block(s.theirs, w), place.partner)
            if s.own is not None:
                loads[k, i] = keeps.start(s.own(w), s.block(s.total, w))
    yield

    def joined(k, i, s, w):
        if s.own is not None:
            loads[k, i].wait()
        if s.other is not None:
            swaps[k, i].wait_recv()
            add_to(s.block(s.total, w), s.block(s.theirs, w))

    def big(s, w, h):
        span = pl.ds(2 * h, 2)
        return s.total.at[w, span] if s.y_first else s.total.at[span, w]

    def small(s, w, h):
        half = s.total.shape[2] // 2
        at = pl.ds(h * half, half)
        return s.total.at[y, w, at] if s.y_first else s.total.at[w, z, at]

    def rings(first):
        view = big if first else small
        return [
            Ring(
                s.y_first == first,
                functools.partial(view, s),
                s.big if first else s.mid,
                s.far if first else s.midfar,
            )
            for s in strips
        ]

    yield from ring_sum(place, sends, rings(True), lambda k, i, w: joined(k, i, strips[i], w))
    yield from ring_sum(place, sends, rings(False))

    shares, back = [], []
    for s in strips:
        shares.append(
            [sends.start(s.total.at[y, z], s.near.at[i], place.x_to[i]) for i in range(3)]
        )
    yield
    for s, share in zip(strips, shares):
        for copy in share:
            copy.wait_recv()
        got = s.total[y, z].astype(F32)
        for i in range(3):
            got += s.near[i].astype(F32)
        s.result = s.theirs.at[y, z] if s.other is not None else s.theirs.at[0, 0]
        s.result[...] = got.astype(BF16)
        back.append(sends.start(s.result, s.near.at[3], place.partner))
    yield
    for copy in back:
        copy.wait_recv()
    yield


def begin_kernel(
    wq_hbm, wk_hbm, wv_hbm, wo_hbm, small_ref, rows_hbm, note_ref, tokens_hbm, cos_ref, sin_ref,
    w_out, small_out, wo_part, rows_out, notes_out, normed_ref, query_ref, kv_ref,
    strips_ref, w_all, own_kv, wq_ref, wk_ref, wv_ref, wo_ref, rows_ref, tokens_ref,
    fetch_sems, local_sems, send_sems, recv_sems,
):
    fetches = Keeps(fetch_sems)
    for src, dst in (
        (wq_hbm, wq_ref), (wk_hbm, wk_ref), (wv_hbm, wv_ref), (wo_hbm, wo_ref),
        (rows_hbm, rows_ref), (tokens_hbm, tokens_ref),
    ):
        fetches.start(src, dst)
    place = Place()
    y, z, core, part = place.y, place.z, place.core, place.part
    neighbours = [*place.others, *place.y_to, *place.z_to]
    greet(neighbours)
    rows = wq_ref.shape[0]
    wide, narrow = wq_ref.shape[1] // 4, wk_ref.shape[1] // 2
    strip = wide + narrow
    for fetch in fetches.made[:4]:
        fetch.wait()
    for s in range(4):
        strips_ref[:, s * strip : s * strip + wide] = wq_ref[:, s * wide : (s + 1) * wide]
        other = (wk_ref, wv_ref)[s % 2]
        begin = s // 2 * narrow
        strips_ref[:, s * strip + wide : (s + 1) * strip] = other[:, begin : begin + narrow]
    await_greetings(neighbours)
    sends, keeps = Sends(send_sems, recv_sems), Keeps(local_sems)

    def columns(p, size):
        return pl.ds(pl.multiple_of((2 * core + p) * size, 128), size)

    across = []

    def send_across(view):
        across.append(sends.start(view, view, place.partner))

    def spread(first, src, out, cols, y_first, landed):
        def near(where):
            return out.at[where, z, :, cols] if y_first else out.at[y, where, :, cols]

        def wider(where):
            return out.at[:, where, :, cols] if y_first else out.at[where, :, :, cols]

        if first:
            return Spread(y_first, src, near, half_rows)
        source = wider(z if y_first else y)
        landed(source)
        return Spread(not y_first, source, wider, half_span, landed)

    def both_strips(first):
        every = pl.ds(0, small_ref.shape[1])
        return [
            *(
                spread(
                    first, strips_ref.at[:, columns(p, strip)], w_all, columns(p, strip), p == 1,
                    send_across,
                )
                for p in range(2)
            ),
            spread(first, small_ref, small_out, every, False, lambda _: None),
        ]

    def out_spread(p):
        ring_of = (z, y)[p]

        keeps.start(wo_ref.at[:, columns(p, wide)], wo_part.at[p, ring_of])
        return Spread(
            p == 1, wo_ref.at[:, columns(p, wide)], lambda where: wo_part.at[p, where], half_rows
        )

    first_steps = ring_gather(place, sends, [*both_strips(True), *map(out_spread, range(2))])
    next(first_steps)
    next(first_steps)
    for p in range(2):
        w_all[y, z, :, columns(p, strip)] = strips_ref[:, columns(p, strip)]
    small_out[y, z] = small_ref[...]

    half = rows_ref.shape[0] // 2
    fetches.made[4].wait()
    x_halves = [pl.ds(h * half, half) for h in range(2)]
    x_came = [
        [
            sends.start(rows_ref.at[x_halves[h]], rows_out.at[part, x_halves[h]], place.x_to[d])
            for h in (d, 1 - d)
        ]
        for d in range(2)
    ]
    across.append(sends.start(rows_ref, rows_out.at[part], place.partner))
    across += [sends.start(note_ref, notes_out.at[part], to) for to in place.others]
    keeps.start(rows_ref, rows_out.at[part])
    keeps.start(note_ref, notes_out.at[part])
    next(first_steps)
    next(first_steps)
    second_steps = ring_gather(place, sends, both_strips(False))
    next(second_steps)
    next(second_steps)
    far_rows = []
    for d, origin in enumerate((place.left, place.right)):
        x_came[d][0].wait_recv()
        view = rows_out.at[origin, x_halves[d]]
        far_rows.append(sends.start(view, view, place.x_to[d]))
    next(second_steps)
    for d, origin in enumerate((place.left, place.right)):
        x_came[d][1].wait_recv()
        send_across(rows_out.at[origin])
    next(second_steps)
    for d in range(2):
        far_rows[d].wait_recv()
        send_across(rows_out.at[place.far, x_halves[d]])
    for copy in across:
        copy.wait_recv()
    keeps.start(w_all, w_out)

    width = tokens_ref.shape[1]
    gain = small_out[...].reshape(width, -1).astype(F32).T[EXPERTS + 1 : EXPERTS + 2]
    cosine, sine = cos_ref[...], sin_ref[...]
    fetches.made[5].wait()
    inputs = tokens_ref[...].astype(F32)
    normed_ref[...] = (inputs * inverse_rms(inputs) * gain).astype(BF16)

    def project(at, size):
        w = w_all[:, :, :, at : at + size].reshape(width, size)
        return mm(normed_ref[...], w)

    for s in range(4):
        got = project(s * strip + wide, HEAD_SIZE)
        if s % 2 == 0:
            got = spin(got, cosine, sine)
        own_kv[:, s * HEAD_SIZE : (s + 1) * HEAD_SIZE] = got.astype(BF16)

    def queries(s):
        got = project(s * strip, wide)
        for h in range(0, wide, HEAD_SIZE):
            head = spin(got[:, h : h + HEAD_SIZE], cosine, sine)
            query_ref[:, s * wide + h : s * wide + h + HEAD_SIZE] = head.astype(BF16)

    slot = kv_ref.at[part]
    kv_came = [
        [
            sends.start(own_kv.at[x_halves[h]], slot.at[x_halves[h]], place.x_to[d])
            for h in (d, 1 - d)
        ]
        for d in range(2)
    ]
    kv_across = [sends.start(own_kv, slot, place.partner)]
    keeps.start(own_kv, slot)
    queries(0)
    queries(1)
    onward = []
    for d, origin in enumerate((place.left, place.right)):
        kv_came[d][0].wait_recv()
        view = kv_ref.at[origin, x_halves[d]]
        onward.append(sends.start(view, view, place.x_to[d]))
    queries(2)
    queries(3)
    for d, origin in enumerate((place.left, place.right)):
        kv_came[d][1].wait_recv()
        view = kv_ref.at[origin]
        kv_across.append(sends.start(view, view, place.partner))
    for d in range(2):
        onward[d].wait_recv()
        view = kv_ref.at[place.far, x_halves[d]]
        kv_across.append(sends.start(view, view, place.partner))
    for copy in kv_across:
        copy.wait_recv()
    for copy in keeps.made:
        copy.wait()
    sends.finish()


def begin(wq, wk, wv, wo, small, rows, note, tokens, cosine, sine, collective_id):
    height, width = wq.shape
    kv_width = wk.shape[1] + wv.shape[1]
    total = width + kv_width
    count = tokens.shape[0]
    vmem = pltpu.VMEM
    return pl.pallas_call(
        begin_kernel,
        out_shape=[
            sds((4, 4, height, total), BF16),
            sds((4, 4, *small.shape), BF16),
            sds((2, 4, height, width // 4), BF16),
            sds((8, *rows.shape), BF16),
            sds((8, *note.shape), note.dtype),
            sds((count, width), BF16),
            sds((count, width), BF16),
            sds((8, count, kv_width), BF16),
        ],
        in_specs=[ANY] * 4 + [VMEM, ANY, VMEM, ANY, VMEM, VMEM],
        out_specs=[ANY, VMEM, VMEM, ANY, ANY, VMEM, VMEM, ANY],
        scratch_shapes=[
            vmem((height, total), BF16),
            vmem((4, 4, height, total), BF16),
            vmem((count, kv_width), BF16),
            *[vmem(a.shape, BF16) for a in (wq, wk, wv, wo, rows, tokens)],
            semaphores(6),
            semaphores(6),
            semaphores(90),
            semaphores(90),
        ],
        compiler_params=remote_params(collective_id),
    )(wq, wk, wv, wo, small, rows, note, tokens, cosine, sine)


def fill_bias(bias, start_ref, first_row):
    length, rows = bias.shape
    places = lax.broadcasted_iota(jnp.int32, (length, rows), 0)
    mine = first_row + lax.broadcasted_iota(jnp.int32, (length, rows), 1)
    keep = (places >= start_ref[...]) & (places <= mine)
    bias[...] = jnp.where(keep, 0.0, MASK_FILL)


def head_columns(head):
    return pl.ds(pl.multiple_of(head * HEAD_SIZE, HEAD_SIZE), HEAD_SIZE)


def attend_kernel(
    start_ref, q_ref, kv_ref, wo_part, ctx_ref, lse_ref, wo_all,
    bias, v_t, scores, local_sems, send_sems, recv_sems,
):
    place = Place()
    neighbours = [place.partner, *place.y_to, *place.z_to]
    greet(neighbours)
    length, rows = bias.shape
    fill_bias(bias, start_ref, rows * place.part)
    await_greetings(neighbours)
    sends, keeps = Sends(send_sems, recv_sems), Keeps(local_sems)
    quarter = wo_part.shape[-1]
    across = []

    def landed(view):
        across.append(sends.start(view, view, place.partner))

    def spread(p):
        cols = pl.ds(pl.multiple_of((2 * place.core + p) * quarter, 128), quarter)

        def view(where):
            return wo_all.at[:, where, :, cols] if p else wo_all.at[where, :, :, cols]

        own = view((place.y, place.z)[p])
        keeps.start(wo_part.at[p], own)
        across.append(sends.start(wo_part.at[p], own, place.partner))
        return Spread(p == 0, wo_part.at[p], view, half_span, landed)

    steps = ring_gather(place, sends, [spread(p) for p in range(2)])
    next(steps)
    next(steps)
    for group in range(KEY_VALUE_HEADS):
        keys = slice(2 * group * HEAD_SIZE, (2 * group + 1) * HEAD_SIZE)
        values = slice((2 * group + 1) * HEAD_SIZE, (2 * group + 2) * HEAD_SIZE)
        v_t[...] = kv_ref[:, values].astype(F32).T.astype(BF16)

        def one_head(i, carry, base):
            head = base + i
            query = q_ref[:, head_columns(head)]
            top = None
            for at in range(0, length, BLOCK):
                span = pl.ds(at, BLOCK)
                s = mm_nt(kv_ref[span, keys], query) + bias[span]
                scores[span] = s
                here = jnp.max(s, axis=0, keepdims=True)
                top = here if top is None else jnp.maximum(top, here)
            total = jnp.zeros_like(top)
            context = jnp.zeros((HEAD_SIZE, rows), F32)
            for at in range(0, length, BLOCK):
                span = pl.ds(at, BLOCK)
                p = jnp.exp2((scores[span] - top) * (SCALE * LOG2E))
                total += jnp.sum(p, axis=0, keepdims=True)
                context += mm(v_t[:, span], p.astype(BF16))
            ctx_ref[:, head_columns(head)] = (context / total).T.astype(BF16)
            lse_ref[head] = top * (SCALE * LOG2E) + jnp.log2(total)
            return carry

        for base in (group * GROUP, group * GROUP + GROUP // 2):
            lax.fori_loop(
                0, GROUP // 2, lambda i, carry, base=base: one_head(i, carry, base), 0
            )
            if base in (GROUP // 2, QUERY_HEADS - GROUP // 2):
                next(steps)
    run_out(steps)
    for copy in across:
        copy.wait_recv()
    for copy in keeps.made:
        copy.wait()
    sends.finish()


def attend(start, query, kv, wo_part, collective_id):
    rows, width = query.shape
    length = kv.shape[0]
    height = wo_part.shape[2]
    return pl.pallas_call(
        attend_kernel,
        out_shape=[
            sds((rows, width), BF16),
            sds((QUERY_HEADS, 1, rows), F32),
            sds((4, 4, height, width), BF16),
        ],
        in_specs=[VMEM] * 4,
        out_specs=[VMEM, VMEM, ANY],
        scratch_shapes=[
            pltpu.VMEM((length, rows), F32),
            pltpu.VMEM((HEAD_SIZE, length), BF16),
            pltpu.VMEM((length, rows), F32),
            semaphores(2),
            semaphores(24),
            semaphores(24),
        ],
        compiler_params=remote_params(collective_id),
    )(start, query, kv, wo_part)


LOW, HIGH = 0, 1


def gelu_parts(a):
    k = (2.0 / jnp.pi) ** 0.5
    square = a * a
    t = jnp.tanh(k * a * (1.0 + 0.044715 * square))
    slope = 0.5 * (1.0 + t) + 0.5 * a * (1.0 - t * t) * k * (1.0 + 3 * 0.044715 * square)
    return 0.5 * a * (1.0 + t), slope


def experts_kernel(
    ctx_ref, tokens_ref, small_ref, gain_ref, member_ref, slot_ref,
    up_all, wo_hbm, wg_hbm, wu_hbm, wd_hbm,
    middle_ref, gates_ref, gg_all, sums_ref, own_ref, back_out, w_grads,
    wo_ref, wg_ref, wu_ref, wd_ref, rows_all, returns, arrived, pair_grad, hidden, grad_pre,
    theirs, far_left, far_right, from_left, from_right, tile, tile_d, back_rows, gates_all, gg_src,
    local_sems, tile_sems, back_sems, send_sems, recv_sems,
):
    place = Place()
    part, core = place.part, place.core
    right, left, far = place.right, place.left, place.far
    to_right, to_left = place.x_to[:2]
    greet(place.others)
    sends, keeps, stores = (
        Sends(send_sems, recv_sems), Keeps(local_sems), Keeps(back_sems)
    )
    rows, width = ctx_ref.shape
    half = rows // 2
    halves = (pl.ds(0, half), pl.ds(half, half))
    ff = wg_ref.shape[1]
    capacity = arrived.shape[0] // 8

    for src, dst in ((wo_hbm, wo_ref), (wg_hbm, wg_ref), (wu_hbm, wu_ref), (wd_hbm, wd_ref)):
        keeps.start(src, dst)
    chips = [lax.rem(place.chip + d, 4) for d in (0, 3, 1, 2)]
    for u in range(4):
        keeps.start(up_all.at[pl.ds(2 * chips[u], 2)], returns.at[u])

    keeps.made[0].wait()
    middle = tokens_ref[...].astype(F32) + mm(ctx_ref[...], wo_ref[...])
    middle_ref[...] = middle
    normed = (middle * inverse_rms(middle) * gain_ref[...]).astype(BF16)
    rows_all[part] = normed
    member = member_ref[...]
    logits = jnp.where(member > 0.0, mm(normed, small_ref[...]), MASK_FILL)
    weight = jnp.exp(logits - jnp.max(logits, axis=-1, keepdims=True)) * member
    gates = weight / jnp.sum(weight, axis=-1, keepdims=True)
    gates_ref[...] = gates.T[:EXPERTS]

    await_greetings(place.others)
    mine = rows_all.at[part]
    go = [
        [sends.start(mine.at[halves[h]], mine.at[halves[h]], way) for h in (d, 1 - d)]
        for d, way in enumerate((to_right, to_left))
    ]
    swap_own = sends.start(mine, mine, place.partner)
    note_sends = [sends.start(gates_ref, gates_all.at[part], to) for to in place.others]
    gates_all[part] = gates_ref[...]

    def pick_of(source):
        slots = lax.broadcasted_iota(jnp.int32, (capacity, rows), 0)
        return slots == slot_ref[source]

    for u in range(4):
        keeps.made[4 + u].wait()
        for c in range(2):
            pick = pick_of(2 * chips[u] + c).astype(BF16)
            got = mm(pick, returns[u, c])
            pair_grad[pl.ds((2 * u + c) * capacity, capacity)] = got.astype(BF16)
    for load in keeps.made[1:4]:
        load.wait()

    swaps, gg_sends = [], []

    def unit(u):
        at = chips[u]
        picks = [pick_of(2 * at + c) for c in range(2)]
        picks_b = [pick.astype(BF16) for pick in picks]
        spans = [pl.ds((2 * u + c) * capacity, capacity) for c in range(2)]
        both = pl.ds(2 * u * capacity, 2 * capacity)
        gate = []
        for c in range(2):
            arrived[spans[c]] = mm(picks_b[c], rows_all[2 * at + c]).astype(BF16)
            row = gates_all[2 * at + c, pl.ds(part, 1)]
            gate.append(jnp.sum(jnp.where(picks[c], row, 0.0), axis=-1, keepdims=True))
        gate = jnp.concatenate(gate, axis=0)
        x = arrived[both]
        a, b = mm(x, wg_ref[...]), mm(x, wu_ref[...])
        act, slope = gelu_parts(a)
        h = (act * b).astype(BF16)
        hidden[both] = h
        out = mm(h, wd_ref[...]).astype(BF16).astype(F32)
        up = pair_grad[both].astype(F32)
        gg = jnp.sum(up * out, axis=-1, keepdims=True)
        weighted = (gate * out).astype(BF16)
        pg = (gate * up).astype(BF16)
        pair_grad[both] = pg
        for c in range(2):
            if u > 0:
                stores.made[2 * (u - 1) + c].wait()
            back_rows[c] = mm_tn(picks_b[c], weighted[c * capacity : (c + 1) * capacity]).astype(
                BF16
            )
            stores.start(back_rows.at[c], back_out.at[2 * at + c])
            gg_c = gg[c * capacity : (c + 1) * capacity]
            row = jnp.sum(jnp.where(picks[c], gg_c, 0.0), axis=0, keepdims=True)
            gg_src[u, c] = jnp.broadcast_to(row, (8, rows))
        grad_h = mm_nt(pg, wd_ref[...])
        grad_a = (grad_h * b * slope).astype(BF16)
        grad_b = (grad_h * act).astype(BF16)
        grad_pre[both, :ff] = grad_a
        grad_pre[both, ff:] = grad_b
        grad_rows = (mm_nt(grad_a, wg_ref[...]) + mm_nt(grad_b, wu_ref[...])).astype(BF16)
        for c in range(2):
            returns[u, c] = mm_tn(
                picks_b[c], grad_rows[c * capacity : (c + 1) * capacity]
            ).astype(BF16)
        swaps.append(sends.start(returns.at[u, 1 - core], theirs.at[u], place.partner))
        if u == 0:
            gg_all[part] = gg_src[0, core]
            gg_sends.append(sends.start(gg_src.at[0, 1 - core], gg_all.at[part], place.partner))
        else:
            for c in (core, 1 - core):
                gg_sends.append(
                    sends.start(gg_src.at[u, c], gg_all.at[part], {"expert": 2 * at + c})
                )

    def joined(u):
        swaps[u].wait_recv()
        add_to(theirs.at[u], returns.at[u, core])

    swap_own.wait_recv()
    for copy in note_sends:
        copy.wait_recv()
    unit(0)
    passed = []
    for d, (origin, way) in enumerate(((left, to_right), (right, to_left))):
        go[d][0].wait_recv()
        view = rows_all.at[origin, halves[d]]
        passed.append(sends.start(view, view, way))
    far_low, far_high = passed
    go[0][1].wait_recv()
    swap_left = sends.start(rows_all.at[left], rows_all.at[left], place.partner)
    go[1][1].wait_recv()
    swap_right = sends.start(rows_all.at[right], rows_all.at[right], place.partner)
    swap_left.wait_recv()
    unit(1)
    swap_right.wait_recv()
    unit(2)
    swap_far = []
    for h, copy in enumerate((far_low, far_high)):
        copy.wait_recv()
        piece = rows_all.at[far, halves[h]]
        swap_far.append(sends.start(piece, piece, place.partner))
    joined(1)
    joined(2)
    back_right = sends.start(theirs.at[2, halves[HIGH]], from_left, to_right)
    back_left = sends.start(theirs.at[1, halves[LOW]], from_right, to_left)
    for copy in swap_far:
        copy.wait_recv()
    unit(3)
    joined(3)
    back_far_low = sends.start(theirs.at[3, halves[LOW]], far_left, to_right)
    back_far_high = sends.start(theirs.at[3, halves[HIGH]], far_right, to_left)

    tall = 4 * w_grads.shape[2] * 2 // 3
    high = tall // 4
    w_stores = Keeps(tile_sems)
    for i in range(ff // tall):
        got = mm_tn(hidden[:, i * tall : (i + 1) * tall], pair_grad[...]).astype(BF16)
        tile_d[i] = got.reshape(tile_d.shape[1:])
        w_stores.start(tile_d.at[i], w_grads.at[pl.ds(2 * i, 2), :, pl.ds(high, high // 2)])
    for i in range(width // tall):
        if i >= 2:
            w_stores.made[ff // tall + i - 2].wait()
        got = mm_tn(arrived[:, i * tall : (i + 1) * tall], grad_pre[...]).astype(BF16)
        tile[i % 2] = got.reshape(tile.shape[1:])
        w_stores.start(tile.at[i % 2], w_grads.at[i, :, pl.ds(0, high)])

    swaps[0].wait_recv()
    back_right.wait_recv()
    back_left.wait_recv()
    own_ref[...] = theirs[0].astype(F32) + returns[0, core].astype(F32)
    add_to(own_ref.at[halves[HIGH]], from_left)
    add_to(own_ref.at[halves[LOW]], from_right)
    back_far_low.wait_recv()
    sums_ref[0] = (theirs[2, halves[LOW]].astype(F32) + far_left[...].astype(F32)).astype(BF16)
    back_far_high.wait_recv()
    sums_ref[1] = (theirs[1, halves[HIGH]].astype(F32) + far_right[...].astype(F32)).astype(BF16)
    for copy in gg_sends:
        copy.wait_recv()
    for copy in [*stores.made[6:], *w_stores.made[: ff // tall], *w_stores.made[-2:]]:
        copy.wait()
    sends.finish()


def experts(ctx, tokens, small, gain, member, slots, up_all, wo, wg, wu, wd, collective_id):
    rows, width = ctx.shape
    ff = wg.shape[1]
    capacity = rows * 9 // 16
    high = width // 16
    vmem = pltpu.VMEM
    return pl.pallas_call(
        experts_kernel,
        out_shape=[
            sds((rows, width), F32),
            sds((EXPERTS, rows), F32),
            sds((8, 8, rows), F32),
            sds((2, rows // 2, width), BF16),
            sds((rows, width), F32),
            sds((8, rows, width), BF16),
            sds((4, 4, high * 3 // 2, width), BF16),
        ],
        in_specs=[VMEM] * 6 + [ANY] * 5,
        out_specs=[VMEM] * 5 + [ANY] * 2,
        scratch_shapes=[
            vmem((width, width), BF16),
            vmem((width, ff), BF16),
            vmem((width, ff), BF16),
            vmem((ff, width), BF16),
            vmem((8, rows, width), BF16),
            vmem((4, 2, rows, width), BF16),
            vmem((8 * capacity, width), BF16),
            vmem((8 * capacity, width), BF16),
            vmem((8 * capacity, ff), BF16),
            vmem((8 * capacity, 2 * ff), BF16),
            vmem((4, rows, width), BF16),
            *[vmem((rows // 2, width), BF16)] * 4,
            vmem((2, 4, high, width), BF16),
            vmem((2, 2, 4, high // 2, width), BF16),
            vmem((2, rows, width), BF16),
            vmem((8, EXPERTS, rows), F32),
            vmem((4, 2, 8, rows), F32),
            semaphores(8),
            semaphores(6),
            semaphores(8),
            semaphores(40),
            semaphores(40),
        ],
        compiler_params=remote_params(collective_id),
    )(ctx, tokens, small, gain, member, slots, up_all, wo, wg, wu, wd)


def middle_kernel(
    middle_ref, gates_ref, gg_all, sums_ref, own_ref, d_out_ref, ctx_ref, small_ref, gain_ref,
    start_ref, q_ref, kv_ref, lse_ref, cos_ref, sin_ref, normed_ref, wo_hbm, w_grads,
    grad_middle_ref, small_grad_ref, gq_ref, lin_kv, wo_out, w_done, grads_out,
    wo_ref, g_ref, from_left, from_right, w_total_0, w_total_1, w_whole, w_far,
    bias, k_t, gkv, probs, grad_probs, second_whole, second_far, kv_terms, kv_sum, normed_t, tile,
    *refs,
):
    place = Place()
    core = place.core
    neighbours = [place.partner, *place.x_to, *place.y_to, *place.z_to]
    greet(neighbours)
    bufs, x_bufs = refs[:12], refs[12:17]
    wo_sem, tile_sems, local_sems, send_sems, recv_sems = refs[17:]
    keeps = Keeps(local_sems)
    cols = w_total_0.shape[-1]
    totals = (w_total_0, w_total_1)
    length, rows = bias.shape
    width = middle_ref.shape[1]
    quarter, height = width // 4, wo_ref.shape[2]

    def part_of(ref, p, w):
        return ref.at[:, w] if p else ref.at[w]

    loads = {}
    for k in range(4):
        for p in range(2):
            me, (right, left, far), _ = place.ring(p == 0)
            w = (far, right, left, me)[k]
            src = part_of(w_grads, p, w).at[:, :, pl.ds(p * cols, cols)]
            loads[k, p] = keeps.start(src, part_of(totals[p], p, w))
    wo_load = pltpu.make_async_copy(wo_hbm, wo_ref, wo_sem)
    wo_load.start()
    await_greetings(neighbours)
    sends = Sends(send_sems, recv_sems)
    came = [
        sends.start(sums_ref.at[i], dst, place.x_to[i])
        for i, dst in enumerate((from_left, from_right))
    ]

    def first_half(p):
        def view(w, h):
            span = pl.ds(2 * h, 2)
            return totals[p].at[span, w] if p else totals[p].at[w, span]

        return view

    def expert_steps():
        rings = [Ring(p == 0, first_half(p), w_whole.at[p], w_far.at[p]) for p in range(2)]
        yield from ring_sum(place, sends, rings, lambda k, i, w: loads[k, i].wait())
        half = cols // 2

        def second_half(p):
            def view(w, h):
                at = pl.ds(h * half, half)
                return totals[p].at[w, place.z, :, at] if p else totals[p].at[place.y, w, :, at]

            return view

        rings = [
            Ring(p == 1, second_half(p), second_whole.at[p], second_far.at[p]) for p in range(2)
        ]
        yield from ring_sum(place, sends, rings)
        spreads = []
        for p in range(2):
            me = place.ring(p == 1)[0]
            w_done[p, me] = totals[p][place.y, place.z]

            view = lambda w, p=p: w_done.at[p, w]
            spreads.append(Spread(p == 1, w_done.at[p, me], view, half_columns))
        yield from ring_gather(place, sends, spreads)

    def columns(c, p):
        return pl.ds(pl.multiple_of((2 * c + p) * quarter, 128), quarter)

    def theirs_of(p):
        at = columns(1 - core, p)
        if p == 0:
            return lambda w: wo_ref.at[w, :, :, at]
        return lambda w: wo_ref.at[:, w, :, at]

    strips = [
        Strip(
            p == 0, wo_ref.at[:, :, :, columns(core, p)], bufs[6 * p : 6 * p + 6],
            None, theirs_of(p),
        )
        for p in range(2)
    ]
    expert = expert_steps()
    dense = dp_sum(place, sends, strips, ())
    next(expert)

    grad_gates = jnp.concatenate([gg_all[e, :1] for e in range(EXPERTS)], axis=0)
    gates_t = gates_ref[...]
    products = gates_t * grad_gates
    grad_logits = products - gates_t * jnp.sum(products, axis=0, keepdims=True)
    grad_logits = jnp.concatenate(
        [grad_logits, jnp.zeros((128 - EXPERTS, rows), F32)], axis=0
    ).T.astype(BF16)
    total = own_ref[...] + mm_nt(grad_logits, small_ref[...])
    middle, gain = middle_ref[...], gain_ref[...]
    inverse = inverse_rms(middle)
    scaled = middle * inverse
    small_grad = mm_tn((scaled * gain).astype(BF16), grad_logits)
    fill_bias(bias, start_ref, rows * place.part)
    for copy in came:
        copy.wait_recv()
    total += jnp.concatenate([from_left[...], from_right[...]], axis=0).astype(F32)
    grad_gain = jnp.sum(total * scaled, axis=0, keepdims=True)
    lanes = lax.broadcasted_iota(jnp.int32, (width, 128), 1)
    small_grad += jnp.where(lanes == EXPERTS, as_column(grad_gain, 128), 0.0)
    small_grad_ref[...] = small_grad.astype(BF16)
    weighted = total * gain
    inner = jnp.mean(weighted * scaled, axis=-1, keepdims=True)
    grad_middle = d_out_ref[...].astype(F32) + inverse * (weighted - scaled * inner)
    grad_middle_ref[...] = grad_middle
    grad_attn = grad_middle.astype(BF16)
    wo_load.wait()
    g_ref[...] = mm_nt(grad_attn, wo_ref[...].reshape(width, width)).astype(BF16)
    next(expert)
    tall = width // 4
    for i in range(4):
        got = mm_tn(ctx_ref[:, i * tall : (i + 1) * tall], grad_attn).astype(BF16)
        wo_ref[i] = got.reshape(wo_ref.shape[1:])
    next(dense)

    when = {2: (dense,), 6: (dense,), 8: (expert,), 10: (dense,)}
    for group in range(KEY_VALUE_HEADS):
        keys = slice(2 * group * HEAD_SIZE, (2 * group + 1) * HEAD_SIZE)
        values = slice((2 * group + 1) * HEAD_SIZE, (2 * group + 2) * HEAD_SIZE)
        k_t[...] = kv_ref[:, keys].astype(F32).T.astype(BF16)
        gkv[...] = jnp.zeros_like(gkv)

        def one_head(i, carry, base):
            head = base + i
            query, grad = q_ref[:, head_columns(head)], g_ref[:, head_columns(head)]
            lse = lse_ref[head]
            inner = jnp.zeros_like(lse)
            for at in range(0, length, BLOCK):
                span = pl.ds(at, BLOCK)
                s = mm_nt(kv_ref[span, keys], query) + bias[span]
                p = jnp.exp2(s * (SCALE * LOG2E) - lse)
                gp = mm_nt(kv_ref[span, values], grad)
                inner += jnp.sum(p * gp, axis=0, keepdims=True)
                probs[span] = p
                grad_probs[span] = gp
                gkv[span, HEAD_SIZE:] += mm(p.astype(BF16), grad)
            gq = jnp.zeros((HEAD_SIZE, rows), F32)
            for at in range(0, length, BLOCK):
                span = pl.ds(at, BLOCK)
                gs = (probs[span] * (grad_probs[span] - inner)).astype(BF16)
                gkv[span, :HEAD_SIZE] += mm(gs, query)
                gq += mm(k_t[:, span], gs)
            turned = spin(gq.T * SCALE, cos_ref[...], -sin_ref[...])
            gq_ref[:, head_columns(head)] = turned.astype(BF16)
            return carry

        for base in range(group * GROUP, (group + 1) * GROUP, 2):
            lax.fori_loop(0, 2, lambda i, carry, base=base: one_head(i, carry, base), 0)
            for steps in when.get(base + 2, ()):
                next(steps)
        shape = (8, rows, HEAD_SIZE)
        kv_terms[:, :, keys] = (gkv[:, :HEAD_SIZE] * SCALE).astype(BF16).reshape(shape)
        kv_terms[:, :, values] = gkv[:, HEAD_SIZE:].astype(BF16).reshape(shape)

    kv_steps = x_sum(place, sends, kv_terms, kv_sum, *x_bufs)
    next(kv_steps)
    stores = Keeps(tile_sems)
    wide = width // 4

    def put(s, at, right_side):
        slot, size = len(stores.made) % 2, right_side.shape[1]
        if len(stores.made) > 1:
            stores.made[-2].wait()
        got = mm(normed_t[...], right_side).astype(BF16)
        tile[slot, :, :, :, :size] = got.reshape(4, 4, height, size)
        stores.start(
            tile.at[slot, :, :, :, pl.ds(0, size)], grads_out.at[s, :, :, :, pl.ds(at, size)]
        )

    next(expert)
    normed_t[...] = normed_ref[...].astype(F32).T.astype(BF16)
    for s in range(2):
        put(s, 0, gq_ref[:, s * wide : (s + 1) * wide])
    next(kv_steps)
    next(dense)
    next(expert)
    for s in range(2, 4):
        put(s, 0, gq_ref[:, s * wide : (s + 1) * wide])
    run_out(kv_steps)
    cosine, sine = cos_ref[...], sin_ref[...]
    for s in range(4):
        got = kv_sum[:, s * HEAD_SIZE : (s + 1) * HEAD_SIZE]
        if s % 2 == 0:
            got = spin(got, cosine, -sine)
        got = got.astype(BF16)
        lin_kv[:, s * HEAD_SIZE : (s + 1) * HEAD_SIZE] = got
        put(s, wide, got)
    run_out(expert, dense)
    for copy in stores.made[-2:]:
        copy.wait()
    for p, s in enumerate(strips):
        wo_out[:, columns(core, p)] = s.result[...]
        wo_out[:, columns(1 - core, p)] = s.near[3]
    sends.finish()


def between(
    middle, gates, gg, sums, own, d_out, ctx, small, gain, start, query, kv, lse, cosine, sine,
    normed, wo, w_grads, collective_id,
):
    rows, width = query.shape
    length = kv.shape[0]
    height, quarter = width // 16, width // 4
    high, cols = w_grads.shape[2], width // 2
    vmem = pltpu.VMEM
    return pl.pallas_call(
        middle_kernel,
        out_shape=[
            sds((rows, width), F32),
            sds((width, 128), BF16),
            sds((rows, width), BF16),
            sds((rows, kv.shape[1]), BF16),
            sds((height, width), BF16),
            sds((2, 4, high, cols), BF16),
            sds((4, 4, 4, height, quarter + HEAD_SIZE), BF16),
        ],
        in_specs=[VMEM] * 16 + [ANY] * 2,
        out_specs=[VMEM] * 6 + [ANY],
        scratch_shapes=[
            vmem((4, 4, height, width), BF16),
            vmem((rows, width), BF16),
            vmem((rows // 2, width), BF16),
            vmem((rows // 2, width), BF16),
            vmem((4, 4, high, cols), BF16),
            vmem((4, 4, high, cols), BF16),
            vmem((2, 2, 2, 2, high, cols), BF16),
            vmem((2, 2, 2, high, cols), BF16),
            vmem((length, rows), F32),
            vmem((HEAD_SIZE, length), BF16),
            vmem((length, 2 * HEAD_SIZE), F32),
            vmem((length, rows), F32),
            vmem((length, rows), F32),
            vmem((2, 2, 2, high, cols // 2), BF16),
            vmem((2, 2, high, cols // 2), BF16),
            vmem((8, rows, kv.shape[1]), BF16),
            vmem((rows, kv.shape[1]), F32),
            vmem((width, rows), BF16),
            vmem((2, 4, 4, height, quarter), BF16),
            *strip_buffers(height, quarter),
            *strip_buffers(height, quarter),
            *x_buffers(rows, kv.shape[1]),
            pltpu.SemaphoreType.DMA,
            semaphores(8),
            semaphores(8),
            semaphores(90),
            semaphores(90),
        ],
        compiler_params=remote_params(collective_id),
    )(
        middle, gates, gg, sums, own, d_out, ctx, small, gain, start, query, kv, lse, cosine, sine,
        normed, wo, w_grads,
    )


def last_kernel(
    gq_ref, lin_kv, tokens_ref, gain_ref, small_ref, w_done, grads, blocks_ref, w_hbm,
    grad_inputs_ref, strips_out, small_out, combined, w_sums,
    small_total, w_ref, total_0, total_1, *refs,
):
    place = Place()
    core = place.core
    neighbours = [place.partner, *place.x_to, *place.y_to, *place.z_to]
    greet(neighbours)
    bufs, x_bufs = refs[:18], refs[18:23]
    w_sem, strip_sems, local_sems, send_sems, recv_sems = refs[23:]
    load = pltpu.make_async_copy(w_hbm, w_ref, w_sem)
    load.start()
    width = w_ref.shape[0]
    strip = total_0.shape[-1]
    wide = strip - HEAD_SIZE

    def terms(c, p):
        s = 2 * c + p
        if p == 0:
            return lambda w: grads.at[s, w]
        return lambda w: grads.at[s, :, w]

    strips = [
        Strip(
            p == 0, total, bufs[6 * p : 6 * p + 6], terms(core, p), terms(1 - core, p)
        )
        for p, total in enumerate((total_0, total_1))
    ]

    keeps = Keeps(local_sems)

    def spread(p):
        cols = pl.ds(p * w_done.shape[-1], w_done.shape[-1])

        def view(w):
            return w_sums.at[:, w, :, cols] if p else w_sums.at[w, :, :, cols]

        keeps.start(w_done.at[p], view(place.ring(p == 0)[0]))
        return Spread(p == 0, w_done.at[p], view, half_span)

    spreads = [spread(p) for p in range(2)]
    await_greetings(neighbours)
    sends = Sends(send_sems, recv_sems)
    wide_steps = dp_sum(place, sends, strips, strip_sems)
    expert_steps = ring_gather(place, sends, spreads)
    rest = x_sum(place, sends, blocks_ref, combined, *x_bufs)
    next(wide_steps)
    next(expert_steps)
    next(rest)
    next(wide_steps)
    next(expert_steps)

    load.wait()
    grad_normed = None
    for s in range(4):
        at = s * strip
        term = mm_nt(gq_ref[:, s * wide : (s + 1) * wide], w_ref[:, at : at + wide])
        term += mm_nt(
            lin_kv[:, s * HEAD_SIZE : (s + 1) * HEAD_SIZE], w_ref[:, at + wide : at + strip]
        )
        grad_normed = term if grad_normed is None else grad_normed + term
    grad_inputs, grad_gain = rms_back(tokens_ref[...].astype(F32), gain_ref[...], grad_normed)
    grad_inputs_ref[...] = grad_inputs
    lanes = lax.broadcasted_iota(jnp.int32, (width, 128), 1)
    small = jnp.where(
        lanes == EXPERTS + 1, as_column(grad_gain, 128), small_ref[...].astype(F32)
    )
    small_total[...] = small.astype(BF16).reshape(small_total.shape)
    small_strip = Strip(True, small_total, bufs[12:])
    small_steps = dp_sum(place, sends, [small_strip], ())
    next(small_steps)
    next(small_steps)
    next(rest)
    next(expert_steps)
    run_out(wide_steps, small_steps, rest, expert_steps)
    small_out[...] = small_strip.result[...].astype(F32) + small_strip.near[3].astype(F32)
    for p, s in enumerate(strips):
        for c, got in ((core, s.result), (1 - core, s.near.at[3])):
            strips_out[:, pl.ds(pl.multiple_of((2 * c + p) * strip, 128), strip)] = got[...]
    for copy in keeps.made:
        copy.wait()
    sends.finish()


def last(grad_query, lin_kv, tokens, gain, small, w_done, grads, back_out, w, collective_id):
    rows, width = tokens.shape
    total = w.shape[1]
    height, strip = width // 16, total // 4
    vmem = pltpu.VMEM
    return pl.pallas_call(
        last_kernel,
        out_shape=[
            sds((rows, width), F32),
            sds((height, total), BF16),
            sds((height, 128), F32),
            sds((rows, width), F32),
            sds((4, 4, w_done.shape[2], width), BF16),
        ],
        in_specs=[VMEM] * 6 + [ANY] * 3,
        out_specs=[VMEM] * 4 + [ANY],
        scratch_shapes=[
            vmem((4, 4, height, 128), BF16),
            vmem((width, total), BF16),
            vmem((4, 4, height, strip), BF16),
            vmem((4, 4, height, strip), BF16),
            *strip_buffers(height, strip),
            *strip_buffers(height, strip),
            *strip_buffers(height, 128, shared=False),
            *x_buffers(rows, width),
            pltpu.SemaphoreType.DMA,
            semaphores(8),
            semaphores(2),
            semaphores(100),
            semaphores(100),
        ],
        compiler_params=remote_params(collective_id),
    )(grad_query, lin_kv, tokens, gain, small, w_done, grads, back_out, w)


def finish_kernel(
    sums_ref, grad_middle_ref, grad_inputs_ref, middle_ref, combined_ref, strips_ref, wo_ref,
    small_ref, g_out, u_out, d_out, tokens_out, mixed_out, wq_out, wk_out, wv_out, wo_out,
    small_out,
):
    owners, high, width = sums_ref.shape
    ff = width // 2
    gu = high * 2 // 3
    g_out[...] = sums_ref[:, :gu, :ff].astype(F32).reshape(owners * gu, ff)
    u_out[...] = sums_ref[:, :gu, ff:].astype(F32).reshape(owners * gu, ff)
    d_out[...] = sums_ref[:, gu:].astype(F32).reshape(owners * (high - gu), width)
    tokens_out[...] = grad_middle_ref[...] + grad_inputs_ref[...]
    mixed_out[...] = (middle_ref[...] + combined_ref[...]).astype(BF16)

    @pl.when(pl.program_id(0) == 0)
    def _():
        strip = strips_ref.shape[1] // 4
        wide = strip - HEAD_SIZE
        for s in range(4):
            at = s * strip
            wq_out[:, s * wide : (s + 1) * wide] = strips_ref[:, at : at + wide].astype(F32)
            other = (wk_out, wv_out)[s % 2]
            begin_at = s // 2 * HEAD_SIZE
            got = strips_ref[:, at + wide : at + strip].astype(F32)
            other[:, begin_at : begin_at + HEAD_SIZE] = got
        wo_out[...] = wo_ref[...].astype(F32)
        small_out[...] = small_ref[...]


def finish(sums, grad_middle, grad_inputs, middle, combined, strips, wo, small):
    owners, high, width = sums.shape
    rows = middle.shape[0]
    height, total = strips.shape
    kv_half = (total - width) // 2
    ff = width // 2
    gu, d = high * 2 // 3, high // 3
    steps = 8
    each, part = owners // steps, rows // steps
    by_step = lambda a, b: pl.BlockSpec((a, b), lambda i: (i, 0))
    whole = lambda a, b: pl.BlockSpec((a, b), lambda i: (0, 0))
    return pl.pallas_call(
        finish_kernel,
        grid=(steps,),
        out_shape=[
            sds((owners * gu, ff), F32),
            sds((owners * gu, ff), F32),
            sds((owners * d, width), F32),
            sds((rows, width), F32),
            sds((rows, width), BF16),
            sds((height, width), F32),
            sds((height, kv_half), F32),
            sds((height, kv_half), F32),
            sds((height, width), F32),
            sds((height, 128), F32),
        ],
        in_specs=[pl.BlockSpec((each, high, width), lambda i: (i, 0, 0))]
        + [by_step(part, width)] * 4
        + [whole(height, total), whole(height, width), whole(height, 128)],
        out_specs=[
            by_step(each * gu, ff),
            by_step(each * gu, ff),
            by_step(each * d, width),
            by_step(part, width),
            by_step(part, width),
            whole(height, width),
            whole(height, kv_half),
            whole(height, kv_half),
            whole(height, width),
            whole(height, 128),
        ],
        compiler_params=pltpu.CompilerParams(vmem_limit_bytes=63 * MIB),
        cost_estimate=pl.CostEstimate(flops=0, bytes_accessed=30 * MIB, transcendentals=0),
    )(sums, grad_middle, grad_inputs, middle, combined, strips, wo, small)


def on_device(
    tokens,
    d_out,
    gain_in,
    w_query,
    key_projection_weight,
    value_projection_weight,
    w_out,
    gain_mid,
    w_router,
    w_gate,
    w_up,
    w_down,
    routes,
    segments,
):
    rows, width = tokens.shape
    length = segments.shape[1]
    part = lax.axis_index("expert")
    seg_row = segments[0]
    offset = part * rows
    my_seg = lax.dynamic_slice_in_dim(seg_row, offset, rows, 0)
    start = jnp.sum((seg_row[None, :] < my_seg[:, None]).astype(jnp.int32), axis=1)
    angles = angles_for(offset + jnp.arange(rows, dtype=jnp.int32) - start)
    cosine, sine = jnp.cos(angles), jnp.sin(angles)
    cosine = jnp.concatenate([cosine, cosine], axis=1)
    sine = jnp.concatenate([-sine, sine], axis=1)
    start = start[None, :]

    small = jnp.concatenate([w_router, gain_mid[:, None], gain_in[:, None]], axis=1)
    small = jnp.pad(small, ((0, 0), (0, 128 - small.shape[1])))
    note = jnp.pad(routes.T, ((0, 8 - TOPK), (0, 0)))
    w_strips, small, wo_part, upstream_all, notes, normed, query, kv_all = begin(
        w_query, key_projection_weight, value_projection_weight, w_out, small, d_out, note,
        tokens, cosine, sine, 1,
    )
    w_strips = w_strips.reshape(width, -1)
    small = small.reshape(width, -1)
    gain_mid_row = small[:, EXPERTS].astype(F32)[None, :]
    gain_in_row = small[:, EXPERTS + 1].astype(F32)[None, :]
    kv_all = kv_all.reshape(length, -1)
    context, lse, wo = attend(start, query, kv_all, wo_part, 2)

    member = jnp.any(routes[:, :, None] == jnp.arange(128, dtype=jnp.int32), axis=1).astype(F32)
    chosen = jnp.any(notes[:, :TOPK] == part, axis=1)
    slots = jnp.where(chosen, jnp.cumsum(chosen.astype(jnp.int32), axis=1) - 1, -1)[:, None, :]
    middle, gates, gg, sums, own, back_out, w_grads = experts(
        context, tokens, small, gain_mid_row, member, slots, upstream_all,
        wo.reshape(width, width), w_gate[0], w_up[0], w_down[0], 3,
    )
    grad_middle, small_grads, grad_query, grad_kv, wo_sum, w_done, strip_grads = between(
        middle, gates, gg, sums, own, d_out, context, small, gain_mid_row, start, query, kv_all,
        lse, cosine, sine, normed, wo, w_grads, 4,
    )
    grad_inputs, strips_sum, small_sum, combined, w_sums = last(
        grad_query, grad_kv, tokens, gain_in_row, small_grads, w_done, strip_grads, back_out,
        w_strips, 5,
    )
    g_wg, g_wu, g_wd, grad_tokens, mixed, g_wq, g_wk, g_wv, g_wo, small_sum = finish(
        w_sums.reshape(16, -1, width), grad_middle, grad_inputs, middle, combined, strips_sum,
        wo_sum, small_sum,
    )
    return (
        mixed,
        grad_tokens,
        small_sum[:, EXPERTS + 1],
        g_wq,
        g_wk,
        g_wv,
        g_wo,
        small_sum[:, EXPERTS],
        small_sum[:, :EXPERTS],
        g_wg[None],
        g_wu[None],
        g_wd[None],
    )


def solution(mesh):
    whole = P(("dp", "expert"), None)
    over_dp, by_dp, over_expert = P("dp"), P("dp", None), P("expert", None, None)
    return jax.shard_map(
        on_device,
        mesh=mesh,
        in_specs=(whole, whole, over_dp, by_dp, by_dp, by_dp, by_dp, over_dp, by_dp)
        + (over_expert,) * 3
        + (whole, by_dp),
        out_specs=(whole, whole, over_dp, by_dp, by_dp, by_dp, by_dp, over_dp, by_dp)
        + (over_expert,) * 3,
        check_vma=False,
    )
```

```python
import functools

import jax
import jax.numpy as jnp
from jax import lax
from jax.experimental import pallas as pl
from jax.experimental.pallas import tpu as pltpu
from jax.sharding import PartitionSpec as P

QUERY_HEADS = 12
KEY_VALUE_HEADS = 2
HEAD_SIZE = 128
TOPK = 4
EXPERTS = 8
GROUP = QUERY_HEADS // KEY_VALUE_HEADS
SCALE = HEAD_SIZE**-0.5
LOG2E = 1.4426950408889634
BLOCK = 512

EPSILON = 1e-06
ROPE_BASE = 1000000.0
MASK_FILL = -1e30
F32 = jnp.float32
BF16 = jnp.bfloat16

MESH = pl.DeviceIdType.MESH
ANY = pl.BlockSpec(memory_space=pl.ANY)
VMEM = pl.BlockSpec(memory_space=pltpu.VMEM)
MIB = 2**20


def dot(a, b, dims):
    return lax.dot_general(a, b, (dims, ((), ())), preferred_element_type=F32)


def mm(a, b):
    return dot(a, b, ((1,), (0,)))


def mm_nt(a, b):
    return dot(a, b, ((1,), (1,)))


def mm_tn(a, b):
    return dot(a, b, ((0,), (0,)))


def sds(shape, dtype):
    return jax.ShapeDtypeStruct(tuple(shape), dtype)


def remote_params(collective_id):
    return pltpu.CompilerParams(
        collective_id=collective_id, has_side_effects=True, vmem_limit_bytes=63 * MIB
    )


def semaphores(count):
    return pltpu.SemaphoreType.DMA((count,))


def inverse_rms(rows):
    return lax.rsqrt(jnp.mean(rows * rows, axis=-1, keepdims=True) + EPSILON)


def rms_back(rows, gain, grad):
    inverse = inverse_rms(rows)
    scaled = rows * inverse
    weighted = grad * gain
    inner = jnp.mean(weighted * scaled, axis=-1, keepdims=True)
    return inverse * (weighted - scaled * inner), jnp.sum(grad * scaled, axis=0, keepdims=True)


def as_column(row, lanes):
    return jnp.broadcast_to(row, (lanes, row.shape[1])).T


def angles_for(positions):
    half_width = HEAD_SIZE // 2
    freqs = ROPE_BASE ** (-2.0 * jnp.arange(half_width, dtype=F32) / HEAD_SIZE)
    return positions.astype(F32)[:, None] * freqs[None, :]


def spin(z, cosine, sine):
    return z * cosine + pltpu.roll(z, HEAD_SIZE // 2, 1) * sine


class Sends:
    def __init__(self, send_sems, recv_sems):
        self.send_sems, self.recv_sems, self.made = send_sems, recv_sems, []

    def start(self, src, dst, to):
        at = len(self.made)
        copy = pltpu.make_async_remote_copy(
            src_ref=src,
            dst_ref=dst,
            send_sem=self.send_sems.at[at],
            recv_sem=self.recv_sems.at[at],
            device_id=to,
            device_id_type=MESH,
        )
        copy.start()
        self.made.append(copy)
        return copy

    def finish(self):
        for copy in self.made:
            copy.wait_send()


class Keeps:
    def __init__(self, sems):
        self.sems, self.made = sems, []

    def start(self, src, dst):
        copy = pltpu.make_async_copy(src, dst, self.sems.at[len(self.made)])
        copy.start()
        self.made.append(copy)
        return copy


class Place:
    def __init__(self):
        self.part = lax.axis_index("expert")
        self.core = self.part % 2
        self.chip = self.part // 2
        at = lambda d: lax.rem(self.chip + d, 4) * 2 + self.core
        self.right, self.left, self.far = at(1), at(3), at(2)
        to = lambda i: {"expert": i}
        self.partner = to(2 * self.chip + (1 - self.core))
        self.x_to = [to(self.right), to(self.left), to(self.far)]
        self.others = [to(lax.rem(self.part + d, 8)) for d in range(1, 8)]
        place = lax.axis_index("dp")
        self.y, self.z = place // 4, place % 4
        ring = lambda v: [lax.rem(v + d, 4) for d in (1, 3, 2)]
        self.y_ring, self.z_ring = ring(self.y), ring(self.z)
        self.y_to = [{"dp": v * 4 + self.z} for v in self.y_ring[:2]]
        self.z_to = [{"dp": self.y * 4 + v} for v in self.z_ring[:2]]

    def ring(self, along_y):
        if along_y:
            return self.y, self.y_ring, self.y_to
        return self.z, self.z_ring, self.z_to


def greet(others):
    barrier = pltpu.get_barrier_semaphore()
    for other in others:
        pl.semaphore_signal(barrier, inc=1, device_id=other, device_id_type=MESH)


def await_greetings(others):
    pl.semaphore_wait(pltpu.get_barrier_semaphore(), len(others))


def add_to(ref, *others):
    got = ref[...].astype(F32)
    for other in others:
        got += other[...].astype(F32)
    ref[...] = got.astype(ref.dtype)


def run_out(*steps):
    steps = list(steps)
    while steps:
        for s in list(steps):
            if next(s, "done") == "done":
                steps.remove(s)


def x_sum(place, sends, blocks_ref, out_ref, mine, total, from_left, from_right, sems):
    rows = out_ref.shape[0]
    half = rows // 2
    low, high = pl.ds(0, half), pl.ds(half, half)
    to_right, to_left = place.x_to[:2]
    flip = 1 - 2 * place.core
    keeps = Keeps(sems)
    swaps, loads = [], []
    for k, dest in enumerate((place.far, place.right, place.left, place.part)):
        swaps.append(sends.start(blocks_ref.at[dest + flip], total.at[k], place.partner))
        loads.append(keeps.start(blocks_ref.at[dest], mine.at[k]))

    def add_up(k):
        loads[k].wait()
        swaps[k].wait_recv()
        add_to(total.at[k], mine.at[k])

    yield
    add_up(0)
    far_low = sends.start(total.at[0, low], from_left.at[0], to_right)
    far_high = sends.start(total.at[0, high], from_right.at[0], to_left)
    add_up(1)
    right_high = sends.start(total.at[1, high], from_left.at[2], to_right)
    add_up(2)
    left_low = sends.start(total.at[2, low], from_right.at[2], to_left)
    yield
    far_low.wait_recv()
    add_to(total.at[1, low], from_left.at[0])
    right_low = sends.start(total.at[1, low], from_left.at[1], to_right)
    far_high.wait_recv()
    add_to(total.at[2, high], from_right.at[0])
    left_high = sends.start(total.at[2, high], from_right.at[1], to_left)
    yield
    loads[3].wait()
    swaps[3].wait_recv()
    out_ref[...] = mine[3].astype(F32) + total[3].astype(F32)
    right_high.wait_recv()
    left_low.wait_recv()
    right_low.wait_recv()
    left_high.wait_recv()
    add_to(out_ref.at[low], from_left.at[1], from_right.at[2])
    add_to(out_ref.at[high], from_left.at[2], from_right.at[1])
    yield


def x_buffers(rows, columns):
    return [
        pltpu.VMEM((4, rows, columns), BF16),
        pltpu.VMEM((4, rows, columns), BF16),
        pltpu.VMEM((3, rows // 2, columns), BF16),
        pltpu.VMEM((3, rows // 2, columns), BF16),
        semaphores(4),
    ]


class Ring:
    def __init__(self, along_y, view, whole, farther):
        self.along_y, self.view, self.whole, self.farther = along_y, view, whole, farther


def ring_sum(place, sends, rings, ready=lambda *_: None):
    going = []
    for i, r in enumerate(rings):
        _, (right, left, far), to = place.ring(r.along_y)
        ready(0, i, far)
        going.append([sends.start(r.view(far, h), r.farther.at[h], to[h]) for h in range(2)])
    for i, r in enumerate(rings):
        _, (right, left, far), to = place.ring(r.along_y)
        ready(1, i, right)
        ready(2, i, left)
        going[i].append(sends.start(r.view(right, 1), r.whole.at[0, 1], to[0]))
        going[i].append(sends.start(r.view(left, 0), r.whole.at[1, 0], to[1]))
    yield
    for i, r in enumerate(rings):
        _, (right, left, far), to = place.ring(r.along_y)
        for h, w in enumerate((right, left)):
            going[i][h].wait_recv()
            add_to(r.view(w, h), r.farther.at[h])
            going[i].append(sends.start(r.view(w, h), r.whole.at[h, h], to[h]))
    yield
    for i, r in enumerate(rings):
        me, _, _ = place.ring(r.along_y)
        ready(3, i, me)
        for copy in going[i][2:]:
            copy.wait_recv()
        for h in range(2):
            add_to(r.view(me, h), r.whole.at[0, h], r.whole.at[1, h])


class Spread:
    def __init__(self, along_y, source, view, half, landed=lambda _: None):
        self.along_y, self.source, self.view = along_y, source, view
        self.half, self.landed = half, landed


def ring_gather(place, sends, spreads):
    came, onward = [], []

    def send(s, h, to):
        me = place.ring(s.along_y)[0]
        return sends.start(s.half(s.source, h), s.half(s.view(me), h), to)

    for s in spreads:
        to = place.ring(s.along_y)[2]
        came.append([[send(s, d, to[d])] for d in range(2)])
    yield
    for s, copies in zip(spreads, came):
        to = place.ring(s.along_y)[2]
        for d in range(2):
            copies[d].append(send(s, 1 - d, to[d]))
    yield
    for s, copies in zip(spreads, came):
        _, (right, left, _), to = place.ring(s.along_y)
        onward.append([])
        for d, origin in enumerate((left, right)):
            copies[d][0].wait_recv()
            view = s.half(s.view(origin), d)
            onward[-1].append(sends.start(view, view, to[d]))
    yield
    for s, copies in zip(spreads, came):
        _, (right, left, _), _ = place.ring(s.along_y)
        for d, origin in enumerate((left, right)):
            copies[d][1].wait_recv()
            s.landed(s.view(origin))
    for s, copies in zip(spreads, onward):
        far = place.ring(s.along_y)[1][2]
        for d in range(2):
            copies[d].wait_recv()
            s.landed(s.half(s.view(far), d))
    yield


def half_span(share, h):
    return share.at[pl.ds(2 * h, 2)]


def half_rows(share, h):
    half = share.shape[0] // 2
    return share.at[pl.ds(h * half, half)]


def half_columns(share, h):
    half = share.shape[-1] // 2
    return share.at[:, pl.ds(h * half, half)]


class Strip:
    def __init__(self, y_first, total, bufs, own=None, other=None):
        self.y_first, self.total, self.own, self.other = y_first, total, own, other
        self.theirs, self.big, self.far, self.mid, self.midfar, self.near = bufs

    def block(self, ref, w):
        return ref.at[w] if self.y_first else ref.at[:, w]


def strip_buffers(rows, columns, shared=True):
    return [
        pltpu.VMEM((4, 4, rows, columns) if shared else (1, 1, rows, columns), BF16),
        pltpu.VMEM((2, 2, 2, rows, columns), BF16),
        pltpu.VMEM((2, 2, rows, columns), BF16),
        pltpu.VMEM((2, 2, rows // 2, columns), BF16),
        pltpu.VMEM((2, rows // 2, columns), BF16),
        pltpu.VMEM((4, rows, columns), BF16),
    ]


def dp_sum(place, sends, strips, sems):
    y, z = place.y, place.z
    keeps = Keeps(sems)
    swaps, loads = {}, {}
    for k in range(4):
        for i, s in enumerate(strips):
            me, (right, left, far), _ = place.ring(s.y_first)
            w = (far, right, left, me)[k]
            if s.other is not None:
                swaps[k, i] = sends.start(s.other(w), s.block(s.theirs, w), place.partner)
            if s.own is not None:
                loads[k, i] = keeps.start(s.own(w), s.block(s.total, w))
    yield

    def joined(k, i, s, w):
        if s.own is not None:
            loads[k, i].wait()
        if s.other is not None:
            swaps[k, i].wait_recv()
            add_to(s.block(s.total, w), s.block(s.theirs, w))

    def big(s, w, h):
        span = pl.ds(2 * h, 2)
        return s.total.at[w, span] if s.y_first else s.total.at[span, w]

    def small(s, w, h):
        half = s.total.shape[2] // 2
        at = pl.ds(h * half, half)
        return s.total.at[y, w, at] if s.y_first else s.total.at[w, z, at]

    def rings(first):
        view = big if first else small
        return [
            Ring(
                s.y_first == first,
                functools.partial(view, s),
                s.big if first else s.mid,
                s.far if first else s.midfar,
            )
            for s in strips
        ]

    yield from ring_sum(place, sends, rings(True), lambda k, i, w: joined(k, i, strips[i], w))
    yield from ring_sum(place, sends, rings(False))

    shares, back = [], []
    for s in strips:
        shares.append(
            [sends.start(s.total.at[y, z], s.near.at[i], place.x_to[i]) for i in range(3)]
        )
    yield
    for s, share in zip(strips, shares):
        for copy in share:
            copy.wait_recv()
        got = s.total[y, z].astype(F32)
        for i in range(3):
            got += s.near[i].astype(F32)
        s.result = s.theirs.at[y, z] if s.other is not None else s.theirs.at[0, 0]
        s.result[...] = got.astype(BF16)
        back.append(sends.start(s.result, s.near.at[3], place.partner))
    yield
    for copy in back:
        copy.wait_recv()
    yield


def begin_kernel(
    wq_hbm, wk_hbm, wv_hbm, wo_hbm, small_ref, rows_hbm, note_ref, tokens_hbm, cos_ref, sin_ref,
    w_out, small_out, wo_part, rows_near, notes_out, normed_ref, query_ref, kv_ref, gains_ref,
    strips_ref, w_all, own_kv, wq_ref, wk_ref, wv_ref, wo_ref, rows_ref, tokens_ref,
    fetch_sems, local_sems, send_sems, recv_sems,
):
    fetches = Keeps(fetch_sems)
    for src, dst in (
        (wq_hbm, wq_ref), (wk_hbm, wk_ref), (wv_hbm, wv_ref), (wo_hbm, wo_ref),
        (rows_hbm, rows_ref), (tokens_hbm, tokens_ref),
    ):
        fetches.start(src, dst)
    place = Place()
    y, z, core, part = place.y, place.z, place.core, place.part
    neighbours = [*place.others, *place.y_to, *place.z_to]
    greet(neighbours)
    rows = wq_ref.shape[0]
    wide, narrow = wq_ref.shape[1] // 4, wk_ref.shape[1] // 2
    strip = wide + narrow
    for fetch in fetches.made[:4]:
        fetch.wait()
    for s in range(4):
        strips_ref[:, s * strip : s * strip + wide] = wq_ref[:, s * wide : (s + 1) * wide]
        other = (wk_ref, wv_ref)[s % 2]
        begin = s // 2 * narrow
        strips_ref[:, s * strip + wide : (s + 1) * strip] = other[:, begin : begin + narrow]
    await_greetings(neighbours)
    sends, keeps = Sends(send_sems, recv_sems), Keeps(local_sems)

    def columns(p, size):
        return pl.ds(pl.multiple_of((2 * core + p) * size, 128), size)

    across = []

    def send_across(view):
        across.append(sends.start(view, view, place.partner))

    def spread(first, src, out, cols, y_first, landed):
        def near(where):
            return out.at[where, z, :, cols] if y_first else out.at[y, where, :, cols]

        def wider(where):
            return out.at[:, where, :, cols] if y_first else out.at[where, :, :, cols]

        if first:
            return Spread(y_first, src, near, half_rows)
        source = wider(z if y_first else y)
        landed(source)
        return Spread(not y_first, source, wider, half_span, landed)

    def strips(first, at, size):
        def part(p):
            return pl.ds(pl.multiple_of((2 * core + p) * strip + at, 128), size)

        return [
            spread(first, strips_ref.at[:, part(p)], w_all, part(p), p == 1, send_across)
            for p in range(2)
        ]

    def small_spread(first):
        every = pl.ds(0, small_ref.shape[1])
        return spread(first, small_ref, small_out, every, False, lambda _: None)

    def out_spread(p):
        ring_of = (z, y)[p]

        keeps.start(wo_ref.at[:, columns(p, wide)], wo_part.at[p, ring_of])
        return Spread(
            p == 1, wo_ref.at[:, columns(p, wide)], lambda where: wo_part.at[p, where], half_rows
        )

    ahead = ring_gather(place, sends, [*strips(True, wide, narrow), small_spread(True)])
    behind = ring_gather(place, sends, [*strips(True, 0, wide), *map(out_spread, range(2))])
    for steps in (ahead, ahead, behind, behind):
        next(steps)
    for p in range(2):
        w_all[y, z, :, columns(p, strip)] = strips_ref[:, columns(p, strip)]
    small_out[y, z] = small_ref[...]

    half = rows_ref.shape[0] // 2
    x_halves = [pl.ds(h * half, half) for h in range(2)]
    fetches.made[4].wait()
    rows_came = [
        sends.start(rows_ref.at[x_halves[h]], rows_near.at[d, x_halves[h]], place.x_to[d])
        for d in range(2)
        for h in (d, 1 - d)
    ]
    notes = [sends.start(note_ref, notes_out.at[part], to) for to in place.others]
    keeps.start(note_ref, notes_out.at[part])
    next(ahead)
    next(ahead)
    ahead = ring_gather(place, sends, [*strips(False, wide, narrow), small_spread(False)])
    next(ahead)
    next(ahead)
    next(behind)
    next(behind)
    behind = ring_gather(place, sends, strips(False, 0, wide))
    next(behind)
    next(behind)
    next(ahead)
    next(ahead)
    small_t = small_out[...].reshape(tokens_ref.shape[1], -1).astype(F32).T
    gains_ref[...] = small_t[EXPERTS : EXPERTS + 8]
    fetches.made[5].wait()
    inputs = tokens_ref[...].astype(F32)
    gain = small_t[EXPERTS + 1 : EXPERTS + 2]
    normed_ref[...] = (inputs * inverse_rms(inputs) * gain).astype(BF16)
    for copy in across:
        copy.wait_recv()
    del across[:]

    cosine, sine = cos_ref[...], sin_ref[...]
    width = tokens_ref.shape[1]

    def project(at, size):
        w = w_all[:, :, :, at : at + size].reshape(width, size)
        return mm(normed_ref[...], w)

    for s in range(4):
        got = project(s * strip + wide, HEAD_SIZE)
        if s % 2 == 0:
            got = spin(got, cosine, sine)
        own_kv[:, s * HEAD_SIZE : (s + 1) * HEAD_SIZE] = got.astype(BF16)
    slot = kv_ref.at[part]
    kv_came = [
        [
            sends.start(own_kv.at[x_halves[h]], slot.at[x_halves[h]], place.x_to[d])
            for h in (d, 1 - d)
        ]
        for d in range(2)
    ]
    kv_across = [sends.start(own_kv, slot, place.partner)]
    keeps.start(own_kv, slot)
    next(behind)
    next(behind)
    onward = []
    for d, origin in enumerate((place.left, place.right)):
        kv_came[d][0].wait_recv()
        view = kv_ref.at[origin, x_halves[d]]
        onward.append(sends.start(view, view, place.x_to[d]))
    for copy in across:
        copy.wait_recv()
    keeps.start(w_all, w_out)

    def queries(s):
        got = project(s * strip, wide)
        for h in range(0, wide, HEAD_SIZE):
            head = spin(got[:, h : h + HEAD_SIZE], cosine, sine)
            query_ref[:, s * wide + h : s * wide + h + HEAD_SIZE] = head.astype(BF16)

    for s in range(4):
        queries(s)
    for d, origin in enumerate((place.left, place.right)):
        kv_came[d][1].wait_recv()
        view = kv_ref.at[origin]
        kv_across.append(sends.start(view, view, place.partner))
    for d in range(2):
        onward[d].wait_recv()
        view = kv_ref.at[place.far, x_halves[d]]
        kv_across.append(sends.start(view, view, place.partner))
    for copy in [*kv_across, *notes, *rows_came]:
        copy.wait_recv()
    for copy in keeps.made:
        copy.wait()
    sends.finish()


def begin(wq, wk, wv, wo, small, rows, note, tokens, cosine, sine, collective_id):
    height, width = wq.shape
    kv_width = wk.shape[1] + wv.shape[1]
    total = width + kv_width
    count = tokens.shape[0]
    vmem = pltpu.VMEM
    return pl.pallas_call(
        begin_kernel,
        out_shape=[
            sds((4, 4, height, total), BF16),
            sds((4, 4, *small.shape), BF16),
            sds((2, 4, height, width // 4), BF16),
            sds((2, *rows.shape), BF16),
            sds((8, *note.shape), note.dtype),
            sds((count, width), BF16),
            sds((count, width), BF16),
            sds((8, count, kv_width), BF16),
            sds((8, width), F32),
        ],
        in_specs=[ANY] * 4 + [VMEM, ANY, VMEM, ANY, VMEM, VMEM],
        out_specs=[ANY, VMEM, VMEM, ANY, ANY, VMEM, VMEM, ANY, VMEM],
        scratch_shapes=[
            vmem((height, total), BF16),
            vmem((4, 4, height, total), BF16),
            vmem((count, kv_width), BF16),
            *[vmem(a.shape, BF16) for a in (wq, wk, wv, wo, rows, tokens)],
            semaphores(6),
            semaphores(6),
            semaphores(125),
            semaphores(125),
        ],
        compiler_params=remote_params(collective_id),
    )(wq, wk, wv, wo, small, rows, note, tokens, cosine, sine)


def fill_bias(bias, start_ref, first_row):
    length, rows = bias.shape
    places = lax.broadcasted_iota(jnp.int32, (length, rows), 0)
    mine = first_row + lax.broadcasted_iota(jnp.int32, (length, rows), 1)
    keep = (places >= start_ref[...]) & (places <= mine)
    bias[...] = jnp.where(keep, 0.0, MASK_FILL)


def head_columns(head):
    return pl.ds(pl.multiple_of(head * HEAD_SIZE, HEAD_SIZE), HEAD_SIZE)


def attend_kernel(
    start_ref, q_ref, kv_ref, wo_part, rows_own, rows_near, ctx_ref, lse_ref, wo_all, rows_far,
    rows_other, bias, v_t, scores, local_sems, send_sems, recv_sems,
):
    place = Place()
    neighbours = [place.partner, *place.x_to[:2], *place.y_to, *place.z_to]
    greet(neighbours)
    length, rows = bias.shape
    fill_bias(bias, start_ref, rows * place.part)
    await_greetings(neighbours)
    sends, keeps = Sends(send_sems, recv_sems), Keeps(local_sems)
    quarter = wo_part.shape[-1]
    across = []

    def landed(view):
        across.append(sends.start(view, view, place.partner))

    def spread(p):
        cols = pl.ds(pl.multiple_of((2 * place.core + p) * quarter, 128), quarter)

        def view(where):
            return wo_all.at[:, where, :, cols] if p else wo_all.at[where, :, :, cols]

        own = view((place.y, place.z)[p])
        keeps.start(wo_part.at[p], own)
        across.append(sends.start(wo_part.at[p], own, place.partner))
        return Spread(p == 0, wo_part.at[p], view, half_span, landed)

    steps = ring_gather(place, sends, [spread(p) for p in range(2)])
    next(steps)
    next(steps)

    half = rows // 2
    x_halves = [pl.ds(h * half, half) for h in range(2)]
    far_came = [
        sends.start(rows_near.at[d, x_halves[d]], rows_far.at[x_halves[d]], place.x_to[d])
        for d in range(2)
    ]
    for i, view in enumerate((rows_own, rows_near.at[0], rows_near.at[1])):
        across.append(sends.start(view, rows_other.at[i], place.partner))
    for group in range(KEY_VALUE_HEADS):
        keys = slice(2 * group * HEAD_SIZE, (2 * group + 1) * HEAD_SIZE)
        values = slice((2 * group + 1) * HEAD_SIZE, (2 * group + 2) * HEAD_SIZE)
        v_t[...] = kv_ref[:, values].astype(F32).T.astype(BF16)

        def one_head(i, carry, base):
            head = base + i
            query = q_ref[:, head_columns(head)]
            top = None
            for at in range(0, length, BLOCK):
                span = pl.ds(at, BLOCK)
                s = mm_nt(kv_ref[span, keys], query) + bias[span]
                scores[span] = s
                here = jnp.max(s, axis=0, keepdims=True)
                top = here if top is None else jnp.maximum(top, here)
            total = jnp.zeros_like(top)
            context = jnp.zeros((HEAD_SIZE, rows), F32)
            for at in range(0, length, BLOCK):
                span = pl.ds(at, BLOCK)
                p = jnp.exp2((scores[span] - top) * (SCALE * LOG2E))
                total += jnp.sum(p, axis=0, keepdims=True)
                context += mm(v_t[:, span], p.astype(BF16))
            ctx_ref[:, head_columns(head)] = (context / total).T.astype(BF16)
            lse_ref[head] = top * (SCALE * LOG2E) + jnp.log2(total)
            return carry

        for base in (group * GROUP, group * GROUP + GROUP // 2):
            lax.fori_loop(
                0, GROUP // 2, lambda i, carry, base=base: one_head(i, carry, base), 0
            )
            if base in (GROUP // 2, QUERY_HEADS - GROUP // 2):
                next(steps)
            if base == GROUP:
                for d, copy in enumerate(far_came):
                    copy.wait_recv()
                    view = rows_far.at[x_halves[d]]
                    across.append(
                        sends.start(view, rows_other.at[3, x_halves[d]], place.partner)
                    )
    run_out(steps)
    for copy in across:
        copy.wait_recv()
    for copy in keeps.made:
        copy.wait()
    sends.finish()


def attend(start, query, kv, wo_part, rows_own, rows_near, collective_id):
    rows, width = query.shape
    length = kv.shape[0]
    height = wo_part.shape[2]
    return pl.pallas_call(
        attend_kernel,
        out_shape=[
            sds((rows, width), BF16),
            sds((QUERY_HEADS, 1, rows), F32),
            sds((4, 4, height, width), BF16),
            sds((rows, width), BF16),
            sds((4, rows, width), BF16),
        ],
        in_specs=[VMEM] * 4 + [ANY] * 2,
        out_specs=[VMEM, VMEM, ANY, ANY, ANY],
        scratch_shapes=[
            pltpu.VMEM((length, rows), F32),
            pltpu.VMEM((HEAD_SIZE, length), BF16),
            pltpu.VMEM((length, rows), F32),
            semaphores(2),
            semaphores(32),
            semaphores(32),
        ],
        compiler_params=remote_params(collective_id),
    )(start, query, kv, wo_part, rows_own, rows_near)


LOW, HIGH = 0, 1


def gelu_parts(a):
    k = (2.0 / jnp.pi) ** 0.5
    square = a * a
    t = jnp.tanh(k * a * (1.0 + 0.044715 * square))
    slope = 0.5 * (1.0 + t) + 0.5 * a * (1.0 - t * t) * k * (1.0 + 3 * 0.044715 * square)
    return 0.5 * a * (1.0 + t), slope


def experts_kernel(
    ctx_ref, tokens_ref, small_ref, gains_ref, routes_ref, notes_ref,
    rows_own, rows_near, rows_far, rows_other, wo_hbm, wg_hbm, wu_hbm, wd_hbm,
    middle_ref, gates_ref, gg_all, sums_ref, own_ref, back_out, w_grads,
    wo_ref, wg_ref, wu_ref, wd_ref, rows_all, returns, arrived, pair_grad, hidden, grad_pre,
    theirs, far_left, far_right, from_left, from_right, tile, tile_d, back_rows, gates_all, gg_src,
    slot_ref,
    local_sems, tile_sems, back_sems, send_sems, recv_sems,
):
    place = Place()
    part, core = place.part, place.core
    right, left, far = place.right, place.left, place.far
    to_right, to_left = place.x_to[:2]
    greet(place.others)
    sends, keeps, stores = (
        Sends(send_sems, recv_sems), Keeps(local_sems), Keeps(back_sems)
    )
    rows, width = ctx_ref.shape
    half = rows // 2
    halves = (pl.ds(0, half), pl.ds(half, half))
    ff = wg_ref.shape[1]
    capacity = arrived.shape[0] // 8

    for src, dst in ((wo_hbm, wo_ref), (wg_hbm, wg_ref), (wu_hbm, wu_ref), (wd_hbm, wd_ref)):
        keeps.start(src, dst)
    chips = [lax.rem(place.chip + d, 4) for d in (0, 3, 1, 2)]
    for u, src in enumerate((rows_own, rows_near.at[0], rows_near.at[1], rows_far)):
        keeps.start(src, returns.at[u, core])
        keeps.start(rows_other.at[u], returns.at[u, 1 - core])

    keeps.made[0].wait()
    middle = tokens_ref[...].astype(F32) + mm(ctx_ref[...], wo_ref[...])
    middle_ref[...] = middle
    normed = (middle * inverse_rms(middle) * gains_ref[:1]).astype(BF16)
    rows_all[part] = normed
    lanes = lax.broadcasted_iota(jnp.int32, (rows, 128), 1)
    member = functools.reduce(
        jnp.logical_or, [lanes == routes_ref[:, k : k + 1] for k in range(TOPK)]
    ).astype(F32)
    logits = jnp.where(member > 0.0, mm(normed, small_ref[...]), MASK_FILL)
    weight = jnp.exp(logits - jnp.max(logits, axis=-1, keepdims=True)) * member
    gates = weight / jnp.sum(weight, axis=-1, keepdims=True)
    gates_ref[...] = gates.T[:EXPERTS]

    await_greetings(place.others)
    mine = rows_all.at[part]
    go = [
        [sends.start(mine.at[halves[h]], mine.at[halves[h]], way) for h in (d, 1 - d)]
        for d, way in enumerate((to_right, to_left))
    ]
    swap_own = sends.start(mine, mine, place.partner)
    note_sends = [sends.start(gates_ref, gates_all.at[part], to) for to in place.others]
    gates_all[part] = gates_ref[...]

    chosen = jnp.concatenate(
        [
            functools.reduce(
                jnp.logical_or, [notes_ref[s, k : k + 1] == part for k in range(TOPK)]
            ).astype(F32)
            for s in range(8)
        ],
        axis=0,
    )
    earlier = lax.broadcasted_iota(jnp.int32, (rows, rows), 0) < lax.broadcasted_iota(
        jnp.int32, (rows, rows), 1
    )
    ranks = mm(chosen.astype(BF16), earlier.astype(F32).astype(BF16))
    slots_of = jnp.where(chosen > 0.0, ranks, -1.0)
    for s in range(8):
        slot_ref[s] = slots_of[s : s + 1].astype(jnp.int32)

    def pick_of(source):
        slots = lax.broadcasted_iota(jnp.int32, (capacity, rows), 0)
        return slots == slot_ref[source]

    for u in range(4):
        keeps.made[4 + 2 * u].wait()
        keeps.made[5 + 2 * u].wait()
        for c in range(2):
            pick = pick_of(2 * chips[u] + c).astype(BF16)
            got = mm(pick, returns[u, c])
            pair_grad[pl.ds((2 * u + c) * capacity, capacity)] = got.astype(BF16)
    for load in keeps.made[1:4]:
        load.wait()

    swaps, gg_sends = [], []

    def unit(u):
        at = chips[u]
        picks = [pick_of(2 * at + c) for c in range(2)]
        picks_b = [pick.astype(BF16) for pick in picks]
        spans = [pl.ds((2 * u + c) * capacity, capacity) for c in range(2)]
        both = pl.ds(2 * u * capacity, 2 * capacity)
        gate = []
        for c in range(2):
            arrived[spans[c]] = mm(picks_b[c], rows_all[2 * at + c]).astype(BF16)
            row = gates_all[2 * at + c, pl.ds(part, 1)]
            gate.append(jnp.sum(jnp.where(picks[c], row, 0.0), axis=-1, keepdims=True))
        gate = jnp.concatenate(gate, axis=0)
        x = arrived[both]
        a, b = mm(x, wg_ref[...]), mm(x, wu_ref[...])
        act, slope = gelu_parts(a)
        h = (act * b).astype(BF16)
        hidden[both] = h
        out = mm(h, wd_ref[...]).astype(BF16).astype(F32)
        up = pair_grad[both].astype(F32)
        gg = jnp.sum(up * out, axis=-1, keepdims=True)
        weighted = (gate * out).astype(BF16)
        pg = (gate * up).astype(BF16)
        pair_grad[both] = pg
        for c in range(2):
            if u > 0:
                stores.made[2 * (u - 1) + c].wait()
            back_rows[c] = mm_tn(picks_b[c], weighted[c * capacity : (c + 1) * capacity]).astype(
                BF16
            )
            stores.start(back_rows.at[c], back_out.at[2 * at + c])
            gg_c = gg[c * capacity : (c + 1) * capacity]
            row = jnp.sum(jnp.where(picks[c], gg_c, 0.0), axis=0, keepdims=True)
            gg_src[u, c] = jnp.broadcast_to(row, (8, rows))
        grad_h = mm_nt(pg, wd_ref[...])
        grad_a = (grad_h * b * slope).astype(BF16)
        grad_b = (grad_h * act).astype(BF16)
        grad_pre[both, :ff] = grad_a
        grad_pre[both, ff:] = grad_b
        grad_rows = (mm_nt(grad_a, wg_ref[...]) + mm_nt(grad_b, wu_ref[...])).astype(BF16)
        for c in range(2):
            returns[u, c] = mm_tn(
                picks_b[c], grad_rows[c * capacity : (c + 1) * capacity]
            ).astype(BF16)
        swaps.append(sends.start(returns.at[u, 1 - core], theirs.at[u], place.partner))
        if u == 0:
            gg_all[part] = gg_src[0, core]
            gg_sends.append(sends.start(gg_src.at[0, 1 - core], gg_all.at[part], place.partner))
        else:
            for c in (core, 1 - core):
                gg_sends.append(
                    sends.start(gg_src.at[u, c], gg_all.at[part], {"expert": 2 * at + c})
                )

    def joined(u):
        swaps[u].wait_recv()
        add_to(theirs.at[u], returns.at[u, core])

    swap_own.wait_recv()
    for copy in note_sends:
        copy.wait_recv()
    unit(0)
    passed = []
    for d, (origin, way) in enumerate(((left, to_right), (right, to_left))):
        go[d][0].wait_recv()
        view = rows_all.at[origin, halves[d]]
        passed.append(sends.start(view, view, way))
    far_low, far_high = passed
    go[0][1].wait_recv()
    swap_left = sends.start(rows_all.at[left], rows_all.at[left], place.partner)
    go[1][1].wait_recv()
    swap_right = sends.start(rows_all.at[right], rows_all.at[right], place.partner)
    swap_left.wait_recv()
    unit(1)
    swap_right.wait_recv()
    unit(2)
    swap_far = []
    for h, copy in enumerate((far_low, far_high)):
        copy.wait_recv()
        piece = rows_all.at[far, halves[h]]
        swap_far.append(sends.start(piece, piece, place.partner))
    joined(1)
    joined(2)
    back_right = sends.start(theirs.at[2, halves[HIGH]], from_left, to_right)
    back_left = sends.start(theirs.at[1, halves[LOW]], from_right, to_left)
    for copy in swap_far:
        copy.wait_recv()
    unit(3)
    joined(3)
    back_far_low = sends.start(theirs.at[3, halves[LOW]], far_left, to_right)
    back_far_high = sends.start(theirs.at[3, halves[HIGH]], far_right, to_left)

    tall = 4 * w_grads.shape[2] * 2 // 3
    high = tall // 4
    w_stores = Keeps(tile_sems)
    for i in range(ff // tall):
        got = mm_tn(hidden[:, i * tall : (i + 1) * tall], pair_grad[...]).astype(BF16)
        tile_d[i] = got.reshape(tile_d.shape[1:])
        w_stores.start(tile_d.at[i], w_grads.at[pl.ds(2 * i, 2), :, pl.ds(high, high // 2)])
    for i in range(width // tall):
        if i >= 2:
            w_stores.made[ff // tall + i - 2].wait()
        got = mm_tn(arrived[:, i * tall : (i + 1) * tall], grad_pre[...]).astype(BF16)
        tile[i % 2] = got.reshape(tile.shape[1:])
        w_stores.start(tile.at[i % 2], w_grads.at[i, :, pl.ds(0, high)])

    swaps[0].wait_recv()
    back_right.wait_recv()
    back_left.wait_recv()
    own_ref[...] = theirs[0].astype(F32) + returns[0, core].astype(F32)
    add_to(own_ref.at[halves[HIGH]], from_left)
    add_to(own_ref.at[halves[LOW]], from_right)
    back_far_low.wait_recv()
    sums_ref[0] = (theirs[2, halves[LOW]].astype(F32) + far_left[...].astype(F32)).astype(BF16)
    back_far_high.wait_recv()
    sums_ref[1] = (theirs[1, halves[HIGH]].astype(F32) + far_right[...].astype(F32)).astype(BF16)
    for copy in gg_sends:
        copy.wait_recv()
    for copy in [*stores.made[6:], *w_stores.made[: ff // tall], *w_stores.made[-2:]]:
        copy.wait()
    sends.finish()


def experts(ctx, tokens, small, gains, routes, notes, rows_by, wo, wg, wu, wd, collective_id):
    rows, width = ctx.shape
    ff = wg.shape[1]
    capacity = rows * 9 // 16
    high = width // 16
    vmem = pltpu.VMEM
    return pl.pallas_call(
        experts_kernel,
        out_shape=[
            sds((rows, width), F32),
            sds((EXPERTS, rows), F32),
            sds((8, 8, rows), F32),
            sds((2, rows // 2, width), BF16),
            sds((rows, width), F32),
            sds((8, rows, width), BF16),
            sds((4, 4, high * 3 // 2, width), BF16),
        ],
        in_specs=[VMEM] * 6 + [ANY] * 8,
        out_specs=[VMEM] * 5 + [ANY] * 2,
        scratch_shapes=[
            vmem((width, width), BF16),
            vmem((width, ff), BF16),
            vmem((width, ff), BF16),
            vmem((ff, width), BF16),
            vmem((8, rows, width), BF16),
            vmem((4, 2, rows, width), BF16),
            vmem((8 * capacity, width), BF16),
            vmem((8 * capacity, width), BF16),
            vmem((8 * capacity, ff), BF16),
            vmem((8 * capacity, 2 * ff), BF16),
            vmem((4, rows, width), BF16),
            *[vmem((rows // 2, width), BF16)] * 4,
            vmem((2, 4, high, width), BF16),
            vmem((2, 2, 4, high // 2, width), BF16),
            vmem((2, rows, width), BF16),
            vmem((8, EXPERTS, rows), F32),
            vmem((4, 2, 8, rows), F32),
            vmem((8, 1, rows), jnp.int32),
            semaphores(12),
            semaphores(6),
            semaphores(8),
            semaphores(40),
            semaphores(40),
        ],
        compiler_params=remote_params(collective_id),
    )(ctx, tokens, small, gains, routes, notes, *rows_by, wo, wg, wu, wd)


def middle_kernel(
    middle_ref, gates_ref, gg_all, sums_ref, own_ref, d_out_ref, ctx_ref, small_ref, gains_ref,
    start_ref, q_ref, kv_ref, lse_ref, cos_ref, sin_ref, wo_hbm, w_grads, blocks_ref,
    grad_middle_ref, small_grad_ref, gq_ref, gkv_ref, wo_out, combined, w_done,
    wo_ref, g_ref, from_left, from_right, w_total_0, w_total_1, w_whole, w_far,
    bias, k_t, gkv, probs, grad_probs, second_whole, second_far, *refs,
):
    place = Place()
    core = place.core
    neighbours = [place.partner, *place.x_to, *place.y_to, *place.z_to]
    greet(neighbours)
    bufs, x_bufs = refs[:12], refs[12:17]
    wo_sem, local_sems, send_sems, recv_sems = refs[17:]
    keeps = Keeps(local_sems)
    cols = w_total_0.shape[-1]
    totals = (w_total_0, w_total_1)
    length, rows = bias.shape
    width = middle_ref.shape[1]
    quarter = width // 4

    def part_of(ref, p, w):
        return ref.at[:, w] if p else ref.at[w]

    loads = {}
    for k in range(4):
        for p in range(2):
            me, (right, left, far), _ = place.ring(p == 0)
            w = (far, right, left, me)[k]
            src = part_of(w_grads, p, w).at[:, :, pl.ds(p * cols, cols)]
            loads[k, p] = keeps.start(src, part_of(totals[p], p, w))
    wo_load = pltpu.make_async_copy(wo_hbm, wo_ref, wo_sem)
    wo_load.start()
    await_greetings(neighbours)
    sends = Sends(send_sems, recv_sems)
    came = [
        sends.start(sums_ref.at[i], dst, place.x_to[i])
        for i, dst in enumerate((from_left, from_right))
    ]

    def first_half(p):
        def view(w, h):
            span = pl.ds(2 * h, 2)
            return totals[p].at[span, w] if p else totals[p].at[w, span]

        return view

    def expert_steps():
        rings = [Ring(p == 0, first_half(p), w_whole.at[p], w_far.at[p]) for p in range(2)]
        yield from ring_sum(place, sends, rings, lambda k, i, w: loads[k, i].wait())
        half = cols // 2

        def second_half(p):
            def view(w, h):
                at = pl.ds(h * half, half)
                return totals[p].at[w, place.z, :, at] if p else totals[p].at[place.y, w, :, at]

            return view

        rings = [
            Ring(p == 1, second_half(p), second_whole.at[p], second_far.at[p]) for p in range(2)
        ]
        yield from ring_sum(place, sends, rings)
        spreads = []
        for p in range(2):
            me = place.ring(p == 1)[0]
            w_done[p, me] = totals[p][place.y, place.z]

            view = lambda w, p=p: w_done.at[p, w]
            spreads.append(Spread(p == 1, w_done.at[p, me], view, half_columns))
        yield from ring_gather(place, sends, spreads)

    def columns(c, p):
        return pl.ds(pl.multiple_of((2 * c + p) * quarter, 128), quarter)

    def theirs_of(p):
        at = columns(1 - core, p)
        if p == 0:
            return lambda w: wo_ref.at[w, :, :, at]
        return lambda w: wo_ref.at[:, w, :, at]

    strips = [
        Strip(
            p == 0, wo_ref.at[:, :, :, columns(core, p)], bufs[6 * p : 6 * p + 6],
            None, theirs_of(p),
        )
        for p in range(2)
    ]
    expert = expert_steps()
    dense = dp_sum(place, sends, strips, ())
    rest = x_sum(place, sends, blocks_ref, combined, *x_bufs)
    next(expert)
    next(rest)

    grad_gates = jnp.concatenate([gg_all[e, :1] for e in range(EXPERTS)], axis=0)
    gates_t = gates_ref[...]
    products = gates_t * grad_gates
    grad_logits = products - gates_t * jnp.sum(products, axis=0, keepdims=True)
    grad_logits = jnp.concatenate(
        [grad_logits, jnp.zeros((128 - EXPERTS, rows), F32)], axis=0
    ).T.astype(BF16)
    total = own_ref[...] + mm_nt(grad_logits, small_ref[...])
    middle, gain = middle_ref[...], gains_ref[:1]
    inverse = inverse_rms(middle)
    scaled = middle * inverse
    small_grad = mm_tn((scaled * gain).astype(BF16), grad_logits)
    fill_bias(bias, start_ref, rows * place.part)
    for copy in came:
        copy.wait_recv()
    total += jnp.concatenate([from_left[...], from_right[...]], axis=0).astype(F32)
    grad_gain = jnp.sum(total * scaled, axis=0, keepdims=True)
    lanes = lax.broadcasted_iota(jnp.int32, (width, 128), 1)
    small_grad += jnp.where(lanes == EXPERTS, as_column(grad_gain, 128), 0.0)
    small_grad_ref[...] = small_grad.astype(BF16)
    weighted = total * gain
    inner = jnp.mean(weighted * scaled, axis=-1, keepdims=True)
    grad_middle = d_out_ref[...].astype(F32) + inverse * (weighted - scaled * inner)
    grad_middle_ref[...] = grad_middle
    grad_attn = grad_middle.astype(BF16)
    wo_load.wait()
    g_ref[...] = mm_nt(grad_attn, wo_ref[...].reshape(width, width)).astype(BF16)
    next(rest)
    next(expert)
    tall = width // 4
    for i in range(4):
        got = mm_tn(ctx_ref[:, i * tall : (i + 1) * tall], grad_attn).astype(BF16)
        wo_ref[i] = got.reshape(wo_ref.shape[1:])
    next(dense)

    when = {2: (dense,), 4: (rest,), 6: (dense,), 8: (expert,), 10: (dense,)}
    for group in range(KEY_VALUE_HEADS):
        keys = slice(2 * group * HEAD_SIZE, (2 * group + 1) * HEAD_SIZE)
        values = slice((2 * group + 1) * HEAD_SIZE, (2 * group + 2) * HEAD_SIZE)
        k_t[...] = kv_ref[:, keys].astype(F32).T.astype(BF16)
        gkv[...] = jnp.zeros_like(gkv)

        def one_head(i, carry, base):
            head = base + i
            query, grad = q_ref[:, head_columns(head)], g_ref[:, head_columns(head)]
            lse = lse_ref[head]
            inner = jnp.zeros_like(lse)
            for at in range(0, length, BLOCK):
                span = pl.ds(at, BLOCK)
                s = mm_nt(kv_ref[span, keys], query) + bias[span]
                p = jnp.exp2(s * (SCALE * LOG2E) - lse)
                gp = mm_nt(kv_ref[span, values], grad)
                inner += jnp.sum(p * gp, axis=0, keepdims=True)
                probs[span] = p
                grad_probs[span] = gp
                gkv[span, HEAD_SIZE:] += mm(p.astype(BF16), grad)
            gq = jnp.zeros((HEAD_SIZE, rows), F32)
            for at in range(0, length, BLOCK):
                span = pl.ds(at, BLOCK)
                gs = (probs[span] * (grad_probs[span] - inner)).astype(BF16)
                gkv[span, :HEAD_SIZE] += mm(gs, query)
                gq += mm(k_t[:, span], gs)
            turned = spin(gq.T * SCALE, cos_ref[...], -sin_ref[...])
            gq_ref[:, head_columns(head)] = turned.astype(BF16)
            return carry

        for base in range(group * GROUP, (group + 1) * GROUP, 2):
            lax.fori_loop(0, 2, lambda i, carry, base=base: one_head(i, carry, base), 0)
            for steps in when.get(base + 2, ()):
                next(steps)
        gkv_ref[:, keys] = (gkv[:, :HEAD_SIZE] * SCALE).astype(BF16)
        gkv_ref[:, values] = gkv[:, HEAD_SIZE:].astype(BF16)
    run_out(expert, dense, rest)
    for p, s in enumerate(strips):
        wo_out[:, columns(core, p)] = s.result[...]
        wo_out[:, columns(1 - core, p)] = s.near[3]
    sends.finish()


def between(
    middle, gates, gg, sums, own, d_out, ctx, small, gain, start, query, kv, lse, cosine, sine,
    wo, w_grads, back_out, collective_id,
):
    rows, width = query.shape
    length = kv.shape[0]
    height, quarter = width // 16, width // 4
    high, cols = w_grads.shape[2], width // 2
    vmem = pltpu.VMEM
    return pl.pallas_call(
        middle_kernel,
        out_shape=[
            sds((rows, width), F32),
            sds((width, 128), BF16),
            sds((rows, width), BF16),
            sds(kv.shape, BF16),
            sds((height, width), BF16),
            sds((rows, width), F32),
            sds((2, 4, high, cols), BF16),
        ],
        in_specs=[VMEM] * 15 + [ANY] * 3,
        out_specs=[VMEM] * 7,
        scratch_shapes=[
            vmem((4, 4, height, width), BF16),
            vmem((rows, width), BF16),
            vmem((rows // 2, width), BF16),
            vmem((rows // 2, width), BF16),
            vmem((4, 4, high, cols), BF16),
            vmem((4, 4, high, cols), BF16),
            vmem((2, 2, 2, 2, high, cols), BF16),
            vmem((2, 2, 2, high, cols), BF16),
            vmem((length, rows), F32),
            vmem((HEAD_SIZE, length), BF16),
            vmem((length, 2 * HEAD_SIZE), F32),
            vmem((length, rows), F32),
            vmem((length, rows), F32),
            vmem((2, 2, 2, high, cols // 2), BF16),
            vmem((2, 2, high, cols // 2), BF16),
            *strip_buffers(height, quarter),
            *strip_buffers(height, quarter),
            *x_buffers(rows, width),
            pltpu.SemaphoreType.DMA,
            semaphores(8),
            semaphores(100),
            semaphores(100),
        ],
        compiler_params=remote_params(collective_id),
    )(
        middle, gates, gg, sums, own, d_out, ctx, small, gain, start, query, kv, lse, cosine, sine,
        wo, w_grads, back_out,
    )


def last_kernel(
    kv_terms, gq_ref, normed_ref, tokens_ref, gains_ref, cos_ref, sin_ref,
    small_ref, w_done, w_hbm,
    grad_inputs_ref, strips_out, small_out, w_sums,
    grads, small_total, w_ref, normed_t, kv_sum, *refs,
):
    place = Place()
    core = place.core
    neighbours = [place.partner, *place.x_to, *place.y_to, *place.z_to]
    greet(neighbours)
    bufs, x_bufs = refs[:30], refs[30:35]
    w_sem, local_sems, send_sems, recv_sems = refs[35:]
    load = pltpu.make_async_copy(w_hbm, w_ref, w_sem)
    load.start()
    await_greetings(neighbours)
    sends, keeps = Sends(send_sems, recv_sems), Keeps(local_sems)
    kv_steps = x_sum(place, sends, kv_terms, kv_sum, *x_bufs)
    next(kv_steps)

    def spread(p):
        cols = pl.ds(p * w_done.shape[-1], w_done.shape[-1])

        def view(w):
            return w_sums.at[:, w, :, cols] if p else w_sums.at[w, :, :, cols]

        keeps.start(w_done.at[p], view(place.ring(p == 0)[0]))
        return Spread(p == 0, w_done.at[p], view, half_span)

    expert_steps = ring_gather(place, sends, [spread(p) for p in range(2)])
    next(expert_steps)
    strip = grads.shape[-1]
    wide = strip - HEAD_SIZE
    rows, width = normed_ref.shape
    height = grads.shape[3]

    def put(s, cols, right_side):
        got = mm(normed_t[...], right_side).astype(BF16)
        grads[s, :, :, :, cols] = got.reshape(4, 4, height, right_side.shape[1])

    def shared(at, size, bufs):
        cols = pl.ds(at, size)

        def theirs_of(p):
            s = 2 * (1 - core) + p
            if p == 0:
                return lambda w: grads.at[s, w, :, :, cols]
            return lambda w: grads.at[s, :, w, :, cols]

        return [
            Strip(
                p == 0, grads.at[2 * core + p, :, :, :, cols], bufs[6 * p : 6 * p + 6],
                None, theirs_of(p),
            )
            for p in range(2)
        ]

    wide_strips = shared(0, wide, bufs[:12])
    narrow_strips = shared(wide, HEAD_SIZE, bufs[12:24])
    wide_steps = dp_sum(place, sends, wide_strips, ())
    narrow_steps = dp_sum(place, sends, narrow_strips, ())
    normed_t[...] = normed_ref[...].astype(F32).T.astype(BF16)
    for s in range(4):
        put(s, pl.ds(0, wide), gq_ref[:, s * wide : (s + 1) * wide])
    next(wide_steps)
    next(kv_steps)
    load.wait()
    grad_normed = None
    for s in range(4):
        at = s * strip
        term = mm_nt(gq_ref[:, s * wide : (s + 1) * wide], w_ref[:, at : at + wide])
        grad_normed = term if grad_normed is None else grad_normed + term
    next(wide_steps)
    next(kv_steps)
    run_out(kv_steps)
    cosine, sine = cos_ref[...], sin_ref[...]
    for s in range(4):
        got = kv_sum[:, s * HEAD_SIZE : (s + 1) * HEAD_SIZE]
        if s % 2 == 0:
            got = spin(got, cosine, -sine)
        got = got.astype(BF16)
        put(s, pl.ds(wide, HEAD_SIZE), got)
        grad_normed += mm_nt(got, w_ref[:, s * strip + wide : (s + 1) * strip])
    next(narrow_steps)
    next(wide_steps)
    next(narrow_steps)
    next(expert_steps)

    grad_inputs, grad_gain = rms_back(tokens_ref[...].astype(F32), gains_ref[1:2], grad_normed)
    grad_inputs_ref[...] = grad_inputs
    lanes = lax.broadcasted_iota(jnp.int32, (width, 128), 1)
    small = jnp.where(
        lanes == EXPERTS + 1, as_column(grad_gain, 128), small_ref[...].astype(F32)
    )
    small_total[...] = small.astype(BF16).reshape(small_total.shape)
    small_strip = Strip(True, small_total, bufs[24:])
    small_steps = dp_sum(place, sends, [small_strip], ())
    next(small_steps)
    next(small_steps)
    next(wide_steps)
    next(narrow_steps)
    next(expert_steps)
    run_out(wide_steps, narrow_steps, small_steps, expert_steps)
    small_out[...] = small_strip.result[...].astype(F32) + small_strip.near[3].astype(F32)
    for p in range(2):
        for at, size, s in ((0, wide, wide_strips[p]), (wide, HEAD_SIZE, narrow_strips[p])):
            for c, got in ((core, s.result), (1 - core, s.near.at[3])):
                begin_at = pl.multiple_of((2 * c + p) * strip + at, 128)
                strips_out[:, pl.ds(begin_at, size)] = got[...]
    for copy in keeps.made:
        copy.wait()
    sends.finish()


def last(
    kv_terms, grad_query, normed, tokens, gain, cosine, sine, small, w_done, w, collective_id
):
    rows, width = normed.shape
    total = w.shape[1]
    height, strip = width // 16, total // 4
    kv_width = total - width
    vmem = pltpu.VMEM
    return pl.pallas_call(
        last_kernel,
        out_shape=[
            sds((rows, width), F32),
            sds((height, total), BF16),
            sds((height, 128), F32),
            sds((4, 4, w_done.shape[2], width), BF16),
        ],
        in_specs=[ANY] + [VMEM] * 8 + [ANY],
        out_specs=[VMEM] * 3 + [ANY],
        scratch_shapes=[
            vmem((4, 4, 4, height, strip), BF16),
            vmem((4, 4, height, 128), BF16),
            vmem((width, total), BF16),
            vmem((width, rows), BF16),
            vmem((rows, kv_width), F32),
            *strip_buffers(height, strip - HEAD_SIZE),
            *strip_buffers(height, strip - HEAD_SIZE),
            *strip_buffers(height, HEAD_SIZE),
            *strip_buffers(height, HEAD_SIZE),
            *strip_buffers(height, 128, shared=False),
            *x_buffers(rows, kv_width),
            pltpu.SemaphoreType.DMA,
            semaphores(2),
            semaphores(120),
            semaphores(120),
        ],
        compiler_params=remote_params(collective_id),
    )(kv_terms, grad_query, normed, tokens, gain, cosine, sine, small, w_done, w)


def finish_kernel(
    sums_ref, grad_middle_ref, grad_inputs_ref, middle_ref, combined_ref, strips_ref, wo_ref,
    small_ref, g_out, u_out, d_out, tokens_out, mixed_out, wq_out, wk_out, wv_out, wo_out,
    router_out, gains_out,
):
    owners, high, width = sums_ref.shape
    ff = width // 2
    gu = high * 2 // 3
    g_out[...] = sums_ref[:, :gu, :ff].astype(F32).reshape(owners * gu, ff)
    u_out[...] = sums_ref[:, :gu, ff:].astype(F32).reshape(owners * gu, ff)
    d_out[...] = sums_ref[:, gu:].astype(F32).reshape(owners * (high - gu), width)
    tokens_out[...] = grad_middle_ref[...] + grad_inputs_ref[...]
    mixed_out[...] = (middle_ref[...] + combined_ref[...]).astype(BF16)

    @pl.when(pl.program_id(0) == 0)
    def _():
        strip = strips_ref.shape[1] // 4
        wide = strip - HEAD_SIZE
        for s in range(4):
            at = s * strip
            wq_out[:, s * wide : (s + 1) * wide] = strips_ref[:, at : at + wide].astype(F32)
            other = (wk_out, wv_out)[s % 2]
            begin_at = s // 2 * HEAD_SIZE
            got = strips_ref[:, at + wide : at + strip].astype(F32)
            other[:, begin_at : begin_at + HEAD_SIZE] = got
        wo_out[...] = wo_ref[...].astype(F32)
        router_out[...] = small_ref[:, :EXPERTS]
        gains_out[...] = small_ref[...].T[EXPERTS : EXPERTS + 8]


def finish(sums, grad_middle, grad_inputs, middle, combined, strips, wo, small):
    owners, high, width = sums.shape
    rows = middle.shape[0]
    height, total = strips.shape
    kv_half = (total - width) // 2
    ff = width // 2
    gu, d = high * 2 // 3, high // 3
    steps = 8
    each, part = owners // steps, rows // steps
    by_step = lambda a, b: pl.BlockSpec((a, b), lambda i: (i, 0))
    whole = lambda a, b: pl.BlockSpec((a, b), lambda i: (0, 0))
    return pl.pallas_call(
        finish_kernel,
        grid=(steps,),
        out_shape=[
            sds((owners * gu, ff), F32),
            sds((owners * gu, ff), F32),
            sds((owners * d, width), F32),
            sds((rows, width), F32),
            sds((rows, width), BF16),
            sds((height, width), F32),
            sds((height, kv_half), F32),
            sds((height, kv_half), F32),
            sds((height, width), F32),
            sds((height, EXPERTS), F32),
            sds((8, height), F32),
        ],
        in_specs=[pl.BlockSpec((each, high, width), lambda i: (i, 0, 0))]
        + [by_step(part, width)] * 4
        + [whole(height, total), whole(height, width), whole(height, 128)],
        out_specs=[
            by_step(each * gu, ff),
            by_step(each * gu, ff),
            by_step(each * d, width),
            by_step(part, width),
            by_step(part, width),
            whole(height, width),
            whole(height, kv_half),
            whole(height, kv_half),
            whole(height, width),
            whole(height, EXPERTS),
            whole(8, height),
        ],
        compiler_params=pltpu.CompilerParams(vmem_limit_bytes=63 * MIB),
        cost_estimate=pl.CostEstimate(flops=0, bytes_accessed=30 * MIB, transcendentals=0),
    )(sums, grad_middle, grad_inputs, middle, combined, strips, wo, small)


def on_device(
    tokens,
    d_out,
    gain_in,
    w_query,
    key_projection_weight,
    value_projection_weight,
    w_out,
    gain_mid,
    w_router,
    w_gate,
    w_up,
    w_down,
    routes,
    segments,
):
    rows, width = tokens.shape
    length = segments.shape[1]
    part = lax.axis_index("expert")
    seg_row = segments[0]
    offset = part * rows
    my_seg = lax.dynamic_slice_in_dim(seg_row, offset, rows, 0)
    start = jnp.sum((seg_row[None, :] < my_seg[:, None]).astype(jnp.int32), axis=1)
    angles = angles_for(offset + jnp.arange(rows, dtype=jnp.int32) - start)
    cosine, sine = jnp.cos(angles), jnp.sin(angles)
    cosine = jnp.concatenate([cosine, cosine], axis=1)
    sine = jnp.concatenate([-sine, sine], axis=1)
    start = start[None, :]

    small = jnp.concatenate([w_router, gain_mid[:, None], gain_in[:, None]], axis=1)
    small = jnp.pad(small, ((0, 0), (0, 128 - small.shape[1])))
    note = jnp.pad(routes.T, ((0, 8 - TOPK), (0, 0)))
    w_strips, small, wo_part, rows_near, notes, normed, query, kv_all, gains = begin(
        w_query, key_projection_weight, value_projection_weight, w_out, small, d_out, note,
        tokens, cosine, sine, 1,
    )
    w_strips = w_strips.reshape(width, -1)
    small = small.reshape(width, -1)
    kv_all = kv_all.reshape(length, -1)
    context, lse, wo, rows_far, rows_other = attend(
        start, query, kv_all, wo_part, d_out, rows_near, 2
    )

    middle, gates, gg, sums, own, back_out, w_grads = experts(
        context, tokens, small, gains, routes, notes, (d_out, rows_near, rows_far, rows_other),
        wo.reshape(width, width), w_gate[0], w_up[0], w_down[0], 3,
    )
    grad_middle, small_grads, grad_query, kv_terms, wo_sum, combined, w_done = between(
        middle, gates, gg, sums, own, d_out, context, small, gains, start, query, kv_all,
        lse, cosine, sine, wo, w_grads, back_out, 4,
    )
    grad_inputs, strips_sum, small_sum, w_sums = last(
        kv_terms.reshape(8, rows, -1), grad_query, normed, tokens, gains, cosine, sine,
        small_grads, w_done, w_strips, 5,
    )
    g_wg, g_wu, g_wd, grad_tokens, mixed, g_wq, g_wk, g_wv, g_wo, g_router, g_gains = finish(
        w_sums.reshape(16, -1, width), grad_middle, grad_inputs, middle, combined, strips_sum,
        wo_sum, small_sum,
    )
    return (
        mixed,
        grad_tokens,
        g_gains[1],
        g_wq,
        g_wk,
        g_wv,
        g_wo,
        g_gains[0],
        g_router,
        g_wg[None],
        g_wu[None],
        g_wd[None],
    )


def solution(mesh):
    whole = P(("dp", "expert"), None)
    over_dp, by_dp, over_expert = P("dp"), P("dp", None), P("expert", None, None)
    return jax.shard_map(
        on_device,
        mesh=mesh,
        in_specs=(whole, whole, over_dp, by_dp, by_dp, by_dp, by_dp, over_dp, by_dp)
        + (over_expert,) * 3
        + (whole, by_dp),
        out_specs=(whole, whole, over_dp, by_dp, by_dp, by_dp, by_dp, over_dp, by_dp)
        + (over_expert,) * 3,
        check_vma=False,
    )
```

```python
import functools

import jax
import jax.numpy as jnp
from jax import lax
from jax.experimental import pallas as pl
from jax.experimental.pallas import tpu as pltpu
from jax.sharding import PartitionSpec as P

QUERY_HEADS = 12
KEY_VALUE_HEADS = 2
HEAD_SIZE = 128
TOPK = 4
EXPERTS = 8
GROUP = QUERY_HEADS // KEY_VALUE_HEADS
SCALE = HEAD_SIZE**-0.5
LOG2E = 1.4426950408889634
BLOCK = 512

EPSILON = 1e-06
ROPE_BASE = 1000000.0
MASK_FILL = -1e30
F32 = jnp.float32
BF16 = jnp.bfloat16

MESH = pl.DeviceIdType.MESH
ANY = pl.BlockSpec(memory_space=pl.ANY)
VMEM = pl.BlockSpec(memory_space=pltpu.VMEM)
MIB = 2**20


def dot(a, b, dims):
    return lax.dot_general(a, b, (dims, ((), ())), preferred_element_type=F32)


def mm(a, b):
    return dot(a, b, ((1,), (0,)))


def mm_nt(a, b):
    return dot(a, b, ((1,), (1,)))


def mm_tn(a, b):
    return dot(a, b, ((0,), (0,)))


def sds(shape, dtype):
    return jax.ShapeDtypeStruct(tuple(shape), dtype)


def remote_params(collective_id):
    return pltpu.CompilerParams(
        collective_id=collective_id, has_side_effects=True, vmem_limit_bytes=63 * MIB
    )


def semaphores(count):
    return pltpu.SemaphoreType.DMA((count,))


def inverse_rms(rows):
    return lax.rsqrt(jnp.mean(rows * rows, axis=-1, keepdims=True) + EPSILON)


def rms_back(rows, gain, grad):
    inverse = inverse_rms(rows)
    scaled = rows * inverse
    weighted = grad * gain
    inner = jnp.mean(weighted * scaled, axis=-1, keepdims=True)
    return inverse * (weighted - scaled * inner), jnp.sum(grad * scaled, axis=0, keepdims=True)


def as_column(row, lanes):
    return jnp.broadcast_to(row, (lanes, row.shape[1])).T


def angles_for(positions):
    half_width = HEAD_SIZE // 2
    freqs = ROPE_BASE ** (-2.0 * jnp.arange(half_width, dtype=F32) / HEAD_SIZE)
    return positions.astype(F32)[:, None] * freqs[None, :]


def spin(z, cosine, sine):
    return z * cosine + pltpu.roll(z, HEAD_SIZE // 2, 1) * sine


class Sends:
    def __init__(self, send_sems, recv_sems):
        self.send_sems, self.recv_sems, self.made = send_sems, recv_sems, []

    def start(self, src, dst, to):
        at = len(self.made)
        copy = pltpu.make_async_remote_copy(
            src_ref=src,
            dst_ref=dst,
            send_sem=self.send_sems.at[at],
            recv_sem=self.recv_sems.at[at],
            device_id=to,
            device_id_type=MESH,
        )
        copy.start()
        self.made.append(copy)
        return copy

    def finish(self):
        for copy in self.made:
            copy.wait_send()


class Keeps:
    def __init__(self, sems):
        self.sems, self.made = sems, []

    def start(self, src, dst):
        copy = pltpu.make_async_copy(src, dst, self.sems.at[len(self.made)])
        copy.start()
        self.made.append(copy)
        return copy


class Place:
    def __init__(self):
        self.part = lax.axis_index("expert")
        self.core = self.part % 2
        self.chip = self.part // 2
        at = lambda d: lax.rem(self.chip + d, 4) * 2 + self.core
        self.right, self.left, self.far = at(1), at(3), at(2)
        to = lambda i: {"expert": i}
        self.partner = to(2 * self.chip + (1 - self.core))
        self.x_to = [to(self.right), to(self.left), to(self.far)]
        self.others = [to(lax.rem(self.part + d, 8)) for d in range(1, 8)]
        place = lax.axis_index("dp")
        self.y, self.z = place // 4, place % 4
        ring = lambda v: [lax.rem(v + d, 4) for d in (1, 3, 2)]
        self.y_ring, self.z_ring = ring(self.y), ring(self.z)
        self.y_to = [{"dp": v * 4 + self.z} for v in self.y_ring[:2]]
        self.z_to = [{"dp": self.y * 4 + v} for v in self.z_ring[:2]]

    def ring(self, along_y):
        if along_y:
            return self.y, self.y_ring, self.y_to
        return self.z, self.z_ring, self.z_to


def greet(others):
    barrier = pltpu.get_barrier_semaphore()
    for other in others:
        pl.semaphore_signal(barrier, inc=1, device_id=other, device_id_type=MESH)


def await_greetings(others):
    pl.semaphore_wait(pltpu.get_barrier_semaphore(), len(others))


def add_to(ref, *others):
    got = ref[...].astype(F32)
    for other in others:
        got += other[...].astype(F32)
    ref[...] = got.astype(ref.dtype)


def run_out(*steps):
    steps = list(steps)
    while steps:
        for s in list(steps):
            if next(s, "done") == "done":
                steps.remove(s)


def x_sum(place, sends, blocks_ref, out_ref, mine, total, from_left, from_right, sems):
    rows = out_ref.shape[0]
    half = rows // 2
    low, high = pl.ds(0, half), pl.ds(half, half)
    to_right, to_left = place.x_to[:2]
    flip = 1 - 2 * place.core
    keeps = Keeps(sems)
    swaps, loads = [], []
    for k, dest in enumerate((place.far, place.right, place.left, place.part)):
        swaps.append(sends.start(blocks_ref.at[dest + flip], total.at[k], place.partner))
        loads.append(keeps.start(blocks_ref.at[dest], mine.at[k]))

    def add_up(k):
        loads[k].wait()
        swaps[k].wait_recv()
        add_to(total.at[k], mine.at[k])

    yield
    add_up(0)
    far_low = sends.start(total.at[0, low], from_left.at[0], to_right)
    far_high = sends.start(total.at[0, high], from_right.at[0], to_left)
    add_up(1)
    right_high = sends.start(total.at[1, high], from_left.at[2], to_right)
    add_up(2)
    left_low = sends.start(total.at[2, low], from_right.at[2], to_left)
    yield
    far_low.wait_recv()
    add_to(total.at[1, low], from_left.at[0])
    right_low = sends.start(total.at[1, low], from_left.at[1], to_right)
    far_high.wait_recv()
    add_to(total.at[2, high], from_right.at[0])
    left_high = sends.start(total.at[2, high], from_right.at[1], to_left)
    yield
    loads[3].wait()
    swaps[3].wait_recv()
    out_ref[...] = mine[3].astype(F32) + total[3].astype(F32)
    right_high.wait_recv()
    left_low.wait_recv()
    right_low.wait_recv()
    left_high.wait_recv()
    add_to(out_ref.at[low], from_left.at[1], from_right.at[2])
    add_to(out_ref.at[high], from_left.at[2], from_right.at[1])
    yield


def x_buffers(rows, columns):
    return [
        pltpu.VMEM((4, rows, columns), BF16),
        pltpu.VMEM((4, rows, columns), BF16),
        pltpu.VMEM((3, rows // 2, columns), BF16),
        pltpu.VMEM((3, rows // 2, columns), BF16),
        semaphores(4),
    ]


class Ring:
    def __init__(self, along_y, view, whole, farther):
        self.along_y, self.view, self.whole, self.farther = along_y, view, whole, farther


def ring_sum(place, sends, rings, ready=lambda *_: None):
    going = []
    for i, r in enumerate(rings):
        _, (right, left, far), to = place.ring(r.along_y)
        ready(0, i, far)
        going.append([sends.start(r.view(far, h), r.farther.at[h], to[h]) for h in range(2)])
    for i, r in enumerate(rings):
        _, (right, left, far), to = place.ring(r.along_y)
        ready(1, i, right)
        ready(2, i, left)
        going[i].append(sends.start(r.view(right, 1), r.whole.at[0, 1], to[0]))
        going[i].append(sends.start(r.view(left, 0), r.whole.at[1, 0], to[1]))
    yield
    for i, r in enumerate(rings):
        _, (right, left, far), to = place.ring(r.along_y)
        for h, w in enumerate((right, left)):
            going[i][h].wait_recv()
            add_to(r.view(w, h), r.farther.at[h])
            going[i].append(sends.start(r.view(w, h), r.whole.at[h, h], to[h]))
    yield
    for i, r in enumerate(rings):
        me, _, _ = place.ring(r.along_y)
        ready(3, i, me)
        for copy in going[i][2:]:
            copy.wait_recv()
        for h in range(2):
            add_to(r.view(me, h), r.whole.at[0, h], r.whole.at[1, h])


class Spread:
    def __init__(self, along_y, source, view, half, landed=lambda _: None):
        self.along_y, self.source, self.view = along_y, source, view
        self.half, self.landed = half, landed


def ring_gather(place, sends, spreads):
    came, onward = [], []

    def send(s, h, to):
        me = place.ring(s.along_y)[0]
        return sends.start(s.half(s.source, h), s.half(s.view(me), h), to)

    for s in spreads:
        to = place.ring(s.along_y)[2]
        came.append([[send(s, d, to[d])] for d in range(2)])
    yield
    for s, copies in zip(spreads, came):
        to = place.ring(s.along_y)[2]
        for d in range(2):
            copies[d].append(send(s, 1 - d, to[d]))
    yield
    for s, copies in zip(spreads, came):
        _, (right, left, _), to = place.ring(s.along_y)
        onward.append([])
        for d, origin in enumerate((left, right)):
            copies[d][0].wait_recv()
            view = s.half(s.view(origin), d)
            onward[-1].append(sends.start(view, view, to[d]))
    yield
    for s, copies in zip(spreads, came):
        _, (right, left, _), _ = place.ring(s.along_y)
        for d, origin in enumerate((left, right)):
            copies[d][1].wait_recv()
            s.landed(s.view(origin))
    for s, copies in zip(spreads, onward):
        far = place.ring(s.along_y)[1][2]
        for d in range(2):
            copies[d].wait_recv()
            s.landed(s.half(s.view(far), d))
    yield


def half_span(share, h):
    return share.at[pl.ds(2 * h, 2)]


def half_rows(share, h):
    half = share.shape[0] // 2
    return share.at[pl.ds(h * half, half)]


def half_columns(share, h):
    half = share.shape[-1] // 2
    return share.at[:, pl.ds(h * half, half)]


class Strip:
    def __init__(self, y_first, total, bufs, own=None, other=None):
        self.y_first, self.total, self.own, self.other = y_first, total, own, other
        self.theirs, self.big, self.far, self.mid, self.midfar, self.near = bufs

    def block(self, ref, w):
        return ref.at[w] if self.y_first else ref.at[:, w]


def strip_buffers(rows, columns, shared=True):
    return [
        pltpu.VMEM((4, 4, rows, columns) if shared else (1, 1, rows, columns), BF16),
        pltpu.VMEM((2, 2, 2, rows, columns), BF16),
        pltpu.VMEM((2, 2, rows, columns), BF16),
        pltpu.VMEM((2, 2, rows // 2, columns), BF16),
        pltpu.VMEM((2, rows // 2, columns), BF16),
        pltpu.VMEM((4, rows, columns), BF16),
    ]


def dp_sum(place, sends, strips, sems):
    y, z = place.y, place.z
    keeps = Keeps(sems)
    swaps, loads = {}, {}
    for k in range(4):
        for i, s in enumerate(strips):
            me, (right, left, far), _ = place.ring(s.y_first)
            w = (far, right, left, me)[k]
            if s.other is not None:
                swaps[k, i] = sends.start(s.other(w), s.block(s.theirs, w), place.partner)
            if s.own is not None:
                loads[k, i] = keeps.start(s.own(w), s.block(s.total, w))
    yield

    def joined(k, i, s, w):
        if s.own is not None:
            loads[k, i].wait()
        if s.other is not None:
            swaps[k, i].wait_recv()
            add_to(s.block(s.total, w), s.block(s.theirs, w))

    def big(s, w, h):
        span = pl.ds(2 * h, 2)
        return s.total.at[w, span] if s.y_first else s.total.at[span, w]

    def small(s, w, h):
        half = s.total.shape[2] // 2
        at = pl.ds(h * half, half)
        return s.total.at[y, w, at] if s.y_first else s.total.at[w, z, at]

    def rings(first):
        view = big if first else small
        return [
            Ring(
                s.y_first == first,
                functools.partial(view, s),
                s.big if first else s.mid,
                s.far if first else s.midfar,
            )
            for s in strips
        ]

    yield from ring_sum(place, sends, rings(True), lambda k, i, w: joined(k, i, strips[i], w))
    yield from ring_sum(place, sends, rings(False))

    shares, back = [], []
    for s in strips:
        shares.append(
            [sends.start(s.total.at[y, z], s.near.at[i], place.x_to[i]) for i in range(3)]
        )
    yield
    for s, share in zip(strips, shares):
        for copy in share:
            copy.wait_recv()
        got = s.total[y, z].astype(F32)
        for i in range(3):
            got += s.near[i].astype(F32)
        s.result = s.theirs.at[y, z] if s.other is not None else s.theirs.at[0, 0]
        s.result[...] = got.astype(BF16)
        back.append(sends.start(s.result, s.near.at[3], place.partner))
    yield
    for copy in back:
        copy.wait_recv()
    yield


def begin_kernel(
    wq_hbm, wk_hbm, wv_hbm, wo_hbm, small_ref, rows_hbm, note_ref, tokens_hbm, cos_ref, sin_ref,
    w_out, small_out, wo_part, rows_near, notes_out, normed_ref, query_ref, kv_ref, gains_ref,
    strips_ref, w_all, own_kv, wq_ref, wk_ref, wv_ref, wo_ref, rows_ref, tokens_ref,
    fetch_sems, local_sems, send_sems, recv_sems,
):
    fetches = Keeps(fetch_sems)
    for src, dst in (
        (wq_hbm, wq_ref), (wk_hbm, wk_ref), (wv_hbm, wv_ref), (wo_hbm, wo_ref),
        (rows_hbm, rows_ref), (tokens_hbm, tokens_ref),
    ):
        fetches.start(src, dst)
    place = Place()
    y, z, core, part = place.y, place.z, place.core, place.part
    neighbours = [*place.others, *place.y_to, *place.z_to]
    greet(neighbours)
    rows = wq_ref.shape[0]
    wide, narrow = wq_ref.shape[1] // 4, wk_ref.shape[1] // 2
    strip = wide + narrow
    for fetch in fetches.made[:4]:
        fetch.wait()
    for s in range(4):
        strips_ref[:, s * strip : s * strip + wide] = wq_ref[:, s * wide : (s + 1) * wide]
        other = (wk_ref, wv_ref)[s % 2]
        begin = s // 2 * narrow
        strips_ref[:, s * strip + wide : (s + 1) * strip] = other[:, begin : begin + narrow]
    await_greetings(neighbours)
    sends, keeps = Sends(send_sems, recv_sems), Keeps(local_sems)

    def columns(p, size):
        return pl.ds(pl.multiple_of((2 * core + p) * size, 128), size)

    across = []

    def send_across(view):
        across.append(sends.start(view, view, place.partner))

    def spread(first, src, out, cols, y_first, landed):
        def near(where):
            return out.at[where, z, :, cols] if y_first else out.at[y, where, :, cols]

        def wider(where):
            return out.at[:, where, :, cols] if y_first else out.at[where, :, :, cols]

        if first:
            return Spread(y_first, src, near, half_rows)
        source = wider(z if y_first else y)
        landed(source)
        return Spread(not y_first, source, wider, half_span, landed)

    def strips(first, at, size):
        def part(p):
            return pl.ds(pl.multiple_of((2 * core + p) * strip + at, 128), size)

        return [
            spread(first, strips_ref.at[:, part(p)], w_all, part(p), p == 1, send_across)
            for p in range(2)
        ]

    def small_spread(first):
        every = pl.ds(0, small_ref.shape[1])
        return spread(first, small_ref, small_out, every, False, lambda _: None)

    def out_spread(p):
        ring_of = (z, y)[p]

        keeps.start(wo_ref.at[:, columns(p, wide)], wo_part.at[p, ring_of])
        return Spread(
            p == 1, wo_ref.at[:, columns(p, wide)], lambda where: wo_part.at[p, where], half_rows
        )

    ahead = ring_gather(place, sends, [*strips(True, wide, narrow), small_spread(True)])
    behind = ring_gather(place, sends, [*strips(True, 0, wide), *map(out_spread, range(2))])
    for steps in (ahead, ahead, behind, behind):
        next(steps)
    for p in range(2):
        w_all[y, z, :, columns(p, strip)] = strips_ref[:, columns(p, strip)]
    small_out[y, z] = small_ref[...]

    half = rows_ref.shape[0] // 2
    x_halves = [pl.ds(h * half, half) for h in range(2)]
    fetches.made[4].wait()
    rows_came = [
        sends.start(rows_ref.at[x_halves[h]], rows_near.at[d, x_halves[h]], place.x_to[d])
        for d in range(2)
        for h in (d, 1 - d)
    ]
    notes = [sends.start(note_ref, notes_out.at[part], to) for to in place.others]
    keeps.start(note_ref, notes_out.at[part])
    next(ahead)
    next(ahead)
    ahead = ring_gather(place, sends, [*strips(False, wide, narrow), small_spread(False)])
    next(ahead)
    next(ahead)
    next(behind)
    next(behind)
    behind = ring_gather(place, sends, strips(False, 0, wide))
    next(behind)
    next(behind)
    next(ahead)
    next(ahead)
    small_t = small_out[...].reshape(tokens_ref.shape[1], -1).astype(F32).T
    gains_ref[...] = small_t[EXPERTS : EXPERTS + 8]
    fetches.made[5].wait()
    inputs = tokens_ref[...].astype(F32)
    gain = small_t[EXPERTS + 1 : EXPERTS + 2]
    normed_ref[...] = (inputs * inverse_rms(inputs) * gain).astype(BF16)
    for copy in across:
        copy.wait_recv()
    del across[:]

    cosine, sine = cos_ref[...], sin_ref[...]
    width = tokens_ref.shape[1]

    def project(at, size):
        w = w_all[:, :, :, at : at + size].reshape(width, size)
        return mm(normed_ref[...], w)

    for s in range(4):
        got = project(s * strip + wide, HEAD_SIZE)
        if s % 2 == 0:
            got = spin(got, cosine, sine)
        own_kv[:, s * HEAD_SIZE : (s + 1) * HEAD_SIZE] = got.astype(BF16)
    slot = kv_ref.at[part]
    kv_came = [
        [
            sends.start(own_kv.at[x_halves[h]], slot.at[x_halves[h]], place.x_to[d])
            for h in (d, 1 - d)
        ]
        for d in range(2)
    ]
    kv_across = [sends.start(own_kv, slot, place.partner)]
    keeps.start(own_kv, slot)
    next(behind)
    next(behind)
    onward = []
    for d, origin in enumerate((place.left, place.right)):
        kv_came[d][0].wait_recv()
        view = kv_ref.at[origin, x_halves[d]]
        onward.append(sends.start(view, view, place.x_to[d]))
    for copy in across:
        copy.wait_recv()
    keeps.start(w_all, w_out)

    def queries(s):
        got = project(s * strip, wide)
        for h in range(0, wide, HEAD_SIZE):
            head = spin(got[:, h : h + HEAD_SIZE], cosine, sine)
            query_ref[:, s * wide + h : s * wide + h + HEAD_SIZE] = head.astype(BF16)

    for s in range(4):
        queries(s)
    for d, origin in enumerate((place.left, place.right)):
        kv_came[d][1].wait_recv()
        view = kv_ref.at[origin]
        kv_across.append(sends.start(view, view, place.partner))
    for d in range(2):
        onward[d].wait_recv()
        view = kv_ref.at[place.far, x_halves[d]]
        kv_across.append(sends.start(view, view, place.partner))
    for copy in [*kv_across, *notes, *rows_came]:
        copy.wait_recv()
    for copy in keeps.made:
        copy.wait()
    sends.finish()


def begin(wq, wk, wv, wo, small, rows, note, tokens, cosine, sine, collective_id):
    height, width = wq.shape
    kv_width = wk.shape[1] + wv.shape[1]
    total = width + kv_width
    count = tokens.shape[0]
    vmem = pltpu.VMEM
    return pl.pallas_call(
        begin_kernel,
        out_shape=[
            sds((4, 4, height, total), BF16),
            sds((4, 4, *small.shape), BF16),
            sds((2, 4, height, width // 4), BF16),
            sds((2, *rows.shape), BF16),
            sds((8, *note.shape), note.dtype),
            sds((count, width), BF16),
            sds((count, width), BF16),
            sds((8, count, kv_width), BF16),
            sds((8, width), F32),
        ],
        in_specs=[ANY] * 4 + [VMEM, ANY, VMEM, ANY, VMEM, VMEM],
        out_specs=[ANY, VMEM, VMEM, ANY, ANY, VMEM, VMEM, ANY, VMEM],
        scratch_shapes=[
            vmem((height, total), BF16),
            vmem((4, 4, height, total), BF16),
            vmem((count, kv_width), BF16),
            *[vmem(a.shape, BF16) for a in (wq, wk, wv, wo, rows, tokens)],
            semaphores(6),
            semaphores(6),
            semaphores(125),
            semaphores(125),
        ],
        compiler_params=remote_params(collective_id),
    )(wq, wk, wv, wo, small, rows, note, tokens, cosine, sine)


def fill_bias(bias, start_ref, first_row):
    length, rows = bias.shape
    places = lax.broadcasted_iota(jnp.int32, (length, rows), 0)
    mine = first_row + lax.broadcasted_iota(jnp.int32, (length, rows), 1)
    keep = (places >= start_ref[...]) & (places <= mine)
    bias[...] = jnp.where(keep, 0.0, MASK_FILL)


def head_columns(head):
    return pl.ds(pl.multiple_of(head * HEAD_SIZE, HEAD_SIZE), HEAD_SIZE)


def attend_kernel(
    start_ref, q_ref, kv_ref, wo_part, rows_own, rows_near, ctx_ref, lse_ref, wo_all, rows_far,
    rows_other, bias, v_t, scores, local_sems, send_sems, recv_sems,
):
    place = Place()
    neighbours = [place.partner, *place.x_to[:2], *place.y_to, *place.z_to]
    greet(neighbours)
    length, rows = bias.shape
    fill_bias(bias, start_ref, rows * place.part)
    await_greetings(neighbours)
    sends, keeps = Sends(send_sems, recv_sems), Keeps(local_sems)
    quarter = wo_part.shape[-1]
    across = []

    def landed(view):
        across.append(sends.start(view, view, place.partner))

    def spread(p):
        cols = pl.ds(pl.multiple_of((2 * place.core + p) * quarter, 128), quarter)

        def view(where):
            return wo_all.at[:, where, :, cols] if p else wo_all.at[where, :, :, cols]

        own = view((place.y, place.z)[p])
        keeps.start(wo_part.at[p], own)
        across.append(sends.start(wo_part.at[p], own, place.partner))
        return Spread(p == 0, wo_part.at[p], view, half_span, landed)

    steps = ring_gather(place, sends, [spread(p) for p in range(2)])
    next(steps)
    next(steps)

    half = rows // 2
    x_halves = [pl.ds(h * half, half) for h in range(2)]
    far_came = [
        sends.start(rows_near.at[d, x_halves[d]], rows_far.at[x_halves[d]], place.x_to[d])
        for d in range(2)
    ]
    for i, view in enumerate((rows_own, rows_near.at[0], rows_near.at[1])):
        across.append(sends.start(view, rows_other.at[i], place.partner))
    for group in range(KEY_VALUE_HEADS):
        keys = slice(2 * group * HEAD_SIZE, (2 * group + 1) * HEAD_SIZE)
        values = slice((2 * group + 1) * HEAD_SIZE, (2 * group + 2) * HEAD_SIZE)
        v_t[...] = kv_ref[:, values].astype(F32).T.astype(BF16)

        def one_head(i, carry, base):
            head = base + i
            query = q_ref[:, head_columns(head)]
            top = None
            for at in range(0, length, BLOCK):
                span = pl.ds(at, BLOCK)
                s = mm_nt(kv_ref[span, keys], query) + bias[span]
                scores[span] = s
                here = jnp.max(s, axis=0, keepdims=True)
                top = here if top is None else jnp.maximum(top, here)
            total = jnp.zeros_like(top)
            context = jnp.zeros((HEAD_SIZE, rows), F32)
            for at in range(0, length, BLOCK):
                span = pl.ds(at, BLOCK)
                p = jnp.exp2((scores[span] - top) * (SCALE * LOG2E))
                total += jnp.sum(p, axis=0, keepdims=True)
                context += mm(v_t[:, span], p.astype(BF16))
            ctx_ref[:, head_columns(head)] = (context / total).T.astype(BF16)
            lse_ref[head] = top * (SCALE * LOG2E) + jnp.log2(total)
            return carry

        for base in (group * GROUP, group * GROUP + GROUP // 2):
            lax.fori_loop(
                0, GROUP // 2, lambda i, carry, base=base: one_head(i, carry, base), 0
            )
            if base in (GROUP // 2, QUERY_HEADS - GROUP // 2):
                next(steps)
            if base == GROUP:
                for d, copy in enumerate(far_came):
                    copy.wait_recv()
                    view = rows_far.at[x_halves[d]]
                    across.append(
                        sends.start(view, rows_other.at[3, x_halves[d]], place.partner)
                    )
    run_out(steps)
    for copy in across:
        copy.wait_recv()
    for copy in keeps.made:
        copy.wait()
    sends.finish()


def attend(start, query, kv, wo_part, rows_own, rows_near, collective_id):
    rows, width = query.shape
    length = kv.shape[0]
    height = wo_part.shape[2]
    return pl.pallas_call(
        attend_kernel,
        out_shape=[
            sds((rows, width), BF16),
            sds((QUERY_HEADS, 1, rows), F32),
            sds((4, 4, height, width), BF16),
            sds((rows, width), BF16),
            sds((4, rows, width), BF16),
        ],
        in_specs=[VMEM] * 4 + [ANY] * 2,
        out_specs=[VMEM, VMEM, ANY, ANY, ANY],
        scratch_shapes=[
            pltpu.VMEM((length, rows), F32),
            pltpu.VMEM((HEAD_SIZE, length), BF16),
            pltpu.VMEM((length, rows), F32),
            semaphores(2),
            semaphores(32),
            semaphores(32),
        ],
        compiler_params=remote_params(collective_id),
    )(start, query, kv, wo_part, rows_own, rows_near)


LOW, HIGH = 0, 1


def gelu_parts(a):
    k = (2.0 / jnp.pi) ** 0.5
    square = a * a
    t = jnp.tanh(k * a * (1.0 + 0.044715 * square))
    slope = 0.5 * (1.0 + t) + 0.5 * a * (1.0 - t * t) * k * (1.0 + 3 * 0.044715 * square)
    return 0.5 * a * (1.0 + t), slope


def experts_kernel(
    ctx_ref, tokens_ref, small_ref, gains_ref, notes_ref,
    rows_own, rows_near, rows_far, rows_other, wo_hbm, wg_hbm, wu_hbm, wd_hbm,
    middle_ref, gates_ref, gg_all, sums_ref, own_ref, back_out, w_grads,
    wo_ref, wg_ref, wu_ref, wd_ref, rows_all, returns, arrived, pair_grad, hidden, grad_pre,
    theirs, far_left, far_right, from_left, from_right, tile, tile_d, back_rows, gates_all, gg_src,
    slot_ref,
    local_sems, tile_sems, back_sems, send_sems, recv_sems,
):
    place = Place()
    part, core = place.part, place.core
    right, left, far = place.right, place.left, place.far
    to_right, to_left = place.x_to[:2]
    greet(place.others)
    sends, keeps, stores = (
        Sends(send_sems, recv_sems), Keeps(local_sems), Keeps(back_sems)
    )
    rows, width = ctx_ref.shape
    half = rows // 2
    halves = (pl.ds(0, half), pl.ds(half, half))
    ff = wg_ref.shape[1]
    capacity = arrived.shape[0] // 8

    for src, dst in ((wo_hbm, wo_ref), (wg_hbm, wg_ref), (wu_hbm, wu_ref), (wd_hbm, wd_ref)):
        keeps.start(src, dst)
    chips = [lax.rem(place.chip + d, 4) for d in (0, 3, 1, 2)]
    for u, src in enumerate((rows_own, rows_near.at[0], rows_near.at[1], rows_far)):
        keeps.start(src, returns.at[u, core])
        keeps.start(rows_other.at[u], returns.at[u, 1 - core])

    keeps.made[0].wait()
    middle = tokens_ref[...].astype(F32) + mm(ctx_ref[...], wo_ref[...])
    middle_ref[...] = middle
    normed = (middle * inverse_rms(middle) * gains_ref[:1]).astype(BF16)
    rows_all[part] = normed
    ids = lax.broadcasted_iota(jnp.int32, (128, rows), 0)
    named = notes_ref[part]
    member = functools.reduce(jnp.logical_or, [ids == named[k : k + 1] for k in range(TOPK)])
    member = member.astype(F32).T
    logits = jnp.where(member > 0.0, mm(normed, small_ref[...]), MASK_FILL)
    weight = jnp.exp(logits - jnp.max(logits, axis=-1, keepdims=True)) * member
    gates = weight / jnp.sum(weight, axis=-1, keepdims=True)
    gates_ref[...] = gates.T[:EXPERTS]

    await_greetings(place.others)
    mine = rows_all.at[part]
    go = [
        [sends.start(mine.at[halves[h]], mine.at[halves[h]], way) for h in (d, 1 - d)]
        for d, way in enumerate((to_right, to_left))
    ]
    swap_own = sends.start(mine, mine, place.partner)
    note_sends = [sends.start(gates_ref, gates_all.at[part], to) for to in place.others]
    gates_all[part] = gates_ref[...]

    chosen = jnp.concatenate(
        [
            functools.reduce(
                jnp.logical_or, [notes_ref[s, k : k + 1] == part for k in range(TOPK)]
            ).astype(F32)
            for s in range(8)
        ],
        axis=0,
    )
    earlier = lax.broadcasted_iota(jnp.int32, (rows, rows), 0) < lax.broadcasted_iota(
        jnp.int32, (rows, rows), 1
    )
    ranks = mm(chosen.astype(BF16), earlier.astype(F32).astype(BF16))
    slots_of = jnp.where(chosen > 0.0, ranks, -1.0)
    for s in range(8):
        slot_ref[s] = slots_of[s : s + 1].astype(jnp.int32)

    def pick_of(source):
        slots = lax.broadcasted_iota(jnp.int32, (capacity, rows), 0)
        return slots == slot_ref[source]

    for u in range(4):
        keeps.made[4 + 2 * u].wait()
        keeps.made[5 + 2 * u].wait()
        for c in range(2):
            pick = pick_of(2 * chips[u] + c).astype(BF16)
            got = mm(pick, returns[u, c])
            pair_grad[pl.ds((2 * u + c) * capacity, capacity)] = got.astype(BF16)
    for load in keeps.made[1:4]:
        load.wait()

    swaps, gg_sends = [], []

    def unit(u):
        at = chips[u]
        picks = [pick_of(2 * at + c) for c in range(2)]
        picks_b = [pick.astype(BF16) for pick in picks]
        spans = [pl.ds((2 * u + c) * capacity, capacity) for c in range(2)]
        both = pl.ds(2 * u * capacity, 2 * capacity)
        gate = []
        for c in range(2):
            arrived[spans[c]] = mm(picks_b[c], rows_all[2 * at + c]).astype(BF16)
            row = gates_all[2 * at + c, pl.ds(part, 1)]
            gate.append(jnp.sum(jnp.where(picks[c], row, 0.0), axis=-1, keepdims=True))
        gate = jnp.concatenate(gate, axis=0)
        x = arrived[both]
        a, b = mm(x, wg_ref[...]), mm(x, wu_ref[...])
        act, slope = gelu_parts(a)
        h = (act * b).astype(BF16)
        hidden[both] = h
        out = mm(h, wd_ref[...]).astype(BF16).astype(F32)
        up = pair_grad[both].astype(F32)
        gg = jnp.sum(up * out, axis=-1, keepdims=True)
        weighted = (gate * out).astype(BF16)
        pg = (gate * up).astype(BF16)
        pair_grad[both] = pg
        grad_h = mm_nt(pg, wd_ref[...])
        grad_a = (grad_h * b * slope).astype(BF16)
        grad_b = (grad_h * act).astype(BF16)
        grad_pre[both, :ff] = grad_a
        grad_pre[both, ff:] = grad_b
        grad_rows = (mm_nt(grad_a, wg_ref[...]) + mm_nt(grad_b, wu_ref[...])).astype(BF16)
        for c in range(2):
            returns[u, c] = mm_tn(
                picks_b[c], grad_rows[c * capacity : (c + 1) * capacity]
            ).astype(BF16)
        swaps.append(sends.start(returns.at[u, 1 - core], theirs.at[u], place.partner))
        for c in range(2):
            if u > 0:
                stores.made[2 * (u - 1) + c].wait()
            back_rows[c] = mm_tn(picks_b[c], weighted[c * capacity : (c + 1) * capacity]).astype(
                BF16
            )
            stores.start(back_rows.at[c], back_out.at[2 * at + c])
            gg_c = gg[c * capacity : (c + 1) * capacity]
            row = jnp.sum(jnp.where(picks[c], gg_c, 0.0), axis=0, keepdims=True)
            gg_src[u, c] = jnp.broadcast_to(row, (8, rows))
        if u == 0:
            gg_all[part] = gg_src[0, core]
            gg_sends.append(sends.start(gg_src.at[0, 1 - core], gg_all.at[part], place.partner))
        else:
            for c in (core, 1 - core):
                gg_sends.append(
                    sends.start(gg_src.at[u, c], gg_all.at[part], {"expert": 2 * at + c})
                )

    def joined(u):
        swaps[u].wait_recv()
        add_to(theirs.at[u], returns.at[u, core])

    swap_own.wait_recv()
    for copy in note_sends:
        copy.wait_recv()
    unit(0)
    passed = []
    for d, (origin, way) in enumerate(((left, to_right), (right, to_left))):
        go[d][0].wait_recv()
        view = rows_all.at[origin, halves[d]]
        passed.append(sends.start(view, view, way))
    far_low, far_high = passed
    go[0][1].wait_recv()
    swap_left = sends.start(rows_all.at[left], rows_all.at[left], place.partner)
    go[1][1].wait_recv()
    swap_right = sends.start(rows_all.at[right], rows_all.at[right], place.partner)
    swap_left.wait_recv()
    unit(1)
    swap_right.wait_recv()
    unit(2)
    swap_far = []
    for h, copy in enumerate((far_low, far_high)):
        copy.wait_recv()
        piece = rows_all.at[far, halves[h]]
        swap_far.append(sends.start(piece, piece, place.partner))
    joined(1)
    joined(2)
    back_right = sends.start(theirs.at[2, halves[HIGH]], from_left, to_right)
    back_left = sends.start(theirs.at[1, halves[LOW]], from_right, to_left)
    for copy in swap_far:
        copy.wait_recv()
    unit(3)
    joined(3)
    back_far_low = sends.start(theirs.at[3, halves[LOW]], far_left, to_right)
    back_far_high = sends.start(theirs.at[3, halves[HIGH]], far_right, to_left)

    tall = 4 * w_grads.shape[2] * 2 // 3
    high = tall // 4
    w_stores = Keeps(tile_sems)
    for i in range(ff // tall):
        got = mm_tn(hidden[:, i * tall : (i + 1) * tall], pair_grad[...]).astype(BF16)
        tile_d[i] = got.reshape(tile_d.shape[1:])
        w_stores.start(tile_d.at[i], w_grads.at[pl.ds(2 * i, 2), :, pl.ds(high, high // 2)])
    for i in range(width // tall):
        if i >= 2:
            w_stores.made[ff // tall + i - 2].wait()
        got = mm_tn(arrived[:, i * tall : (i + 1) * tall], grad_pre[...]).astype(BF16)
        tile[i % 2] = got.reshape(tile.shape[1:])
        w_stores.start(tile.at[i % 2], w_grads.at[i, :, pl.ds(0, high)])

    swaps[0].wait_recv()
    back_right.wait_recv()
    back_left.wait_recv()
    own_ref[...] = theirs[0].astype(F32) + returns[0, core].astype(F32)
    add_to(own_ref.at[halves[HIGH]], from_left)
    add_to(own_ref.at[halves[LOW]], from_right)
    back_far_low.wait_recv()
    sums_ref[0] = (theirs[2, halves[LOW]].astype(F32) + far_left[...].astype(F32)).astype(BF16)
    back_far_high.wait_recv()
    sums_ref[1] = (theirs[1, halves[HIGH]].astype(F32) + far_right[...].astype(F32)).astype(BF16)
    for copy in gg_sends:
        copy.wait_recv()
    for copy in [*stores.made[6:], *w_stores.made[: ff // tall], *w_stores.made[-2:]]:
        copy.wait()
    sends.finish()


def experts(ctx, tokens, small, gains, notes, rows_by, wo, wg, wu, wd, collective_id):
    rows, width = ctx.shape
    ff = wg.shape[1]
    capacity = rows * 9 // 16
    high = width // 16
    vmem = pltpu.VMEM
    return pl.pallas_call(
        experts_kernel,
        out_shape=[
            sds((rows, width), F32),
            sds((EXPERTS, rows), F32),
            sds((8, 8, rows), F32),
            sds((2, rows // 2, width), BF16),
            sds((rows, width), F32),
            sds((8, rows, width), BF16),
            sds((4, 4, high * 3 // 2, width), BF16),
        ],
        in_specs=[VMEM] * 5 + [ANY] * 8,
        out_specs=[VMEM] * 5 + [ANY] * 2,
        scratch_shapes=[
            vmem((width, width), BF16),
            vmem((width, ff), BF16),
            vmem((width, ff), BF16),
            vmem((ff, width), BF16),
            vmem((8, rows, width), BF16),
            vmem((4, 2, rows, width), BF16),
            vmem((8 * capacity, width), BF16),
            vmem((8 * capacity, width), BF16),
            vmem((8 * capacity, ff), BF16),
            vmem((8 * capacity, 2 * ff), BF16),
            vmem((4, rows, width), BF16),
            *[vmem((rows // 2, width), BF16)] * 4,
            vmem((2, 4, high, width), BF16),
            vmem((2, 2, 4, high // 2, width), BF16),
            vmem((2, rows, width), BF16),
            vmem((8, EXPERTS, rows), F32),
            vmem((4, 2, 8, rows), F32),
            vmem((8, 1, rows), jnp.int32),
            semaphores(12),
            semaphores(6),
            semaphores(8),
            semaphores(40),
            semaphores(40),
        ],
        compiler_params=remote_params(collective_id),
    )(ctx, tokens, small, gains, notes, *rows_by, wo, wg, wu, wd)


GROUPS = 3


def middle_kernel(
    middle_ref, gates_ref, gg_all, sums_ref, own_ref, d_out_ref, ctx_ref, small_ref, gains_ref,
    start_ref, q_ref, kv_ref, lse_ref, cos_ref, sin_ref, wo_hbm, w_grads, blocks_ref,
    grad_middle_ref, small_grad_ref, gq_ref, gkv_ref, wo_out, combined, w_done,
    wo_ref, g_ref, from_left, from_right, w_total_0, w_total_1, w_whole, w_far,
    bias, k_t, gkv, probs, grad_probs, second_whole, second_far, *refs,
):
    place = Place()
    core = place.core
    neighbours = [place.partner, *place.x_to, *place.y_to, *place.z_to]
    greet(neighbours)
    bufs, x_bufs = refs[:12], refs[12:17]
    wo_sem, local_sems, send_sems, recv_sems = refs[17:]
    keeps = Keeps(local_sems)
    cols = w_total_0.shape[-1]
    totals = (w_total_0, w_total_1)
    length, rows = bias.shape
    width = middle_ref.shape[1]
    quarter = width // 4

    def part_of(ref, p, w):
        return ref.at[:, w] if p else ref.at[w]

    loads = {}
    for k in range(4):
        for p in range(2):
            me, (right, left, far), _ = place.ring(p == 0)
            w = (far, right, left, me)[k]
            src = part_of(w_grads, p, w).at[:, :, pl.ds(p * cols, cols)]
            loads[k, p] = keeps.start(src, part_of(totals[p], p, w))
    wo_load = pltpu.make_async_copy(wo_hbm, wo_ref, wo_sem)
    wo_load.start()
    await_greetings(neighbours)
    sends = Sends(send_sems, recv_sems)
    came = [
        sends.start(sums_ref.at[i], dst, place.x_to[i])
        for i, dst in enumerate((from_left, from_right))
    ]

    def first_half(p):
        def view(w, h):
            span = pl.ds(2 * h, 2)
            return totals[p].at[span, w] if p else totals[p].at[w, span]

        return view

    def expert_steps():
        rings = [Ring(p == 0, first_half(p), w_whole.at[p], w_far.at[p]) for p in range(2)]
        yield from ring_sum(place, sends, rings, lambda k, i, w: loads[k, i].wait())
        half = cols // 2

        def second_half(p):
            def view(w, h):
                at = pl.ds(h * half, half)
                return totals[p].at[w, place.z, :, at] if p else totals[p].at[place.y, w, :, at]

            return view

        rings = [
            Ring(p == 1, second_half(p), second_whole.at[p], second_far.at[p]) for p in range(2)
        ]
        yield from ring_sum(place, sends, rings)
        spreads = []
        for p in range(2):
            me = place.ring(p == 1)[0]
            w_done[p, me] = totals[p][place.y, place.z]

            view = lambda w, p=p: w_done.at[p, w]
            spreads.append(Spread(p == 1, w_done.at[p, me], view, half_columns))
        yield from ring_gather(place, sends, spreads)

    def columns(c, p):
        return pl.ds(pl.multiple_of((2 * c + p) * quarter, 128), quarter)

    def theirs_of(p):
        at = columns(1 - core, p)
        if p == 0:
            return lambda w: wo_ref.at[w, :, :, at]
        return lambda w: wo_ref.at[:, w, :, at]

    strips = [
        Strip(
            p == 0, wo_ref.at[:, :, :, columns(core, p)], bufs[6 * p : 6 * p + 6],
            None, theirs_of(p),
        )
        for p in range(2)
    ]
    expert = expert_steps()
    dense = dp_sum(place, sends, strips, ())
    rest = x_sum(place, sends, blocks_ref, combined, *x_bufs)
    next(expert)
    next(rest)

    grad_gates = jnp.concatenate([gg_all[e, :1] for e in range(EXPERTS)], axis=0)
    gates_t = gates_ref[...]
    products = gates_t * grad_gates
    grad_logits = products - gates_t * jnp.sum(products, axis=0, keepdims=True)
    grad_logits = jnp.concatenate(
        [grad_logits, jnp.zeros((128 - EXPERTS, rows), F32)], axis=0
    ).T.astype(BF16)
    total = own_ref[...] + mm_nt(grad_logits, small_ref[...])
    middle, gain = middle_ref[...], gains_ref[:1]
    inverse = inverse_rms(middle)
    scaled = middle * inverse
    small_grad = mm_tn((scaled * gain).astype(BF16), grad_logits)
    fill_bias(bias, start_ref, rows * place.part)
    for copy in came:
        copy.wait_recv()
    total += jnp.concatenate([from_left[...], from_right[...]], axis=0).astype(F32)
    grad_gain = jnp.sum(total * scaled, axis=0, keepdims=True)
    lanes = lax.broadcasted_iota(jnp.int32, (width, 128), 1)
    small_grad += jnp.where(lanes == EXPERTS, as_column(grad_gain, 128), 0.0)
    small_grad_ref[...] = small_grad.astype(BF16)
    weighted = total * gain
    inner = jnp.mean(weighted * scaled, axis=-1, keepdims=True)
    grad_middle = d_out_ref[...].astype(F32) + inverse * (weighted - scaled * inner)
    grad_middle_ref[...] = grad_middle
    grad_attn = grad_middle.astype(BF16)
    wo_load.wait()
    g_ref[...] = mm_nt(grad_attn, wo_ref[...].reshape(width, width)).astype(BF16)
    next(rest)
    next(expert)
    tall = width // 4
    for i in range(4):
        got = mm_tn(ctx_ref[:, i * tall : (i + 1) * tall], grad_attn).astype(BF16)
        wo_ref[i] = got.reshape(wo_ref.shape[1:])
    next(dense)

    when = {2: (dense,), 4: (rest,), 6: (dense, expert), 8: (dense,), 10: (dense, expert)}
    for group in range(KEY_VALUE_HEADS):
        keys = slice(2 * group * HEAD_SIZE, (2 * group + 1) * HEAD_SIZE)
        values = slice((2 * group + 1) * HEAD_SIZE, (2 * group + 2) * HEAD_SIZE)
        k_t[...] = kv_ref[:, keys].astype(F32).T.astype(BF16)
        gkv[...] = jnp.zeros_like(gkv)

        def one_head(i, carry, base):
            head = base + i
            query, grad = q_ref[:, head_columns(head)], g_ref[:, head_columns(head)]
            lse = lse_ref[head]
            inner = jnp.zeros_like(lse)
            for at in range(0, length, BLOCK):
                span = pl.ds(at, BLOCK)
                s = mm_nt(kv_ref[span, keys], query) + bias[span]
                p = jnp.exp2(s * (SCALE * LOG2E) - lse)
                gp = mm_nt(kv_ref[span, values], grad)
                inner += jnp.sum(p * gp, axis=0, keepdims=True)
                probs[span] = p
                grad_probs[span] = gp
                gkv[span, HEAD_SIZE:] += mm(p.astype(BF16), grad)
            gq = jnp.zeros((HEAD_SIZE, rows), F32)
            for at in range(0, length, BLOCK):
                span = pl.ds(at, BLOCK)
                gs = (probs[span] * (grad_probs[span] - inner)).astype(BF16)
                gkv[span, :HEAD_SIZE] += mm(gs, query)
                gq += mm(k_t[:, span], gs)
            turned = spin(gq.T * SCALE, cos_ref[...], -sin_ref[...])
            gq_ref[:, head_columns(head)] = turned.astype(BF16)
            return carry

        for base in range(group * GROUP, (group + 1) * GROUP, 2):
            lax.fori_loop(0, 2, lambda i, carry, base=base: one_head(i, carry, base), 0)
            for steps in when.get(base + 2, ()):
                next(steps)
        gkv_ref[:, keys] = (gkv[:, :HEAD_SIZE] * SCALE).astype(BF16)
        gkv_ref[:, values] = gkv[:, HEAD_SIZE:].astype(BF16)
    run_out(expert, dense, rest)
    for p, s in enumerate(strips):
        wo_out[:, columns(core, p)] = s.result[...]
        wo_out[:, columns(1 - core, p)] = s.near[3]
    sends.finish()


def between(
    middle, gates, gg, sums, own, d_out, ctx, small, gain, start, query, kv, lse, cosine, sine,
    wo, w_grads, back_out, collective_id,
):
    rows, width = query.shape
    length = kv.shape[0]
    height, quarter = width // 16, width // 4
    high, cols = w_grads.shape[2], width // 2
    vmem = pltpu.VMEM
    return pl.pallas_call(
        middle_kernel,
        out_shape=[
            sds((rows, width), F32),
            sds((width, 128), BF16),
            sds((rows, width), BF16),
            sds(kv.shape, BF16),
            sds((height, width), BF16),
            sds((rows, width), F32),
            sds((2, 4, high, cols), BF16),
        ],
        in_specs=[VMEM] * 15 + [ANY] * 3,
        out_specs=[VMEM] * 7,
        scratch_shapes=[
            vmem((4, 4, height, width), BF16),
            vmem((rows, width), BF16),
            vmem((rows // 2, width), BF16),
            vmem((rows // 2, width), BF16),
            vmem((4, 4, high, cols), BF16),
            vmem((4, 4, high, cols), BF16),
            vmem((2, 2, 2, 2, high, cols), BF16),
            vmem((2, 2, 2, high, cols), BF16),
            vmem((length, rows), F32),
            vmem((HEAD_SIZE, length), BF16),
            vmem((length, 2 * HEAD_SIZE), F32),
            vmem((length, rows), F32),
            vmem((length, rows), F32),
            vmem((2, 2, 2, high, cols // 2), BF16),
            vmem((2, 2, high, cols // 2), BF16),
            *strip_buffers(height, quarter),
            *strip_buffers(height, quarter),
            *x_buffers(rows, width),
            pltpu.SemaphoreType.DMA,
            semaphores(8),
            semaphores(100),
            semaphores(100),
        ],
        compiler_params=remote_params(collective_id),
    )(
        middle, gates, gg, sums, own, d_out, ctx, small, gain, start, query, kv, lse, cosine, sine,
        wo, w_grads, back_out,
    )


def last_kernel(
    kv_terms, gq_ref, normed_ref, tokens_ref, gains_ref, cos_ref, sin_ref,
    small_ref, w_done, w_hbm,
    grad_inputs_ref, strips_out, small_out, w_sums,
    grads, small_total, w_ref, normed_t, kv_sum, *refs,
):
    place = Place()
    core = place.core
    neighbours = [place.partner, *place.x_to, *place.y_to, *place.z_to]
    greet(neighbours)
    bufs, x_bufs = refs[:30], refs[30:35]
    w_sem, local_sems, send_sems, recv_sems = refs[35:]
    load = pltpu.make_async_copy(w_hbm, w_ref, w_sem)
    load.start()
    await_greetings(neighbours)
    sends, keeps = Sends(send_sems, recv_sems), Keeps(local_sems)
    kv_steps = x_sum(place, sends, kv_terms, kv_sum, *x_bufs)
    next(kv_steps)

    def place_of(p, w, at, size):
        cols = pl.ds(p * w_done.shape[-1] + at, size)
        return w_sums.at[:, w, :, cols] if p else w_sums.at[w, :, :, cols]

    def spread(p, i):
        size = w_done.shape[-1] // GROUPS
        source = w_done.at[p, :, :, pl.ds(i * size, size)]
        return Spread(p == 0, source, lambda w: place_of(p, w, i * size, size), half_span)

    for p in range(2):
        keeps.start(w_done.at[p], place_of(p, place.ring(p == 0)[0], 0, w_done.shape[-1]))
    e0, e1, e2 = [
        ring_gather(place, sends, [spread(p, i) for p in range(2)]) for i in range(GROUPS)
    ]
    for steps in (e0, e0, e1):
        next(steps)
    strip = grads.shape[-1]
    wide = strip - HEAD_SIZE
    rows, width = normed_ref.shape
    height = grads.shape[3]

    def put(s, cols, right_side):
        got = mm(normed_t[...], right_side).astype(BF16)
        grads[s, :, :, :, cols] = got.reshape(4, 4, height, right_side.shape[1])

    def shared(at, size, bufs):
        cols = pl.ds(at, size)

        def theirs_of(p):
            s = 2 * (1 - core) + p
            if p == 0:
                return lambda w: grads.at[s, w, :, :, cols]
            return lambda w: grads.at[s, :, w, :, cols]

        return [
            Strip(
                p == 0, grads.at[2 * core + p, :, :, :, cols], bufs[6 * p : 6 * p + 6],
                None, theirs_of(p),
            )
            for p in range(2)
        ]

    wide_strips = shared(0, wide, bufs[:12])
    narrow_strips = shared(wide, HEAD_SIZE, bufs[12:24])
    wide_steps = dp_sum(place, sends, wide_strips, ())
    narrow_steps = dp_sum(place, sends, narrow_strips, ())
    normed_t[...] = normed_ref[...].astype(F32).T.astype(BF16)
    for s in range(4):
        put(s, pl.ds(0, wide), gq_ref[:, s * wide : (s + 1) * wide])
    next(wide_steps)
    next(kv_steps)
    next(e0)
    load.wait()
    grad_normed = None
    for s in range(4):
        at = s * strip
        term = mm_nt(gq_ref[:, s * wide : (s + 1) * wide], w_ref[:, at : at + wide])
        grad_normed = term if grad_normed is None else grad_normed + term
    next(wide_steps)
    next(kv_steps)
    run_out(kv_steps)
    cosine, sine = cos_ref[...], sin_ref[...]
    for s in range(4):
        got = kv_sum[:, s * HEAD_SIZE : (s + 1) * HEAD_SIZE]
        if s % 2 == 0:
            got = spin(got, cosine, -sine)
        got = got.astype(BF16)
        put(s, pl.ds(wide, HEAD_SIZE), got)
        grad_normed += mm_nt(got, w_ref[:, s * strip + wide : (s + 1) * strip])
    for steps in (narrow_steps, wide_steps, narrow_steps):
        next(steps)

    grad_inputs, grad_gain = rms_back(tokens_ref[...].astype(F32), gains_ref[1:2], grad_normed)
    grad_inputs_ref[...] = grad_inputs
    lanes = lax.broadcasted_iota(jnp.int32, (width, 128), 1)
    small = jnp.where(
        lanes == EXPERTS + 1, as_column(grad_gain, 128), small_ref[...].astype(F32)
    )
    small_total[...] = small.astype(BF16).reshape(small_total.shape)
    small_strip = Strip(True, small_total, bufs[24:])
    small_steps = dp_sum(place, sends, [small_strip], ())
    for steps in (
        small_steps, small_steps, wide_steps, narrow_steps, small_steps,
        wide_steps, narrow_steps, small_steps, wide_steps, e1, narrow_steps, e2, small_steps, e2,
        wide_steps, narrow_steps, e1,
    ):
        next(steps)
    run_out(wide_steps, narrow_steps, small_steps, e0, e1, e2)
    small_out[...] = small_strip.result[...].astype(F32) + small_strip.near[3].astype(F32)
    for p in range(2):
        for at, size, s in ((0, wide, wide_strips[p]), (wide, HEAD_SIZE, narrow_strips[p])):
            for c, got in ((core, s.result), (1 - core, s.near.at[3])):
                begin_at = pl.multiple_of((2 * c + p) * strip + at, 128)
                strips_out[:, pl.ds(begin_at, size)] = got[...]
    for copy in keeps.made:
        copy.wait()
    sends.finish()


def last(
    kv_terms, grad_query, normed, tokens, gain, cosine, sine, small, w_done, w, collective_id
):
    rows, width = normed.shape
    total = w.shape[1]
    height, strip = width // 16, total // 4
    kv_width = total - width
    vmem = pltpu.VMEM
    return pl.pallas_call(
        last_kernel,
        out_shape=[
            sds((rows, width), F32),
            sds((height, total), BF16),
            sds((height, 128), F32),
            sds((4, 4, w_done.shape[2], width), BF16),
        ],
        in_specs=[ANY] + [VMEM] * 8 + [ANY],
        out_specs=[VMEM] * 3 + [ANY],
        scratch_shapes=[
            vmem((4, 4, 4, height, strip), BF16),
            vmem((4, 4, height, 128), BF16),
            vmem((width, total), BF16),
            vmem((width, rows), BF16),
            vmem((rows, kv_width), F32),
            *strip_buffers(height, strip - HEAD_SIZE),
            *strip_buffers(height, strip - HEAD_SIZE),
            *strip_buffers(height, HEAD_SIZE),
            *strip_buffers(height, HEAD_SIZE),
            *strip_buffers(height, 128, shared=False),
            *x_buffers(rows, kv_width),
            pltpu.SemaphoreType.DMA,
            semaphores(2),
            semaphores(160),
            semaphores(160),
        ],
        compiler_params=remote_params(collective_id),
    )(kv_terms, grad_query, normed, tokens, gain, cosine, sine, small, w_done, w)


def finish_kernel(
    sums_ref, grad_middle_ref, grad_inputs_ref, middle_ref, combined_ref, strips_ref, wo_ref,
    small_ref, g_out, u_out, d_out, tokens_out, mixed_out, wq_out, wk_out, wv_out, wo_out,
    small_out,
):
    owners, high, width = sums_ref.shape
    ff = width // 2
    gu = high * 2 // 3
    g_out[...] = sums_ref[:, :gu, :ff].astype(F32).reshape(owners * gu, ff)
    u_out[...] = sums_ref[:, :gu, ff:].astype(F32).reshape(owners * gu, ff)
    d_out[...] = sums_ref[:, gu:].astype(F32).reshape(owners * (high - gu), width)
    tokens_out[...] = grad_middle_ref[...] + grad_inputs_ref[...]
    mixed_out[...] = (middle_ref[...] + combined_ref[...]).astype(BF16)

    @pl.when(pl.program_id(0) == 0)
    def _():
        strip = strips_ref.shape[1] // 4
        wide = strip - HEAD_SIZE
        for s in range(4):
            at = s * strip
            wq_out[:, s * wide : (s + 1) * wide] = strips_ref[:, at : at + wide].astype(F32)
            other = (wk_out, wv_out)[s % 2]
            begin_at = s // 2 * HEAD_SIZE
            got = strips_ref[:, at + wide : at + strip].astype(F32)
            other[:, begin_at : begin_at + HEAD_SIZE] = got
        wo_out[...] = wo_ref[...].astype(F32)
        small_out[...] = small_ref[...].T[: EXPERTS + 8]


def finish(sums, grad_middle, grad_inputs, middle, combined, strips, wo, small):
    owners, high, width = sums.shape
    rows = middle.shape[0]
    height, total = strips.shape
    kv_half = (total - width) // 2
    ff = width // 2
    gu, d = high * 2 // 3, high // 3
    steps = 8
    each, part = owners // steps, rows // steps
    by_step = lambda a, b: pl.BlockSpec((a, b), lambda i: (i, 0))
    whole = lambda a, b: pl.BlockSpec((a, b), lambda i: (0, 0))
    return pl.pallas_call(
        finish_kernel,
        grid=(steps,),
        out_shape=[
            sds((owners * gu, ff), F32),
            sds((owners * gu, ff), F32),
            sds((owners * d, width), F32),
            sds((rows, width), F32),
            sds((rows, width), BF16),
            sds((height, width), F32),
            sds((height, kv_half), F32),
            sds((height, kv_half), F32),
            sds((height, width), F32),
            sds((EXPERTS + 8, height), F32),
        ],
        in_specs=[pl.BlockSpec((each, high, width), lambda i: (i, 0, 0))]
        + [by_step(part, width)] * 4
        + [whole(height, total), whole(height, width), whole(height, 128)],
        out_specs=[
            by_step(each * gu, ff),
            by_step(each * gu, ff),
            by_step(each * d, width),
            by_step(part, width),
            by_step(part, width),
            whole(height, width),
            whole(height, kv_half),
            whole(height, kv_half),
            whole(height, width),
            whole(EXPERTS + 8, height),
        ],
        compiler_params=pltpu.CompilerParams(vmem_limit_bytes=63 * MIB),
        cost_estimate=pl.CostEstimate(flops=0, bytes_accessed=30 * MIB, transcendentals=0),
    )(sums, grad_middle, grad_inputs, middle, combined, strips, wo, small)


def on_device(
    tokens,
    d_out,
    gain_in,
    w_query,
    key_projection_weight,
    value_projection_weight,
    w_out,
    gain_mid,
    w_router,
    w_gate,
    w_up,
    w_down,
    routes,
    segments,
):
    rows, width = tokens.shape
    length = segments.shape[1]
    part = lax.axis_index("expert")
    seg_row = segments[0]
    offset = part * rows
    my_seg = lax.dynamic_slice_in_dim(seg_row, offset, rows, 0)
    start = jnp.sum((seg_row[None, :] < my_seg[:, None]).astype(jnp.int32), axis=1)
    angles = angles_for(offset + jnp.arange(rows, dtype=jnp.int32) - start)
    cosine, sine = jnp.cos(angles), jnp.sin(angles)
    cosine = jnp.concatenate([cosine, cosine], axis=1)
    sine = jnp.concatenate([-sine, sine], axis=1)
    start = start[None, :]

    small = jnp.concatenate([w_router, gain_mid[:, None], gain_in[:, None]], axis=1)
    small = jnp.pad(small, ((0, 0), (0, 128 - small.shape[1])))
    note = jnp.pad(routes.T, ((0, 8 - TOPK), (0, 0)))
    w_strips, small, wo_part, rows_near, notes, normed, query, kv_all, gains = begin(
        w_query, key_projection_weight, value_projection_weight, w_out, small, d_out, note,
        tokens, cosine, sine, 1,
    )
    w_strips = w_strips.reshape(width, -1)
    small = small.reshape(width, -1)
    kv_all = kv_all.reshape(length, -1)
    context, lse, wo, rows_far, rows_other = attend(
        start, query, kv_all, wo_part, d_out, rows_near, 2
    )

    middle, gates, gg, sums, own, back_out, w_grads = experts(
        context, tokens, small, gains, notes, (d_out, rows_near, rows_far, rows_other),
        wo.reshape(width, width), w_gate[0], w_up[0], w_down[0], 3,
    )
    grad_middle, small_grads, grad_query, kv_terms, wo_sum, combined, w_done = between(
        middle, gates, gg, sums, own, d_out, context, small, gains, start, query, kv_all,
        lse, cosine, sine, wo, w_grads, back_out, 4,
    )
    grad_inputs, strips_sum, small_sum, w_sums = last(
        kv_terms.reshape(8, rows, -1), grad_query, normed, tokens, gains, cosine, sine,
        small_grads, w_done, w_strips, 5,
    )
    g_wg, g_wu, g_wd, grad_tokens, mixed, g_wq, g_wk, g_wv, g_wo, g_small = finish(
        w_sums.reshape(16, -1, width), grad_middle, grad_inputs, middle, combined, strips_sum,
        wo_sum, small_sum,
    )
    return (
        mixed,
        grad_tokens,
        g_small[EXPERTS + 1],
        g_wq,
        g_wk,
        g_wv,
        g_wo,
        g_small[EXPERTS],
        g_small[:EXPERTS].T,
        g_wg[None],
        g_wu[None],
        g_wd[None],
    )


def solution(mesh):
    whole = P(("dp", "expert"), None)
    over_dp, by_dp, over_expert = P("dp"), P("dp", None), P("expert", None, None)
    return jax.shard_map(
        on_device,
        mesh=mesh,
        in_specs=(whole, whole, over_dp, by_dp, by_dp, by_dp, by_dp, over_dp, by_dp)
        + (over_expert,) * 3
        + (whole, by_dp),
        out_specs=(whole, whole, over_dp, by_dp, by_dp, by_dp, by_dp, over_dp, by_dp)
        + (over_expert,) * 3,
        check_vma=False,
    )
```

```python
import functools

import jax
import jax.numpy as jnp
from jax import lax
from jax.experimental import pallas as pl
from jax.experimental.pallas import tpu as pltpu
from jax.sharding import PartitionSpec as P

QUERY_HEADS = 12
KEY_VALUE_HEADS = 2
HEAD_SIZE = 128
TOPK = 4
EXPERTS = 8
GROUP = QUERY_HEADS // KEY_VALUE_HEADS
SCALE = HEAD_SIZE**-0.5
LOG2E = 1.4426950408889634
BLOCK = 512

EPSILON = 1e-06
ROPE_BASE = 1000000.0
MASK_FILL = -1e30
F32 = jnp.float32
BF16 = jnp.bfloat16

MESH = pl.DeviceIdType.MESH
ANY = pl.BlockSpec(memory_space=pl.ANY)
VMEM = pl.BlockSpec(memory_space=pltpu.VMEM)
MIB = 2**20


def dot(a, b, dims):
    return lax.dot_general(a, b, (dims, ((), ())), preferred_element_type=F32)


def mm(a, b):
    return dot(a, b, ((1,), (0,)))


def mm_nt(a, b):
    return dot(a, b, ((1,), (1,)))


def mm_tn(a, b):
    return dot(a, b, ((0,), (0,)))


def sds(shape, dtype):
    return jax.ShapeDtypeStruct(tuple(shape), dtype)


def remote_params(collective_id):
    return pltpu.CompilerParams(
        collective_id=collective_id, has_side_effects=True, vmem_limit_bytes=63 * MIB
    )


def semaphores(count):
    return pltpu.SemaphoreType.DMA((count,))


def inverse_rms(rows):
    return lax.rsqrt(jnp.mean(rows * rows, axis=-1, keepdims=True) + EPSILON)


def rms_back(rows, gain, grad):
    inverse = inverse_rms(rows)
    scaled = rows * inverse
    weighted = grad * gain
    inner = jnp.mean(weighted * scaled, axis=-1, keepdims=True)
    return inverse * (weighted - scaled * inner), jnp.sum(grad * scaled, axis=0, keepdims=True)


def as_column(row, lanes):
    return jnp.broadcast_to(row, (lanes, row.shape[1])).T


def angles_for(positions):
    half_width = HEAD_SIZE // 2
    freqs = ROPE_BASE ** (-2.0 * jnp.arange(half_width, dtype=F32) / HEAD_SIZE)
    return positions.astype(F32)[:, None] * freqs[None, :]


def spin(z, cosine, sine):
    return z * cosine + pltpu.roll(z, HEAD_SIZE // 2, 1) * sine


class Sends:
    def __init__(self, send_sems, recv_sems):
        self.send_sems, self.recv_sems, self.made = send_sems, recv_sems, []

    def start(self, src, dst, to):
        at = len(self.made)
        copy = pltpu.make_async_remote_copy(
            src_ref=src,
            dst_ref=dst,
            send_sem=self.send_sems.at[at],
            recv_sem=self.recv_sems.at[at],
            device_id=to,
            device_id_type=MESH,
        )
        copy.start()
        self.made.append(copy)
        return copy

    def finish(self):
        for copy in self.made:
            copy.wait_send()


class Keeps:
    def __init__(self, sems):
        self.sems, self.made = sems, []

    def start(self, src, dst):
        copy = pltpu.make_async_copy(src, dst, self.sems.at[len(self.made)])
        copy.start()
        self.made.append(copy)
        return copy


class Place:
    def __init__(self):
        self.part = lax.axis_index("expert")
        self.core = self.part % 2
        self.chip = self.part // 2
        at = lambda d: lax.rem(self.chip + d, 4) * 2 + self.core
        self.right, self.left, self.far = at(1), at(3), at(2)
        to = lambda i: {"expert": i}
        self.partner = to(2 * self.chip + (1 - self.core))
        self.x_to = [to(self.right), to(self.left), to(self.far)]
        self.others = [to(lax.rem(self.part + d, 8)) for d in range(1, 8)]
        place = lax.axis_index("dp")
        self.y, self.z = place // 4, place % 4
        ring = lambda v: [lax.rem(v + d, 4) for d in (1, 3, 2)]
        self.y_ring, self.z_ring = ring(self.y), ring(self.z)
        self.y_to = [{"dp": v * 4 + self.z} for v in self.y_ring[:2]]
        self.z_to = [{"dp": self.y * 4 + v} for v in self.z_ring[:2]]

    def ring(self, along_y):
        if along_y:
            return self.y, self.y_ring, self.y_to
        return self.z, self.z_ring, self.z_to


def greet(others):
    barrier = pltpu.get_barrier_semaphore()
    for other in others:
        pl.semaphore_signal(barrier, inc=1, device_id=other, device_id_type=MESH)


def await_greetings(others):
    pl.semaphore_wait(pltpu.get_barrier_semaphore(), len(others))


def add_to(ref, *others):
    got = ref[...].astype(F32)
    for other in others:
        got += other[...].astype(F32)
    ref[...] = got.astype(ref.dtype)


def run_out(*steps):
    steps = list(steps)
    while steps:
        for s in list(steps):
            if next(s, "done") == "done":
                steps.remove(s)


def x_sum(place, sends, blocks_ref, out_ref, mine, total, from_left, from_right, sems):
    rows = out_ref.shape[0]
    half = rows // 2
    low, high = pl.ds(0, half), pl.ds(half, half)
    to_right, to_left = place.x_to[:2]
    flip = 1 - 2 * place.core
    keeps = Keeps(sems)
    swaps, loads = [], []
    for k, dest in enumerate((place.far, place.right, place.left, place.part)):
        swaps.append(sends.start(blocks_ref.at[dest + flip], total.at[k], place.partner))
        loads.append(keeps.start(blocks_ref.at[dest], mine.at[k]))

    def add_up(k):
        loads[k].wait()
        swaps[k].wait_recv()
        add_to(total.at[k], mine.at[k])

    yield
    add_up(0)
    far_low = sends.start(total.at[0, low], from_left.at[0], to_right)
    far_high = sends.start(total.at[0, high], from_right.at[0], to_left)
    add_up(1)
    right_high = sends.start(total.at[1, high], from_left.at[2], to_right)
    add_up(2)
    left_low = sends.start(total.at[2, low], from_right.at[2], to_left)
    yield
    far_low.wait_recv()
    add_to(total.at[1, low], from_left.at[0])
    right_low = sends.start(total.at[1, low], from_left.at[1], to_right)
    far_high.wait_recv()
    add_to(total.at[2, high], from_right.at[0])
    left_high = sends.start(total.at[2, high], from_right.at[1], to_left)
    yield
    loads[3].wait()
    swaps[3].wait_recv()
    out_ref[...] = mine[3].astype(F32) + total[3].astype(F32)
    right_high.wait_recv()
    left_low.wait_recv()
    right_low.wait_recv()
    left_high.wait_recv()
    add_to(out_ref.at[low], from_left.at[1], from_right.at[2])
    add_to(out_ref.at[high], from_left.at[2], from_right.at[1])
    yield


def x_buffers(rows, columns):
    return [
        pltpu.VMEM((4, rows, columns), BF16),
        pltpu.VMEM((4, rows, columns), BF16),
        pltpu.VMEM((3, rows // 2, columns), BF16),
        pltpu.VMEM((3, rows // 2, columns), BF16),
        semaphores(4),
    ]


class Ring:
    def __init__(self, along_y, view, whole, farther):
        self.along_y, self.view, self.whole, self.farther = along_y, view, whole, farther


def ring_sum(place, sends, rings, ready=lambda *_: None):
    going = []
    for i, r in enumerate(rings):
        _, (right, left, far), to = place.ring(r.along_y)
        ready(0, i, far)
        going.append([sends.start(r.view(far, h), r.farther.at[h], to[h]) for h in range(2)])
    for i, r in enumerate(rings):
        _, (right, left, far), to = place.ring(r.along_y)
        ready(1, i, right)
        ready(2, i, left)
        going[i].append(sends.start(r.view(right, 1), r.whole.at[0, 1], to[0]))
        going[i].append(sends.start(r.view(left, 0), r.whole.at[1, 0], to[1]))
    yield
    for i, r in enumerate(rings):
        _, (right, left, far), to = place.ring(r.along_y)
        for h, w in enumerate((right, left)):
            going[i][h].wait_recv()
            add_to(r.view(w, h), r.farther.at[h])
            going[i].append(sends.start(r.view(w, h), r.whole.at[h, h], to[h]))
    yield
    for i, r in enumerate(rings):
        me, _, _ = place.ring(r.along_y)
        ready(3, i, me)
        for copy in going[i][2:]:
            copy.wait_recv()
        for h in range(2):
            add_to(r.view(me, h), r.whole.at[0, h], r.whole.at[1, h])


class Spread:
    def __init__(self, along_y, source, view, half, landed=lambda _: None):
        self.along_y, self.source, self.view = along_y, source, view
        self.half, self.landed = half, landed


def ring_gather(place, sends, spreads):
    came, onward = [], []

    def send(s, h, to):
        me = place.ring(s.along_y)[0]
        return sends.start(s.half(s.source, h), s.half(s.view(me), h), to)

    for s in spreads:
        to = place.ring(s.along_y)[2]
        came.append([[send(s, d, to[d])] for d in range(2)])
    yield
    for s, copies in zip(spreads, came):
        to = place.ring(s.along_y)[2]
        for d in range(2):
            copies[d].append(send(s, 1 - d, to[d]))
    yield
    for s, copies in zip(spreads, came):
        _, (right, left, _), to = place.ring(s.along_y)
        onward.append([])
        for d, origin in enumerate((left, right)):
            copies[d][0].wait_recv()
            view = s.half(s.view(origin), d)
            onward[-1].append(sends.start(view, view, to[d]))
    yield
    for s, copies in zip(spreads, came):
        _, (right, left, _), _ = place.ring(s.along_y)
        for d, origin in enumerate((left, right)):
            copies[d][1].wait_recv()
            s.landed(s.view(origin))
    for s, copies in zip(spreads, onward):
        far = place.ring(s.along_y)[1][2]
        for d in range(2):
            copies[d].wait_recv()
            s.landed(s.half(s.view(far), d))
    yield


def half_span(share, h):
    return share.at[pl.ds(2 * h, 2)]


def half_rows(share, h):
    half = share.shape[0] // 2
    return share.at[pl.ds(h * half, half)]


def half_columns(share, h):
    half = share.shape[-1] // 2
    return share.at[:, pl.ds(h * half, half)]


class Strip:
    def __init__(self, y_first, total, bufs, own=None, other=None):
        self.y_first, self.total, self.own, self.other = y_first, total, own, other
        self.theirs, self.big, self.far, self.mid, self.midfar, self.near = bufs

    def block(self, ref, w):
        return ref.at[w] if self.y_first else ref.at[:, w]


def strip_buffers(rows, columns, shared=True):
    return [
        pltpu.VMEM((4, 4, rows, columns) if shared else (1, 1, rows, columns), BF16),
        pltpu.VMEM((2, 2, 2, rows, columns), BF16),
        pltpu.VMEM((2, 2, rows, columns), BF16),
        pltpu.VMEM((2, 2, rows // 2, columns), BF16),
        pltpu.VMEM((2, rows // 2, columns), BF16),
        pltpu.VMEM((4, rows, columns), BF16),
    ]


def dp_sum(place, sends, strips, sems):
    y, z = place.y, place.z
    keeps = Keeps(sems)
    swaps, loads = {}, {}
    for k in range(4):
        for i, s in enumerate(strips):
            me, (right, left, far), _ = place.ring(s.y_first)
            w = (far, right, left, me)[k]
            if s.other is not None:
                swaps[k, i] = sends.start(s.other(w), s.block(s.theirs, w), place.partner)
            if s.own is not None:
                loads[k, i] = keeps.start(s.own(w), s.block(s.total, w))
    yield

    def joined(k, i, s, w):
        if s.own is not None:
            loads[k, i].wait()
        if s.other is not None:
            swaps[k, i].wait_recv()
            add_to(s.block(s.total, w), s.block(s.theirs, w))

    def big(s, w, h):
        span = pl.ds(2 * h, 2)
        return s.total.at[w, span] if s.y_first else s.total.at[span, w]

    def small(s, w, h):
        half = s.total.shape[2] // 2
        at = pl.ds(h * half, half)
        return s.total.at[y, w, at] if s.y_first else s.total.at[w, z, at]

    def rings(first):
        view = big if first else small
        return [
            Ring(
                s.y_first == first,
                functools.partial(view, s),
                s.big if first else s.mid,
                s.far if first else s.midfar,
            )
            for s in strips
        ]

    yield from ring_sum(place, sends, rings(True), lambda k, i, w: joined(k, i, strips[i], w))
    yield from ring_sum(place, sends, rings(False))

    shares, back = [], []
    for s in strips:
        shares.append(
            [sends.start(s.total.at[y, z], s.near.at[i], place.x_to[i]) for i in range(3)]
        )
    yield
    for s, share in zip(strips, shares):
        for copy in share:
            copy.wait_recv()
        got = s.total[y, z].astype(F32)
        for i in range(3):
            got += s.near[i].astype(F32)
        s.result = s.theirs.at[y, z] if s.other is not None else s.theirs.at[0, 0]
        s.result[...] = got.astype(BF16)
        back.append(sends.start(s.result, s.near.at[3], place.partner))
    yield
    for copy in back:
        copy.wait_recv()
    yield


def begin_kernel(
    wq_hbm, wk_hbm, wv_hbm, wo_hbm, small_ref, rows_hbm, note_ref, tokens_hbm, cos_ref, sin_ref,
    w_out, small_out, wo_part, rows_near, notes_out, normed_ref, query_ref, kv_ref, gains_ref,
    strips_ref, w_all, own_kv, wq_ref, wk_ref, wv_ref, wo_ref, rows_ref, tokens_ref,
    fetch_sems, local_sems, send_sems, recv_sems,
):
    fetches = Keeps(fetch_sems)
    for src, dst in (
        (wq_hbm, wq_ref), (wk_hbm, wk_ref), (wv_hbm, wv_ref), (wo_hbm, wo_ref),
        (rows_hbm, rows_ref), (tokens_hbm, tokens_ref),
    ):
        fetches.start(src, dst)
    place = Place()
    y, z, core, part = place.y, place.z, place.core, place.part
    neighbours = [*place.others, *place.y_to, *place.z_to]
    greet(neighbours)
    rows = wq_ref.shape[0]
    wide, narrow = wq_ref.shape[1] // 4, wk_ref.shape[1] // 2
    strip = wide + narrow
    for fetch in fetches.made[:4]:
        fetch.wait()
    for s in range(4):
        strips_ref[:, s * strip : s * strip + wide] = wq_ref[:, s * wide : (s + 1) * wide]
        other = (wk_ref, wv_ref)[s % 2]
        begin = s // 2 * narrow
        strips_ref[:, s * strip + wide : (s + 1) * strip] = other[:, begin : begin + narrow]
    await_greetings(neighbours)
    sends, keeps = Sends(send_sems, recv_sems), Keeps(local_sems)

    def columns(p, size):
        return pl.ds(pl.multiple_of((2 * core + p) * size, 128), size)

    across = []

    def send_across(view):
        across.append(sends.start(view, view, place.partner))

    def spread(first, src, out, cols, y_first, landed):
        def near(where):
            return out.at[where, z, :, cols] if y_first else out.at[y, where, :, cols]

        def wider(where):
            return out.at[:, where, :, cols] if y_first else out.at[where, :, :, cols]

        if first:
            return Spread(y_first, src, near, half_rows)
        source = wider(z if y_first else y)
        landed(source)
        return Spread(not y_first, source, wider, half_span, landed)

    def strips(first, at, size):
        def part(p):
            return pl.ds(pl.multiple_of((2 * core + p) * strip + at, 128), size)

        return [
            spread(first, strips_ref.at[:, part(p)], w_all, part(p), p == 1, send_across)
            for p in range(2)
        ]

    def small_spread(first):
        every = pl.ds(0, small_ref.shape[1])
        return spread(first, small_ref, small_out, every, False, lambda _: None)

    def out_spread(p):
        ring_of = (z, y)[p]

        keeps.start(wo_ref.at[:, columns(p, wide)], wo_part.at[p, ring_of])
        return Spread(
            p == 1, wo_ref.at[:, columns(p, wide)], lambda where: wo_part.at[p, where], half_rows
        )

    ahead = ring_gather(place, sends, [*strips(True, wide, narrow), small_spread(True)])
    behind = ring_gather(place, sends, [*strips(True, 0, wide), *map(out_spread, range(2))])
    for steps in (ahead, ahead, behind, behind):
        next(steps)
    for p in range(2):
        w_all[y, z, :, columns(p, strip)] = strips_ref[:, columns(p, strip)]
    small_out[y, z] = small_ref[...]

    half = rows_ref.shape[0] // 2
    x_halves = [pl.ds(h * half, half) for h in range(2)]
    fetches.made[4].wait()
    rows_came = [
        sends.start(rows_ref.at[x_halves[h]], rows_near.at[d, x_halves[h]], place.x_to[d])
        for d in range(2)
        for h in (d, 1 - d)
    ]
    notes = [sends.start(note_ref, notes_out.at[part], to) for to in place.others]
    keeps.start(note_ref, notes_out.at[part])
    next(ahead)
    next(ahead)
    ahead = ring_gather(place, sends, [*strips(False, wide, narrow), small_spread(False)])
    next(ahead)
    next(ahead)
    next(behind)
    next(behind)
    behind = ring_gather(place, sends, strips(False, 0, wide))
    next(behind)
    next(behind)
    next(ahead)
    next(ahead)
    small_t = small_out[...].reshape(tokens_ref.shape[1], -1).astype(F32).T
    gains_ref[...] = small_t[EXPERTS : EXPERTS + 8]
    fetches.made[5].wait()
    inputs = tokens_ref[...].astype(F32)
    gain = small_t[EXPERTS + 1 : EXPERTS + 2]
    normed_ref[...] = (inputs * inverse_rms(inputs) * gain).astype(BF16)
    for copy in across:
        copy.wait_recv()
    del across[:]

    cosine, sine = cos_ref[...], sin_ref[...]
    width = tokens_ref.shape[1]

    def project(at, size):
        w = w_all[:, :, :, at : at + size].reshape(width, size)
        return mm(normed_ref[...], w)

    for s in range(4):
        got = project(s * strip + wide, HEAD_SIZE)
        if s % 2 == 0:
            got = spin(got, cosine, sine)
        own_kv[:, s * HEAD_SIZE : (s + 1) * HEAD_SIZE] = got.astype(BF16)
    slot = kv_ref.at[part]
    kv_came = [
        [
            sends.start(own_kv.at[x_halves[h]], slot.at[x_halves[h]], place.x_to[d])
            for h in (d, 1 - d)
        ]
        for d in range(2)
    ]
    kv_across = [sends.start(own_kv, slot, place.partner)]
    keeps.start(own_kv, slot)
    next(behind)
    next(behind)
    onward = []
    for d, origin in enumerate((place.left, place.right)):
        kv_came[d][0].wait_recv()
        view = kv_ref.at[origin, x_halves[d]]
        onward.append(sends.start(view, view, place.x_to[d]))
    for copy in across:
        copy.wait_recv()
    keeps.start(w_all, w_out)

    def queries(s):
        got = project(s * strip, wide)
        for h in range(0, wide, HEAD_SIZE):
            head = spin(got[:, h : h + HEAD_SIZE], cosine, sine)
            query_ref[:, s * wide + h : s * wide + h + HEAD_SIZE] = head.astype(BF16)

    for s in range(4):
        queries(s)
    for d, origin in enumerate((place.left, place.right)):
        kv_came[d][1].wait_recv()
        view = kv_ref.at[origin]
        kv_across.append(sends.start(view, view, place.partner))
    for d in range(2):
        onward[d].wait_recv()
        view = kv_ref.at[place.far, x_halves[d]]
        kv_across.append(sends.start(view, view, place.partner))
    for copy in [*kv_across, *notes, *rows_came]:
        copy.wait_recv()
    for copy in keeps.made:
        copy.wait()
    sends.finish()


def begin(wq, wk, wv, wo, small, rows, note, tokens, cosine, sine, collective_id):
    height, width = wq.shape
    kv_width = wk.shape[1] + wv.shape[1]
    total = width + kv_width
    count = tokens.shape[0]
    vmem = pltpu.VMEM
    return pl.pallas_call(
        begin_kernel,
        out_shape=[
            sds((4, 4, height, total), BF16),
            sds((4, 4, *small.shape), BF16),
            sds((2, 4, height, width // 4), BF16),
            sds((2, *rows.shape), BF16),
            sds((8, *note.shape), note.dtype),
            sds((count, width), BF16),
            sds((count, width), BF16),
            sds((8, count, kv_width), BF16),
            sds((8, width), F32),
        ],
        in_specs=[ANY] * 4 + [VMEM, ANY, VMEM, ANY, VMEM, VMEM],
        out_specs=[ANY, VMEM, VMEM, ANY, ANY, VMEM, VMEM, ANY, VMEM],
        scratch_shapes=[
            vmem((height, total), BF16),
            vmem((4, 4, height, total), BF16),
            vmem((count, kv_width), BF16),
            *[vmem(a.shape, BF16) for a in (wq, wk, wv, wo, rows, tokens)],
            semaphores(6),
            semaphores(6),
            semaphores(125),
            semaphores(125),
        ],
        compiler_params=remote_params(collective_id),
    )(wq, wk, wv, wo, small, rows, note, tokens, cosine, sine)


def fill_bias(bias, start_ref, first_row):
    length, rows = bias.shape
    places = lax.broadcasted_iota(jnp.int32, (length, rows), 0)
    mine = first_row + lax.broadcasted_iota(jnp.int32, (length, rows), 1)
    keep = (places >= start_ref[...]) & (places <= mine)
    bias[...] = jnp.where(keep, 0.0, MASK_FILL)


def head_columns(head):
    return pl.ds(pl.multiple_of(head * HEAD_SIZE, HEAD_SIZE), HEAD_SIZE)


def attend_kernel(
    start_ref, q_ref, kv_ref, wo_part, rows_own, rows_near, ctx_ref, lse_ref, wo_all, rows_far,
    rows_other, bias, v_t, scores, local_sems, send_sems, recv_sems,
):
    place = Place()
    neighbours = [place.partner, *place.x_to[:2], *place.y_to, *place.z_to]
    greet(neighbours)
    length, rows = bias.shape
    fill_bias(bias, start_ref, rows * place.part)
    await_greetings(neighbours)
    sends, keeps = Sends(send_sems, recv_sems), Keeps(local_sems)
    quarter = wo_part.shape[-1]
    across = []

    def landed(view):
        across.append(sends.start(view, view, place.partner))

    def spread(p):
        cols = pl.ds(pl.multiple_of((2 * place.core + p) * quarter, 128), quarter)

        def view(where):
            return wo_all.at[:, where, :, cols] if p else wo_all.at[where, :, :, cols]

        own = view((place.y, place.z)[p])
        keeps.start(wo_part.at[p], own)
        across.append(sends.start(wo_part.at[p], own, place.partner))
        return Spread(p == 0, wo_part.at[p], view, half_span, landed)

    steps = ring_gather(place, sends, [spread(p) for p in range(2)])
    next(steps)
    next(steps)

    half = rows // 2
    x_halves = [pl.ds(h * half, half) for h in range(2)]
    far_came = [
        sends.start(rows_near.at[d, x_halves[d]], rows_far.at[x_halves[d]], place.x_to[d])
        for d in range(2)
    ]
    for i, view in enumerate((rows_own, rows_near.at[0], rows_near.at[1])):
        across.append(sends.start(view, rows_other.at[i], place.partner))
    for group in range(KEY_VALUE_HEADS):
        keys = slice(2 * group * HEAD_SIZE, (2 * group + 1) * HEAD_SIZE)
        values = slice((2 * group + 1) * HEAD_SIZE, (2 * group + 2) * HEAD_SIZE)
        v_t[...] = kv_ref[:, values].astype(F32).T.astype(BF16)

        def one_head(i, carry, base):
            head = base + i
            query = q_ref[:, head_columns(head)]
            top = None
            for at in range(0, length, BLOCK):
                span = pl.ds(at, BLOCK)
                s = mm_nt(kv_ref[span, keys], query) + bias[span]
                scores[span] = s
                here = jnp.max(s, axis=0, keepdims=True)
                top = here if top is None else jnp.maximum(top, here)
            total = jnp.zeros_like(top)
            context = jnp.zeros((HEAD_SIZE, rows), F32)
            for at in range(0, length, BLOCK):
                span = pl.ds(at, BLOCK)
                p = jnp.exp2((scores[span] - top) * (SCALE * LOG2E))
                total += jnp.sum(p, axis=0, keepdims=True)
                context += mm(v_t[:, span], p.astype(BF16))
            ctx_ref[:, head_columns(head)] = (context / total).T.astype(BF16)
            lse_ref[head] = top * (SCALE * LOG2E) + jnp.log2(total)
            return carry

        for base in (group * GROUP, group * GROUP + GROUP // 2):
            lax.fori_loop(
                0, GROUP // 2, lambda i, carry, base=base: one_head(i, carry, base), 0
            )
            if base in (GROUP // 2, QUERY_HEADS - GROUP // 2):
                next(steps)
            if base == GROUP:
                for d, copy in enumerate(far_came):
                    copy.wait_recv()
                    view = rows_far.at[x_halves[d]]
                    across.append(
                        sends.start(view, rows_other.at[3, x_halves[d]], place.partner)
                    )
    run_out(steps)
    for copy in across:
        copy.wait_recv()
    for copy in keeps.made:
        copy.wait()
    sends.finish()


def attend(start, query, kv, wo_part, rows_own, rows_near, collective_id):
    rows, width = query.shape
    length = kv.shape[0]
    height = wo_part.shape[2]
    return pl.pallas_call(
        attend_kernel,
        out_shape=[
            sds((rows, width), BF16),
            sds((QUERY_HEADS, 1, rows), F32),
            sds((4, 4, height, width), BF16),
            sds((rows, width), BF16),
            sds((4, rows, width), BF16),
        ],
        in_specs=[VMEM] * 4 + [ANY] * 2,
        out_specs=[VMEM, VMEM, ANY, ANY, ANY],
        scratch_shapes=[
            pltpu.VMEM((length, rows), F32),
            pltpu.VMEM((HEAD_SIZE, length), BF16),
            pltpu.VMEM((length, rows), F32),
            semaphores(2),
            semaphores(32),
            semaphores(32),
        ],
        compiler_params=remote_params(collective_id),
    )(start, query, kv, wo_part, rows_own, rows_near)


LOW, HIGH = 0, 1


def gelu_parts(a):
    k = (2.0 / jnp.pi) ** 0.5
    square = a * a
    t = jnp.tanh(k * a * (1.0 + 0.044715 * square))
    slope = 0.5 * (1.0 + t) + 0.5 * a * (1.0 - t * t) * k * (1.0 + 3 * 0.044715 * square)
    return 0.5 * a * (1.0 + t), slope


def experts_kernel(
    ctx_ref, tokens_ref, small_ref, gains_ref, notes_ref,
    rows_own, rows_near, rows_far, rows_other, wo_hbm, wg_hbm, wu_hbm, wd_hbm,
    middle_ref, gates_ref, gg_all, sums_ref, own_ref, back_out, w_grads,
    wo_ref, wg_ref, wu_ref, wd_ref, rows_all, returns, arrived, pair_grad, hidden, grad_pre,
    theirs, far_left, far_right, from_left, from_right, tile, tile_d, back_rows, gates_all, gg_src,
    slot_ref,
    local_sems, tile_sems, back_sems, send_sems, recv_sems,
):
    place = Place()
    part, core = place.part, place.core
    right, left, far = place.right, place.left, place.far
    to_right, to_left = place.x_to[:2]
    greet(place.others)
    sends, keeps, stores = (
        Sends(send_sems, recv_sems), Keeps(local_sems), Keeps(back_sems)
    )
    rows, width = ctx_ref.shape
    half = rows // 2
    halves = (pl.ds(0, half), pl.ds(half, half))
    ff = wg_ref.shape[1]
    capacity = arrived.shape[0] // 8

    for src, dst in ((wo_hbm, wo_ref), (wg_hbm, wg_ref), (wu_hbm, wu_ref), (wd_hbm, wd_ref)):
        keeps.start(src, dst)
    chips = [lax.rem(place.chip + d, 4) for d in (0, 3, 1, 2)]
    for u, src in enumerate((rows_own, rows_near.at[0], rows_near.at[1], rows_far)):
        keeps.start(src, returns.at[u, core])
        keeps.start(rows_other.at[u], returns.at[u, 1 - core])

    keeps.made[0].wait()
    middle = tokens_ref[...].astype(F32) + mm(ctx_ref[...], wo_ref[...])
    middle_ref[...] = middle
    normed = (middle * inverse_rms(middle) * gains_ref[:1]).astype(BF16)
    rows_all[part] = normed
    await_greetings(place.others)
    mine = rows_all.at[part]
    go = [
        [sends.start(mine.at[halves[h]], mine.at[halves[h]], way) for h in (d, 1 - d)]
        for d, way in enumerate((to_right, to_left))
    ]
    swap_own = sends.start(mine, mine, place.partner)

    ids = lax.broadcasted_iota(jnp.int32, (128, rows), 0)
    named = notes_ref[part]
    member = functools.reduce(jnp.logical_or, [ids == named[k : k + 1] for k in range(TOPK)])
    member = member.astype(F32).T
    logits = jnp.where(member > 0.0, mm(normed, small_ref[...]), MASK_FILL)
    weight = jnp.exp(logits - jnp.max(logits, axis=-1, keepdims=True)) * member
    gates = weight / jnp.sum(weight, axis=-1, keepdims=True)
    gates_ref[...] = gates.T[:EXPERTS]
    note_sends = [sends.start(gates_ref, gates_all.at[part], to) for to in place.others]
    gates_all[part] = gates_ref[...]

    chosen = jnp.concatenate(
        [
            functools.reduce(
                jnp.logical_or, [notes_ref[s, k : k + 1] == part for k in range(TOPK)]
            ).astype(F32)
            for s in range(8)
        ],
        axis=0,
    )
    earlier = lax.broadcasted_iota(jnp.int32, (rows, rows), 0) < lax.broadcasted_iota(
        jnp.int32, (rows, rows), 1
    )
    ranks = mm(chosen.astype(BF16), earlier.astype(F32).astype(BF16))
    slots_of = jnp.where(chosen > 0.0, ranks, -1.0)
    for s in range(8):
        slot_ref[s] = slots_of[s : s + 1].astype(jnp.int32)

    def pick_of(source):
        slots = lax.broadcasted_iota(jnp.int32, (capacity, rows), 0)
        return slots == slot_ref[source]

    for u in range(4):
        keeps.made[4 + 2 * u].wait()
        keeps.made[5 + 2 * u].wait()
        for c in range(2):
            pick = pick_of(2 * chips[u] + c).astype(BF16)
            got = mm(pick, returns[u, c])
            pair_grad[pl.ds((2 * u + c) * capacity, capacity)] = got.astype(BF16)
    for load in keeps.made[1:4]:
        load.wait()

    swaps, gg_sends = [], []

    def unit(u):
        at = chips[u]
        picks = [pick_of(2 * at + c) for c in range(2)]
        picks_b = [pick.astype(BF16) for pick in picks]
        spans = [pl.ds((2 * u + c) * capacity, capacity) for c in range(2)]
        both = pl.ds(2 * u * capacity, 2 * capacity)
        gate = []
        for c in range(2):
            arrived[spans[c]] = mm(picks_b[c], rows_all[2 * at + c]).astype(BF16)
            row = gates_all[2 * at + c, pl.ds(part, 1)]
            gate.append(jnp.sum(jnp.where(picks[c], row, 0.0), axis=-1, keepdims=True))
        gate = jnp.concatenate(gate, axis=0)
        x = arrived[both]
        a, b = mm(x, wg_ref[...]), mm(x, wu_ref[...])
        act, slope = gelu_parts(a)
        h = (act * b).astype(BF16)
        hidden[both] = h
        out = mm(h, wd_ref[...]).astype(BF16).astype(F32)
        up = pair_grad[both].astype(F32)
        gg = jnp.sum(up * out, axis=-1, keepdims=True)
        weighted = (gate * out).astype(BF16)
        pg = (gate * up).astype(BF16)
        pair_grad[both] = pg
        grad_h = mm_nt(pg, wd_ref[...])
        grad_a = (grad_h * b * slope).astype(BF16)
        grad_b = (grad_h * act).astype(BF16)
        grad_pre[both, :ff] = grad_a
        grad_pre[both, ff:] = grad_b
        grad_rows = (mm_nt(grad_a, wg_ref[...]) + mm_nt(grad_b, wu_ref[...])).astype(BF16)
        for c in range(2):
            returns[u, c] = mm_tn(
                picks_b[c], grad_rows[c * capacity : (c + 1) * capacity]
            ).astype(BF16)
        swaps.append(sends.start(returns.at[u, 1 - core], theirs.at[u], place.partner))
        for c in range(2):
            if u > 0:
                stores.made[2 * (u - 1) + c].wait()
            back_rows[c] = mm_tn(picks_b[c], weighted[c * capacity : (c + 1) * capacity]).astype(
                BF16
            )
            stores.start(back_rows.at[c], back_out.at[2 * at + c])
            gg_c = gg[c * capacity : (c + 1) * capacity]
            row = jnp.sum(jnp.where(picks[c], gg_c, 0.0), axis=0, keepdims=True)
            gg_src[u, c] = jnp.broadcast_to(row, (8, rows))
        if u == 0:
            gg_all[part] = gg_src[0, core]
            gg_sends.append(sends.start(gg_src.at[0, 1 - core], gg_all.at[part], place.partner))
        else:
            for c in (core, 1 - core):
                gg_sends.append(
                    sends.start(gg_src.at[u, c], gg_all.at[part], {"expert": 2 * at + c})
                )

    def joined(u):
        swaps[u].wait_recv()
        add_to(theirs.at[u], returns.at[u, core])

    swap_own.wait_recv()
    for copy in note_sends:
        copy.wait_recv()
    unit(0)
    passed = []
    for d, (origin, way) in enumerate(((left, to_right), (right, to_left))):
        go[d][0].wait_recv()
        view = rows_all.at[origin, halves[d]]
        passed.append(sends.start(view, view, way))
    far_low, far_high = passed
    go[0][1].wait_recv()
    swap_left = sends.start(rows_all.at[left], rows_all.at[left], place.partner)
    go[1][1].wait_recv()
    swap_right = sends.start(rows_all.at[right], rows_all.at[right], place.partner)
    swap_left.wait_recv()
    unit(1)
    swap_right.wait_recv()
    unit(2)
    swap_far = []
    for h, copy in enumerate((far_low, far_high)):
        copy.wait_recv()
        piece = rows_all.at[far, halves[h]]
        swap_far.append(sends.start(piece, piece, place.partner))
    joined(1)
    joined(2)
    back_right = sends.start(theirs.at[2, halves[HIGH]], from_left, to_right)
    back_left = sends.start(theirs.at[1, halves[LOW]], from_right, to_left)
    for copy in swap_far:
        copy.wait_recv()
    unit(3)
    joined(3)
    back_far_low = sends.start(theirs.at[3, halves[LOW]], far_left, to_right)
    back_far_high = sends.start(theirs.at[3, halves[HIGH]], far_right, to_left)

    tall = 4 * w_grads.shape[2] * 2 // 3
    high = tall // 4
    w_stores = Keeps(tile_sems)
    for i in range(ff // tall):
        got = mm_tn(hidden[:, i * tall : (i + 1) * tall], pair_grad[...]).astype(BF16)
        tile_d[i] = got.reshape(tile_d.shape[1:])
        w_stores.start(tile_d.at[i], w_grads.at[pl.ds(2 * i, 2), :, pl.ds(high, high // 2)])
    for i in range(width // tall):
        if i >= 2:
            w_stores.made[ff // tall + i - 2].wait()
        got = mm_tn(arrived[:, i * tall : (i + 1) * tall], grad_pre[...]).astype(BF16)
        tile[i % 2] = got.reshape(tile.shape[1:])
        w_stores.start(tile.at[i % 2], w_grads.at[i, :, pl.ds(0, high)])

    swaps[0].wait_recv()
    back_right.wait_recv()
    back_left.wait_recv()
    own_ref[...] = theirs[0].astype(F32) + returns[0, core].astype(F32)
    add_to(own_ref.at[halves[HIGH]], from_left)
    add_to(own_ref.at[halves[LOW]], from_right)
    back_far_low.wait_recv()
    sums_ref[0] = (theirs[2, halves[LOW]].astype(F32) + far_left[...].astype(F32)).astype(BF16)
    back_far_high.wait_recv()
    sums_ref[1] = (theirs[1, halves[HIGH]].astype(F32) + far_right[...].astype(F32)).astype(BF16)
    for copy in gg_sends:
        copy.wait_recv()
    for copy in [*stores.made[6:], *w_stores.made[: ff // tall], *w_stores.made[-2:]]:
        copy.wait()
    sends.finish()


def experts(ctx, tokens, small, gains, notes, rows_by, wo, wg, wu, wd, collective_id):
    rows, width = ctx.shape
    ff = wg.shape[1]
    capacity = rows * 9 // 16
    high = width // 16
    vmem = pltpu.VMEM
    return pl.pallas_call(
        experts_kernel,
        out_shape=[
            sds((rows, width), F32),
            sds((EXPERTS, rows), F32),
            sds((8, 8, rows), F32),
            sds((2, rows // 2, width), BF16),
            sds((rows, width), F32),
            sds((8, rows, width), BF16),
            sds((4, 4, high * 3 // 2, width), BF16),
        ],
        in_specs=[VMEM] * 5 + [ANY] * 8,
        out_specs=[VMEM] * 5 + [ANY] * 2,
        scratch_shapes=[
            vmem((width, width), BF16),
            vmem((width, ff), BF16),
            vmem((width, ff), BF16),
            vmem((ff, width), BF16),
            vmem((8, rows, width), BF16),
            vmem((4, 2, rows, width), BF16),
            vmem((8 * capacity, width), BF16),
            vmem((8 * capacity, width), BF16),
            vmem((8 * capacity, ff), BF16),
            vmem((8 * capacity, 2 * ff), BF16),
            vmem((4, rows, width), BF16),
            *[vmem((rows // 2, width), BF16)] * 4,
            vmem((2, 4, high, width), BF16),
            vmem((2, 2, 4, high // 2, width), BF16),
            vmem((2, rows, width), BF16),
            vmem((8, EXPERTS, rows), F32),
            vmem((4, 2, 8, rows), F32),
            vmem((8, 1, rows), jnp.int32),
            semaphores(12),
            semaphores(6),
            semaphores(8),
            semaphores(40),
            semaphores(40),
        ],
        compiler_params=remote_params(collective_id),
    )(ctx, tokens, small, gains, notes, *rows_by, wo, wg, wu, wd)


GROUPS = 3


def middle_kernel(
    middle_ref, gates_ref, gg_all, sums_ref, own_hbm, d_out_hbm, ctx_hbm, small_ref, gains_ref,
    start_ref, q_hbm, kv_hbm, lse_ref, cos_ref, sin_ref, wo_hbm, w_grads, blocks_ref,
    grad_middle_out, small_grad_ref, gq_out, gkv_out, wo_out, combined, w_done,
    own_ref, d_out_ref, ctx_ref, q_ref, kv_ref, grad_middle_ref, gq_ref, gkv_ref,
    wo_ref, g_ref, from_left, from_right, w_total_0, w_total_1, w_whole, w_far,
    bias, k_t, gkv, probs, grad_probs, second_whole, second_far, *refs,
):
    place = Place()
    core = place.core
    neighbours = [place.partner, *place.x_to, *place.y_to, *place.z_to]
    greet(neighbours)
    bufs, x_bufs = refs[:12], refs[12:17]
    wo_sem, fetch_sems, store_sems, local_sems, send_sems, recv_sems = refs[17:]
    keeps = Keeps(local_sems)
    cols = w_total_0.shape[-1]
    totals = (w_total_0, w_total_1)
    length, rows = bias.shape
    width = middle_ref.shape[1]
    quarter = width // 4

    def part_of(ref, p, w):
        return ref.at[:, w] if p else ref.at[w]

    loads = {}
    for k in range(4):
        for p in range(2):
            me, (right, left, far), _ = place.ring(p == 0)
            w = (far, right, left, me)[k]
            src = part_of(w_grads, p, w).at[:, :, pl.ds(p * cols, cols)]
            loads[k, p] = keeps.start(src, part_of(totals[p], p, w))
    wo_load = pltpu.make_async_copy(wo_hbm, wo_ref, wo_sem)
    wo_load.start()
    fetches, stores = Keeps(fetch_sems), Keeps(store_sems)
    own_fetch, d_out_fetch, ctx_fetch, q_fetch, kv_fetch = [
        fetches.start(src, dst)
        for src, dst in (
            (own_hbm, own_ref), (d_out_hbm, d_out_ref), (ctx_hbm, ctx_ref), (q_hbm, q_ref),
            (kv_hbm, kv_ref),
        )
    ]
    await_greetings(neighbours)
    sends = Sends(send_sems, recv_sems)
    came = [
        sends.start(sums_ref.at[i], dst, place.x_to[i])
        for i, dst in enumerate((from_left, from_right))
    ]

    def first_half(p):
        def view(w, h):
            span = pl.ds(2 * h, 2)
            return totals[p].at[span, w] if p else totals[p].at[w, span]

        return view

    def expert_steps():
        rings = [Ring(p == 0, first_half(p), w_whole.at[p], w_far.at[p]) for p in range(2)]
        yield from ring_sum(place, sends, rings, lambda k, i, w: loads[k, i].wait())
        half = cols // 2

        def second_half(p):
            def view(w, h):
                at = pl.ds(h * half, half)
                return totals[p].at[w, place.z, :, at] if p else totals[p].at[place.y, w, :, at]

            return view

        rings = [
            Ring(p == 1, second_half(p), second_whole.at[p], second_far.at[p]) for p in range(2)
        ]
        yield from ring_sum(place, sends, rings)
        spreads = []
        for p in range(2):
            me = place.ring(p == 1)[0]
            w_done[p, me] = totals[p][place.y, place.z]

            view = lambda w, p=p: w_done.at[p, w]
            spreads.append(Spread(p == 1, w_done.at[p, me], view, half_columns))
        yield from ring_gather(place, sends, spreads)

    def columns(c, p):
        return pl.ds(pl.multiple_of((2 * c + p) * quarter, 128), quarter)

    def theirs_of(p):
        at = columns(1 - core, p)
        if p == 0:
            return lambda w: wo_ref.at[w, :, :, at]
        return lambda w: wo_ref.at[:, w, :, at]

    strips = [
        Strip(
            p == 0, wo_ref.at[:, :, :, columns(core, p)], bufs[6 * p : 6 * p + 6],
            None, theirs_of(p),
        )
        for p in range(2)
    ]
    expert = expert_steps()
    dense = dp_sum(place, sends, strips, ())
    rest = x_sum(place, sends, blocks_ref, combined, *x_bufs)
    next(expert)
    next(rest)

    grad_gates = jnp.concatenate([gg_all[e, :1] for e in range(EXPERTS)], axis=0)
    gates_t = gates_ref[...]
    products = gates_t * grad_gates
    grad_logits = products - gates_t * jnp.sum(products, axis=0, keepdims=True)
    grad_logits = jnp.concatenate(
        [grad_logits, jnp.zeros((128 - EXPERTS, rows), F32)], axis=0
    ).T.astype(BF16)
    own_fetch.wait()
    total = own_ref[...] + mm_nt(grad_logits, small_ref[...])
    middle, gain = middle_ref[...], gains_ref[:1]
    inverse = inverse_rms(middle)
    scaled = middle * inverse
    small_grad = mm_tn((scaled * gain).astype(BF16), grad_logits)
    fill_bias(bias, start_ref, rows * place.part)
    for copy in came:
        copy.wait_recv()
    total += jnp.concatenate([from_left[...], from_right[...]], axis=0).astype(F32)
    grad_gain = jnp.sum(total * scaled, axis=0, keepdims=True)
    lanes = lax.broadcasted_iota(jnp.int32, (width, 128), 1)
    small_grad += jnp.where(lanes == EXPERTS, as_column(grad_gain, 128), 0.0)
    small_grad_ref[...] = small_grad.astype(BF16)
    weighted = total * gain
    inner = jnp.mean(weighted * scaled, axis=-1, keepdims=True)
    d_out_fetch.wait()
    grad_middle = d_out_ref[...].astype(F32) + inverse * (weighted - scaled * inner)
    grad_middle_ref[...] = grad_middle
    stores.start(grad_middle_ref, grad_middle_out)
    grad_attn = grad_middle.astype(BF16)
    wo_load.wait()
    g_ref[...] = mm_nt(grad_attn, wo_ref[...].reshape(width, width)).astype(BF16)
    next(rest)
    next(expert)
    ctx_fetch.wait()
    tall = width // 4
    for i in range(4):
        got = mm_tn(ctx_ref[:, i * tall : (i + 1) * tall], grad_attn).astype(BF16)
        wo_ref[i] = got.reshape(wo_ref.shape[1:])
    next(dense)

    q_fetch.wait()
    kv_fetch.wait()
    when = {2: (dense,), 4: (rest,), 6: (dense, expert), 8: (dense,), 10: (dense, expert)}
    for group in range(KEY_VALUE_HEADS):
        keys = slice(2 * group * HEAD_SIZE, (2 * group + 1) * HEAD_SIZE)
        values = slice((2 * group + 1) * HEAD_SIZE, (2 * group + 2) * HEAD_SIZE)
        k_t[...] = kv_ref[:, keys].astype(F32).T.astype(BF16)
        gkv[...] = jnp.zeros_like(gkv)

        def one_head(i, carry, base):
            head = base + i
            query, grad = q_ref[:, head_columns(head)], g_ref[:, head_columns(head)]
            lse = lse_ref[head]
            inner = jnp.zeros_like(lse)
            for at in range(0, length, BLOCK):
                span = pl.ds(at, BLOCK)
                s = mm_nt(kv_ref[span, keys], query) + bias[span]
                p = jnp.exp2(s * (SCALE * LOG2E) - lse)
                gp = mm_nt(kv_ref[span, values], grad)
                inner += jnp.sum(p * gp, axis=0, keepdims=True)
                probs[span] = p
                grad_probs[span] = gp
                gkv[span, HEAD_SIZE:] += mm(p.astype(BF16), grad)
            gq = jnp.zeros((HEAD_SIZE, rows), F32)
            for at in range(0, length, BLOCK):
                span = pl.ds(at, BLOCK)
                gs = (probs[span] * (grad_probs[span] - inner)).astype(BF16)
                gkv[span, :HEAD_SIZE] += mm(gs, query)
                gq += mm(k_t[:, span], gs)
            turned = spin(gq.T * SCALE, cos_ref[...], -sin_ref[...])
            gq_ref[:, head_columns(head)] = turned.astype(BF16)
            return carry

        for base in range(group * GROUP, (group + 1) * GROUP, 2):
            lax.fori_loop(0, 2, lambda i, carry, base=base: one_head(i, carry, base), 0)
            for steps in when.get(base + 2, ()):
                next(steps)
        gkv_ref[:, keys] = (gkv[:, :HEAD_SIZE] * SCALE).astype(BF16)
        gkv_ref[:, values] = gkv[:, HEAD_SIZE:].astype(BF16)
    stores.start(gq_ref, gq_out)
    stores.start(gkv_ref, gkv_out)
    run_out(expert, dense, rest)
    for p, s in enumerate(strips):
        wo_out[:, columns(core, p)] = s.result[...]
        wo_out[:, columns(1 - core, p)] = s.near[3]
    for copy in stores.made:
        copy.wait()
    sends.finish()


def between(
    middle, gates, gg, sums, own, d_out, ctx, small, gain, start, query, kv, lse, cosine, sine,
    wo, w_grads, back_out, collective_id,
):
    rows, width = query.shape
    length = kv.shape[0]
    height, quarter = width // 16, width // 4
    high, cols = w_grads.shape[2], width // 2
    vmem = pltpu.VMEM
    return pl.pallas_call(
        middle_kernel,
        out_shape=[
            sds((rows, width), F32),
            sds((width, 128), BF16),
            sds((rows, width), BF16),
            sds(kv.shape, BF16),
            sds((height, width), BF16),
            sds((rows, width), F32),
            sds((2, 4, high, cols), BF16),
        ],
        in_specs=[VMEM] * 4 + [ANY] * 3 + [VMEM] * 3 + [ANY] * 2 + [VMEM] * 3 + [ANY] * 3,
        out_specs=[ANY, VMEM, ANY, ANY, VMEM, VMEM, VMEM],
        scratch_shapes=[
            vmem((rows, width), F32),
            *[vmem((rows, width), BF16)] * 3,
            vmem(kv.shape, BF16),
            vmem((rows, width), F32),
            vmem((rows, width), BF16),
            vmem(kv.shape, BF16),
            vmem((4, 4, height, width), BF16),
            vmem((rows, width), BF16),
            vmem((rows // 2, width), BF16),
            vmem((rows // 2, width), BF16),
            vmem((4, 4, high, cols), BF16),
            vmem((4, 4, high, cols), BF16),
            vmem((2, 2, 2, 2, high, cols), BF16),
            vmem((2, 2, 2, high, cols), BF16),
            vmem((length, rows), F32),
            vmem((HEAD_SIZE, length), BF16),
            vmem((length, 2 * HEAD_SIZE), F32),
            vmem((length, rows), F32),
            vmem((length, rows), F32),
            vmem((2, 2, 2, high, cols // 2), BF16),
            vmem((2, 2, high, cols // 2), BF16),
            *strip_buffers(height, quarter),
            *strip_buffers(height, quarter),
            *x_buffers(rows, width),
            pltpu.SemaphoreType.DMA,
            semaphores(5),
            semaphores(3),
            semaphores(8),
            semaphores(100),
            semaphores(100),
        ],
        compiler_params=remote_params(collective_id),
    )(
        middle, gates, gg, sums, own, d_out, ctx, small, gain, start, query, kv, lse, cosine, sine,
        wo, w_grads, back_out,
    )


def last_kernel(
    kv_terms, gq_ref, normed_ref, tokens_ref, gains_ref, cos_ref, sin_ref,
    small_ref, w_done, w_hbm,
    grad_inputs_ref, strips_out, small_out, w_sums,
    grads, small_total, w_ref, normed_t, kv_sum, *refs,
):
    place = Place()
    core = place.core
    neighbours = [place.partner, *place.x_to, *place.y_to, *place.z_to]
    greet(neighbours)
    bufs, x_bufs = refs[:30], refs[30:35]
    w_sem, local_sems, send_sems, recv_sems = refs[35:]
    load = pltpu.make_async_copy(w_hbm, w_ref, w_sem)
    load.start()
    await_greetings(neighbours)
    sends, keeps = Sends(send_sems, recv_sems), Keeps(local_sems)
    kv_steps = x_sum(place, sends, kv_terms, kv_sum, *x_bufs)
    next(kv_steps)

    def place_of(p, w, at, size):
        cols = pl.ds(p * w_done.shape[-1] + at, size)
        return w_sums.at[:, w, :, cols] if p else w_sums.at[w, :, :, cols]

    def spread(p, i):
        size = w_done.shape[-1] // GROUPS
        source = w_done.at[p, :, :, pl.ds(i * size, size)]
        return Spread(p == 0, source, lambda w: place_of(p, w, i * size, size), half_span)

    for p in range(2):
        keeps.start(w_done.at[p], place_of(p, place.ring(p == 0)[0], 0, w_done.shape[-1]))
    e0, e1, e2 = [
        ring_gather(place, sends, [spread(p, i) for p in range(2)]) for i in range(GROUPS)
    ]
    for steps in (e0, e0, e1):
        next(steps)
    strip = grads.shape[-1]
    wide = strip - HEAD_SIZE
    rows, width = normed_ref.shape
    height = grads.shape[3]

    def put(s, cols, right_side):
        got = mm(normed_t[...], right_side).astype(BF16)
        grads[s, :, :, :, cols] = got.reshape(4, 4, height, right_side.shape[1])

    def shared(at, size, bufs):
        cols = pl.ds(at, size)

        def theirs_of(p):
            s = 2 * (1 - core) + p
            if p == 0:
                return lambda w: grads.at[s, w, :, :, cols]
            return lambda w: grads.at[s, :, w, :, cols]

        return [
            Strip(
                p == 0, grads.at[2 * core + p, :, :, :, cols], bufs[6 * p : 6 * p + 6],
                None, theirs_of(p),
            )
            for p in range(2)
        ]

    wide_strips = shared(0, wide, bufs[:12])
    narrow_strips = shared(wide, HEAD_SIZE, bufs[12:24])
    wide_steps = dp_sum(place, sends, wide_strips, ())
    narrow_steps = dp_sum(place, sends, narrow_strips, ())
    normed_t[...] = normed_ref[...].astype(F32).T.astype(BF16)
    for s in range(4):
        put(s, pl.ds(0, wide), gq_ref[:, s * wide : (s + 1) * wide])
    next(wide_steps)
    next(kv_steps)
    next(e0)
    load.wait()
    grad_normed = None
    for s in range(4):
        at = s * strip
        term = mm_nt(gq_ref[:, s * wide : (s + 1) * wide], w_ref[:, at : at + wide])
        grad_normed = term if grad_normed is None else grad_normed + term
    next(wide_steps)
    next(kv_steps)
    run_out(kv_steps)
    cosine, sine = cos_ref[...], sin_ref[...]
    for s in range(4):
        got = kv_sum[:, s * HEAD_SIZE : (s + 1) * HEAD_SIZE]
        if s % 2 == 0:
            got = spin(got, cosine, -sine)
        got = got.astype(BF16)
        put(s, pl.ds(wide, HEAD_SIZE), got)
        grad_normed += mm_nt(got, w_ref[:, s * strip + wide : (s + 1) * strip])
    for steps in (narrow_steps, wide_steps, narrow_steps):
        next(steps)

    grad_inputs, grad_gain = rms_back(tokens_ref[...].astype(F32), gains_ref[1:2], grad_normed)
    grad_inputs_ref[...] = grad_inputs
    lanes = lax.broadcasted_iota(jnp.int32, (width, 128), 1)
    small = jnp.where(
        lanes == EXPERTS + 1, as_column(grad_gain, 128), small_ref[...].astype(F32)
    )
    small_total[...] = small.astype(BF16).reshape(small_total.shape)
    small_strip = Strip(True, small_total, bufs[24:])
    small_steps = dp_sum(place, sends, [small_strip], ())
    for steps in (
        small_steps, small_steps, wide_steps, narrow_steps, small_steps,
        wide_steps, narrow_steps, small_steps, wide_steps, e1, narrow_steps, e2, small_steps, e2,
        wide_steps, narrow_steps, e1,
    ):
        next(steps)
    run_out(wide_steps, narrow_steps, small_steps, e0, e1, e2)
    small_out[...] = small_strip.result[...].astype(F32) + small_strip.near[3].astype(F32)
    for p in range(2):
        for at, size, s in ((0, wide, wide_strips[p]), (wide, HEAD_SIZE, narrow_strips[p])):
            for c, got in ((core, s.result), (1 - core, s.near.at[3])):
                begin_at = pl.multiple_of((2 * c + p) * strip + at, 128)
                strips_out[:, pl.ds(begin_at, size)] = got[...]
    for copy in keeps.made:
        copy.wait()
    sends.finish()


def last(
    kv_terms, grad_query, normed, tokens, gain, cosine, sine, small, w_done, w, collective_id
):
    rows, width = normed.shape
    total = w.shape[1]
    height, strip = width // 16, total // 4
    kv_width = total - width
    vmem = pltpu.VMEM
    return pl.pallas_call(
        last_kernel,
        out_shape=[
            sds((rows, width), F32),
            sds((height, total), BF16),
            sds((height, 128), F32),
            sds((4, 4, w_done.shape[2], width), BF16),
        ],
        in_specs=[ANY] + [VMEM] * 8 + [ANY],
        out_specs=[VMEM] * 3 + [ANY],
        scratch_shapes=[
            vmem((4, 4, 4, height, strip), BF16),
            vmem((4, 4, height, 128), BF16),
            vmem((width, total), BF16),
            vmem((width, rows), BF16),
            vmem((rows, kv_width), F32),
            *strip_buffers(height, strip - HEAD_SIZE),
            *strip_buffers(height, strip - HEAD_SIZE),
            *strip_buffers(height, HEAD_SIZE),
            *strip_buffers(height, HEAD_SIZE),
            *strip_buffers(height, 128, shared=False),
            *x_buffers(rows, kv_width),
            pltpu.SemaphoreType.DMA,
            semaphores(2),
            semaphores(160),
            semaphores(160),
        ],
        compiler_params=remote_params(collective_id),
    )(kv_terms, grad_query, normed, tokens, gain, cosine, sine, small, w_done, w)


def finish_kernel(
    sums_ref, grad_middle_ref, grad_inputs_ref, middle_ref, combined_ref, strips_ref, wo_ref,
    small_ref, g_out, u_out, d_out, tokens_out, mixed_out, wq_out, wk_out, wv_out, wo_out,
    small_out,
):
    owners, high, width = sums_ref.shape
    ff = width // 2
    gu = high * 2 // 3
    g_out[...] = sums_ref[:, :gu, :ff].astype(F32).reshape(owners * gu, ff)
    u_out[...] = sums_ref[:, :gu, ff:].astype(F32).reshape(owners * gu, ff)
    d_out[...] = sums_ref[:, gu:].astype(F32).reshape(owners * (high - gu), width)
    tokens_out[...] = grad_middle_ref[...] + grad_inputs_ref[...]
    mixed_out[...] = (middle_ref[...] + combined_ref[...]).astype(BF16)

    @pl.when(pl.program_id(0) == 0)
    def _():
        strip = strips_ref.shape[1] // 4
        wide = strip - HEAD_SIZE
        for s in range(4):
            at = s * strip
            wq_out[:, s * wide : (s + 1) * wide] = strips_ref[:, at : at + wide].astype(F32)
            other = (wk_out, wv_out)[s % 2]
            begin_at = s // 2 * HEAD_SIZE
            got = strips_ref[:, at + wide : at + strip].astype(F32)
            other[:, begin_at : begin_at + HEAD_SIZE] = got
        wo_out[...] = wo_ref[...].astype(F32)
        small_out[...] = small_ref[...].T[: EXPERTS + 8]


def finish(sums, grad_middle, grad_inputs, middle, combined, strips, wo, small):
    owners, high, width = sums.shape
    rows = middle.shape[0]
    height, total = strips.shape
    kv_half = (total - width) // 2
    ff = width // 2
    gu, d = high * 2 // 3, high // 3
    steps = 8
    each, part = owners // steps, rows // steps
    by_step = lambda a, b: pl.BlockSpec((a, b), lambda i: (i, 0))
    whole = lambda a, b: pl.BlockSpec((a, b), lambda i: (0, 0))
    return pl.pallas_call(
        finish_kernel,
        grid=(steps,),
        out_shape=[
            sds((owners * gu, ff), F32),
            sds((owners * gu, ff), F32),
            sds((owners * d, width), F32),
            sds((rows, width), F32),
            sds((rows, width), BF16),
            sds((height, width), F32),
            sds((height, kv_half), F32),
            sds((height, kv_half), F32),
            sds((height, width), F32),
            sds((EXPERTS + 8, height), F32),
        ],
        in_specs=[pl.BlockSpec((each, high, width), lambda i: (i, 0, 0))]
        + [by_step(part, width)] * 4
        + [whole(height, total), whole(height, width), whole(height, 128)],
        out_specs=[
            by_step(each * gu, ff),
            by_step(each * gu, ff),
            by_step(each * d, width),
            by_step(part, width),
            by_step(part, width),
            whole(height, width),
            whole(height, kv_half),
            whole(height, kv_half),
            whole(height, width),
            whole(EXPERTS + 8, height),
        ],
        compiler_params=pltpu.CompilerParams(vmem_limit_bytes=63 * MIB),
        cost_estimate=pl.CostEstimate(flops=0, bytes_accessed=30 * MIB, transcendentals=0),
    )(sums, grad_middle, grad_inputs, middle, combined, strips, wo, small)


def on_device(
    tokens,
    d_out,
    gain_in,
    w_query,
    key_projection_weight,
    value_projection_weight,
    w_out,
    gain_mid,
    w_router,
    w_gate,
    w_up,
    w_down,
    routes,
    segments,
):
    rows, width = tokens.shape
    length = segments.shape[1]
    part = lax.axis_index("expert")
    seg_row = segments[0]
    offset = part * rows
    my_seg = lax.dynamic_slice_in_dim(seg_row, offset, rows, 0)
    start = jnp.sum((seg_row[None, :] < my_seg[:, None]).astype(jnp.int32), axis=1)
    angles = angles_for(offset + jnp.arange(rows, dtype=jnp.int32) - start)
    cosine, sine = jnp.cos(angles), jnp.sin(angles)
    cosine = jnp.concatenate([cosine, cosine], axis=1)
    sine = jnp.concatenate([-sine, sine], axis=1)
    start = start[None, :]

    small = jnp.concatenate([w_router, gain_mid[:, None], gain_in[:, None]], axis=1)
    small = jnp.pad(small, ((0, 0), (0, 128 - small.shape[1])))
    note = jnp.pad(routes.T, ((0, 8 - TOPK), (0, 0)))
    w_strips, small, wo_part, rows_near, notes, normed, query, kv_all, gains = begin(
        w_query, key_projection_weight, value_projection_weight, w_out, small, d_out, note,
        tokens, cosine, sine, 1,
    )
    w_strips = w_strips.reshape(width, -1)
    small = small.reshape(width, -1)
    kv_all = kv_all.reshape(length, -1)
    context, lse, wo, rows_far, rows_other = attend(
        start, query, kv_all, wo_part, d_out, rows_near, 2
    )

    middle, gates, gg, sums, own, back_out, w_grads = experts(
        context, tokens, small, gains, notes, (d_out, rows_near, rows_far, rows_other),
        wo.reshape(width, width), w_gate[0], w_up[0], w_down[0], 3,
    )
    grad_middle, small_grads, grad_query, kv_terms, wo_sum, combined, w_done = between(
        middle, gates, gg, sums, own, d_out, context, small, gains, start, query, kv_all,
        lse, cosine, sine, wo, w_grads, back_out, 4,
    )
    grad_inputs, strips_sum, small_sum, w_sums = last(
        kv_terms.reshape(8, rows, -1), grad_query, normed, tokens, gains, cosine, sine,
        small_grads, w_done, w_strips, 5,
    )
    g_wg, g_wu, g_wd, grad_tokens, mixed, g_wq, g_wk, g_wv, g_wo, g_small = finish(
        w_sums.reshape(16, -1, width), grad_middle, grad_inputs, middle, combined, strips_sum,
        wo_sum, small_sum,
    )
    return (
        mixed,
        grad_tokens,
        g_small[EXPERTS + 1],
        g_wq,
        g_wk,
        g_wv,
        g_wo,
        g_small[EXPERTS],
        g_small[:EXPERTS].T,
        g_wg[None],
        g_wu[None],
        g_wd[None],
    )


def solution(mesh):
    whole = P(("dp", "expert"), None)
    over_dp, by_dp, over_expert = P("dp"), P("dp", None), P("expert", None, None)
    return jax.shard_map(
        on_device,
        mesh=mesh,
        in_specs=(whole, whole, over_dp, by_dp, by_dp, by_dp, by_dp, over_dp, by_dp)
        + (over_expert,) * 3
        + (whole, by_dp),
        out_specs=(whole, whole, over_dp, by_dp, by_dp, by_dp, by_dp, over_dp, by_dp)
        + (over_expert,) * 3,
        check_vma=False,
    )
```

```python
import functools

import jax
import jax.numpy as jnp
from jax import lax
from jax.experimental import pallas as pl
from jax.experimental.pallas import tpu as pltpu
from jax.sharding import PartitionSpec as P

QUERY_HEADS = 12
KEY_VALUE_HEADS = 2
HEAD_SIZE = 128
TOPK = 4
EXPERTS = 8
GROUP = QUERY_HEADS // KEY_VALUE_HEADS
SCALE = HEAD_SIZE**-0.5
LOG2E = 1.4426950408889634
BLOCK = 512

EPSILON = 1e-06
ROPE_BASE = 1000000.0
MASK_FILL = -1e30
F32 = jnp.float32
BF16 = jnp.bfloat16

MESH = pl.DeviceIdType.MESH
ANY = pl.BlockSpec(memory_space=pl.ANY)
VMEM = pl.BlockSpec(memory_space=pltpu.VMEM)
MIB = 2**20


def dot(a, b, dims):
    return lax.dot_general(a, b, (dims, ((), ())), preferred_element_type=F32)


def mm(a, b):
    return dot(a, b, ((1,), (0,)))


def mm_nt(a, b):
    return dot(a, b, ((1,), (1,)))


def mm_tn(a, b):
    return dot(a, b, ((0,), (0,)))


def sds(shape, dtype):
    return jax.ShapeDtypeStruct(tuple(shape), dtype)


def remote_params(collective_id):
    return pltpu.CompilerParams(
        collective_id=collective_id, has_side_effects=True, vmem_limit_bytes=63 * MIB
    )


def semaphores(count):
    return pltpu.SemaphoreType.DMA((count,))


def inverse_rms(rows):
    return lax.rsqrt(jnp.mean(rows * rows, axis=-1, keepdims=True) + EPSILON)


def rms_back(rows, gain, grad):
    inverse = inverse_rms(rows)
    scaled = rows * inverse
    weighted = grad * gain
    inner = jnp.mean(weighted * scaled, axis=-1, keepdims=True)
    return inverse * (weighted - scaled * inner), jnp.sum(grad * scaled, axis=0, keepdims=True)


def as_column(row, lanes):
    return jnp.broadcast_to(row, (lanes, row.shape[1])).T


def angles_for(positions):
    half_width = HEAD_SIZE // 2
    freqs = ROPE_BASE ** (-2.0 * jnp.arange(half_width, dtype=F32) / HEAD_SIZE)
    return positions.astype(F32)[:, None] * freqs[None, :]


def spin(z, cosine, sine):
    return z * cosine + pltpu.roll(z, HEAD_SIZE // 2, 1) * sine


class Sends:
    def __init__(self, send_sems, recv_sems):
        self.send_sems, self.recv_sems, self.made = send_sems, recv_sems, []

    def start(self, src, dst, to):
        at = len(self.made)
        copy = pltpu.make_async_remote_copy(
            src_ref=src,
            dst_ref=dst,
            send_sem=self.send_sems.at[at],
            recv_sem=self.recv_sems.at[at],
            device_id=to,
            device_id_type=MESH,
        )
        copy.start()
        self.made.append(copy)
        return copy

    def finish(self):
        for copy in self.made:
            copy.wait_send()


class Keeps:
    def __init__(self, sems):
        self.sems, self.made = sems, []

    def start(self, src, dst):
        copy = pltpu.make_async_copy(src, dst, self.sems.at[len(self.made)])
        copy.start()
        self.made.append(copy)
        return copy


class Place:
    def __init__(self):
        self.part = lax.axis_index("expert")
        self.core = self.part % 2
        self.chip = self.part // 2
        at = lambda d: lax.rem(self.chip + d, 4) * 2 + self.core
        self.right, self.left, self.far = at(1), at(3), at(2)
        to = lambda i: {"expert": i}
        self.partner = to(2 * self.chip + (1 - self.core))
        self.x_to = [to(self.right), to(self.left), to(self.far)]
        self.others = [to(lax.rem(self.part + d, 8)) for d in range(1, 8)]
        place = lax.axis_index("dp")
        self.y, self.z = place // 4, place % 4
        ring = lambda v: [lax.rem(v + d, 4) for d in (1, 3, 2)]
        self.y_ring, self.z_ring = ring(self.y), ring(self.z)
        self.y_to = [{"dp": v * 4 + self.z} for v in self.y_ring[:2]]
        self.z_to = [{"dp": self.y * 4 + v} for v in self.z_ring[:2]]

    def ring(self, along_y):
        if along_y:
            return self.y, self.y_ring, self.y_to
        return self.z, self.z_ring, self.z_to


def greet(others):
    barrier = pltpu.get_barrier_semaphore()
    for other in others:
        pl.semaphore_signal(barrier, inc=1, device_id=other, device_id_type=MESH)


def await_greetings(others):
    pl.semaphore_wait(pltpu.get_barrier_semaphore(), len(others))


def add_to(ref, *others):
    got = ref[...].astype(F32)
    for other in others:
        got += other[...].astype(F32)
    ref[...] = got.astype(ref.dtype)


def run_out(*steps):
    steps = list(steps)
    while steps:
        for s in list(steps):
            if next(s, "done") == "done":
                steps.remove(s)


def x_sum(place, sends, blocks_ref, out_ref, mine, total, from_left, from_right, sems):
    rows = out_ref.shape[0]
    half = rows // 2
    low, high = pl.ds(0, half), pl.ds(half, half)
    to_right, to_left = place.x_to[:2]
    flip = 1 - 2 * place.core
    keeps = Keeps(sems)
    swaps, loads = [], []
    for k, dest in enumerate((place.far, place.right, place.left, place.part)):
        swaps.append(sends.start(blocks_ref.at[dest + flip], total.at[k], place.partner))
        loads.append(keeps.start(blocks_ref.at[dest], mine.at[k]))

    def add_up(k):
        loads[k].wait()
        swaps[k].wait_recv()
        add_to(total.at[k], mine.at[k])

    yield
    add_up(0)
    far_low = sends.start(total.at[0, low], from_left.at[0], to_right)
    far_high = sends.start(total.at[0, high], from_right.at[0], to_left)
    add_up(1)
    right_high = sends.start(total.at[1, high], from_left.at[2], to_right)
    add_up(2)
    left_low = sends.start(total.at[2, low], from_right.at[2], to_left)
    yield
    far_low.wait_recv()
    add_to(total.at[1, low], from_left.at[0])
    right_low = sends.start(total.at[1, low], from_left.at[1], to_right)
    far_high.wait_recv()
    add_to(total.at[2, high], from_right.at[0])
    left_high = sends.start(total.at[2, high], from_right.at[1], to_left)
    yield
    loads[3].wait()
    swaps[3].wait_recv()
    out_ref[...] = mine[3].astype(F32) + total[3].astype(F32)
    right_high.wait_recv()
    left_low.wait_recv()
    right_low.wait_recv()
    left_high.wait_recv()
    add_to(out_ref.at[low], from_left.at[1], from_right.at[2])
    add_to(out_ref.at[high], from_left.at[2], from_right.at[1])
    yield


def x_buffers(rows, columns):
    return [
        pltpu.VMEM((4, rows, columns), BF16),
        pltpu.VMEM((4, rows, columns), BF16),
        pltpu.VMEM((3, rows // 2, columns), BF16),
        pltpu.VMEM((3, rows // 2, columns), BF16),
        semaphores(4),
    ]


class Ring:
    def __init__(self, along_y, view, whole, farther):
        self.along_y, self.view, self.whole, self.farther = along_y, view, whole, farther


def ring_sum(place, sends, rings, ready=lambda *_: None):
    going = []
    for i, r in enumerate(rings):
        _, (right, left, far), to = place.ring(r.along_y)
        ready(0, i, far)
        going.append([sends.start(r.view(far, h), r.farther.at[h], to[h]) for h in range(2)])
    for i, r in enumerate(rings):
        _, (right, left, far), to = place.ring(r.along_y)
        ready(1, i, right)
        ready(2, i, left)
        going[i].append(sends.start(r.view(right, 1), r.whole.at[0, 1], to[0]))
        going[i].append(sends.start(r.view(left, 0), r.whole.at[1, 0], to[1]))
    yield
    for i, r in enumerate(rings):
        _, (right, left, far), to = place.ring(r.along_y)
        for h, w in enumerate((right, left)):
            going[i][h].wait_recv()
            add_to(r.view(w, h), r.farther.at[h])
            going[i].append(sends.start(r.view(w, h), r.whole.at[h, h], to[h]))
    yield
    for i, r in enumerate(rings):
        me, _, _ = place.ring(r.along_y)
        ready(3, i, me)
        for copy in going[i][2:]:
            copy.wait_recv()
        for h in range(2):
            add_to(r.view(me, h), r.whole.at[0, h], r.whole.at[1, h])


class Spread:
    def __init__(self, along_y, source, view, half, landed=lambda _: None):
        self.along_y, self.source, self.view = along_y, source, view
        self.half, self.landed = half, landed


def ring_gather(place, sends, spreads):
    came, onward = [], []

    def send(s, h, to):
        me = place.ring(s.along_y)[0]
        return sends.start(s.half(s.source, h), s.half(s.view(me), h), to)

    for s in spreads:
        to = place.ring(s.along_y)[2]
        came.append([[send(s, d, to[d])] for d in range(2)])
    yield
    for s, copies in zip(spreads, came):
        to = place.ring(s.along_y)[2]
        for d in range(2):
            copies[d].append(send(s, 1 - d, to[d]))
    yield
    for s, copies in zip(spreads, came):
        _, (right, left, _), to = place.ring(s.along_y)
        onward.append([])
        for d, origin in enumerate((left, right)):
            copies[d][0].wait_recv()
            view = s.half(s.view(origin), d)
            onward[-1].append(sends.start(view, view, to[d]))
    yield
    for s, copies in zip(spreads, came):
        _, (right, left, _), _ = place.ring(s.along_y)
        for d, origin in enumerate((left, right)):
            copies[d][1].wait_recv()
            s.landed(s.view(origin))
    for s, copies in zip(spreads, onward):
        far = place.ring(s.along_y)[1][2]
        for d in range(2):
            copies[d].wait_recv()
            s.landed(s.half(s.view(far), d))
    yield


def half_span(share, h):
    return share.at[pl.ds(2 * h, 2)]


def half_rows(share, h):
    half = share.shape[0] // 2
    return share.at[pl.ds(h * half, half)]


def half_columns(share, h):
    half = share.shape[-1] // 2
    return share.at[:, pl.ds(h * half, half)]


class Strip:
    def __init__(self, y_first, total, bufs, own=None, other=None):
        self.y_first, self.total, self.own, self.other = y_first, total, own, other
        self.theirs, self.big, self.far, self.mid, self.midfar, self.near = bufs

    def block(self, ref, w):
        return ref.at[w] if self.y_first else ref.at[:, w]


def strip_buffers(rows, columns, shared=True):
    return [
        pltpu.VMEM((4, 4, rows, columns) if shared else (1, 1, rows, columns), BF16),
        pltpu.VMEM((2, 2, 2, rows, columns), BF16),
        pltpu.VMEM((2, 2, rows, columns), BF16),
        pltpu.VMEM((2, 2, rows // 2, columns), BF16),
        pltpu.VMEM((2, rows // 2, columns), BF16),
        pltpu.VMEM((4, rows, columns), BF16),
    ]


def dp_sum(place, sends, strips, sems):
    y, z = place.y, place.z
    keeps = Keeps(sems)
    swaps, loads = {}, {}
    for k in range(4):
        for i, s in enumerate(strips):
            me, (right, left, far), _ = place.ring(s.y_first)
            w = (far, right, left, me)[k]
            if s.other is not None:
                swaps[k, i] = sends.start(s.other(w), s.block(s.theirs, w), place.partner)
            if s.own is not None:
                loads[k, i] = keeps.start(s.own(w), s.block(s.total, w))
    yield

    def joined(k, i, s, w):
        if s.own is not None:
            loads[k, i].wait()
        if s.other is not None:
            swaps[k, i].wait_recv()
            add_to(s.block(s.total, w), s.block(s.theirs, w))

    def big(s, w, h):
        span = pl.ds(2 * h, 2)
        return s.total.at[w, span] if s.y_first else s.total.at[span, w]

    def small(s, w, h):
        half = s.total.shape[2] // 2
        at = pl.ds(h * half, half)
        return s.total.at[y, w, at] if s.y_first else s.total.at[w, z, at]

    def rings(first):
        view = big if first else small
        return [
            Ring(
                s.y_first == first,
                functools.partial(view, s),
                s.big if first else s.mid,
                s.far if first else s.midfar,
            )
            for s in strips
        ]

    yield from ring_sum(place, sends, rings(True), lambda k, i, w: joined(k, i, strips[i], w))
    yield from ring_sum(place, sends, rings(False))

    shares, back = [], []
    for s in strips:
        shares.append(
            [sends.start(s.total.at[y, z], s.near.at[i], place.x_to[i]) for i in range(3)]
        )
    yield
    for s, share in zip(strips, shares):
        for copy in share:
            copy.wait_recv()
        got = s.total[y, z].astype(F32)
        for i in range(3):
            got += s.near[i].astype(F32)
        s.result = s.theirs.at[y, z] if s.other is not None else s.theirs.at[0, 0]
        s.result[...] = got.astype(BF16)
        back.append(sends.start(s.result, s.near.at[3], place.partner))
    yield
    for copy in back:
        copy.wait_recv()
    yield


def begin_kernel(
    wq_hbm, wk_hbm, wv_hbm, wo_hbm, small_ref, rows_hbm, note_ref, tokens_hbm, cos_ref, sin_ref,
    w_out, small_out, wo_part, rows_near, notes_out, normed_ref, query_ref, kv_ref, gains_ref,
    strips_ref, w_all, own_kv, wq_ref, wk_ref, wv_ref, wo_ref, rows_ref, tokens_ref,
    fetch_sems, local_sems, send_sems, recv_sems,
):
    fetches = Keeps(fetch_sems)
    for src, dst in (
        (wq_hbm, wq_ref), (wk_hbm, wk_ref), (wv_hbm, wv_ref), (wo_hbm, wo_ref),
        (rows_hbm, rows_ref), (tokens_hbm, tokens_ref),
    ):
        fetches.start(src, dst)
    place = Place()
    y, z, core, part = place.y, place.z, place.core, place.part
    neighbours = [*place.others, *place.y_to, *place.z_to]
    greet(neighbours)
    rows = wq_ref.shape[0]
    wide, narrow = wq_ref.shape[1] // 4, wk_ref.shape[1] // 2
    strip = wide + narrow
    for fetch in fetches.made[:4]:
        fetch.wait()
    for s in range(4):
        strips_ref[:, s * strip : s * strip + wide] = wq_ref[:, s * wide : (s + 1) * wide]
        other = (wk_ref, wv_ref)[s % 2]
        begin = s // 2 * narrow
        strips_ref[:, s * strip + wide : (s + 1) * strip] = other[:, begin : begin + narrow]
    await_greetings(neighbours)
    sends, keeps = Sends(send_sems, recv_sems), Keeps(local_sems)

    def columns(p, size):
        return pl.ds(pl.multiple_of((2 * core + p) * size, 128), size)

    across = []

    def send_across(view):
        across.append(sends.start(view, view, place.partner))

    def spread(first, src, out, cols, y_first, landed):
        def near(where):
            return out.at[where, z, :, cols] if y_first else out.at[y, where, :, cols]

        def wider(where):
            return out.at[:, where, :, cols] if y_first else out.at[where, :, :, cols]

        if first:
            return Spread(y_first, src, near, half_rows)
        source = wider(z if y_first else y)
        landed(source)
        return Spread(not y_first, source, wider, half_span, landed)

    def strips(first, at, size):
        def part(p):
            return pl.ds(pl.multiple_of((2 * core + p) * strip + at, 128), size)

        return [
            spread(first, strips_ref.at[:, part(p)], w_all, part(p), p == 1, send_across)
            for p in range(2)
        ]

    def small_spread(first):
        every = pl.ds(0, small_ref.shape[1])
        return spread(first, small_ref, small_out, every, False, lambda _: None)

    def out_spread(p):
        ring_of = (z, y)[p]

        keeps.start(wo_ref.at[:, columns(p, wide)], wo_part.at[p, ring_of])
        return Spread(
            p == 1, wo_ref.at[:, columns(p, wide)], lambda where: wo_part.at[p, where], half_rows
        )

    ahead = ring_gather(place, sends, [*strips(True, wide, narrow), small_spread(True)])
    behind = ring_gather(place, sends, [*strips(True, 0, wide), *map(out_spread, range(2))])
    for steps in (ahead, ahead, behind, behind):
        next(steps)
    for p in range(2):
        w_all[y, z, :, columns(p, strip)] = strips_ref[:, columns(p, strip)]
    small_out[y, z] = small_ref[...]

    half = rows_ref.shape[0] // 2
    x_halves = [pl.ds(h * half, half) for h in range(2)]
    fetches.made[4].wait()
    rows_came = [
        sends.start(rows_ref.at[x_halves[h]], rows_near.at[d, x_halves[h]], place.x_to[d])
        for d in range(2)
        for h in (d, 1 - d)
    ]
    notes = [sends.start(note_ref, notes_out.at[part], to) for to in place.others]
    keeps.start(note_ref, notes_out.at[part])
    next(ahead)
    next(ahead)
    ahead = ring_gather(place, sends, [*strips(False, wide, narrow), small_spread(False)])
    next(ahead)
    next(ahead)
    next(behind)
    next(behind)
    behind = ring_gather(place, sends, strips(False, 0, wide))
    next(behind)
    next(behind)
    next(ahead)
    next(ahead)
    small_t = small_out[...].reshape(tokens_ref.shape[1], -1).astype(F32).T
    gains_ref[...] = small_t[EXPERTS : EXPERTS + 8]
    fetches.made[5].wait()
    inputs = tokens_ref[...].astype(F32)
    gain = small_t[EXPERTS + 1 : EXPERTS + 2]
    normed_ref[...] = (inputs * inverse_rms(inputs) * gain).astype(BF16)
    for copy in across:
        copy.wait_recv()
    del across[:]

    cosine, sine = cos_ref[...], sin_ref[...]
    width = tokens_ref.shape[1]

    def project(at, size):
        w = w_all[:, :, :, at : at + size].reshape(width, size)
        return mm(normed_ref[...], w)

    for s in range(4):
        got = project(s * strip + wide, HEAD_SIZE)
        if s % 2 == 0:
            got = spin(got, cosine, sine)
        own_kv[:, s * HEAD_SIZE : (s + 1) * HEAD_SIZE] = got.astype(BF16)
    slot = kv_ref.at[part]
    kv_came = [
        [
            sends.start(own_kv.at[x_halves[h]], slot.at[x_halves[h]], place.x_to[d])
            for h in (d, 1 - d)
        ]
        for d in range(2)
    ]
    kv_across = [sends.start(own_kv, slot, place.partner)]
    keeps.start(own_kv, slot)
    next(behind)
    next(behind)
    onward = []
    for d, origin in enumerate((place.left, place.right)):
        kv_came[d][0].wait_recv()
        view = kv_ref.at[origin, x_halves[d]]
        onward.append(sends.start(view, view, place.x_to[d]))
    for copy in across:
        copy.wait_recv()
    keeps.start(w_all, w_out)

    def queries(s):
        got = project(s * strip, wide)
        for h in range(0, wide, HEAD_SIZE):
            head = spin(got[:, h : h + HEAD_SIZE], cosine, sine)
            query_ref[:, s * wide + h : s * wide + h + HEAD_SIZE] = head.astype(BF16)

    for s in range(4):
        queries(s)
    for d, origin in enumerate((place.left, place.right)):
        kv_came[d][1].wait_recv()
        view = kv_ref.at[origin]
        kv_across.append(sends.start(view, view, place.partner))
    for d in range(2):
        onward[d].wait_recv()
        view = kv_ref.at[place.far, x_halves[d]]
        kv_across.append(sends.start(view, view, place.partner))
    for copy in [*kv_across, *notes, *rows_came]:
        copy.wait_recv()
    for copy in keeps.made:
        copy.wait()
    sends.finish()


def begin(wq, wk, wv, wo, small, rows, note, tokens, cosine, sine, collective_id):
    height, width = wq.shape
    kv_width = wk.shape[1] + wv.shape[1]
    total = width + kv_width
    count = tokens.shape[0]
    vmem = pltpu.VMEM
    return pl.pallas_call(
        begin_kernel,
        out_shape=[
            sds((4, 4, height, total), BF16),
            sds((4, 4, *small.shape), BF16),
            sds((2, 4, height, width // 4), BF16),
            sds((2, *rows.shape), BF16),
            sds((8, *note.shape), note.dtype),
            sds((count, width), BF16),
            sds((count, width), BF16),
            sds((8, count, kv_width), BF16),
            sds((8, width), F32),
        ],
        in_specs=[ANY] * 4 + [VMEM, ANY, VMEM, ANY, VMEM, VMEM],
        out_specs=[ANY, VMEM, VMEM, ANY, ANY, VMEM, VMEM, ANY, VMEM],
        scratch_shapes=[
            vmem((height, total), BF16),
            vmem((4, 4, height, total), BF16),
            vmem((count, kv_width), BF16),
            *[vmem(a.shape, BF16) for a in (wq, wk, wv, wo, rows, tokens)],
            semaphores(6),
            semaphores(6),
            semaphores(125),
            semaphores(125),
        ],
        compiler_params=remote_params(collective_id),
    )(wq, wk, wv, wo, small, rows, note, tokens, cosine, sine)


def fill_bias(bias, start_ref, first_row):
    length, rows = bias.shape
    places = lax.broadcasted_iota(jnp.int32, (length, rows), 0)
    mine = first_row + lax.broadcasted_iota(jnp.int32, (length, rows), 1)
    keep = (places >= start_ref[...]) & (places <= mine)
    bias[...] = jnp.where(keep, 0.0, MASK_FILL)


def head_columns(head):
    return pl.ds(pl.multiple_of(head * HEAD_SIZE, HEAD_SIZE), HEAD_SIZE)


def attend_kernel(
    start_ref, q_ref, kv_ref, wo_part, rows_own, rows_near, ctx_ref, lse_ref, wo_all, rows_far,
    rows_other, bias, v_t, scores, local_sems, send_sems, recv_sems,
):
    place = Place()
    neighbours = [place.partner, *place.x_to[:2], *place.y_to, *place.z_to]
    greet(neighbours)
    length, rows = bias.shape
    fill_bias(bias, start_ref, rows * place.part)
    await_greetings(neighbours)
    sends, keeps = Sends(send_sems, recv_sems), Keeps(local_sems)
    quarter = wo_part.shape[-1]
    across = []

    def landed(view):
        across.append(sends.start(view, view, place.partner))

    def spread(p):
        cols = pl.ds(pl.multiple_of((2 * place.core + p) * quarter, 128), quarter)

        def view(where):
            return wo_all.at[:, where, :, cols] if p else wo_all.at[where, :, :, cols]

        own = view((place.y, place.z)[p])
        keeps.start(wo_part.at[p], own)
        across.append(sends.start(wo_part.at[p], own, place.partner))
        return Spread(p == 0, wo_part.at[p], view, half_span, landed)

    steps = ring_gather(place, sends, [spread(p) for p in range(2)])
    next(steps)
    next(steps)

    half = rows // 2
    x_halves = [pl.ds(h * half, half) for h in range(2)]
    far_came = [
        sends.start(rows_near.at[d, x_halves[d]], rows_far.at[x_halves[d]], place.x_to[d])
        for d in range(2)
    ]
    for i, view in enumerate((rows_own, rows_near.at[0], rows_near.at[1])):
        across.append(sends.start(view, rows_other.at[i], place.partner))
    for group in range(KEY_VALUE_HEADS):
        keys = slice(2 * group * HEAD_SIZE, (2 * group + 1) * HEAD_SIZE)
        values = slice((2 * group + 1) * HEAD_SIZE, (2 * group + 2) * HEAD_SIZE)
        v_t[...] = kv_ref[:, values].astype(F32).T.astype(BF16)

        def one_head(i, carry, base):
            head = base + i
            query = q_ref[:, head_columns(head)]
            top = None
            for at in range(0, length, BLOCK):
                span = pl.ds(at, BLOCK)
                s = mm_nt(kv_ref[span, keys], query) + bias[span]
                scores[span] = s
                here = jnp.max(s, axis=0, keepdims=True)
                top = here if top is None else jnp.maximum(top, here)
            total = jnp.zeros_like(top)
            context = jnp.zeros((HEAD_SIZE, rows), F32)
            for at in range(0, length, BLOCK):
                span = pl.ds(at, BLOCK)
                p = jnp.exp2((scores[span] - top) * (SCALE * LOG2E))
                total += jnp.sum(p, axis=0, keepdims=True)
                context += mm(v_t[:, span], p.astype(BF16))
            ctx_ref[:, head_columns(head)] = (context / total).T.astype(BF16)
            lse_ref[head] = top * (SCALE * LOG2E) + jnp.log2(total)
            return carry

        for base in range(group * GROUP, (group + 1) * GROUP, 2):
            lax.fori_loop(0, 2, lambda i, carry, base=base: one_head(i, carry, base), 0)
            if base in (2, GROUP):
                next(steps)
            if base == GROUP:
                for d, copy in enumerate(far_came):
                    copy.wait_recv()
                    view = rows_far.at[x_halves[d]]
                    across.append(
                        sends.start(view, rows_other.at[3, x_halves[d]], place.partner)
                    )
    run_out(steps)
    for copy in across:
        copy.wait_recv()
    for copy in keeps.made:
        copy.wait()
    sends.finish()


def attend(start, query, kv, wo_part, rows_own, rows_near, collective_id):
    rows, width = query.shape
    length = kv.shape[0]
    height = wo_part.shape[2]
    return pl.pallas_call(
        attend_kernel,
        out_shape=[
            sds((rows, width), BF16),
            sds((QUERY_HEADS, 1, rows), F32),
            sds((4, 4, height, width), BF16),
            sds((rows, width), BF16),
            sds((4, rows, width), BF16),
        ],
        in_specs=[VMEM] * 4 + [ANY] * 2,
        out_specs=[VMEM, VMEM, ANY, ANY, ANY],
        scratch_shapes=[
            pltpu.VMEM((length, rows), F32),
            pltpu.VMEM((HEAD_SIZE, length), BF16),
            pltpu.VMEM((length, rows), F32),
            semaphores(2),
            semaphores(32),
            semaphores(32),
        ],
        compiler_params=remote_params(collective_id),
    )(start, query, kv, wo_part, rows_own, rows_near)


LOW, HIGH = 0, 1


def gelu_parts(a):
    k = (2.0 / jnp.pi) ** 0.5
    square = a * a
    t = jnp.tanh(k * a * (1.0 + 0.044715 * square))
    slope = 0.5 * (1.0 + t) + 0.5 * a * (1.0 - t * t) * k * (1.0 + 3 * 0.044715 * square)
    return 0.5 * a * (1.0 + t), slope


def experts_kernel(
    ctx_ref, tokens_ref, small_ref, gains_ref, notes_ref,
    rows_own, rows_near, rows_far, rows_other, wo_hbm, wg_hbm, wu_hbm, wd_hbm,
    middle_ref, gates_ref, gg_all, sums_ref, own_ref, back_out, w_grads,
    wo_ref, wg_ref, wu_ref, wd_ref, rows_all, returns, arrived, pair_grad, hidden, grad_pre,
    theirs, far_left, far_right, from_left, from_right, tile, tile_d, back_rows, gates_all, gg_src,
    slot_ref,
    local_sems, tile_sems, back_sems, send_sems, recv_sems,
):
    place = Place()
    part, core = place.part, place.core
    right, left, far = place.right, place.left, place.far
    to_right, to_left = place.x_to[:2]
    greet(place.others)
    sends, keeps, stores = (
        Sends(send_sems, recv_sems), Keeps(local_sems), Keeps(back_sems)
    )
    rows, width = ctx_ref.shape
    half = rows // 2
    halves = (pl.ds(0, half), pl.ds(half, half))
    ff = wg_ref.shape[1]
    capacity = arrived.shape[0] // 8

    for src, dst in ((wo_hbm, wo_ref), (wg_hbm, wg_ref), (wu_hbm, wu_ref), (wd_hbm, wd_ref)):
        keeps.start(src, dst)
    chips = [lax.rem(place.chip + d, 4) for d in (0, 3, 1, 2)]
    for u, src in enumerate((rows_own, rows_near.at[0], rows_near.at[1], rows_far)):
        keeps.start(src, returns.at[u, core])
        keeps.start(rows_other.at[u], returns.at[u, 1 - core])

    keeps.made[0].wait()
    middle = tokens_ref[...].astype(F32) + mm(ctx_ref[...], wo_ref[...])
    middle_ref[...] = middle
    normed = (middle * inverse_rms(middle) * gains_ref[:1]).astype(BF16)
    rows_all[part] = normed
    await_greetings(place.others)
    mine = rows_all.at[part]
    go = [
        [sends.start(mine.at[halves[h]], mine.at[halves[h]], way) for h in (d, 1 - d)]
        for d, way in enumerate((to_right, to_left))
    ]
    swap_own = sends.start(mine, mine, place.partner)

    ids = lax.broadcasted_iota(jnp.int32, (128, rows), 0)
    named = notes_ref[part]
    member = functools.reduce(jnp.logical_or, [ids == named[k : k + 1] for k in range(TOPK)])
    member = member.astype(F32).T
    logits = jnp.where(member > 0.0, mm(normed, small_ref[...]), MASK_FILL)
    weight = jnp.exp(logits - jnp.max(logits, axis=-1, keepdims=True)) * member
    gates = weight / jnp.sum(weight, axis=-1, keepdims=True)
    gates_ref[...] = gates.T[:EXPERTS]
    note_sends = [sends.start(gates_ref, gates_all.at[part], to) for to in place.others]
    gates_all[part] = gates_ref[...]

    chosen = jnp.concatenate(
        [
            functools.reduce(
                jnp.logical_or, [notes_ref[s, k : k + 1] == part for k in range(TOPK)]
            ).astype(F32)
            for s in range(8)
        ],
        axis=0,
    )
    earlier = lax.broadcasted_iota(jnp.int32, (rows, rows), 0) < lax.broadcasted_iota(
        jnp.int32, (rows, rows), 1
    )
    ranks = mm(chosen.astype(BF16), earlier.astype(F32).astype(BF16))
    slots_of = jnp.where(chosen > 0.0, ranks, -1.0)
    for s in range(8):
        slot_ref[s] = slots_of[s : s + 1].astype(jnp.int32)

    def pick_of(source):
        slots = lax.broadcasted_iota(jnp.int32, (capacity, rows), 0)
        return slots == slot_ref[source]

    for u in range(4):
        keeps.made[4 + 2 * u].wait()
        keeps.made[5 + 2 * u].wait()
        for c in range(2):
            pick = pick_of(2 * chips[u] + c).astype(BF16)
            got = mm(pick, returns[u, c])
            pair_grad[pl.ds((2 * u + c) * capacity, capacity)] = got.astype(BF16)
    for load in keeps.made[1:4]:
        load.wait()

    swaps, gg_sends = [], []

    def unit(u):
        at = chips[u]
        picks = [pick_of(2 * at + c) for c in range(2)]
        picks_b = [pick.astype(BF16) for pick in picks]
        spans = [pl.ds((2 * u + c) * capacity, capacity) for c in range(2)]
        both = pl.ds(2 * u * capacity, 2 * capacity)
        gate = []
        for c in range(2):
            arrived[spans[c]] = mm(picks_b[c], rows_all[2 * at + c]).astype(BF16)
            row = gates_all[2 * at + c, pl.ds(part, 1)]
            gate.append(jnp.sum(jnp.where(picks[c], row, 0.0), axis=-1, keepdims=True))
        gate = jnp.concatenate(gate, axis=0)
        x = arrived[both]
        a, b = mm(x, wg_ref[...]), mm(x, wu_ref[...])
        act, slope = gelu_parts(a)
        h = (act * b).astype(BF16)
        hidden[both] = h
        out = mm(h, wd_ref[...]).astype(BF16).astype(F32)
        up = pair_grad[both].astype(F32)
        gg = jnp.sum(up * out, axis=-1, keepdims=True)
        weighted = (gate * out).astype(BF16)
        pg = (gate * up).astype(BF16)
        pair_grad[both] = pg
        grad_h = mm_nt(pg, wd_ref[...])
        grad_a = (grad_h * b * slope).astype(BF16)
        grad_b = (grad_h * act).astype(BF16)
        grad_pre[both, :ff] = grad_a
        grad_pre[both, ff:] = grad_b
        grad_rows = (mm_nt(grad_a, wg_ref[...]) + mm_nt(grad_b, wu_ref[...])).astype(BF16)
        for c in range(2):
            returns[u, c] = mm_tn(
                picks_b[c], grad_rows[c * capacity : (c + 1) * capacity]
            ).astype(BF16)
        swaps.append(sends.start(returns.at[u, 1 - core], theirs.at[u], place.partner))
        for c in range(2):
            if u > 0:
                stores.made[2 * (u - 1) + c].wait()
            back_rows[c] = mm_tn(picks_b[c], weighted[c * capacity : (c + 1) * capacity]).astype(
                BF16
            )
            stores.start(back_rows.at[c], back_out.at[2 * at + c])
            gg_c = gg[c * capacity : (c + 1) * capacity]
            row = jnp.sum(jnp.where(picks[c], gg_c, 0.0), axis=0, keepdims=True)
            gg_src[u, c] = jnp.broadcast_to(row, (8, rows))
        if u == 0:
            gg_all[part] = gg_src[0, core]
            gg_sends.append(sends.start(gg_src.at[0, 1 - core], gg_all.at[part], place.partner))
        else:
            for c in (core, 1 - core):
                gg_sends.append(
                    sends.start(gg_src.at[u, c], gg_all.at[part], {"expert": 2 * at + c})
                )

    def joined(u):
        swaps[u].wait_recv()
        add_to(theirs.at[u], returns.at[u, core])

    swap_own.wait_recv()
    for copy in note_sends:
        copy.wait_recv()
    unit(0)
    passed = []
    for d, (origin, way) in enumerate(((left, to_right), (right, to_left))):
        go[d][0].wait_recv()
        view = rows_all.at[origin, halves[d]]
        passed.append(sends.start(view, view, way))
    far_low, far_high = passed
    go[0][1].wait_recv()
    swap_left = sends.start(rows_all.at[left], rows_all.at[left], place.partner)
    go[1][1].wait_recv()
    swap_right = sends.start(rows_all.at[right], rows_all.at[right], place.partner)
    swap_left.wait_recv()
    unit(1)
    swap_right.wait_recv()
    unit(2)
    swap_far = []
    for h, copy in enumerate((far_low, far_high)):
        copy.wait_recv()
        piece = rows_all.at[far, halves[h]]
        swap_far.append(sends.start(piece, piece, place.partner))
    joined(1)
    joined(2)
    back_right = sends.start(theirs.at[2, halves[HIGH]], from_left, to_right)
    back_left = sends.start(theirs.at[1, halves[LOW]], from_right, to_left)
    for copy in swap_far:
        copy.wait_recv()
    unit(3)
    joined(3)
    back_far_low = sends.start(theirs.at[3, halves[LOW]], far_left, to_right)
    back_far_high = sends.start(theirs.at[3, halves[HIGH]], far_right, to_left)

    tall = 4 * w_grads.shape[2] * 2 // 3
    high = tall // 4
    w_stores = Keeps(tile_sems)
    for i in range(ff // tall):
        got = mm_tn(hidden[:, i * tall : (i + 1) * tall], pair_grad[...]).astype(BF16)
        tile_d[i] = got.reshape(tile_d.shape[1:])
        w_stores.start(tile_d.at[i], w_grads.at[pl.ds(2 * i, 2), :, pl.ds(high, high // 2)])
    for i in range(width // tall):
        if i >= 2:
            w_stores.made[ff // tall + i - 2].wait()
        got = mm_tn(arrived[:, i * tall : (i + 1) * tall], grad_pre[...]).astype(BF16)
        tile[i % 2] = got.reshape(tile.shape[1:])
        w_stores.start(tile.at[i % 2], w_grads.at[i, :, pl.ds(0, high)])

    swaps[0].wait_recv()
    back_right.wait_recv()
    back_left.wait_recv()
    own_ref[...] = theirs[0].astype(F32) + returns[0, core].astype(F32)
    add_to(own_ref.at[halves[HIGH]], from_left)
    add_to(own_ref.at[halves[LOW]], from_right)
    back_far_low.wait_recv()
    sums_ref[0] = (theirs[2, halves[LOW]].astype(F32) + far_left[...].astype(F32)).astype(BF16)
    back_far_high.wait_recv()
    sums_ref[1] = (theirs[1, halves[HIGH]].astype(F32) + far_right[...].astype(F32)).astype(BF16)
    for copy in gg_sends:
        copy.wait_recv()
    for copy in [*stores.made[6:], *w_stores.made[: ff // tall], *w_stores.made[-2:]]:
        copy.wait()
    sends.finish()


def experts(ctx, tokens, small, gains, notes, rows_by, wo, wg, wu, wd, collective_id):
    rows, width = ctx.shape
    ff = wg.shape[1]
    capacity = rows * 9 // 16
    high = width // 16
    vmem = pltpu.VMEM
    return pl.pallas_call(
        experts_kernel,
        out_shape=[
            sds((rows, width), F32),
            sds((EXPERTS, rows), F32),
            sds((8, 8, rows), F32),
            sds((2, rows // 2, width), BF16),
            sds((rows, width), F32),
            sds((8, rows, width), BF16),
            sds((4, 4, high * 3 // 2, width), BF16),
        ],
        in_specs=[VMEM] * 5 + [ANY] * 8,
        out_specs=[VMEM] * 5 + [ANY] * 2,
        scratch_shapes=[
            vmem((width, width), BF16),
            vmem((width, ff), BF16),
            vmem((width, ff), BF16),
            vmem((ff, width), BF16),
            vmem((8, rows, width), BF16),
            vmem((4, 2, rows, width), BF16),
            vmem((8 * capacity, width), BF16),
            vmem((8 * capacity, width), BF16),
            vmem((8 * capacity, ff), BF16),
            vmem((8 * capacity, 2 * ff), BF16),
            vmem((4, rows, width), BF16),
            *[vmem((rows // 2, width), BF16)] * 4,
            vmem((2, 4, high, width), BF16),
            vmem((2, 2, 4, high // 2, width), BF16),
            vmem((2, rows, width), BF16),
            vmem((8, EXPERTS, rows), F32),
            vmem((4, 2, 8, rows), F32),
            vmem((8, 1, rows), jnp.int32),
            semaphores(12),
            semaphores(6),
            semaphores(8),
            semaphores(40),
            semaphores(40),
        ],
        compiler_params=remote_params(collective_id),
    )(ctx, tokens, small, gains, notes, *rows_by, wo, wg, wu, wd)


GROUPS = 3


def middle_kernel(
    middle_ref, gates_ref, gg_all, sums_ref, own_hbm, d_out_hbm, ctx_hbm, small_ref, gains_ref,
    start_ref, q_hbm, kv_hbm, lse_ref, cos_ref, sin_ref, wo_hbm, w_grads, blocks_ref,
    grad_middle_out, small_grad_ref, gq_out, gkv_out, wo_out, combined, w_done,
    own_ref, d_out_ref, ctx_ref, q_ref, kv_ref, grad_middle_ref, gq_ref, gkv_ref,
    wo_ref, g_ref, from_left, from_right, w_total_0, w_total_1, w_whole, w_far,
    bias, k_t, gkv, probs, grad_probs, second_whole, second_far, *refs,
):
    place = Place()
    core = place.core
    neighbours = [place.partner, *place.x_to, *place.y_to, *place.z_to]
    greet(neighbours)
    bufs, x_bufs = refs[:12], refs[12:17]
    wo_sem, fetch_sems, store_sems, local_sems, send_sems, recv_sems = refs[17:]
    keeps = Keeps(local_sems)
    cols = w_total_0.shape[-1]
    totals = (w_total_0, w_total_1)
    length, rows = bias.shape
    width = middle_ref.shape[1]
    quarter = width // 4

    def part_of(ref, p, w):
        return ref.at[:, w] if p else ref.at[w]

    loads = {}
    for k in range(4):
        for p in range(2):
            me, (right, left, far), _ = place.ring(p == 0)
            w = (far, right, left, me)[k]
            src = part_of(w_grads, p, w).at[:, :, pl.ds(p * cols, cols)]
            loads[k, p] = keeps.start(src, part_of(totals[p], p, w))
    wo_load = pltpu.make_async_copy(wo_hbm, wo_ref, wo_sem)
    wo_load.start()
    fetches, stores = Keeps(fetch_sems), Keeps(store_sems)
    own_fetch, d_out_fetch, ctx_fetch, q_fetch, kv_fetch = [
        fetches.start(src, dst)
        for src, dst in (
            (own_hbm, own_ref), (d_out_hbm, d_out_ref), (ctx_hbm, ctx_ref), (q_hbm, q_ref),
            (kv_hbm, kv_ref),
        )
    ]
    await_greetings(neighbours)
    sends = Sends(send_sems, recv_sems)
    came = [
        sends.start(sums_ref.at[i], dst, place.x_to[i])
        for i, dst in enumerate((from_left, from_right))
    ]

    def first_half(p):
        def view(w, h):
            span = pl.ds(2 * h, 2)
            return totals[p].at[span, w] if p else totals[p].at[w, span]

        return view

    def expert_steps():
        rings = [Ring(p == 0, first_half(p), w_whole.at[p], w_far.at[p]) for p in range(2)]
        yield from ring_sum(place, sends, rings, lambda k, i, w: loads[k, i].wait())
        half = cols // 2

        def second_half(p):
            def view(w, h):
                at = pl.ds(h * half, half)
                return totals[p].at[w, place.z, :, at] if p else totals[p].at[place.y, w, :, at]

            return view

        rings = [
            Ring(p == 1, second_half(p), second_whole.at[p], second_far.at[p]) for p in range(2)
        ]
        yield from ring_sum(place, sends, rings)
        spreads = []
        for p in range(2):
            me = place.ring(p == 1)[0]
            w_done[p, me] = totals[p][place.y, place.z]

            view = lambda w, p=p: w_done.at[p, w]
            spreads.append(Spread(p == 1, w_done.at[p, me], view, half_columns))
        yield from ring_gather(place, sends, spreads)

    def columns(c, p):
        return pl.ds(pl.multiple_of((2 * c + p) * quarter, 128), quarter)

    def theirs_of(p):
        at = columns(1 - core, p)
        if p == 0:
            return lambda w: wo_ref.at[w, :, :, at]
        return lambda w: wo_ref.at[:, w, :, at]

    strips = [
        Strip(
            p == 0, wo_ref.at[:, :, :, columns(core, p)], bufs[6 * p : 6 * p + 6],
            None, theirs_of(p),
        )
        for p in range(2)
    ]
    expert = expert_steps()
    dense = dp_sum(place, sends, strips, ())
    rest = x_sum(place, sends, blocks_ref, combined, *x_bufs)
    next(expert)
    next(rest)

    grad_gates = jnp.concatenate([gg_all[e, :1] for e in range(EXPERTS)], axis=0)
    gates_t = gates_ref[...]
    products = gates_t * grad_gates
    grad_logits = products - gates_t * jnp.sum(products, axis=0, keepdims=True)
    grad_logits = jnp.concatenate(
        [grad_logits, jnp.zeros((128 - EXPERTS, rows), F32)], axis=0
    ).T.astype(BF16)
    own_fetch.wait()
    total = own_ref[...] + mm_nt(grad_logits, small_ref[...])
    middle, gain = middle_ref[...], gains_ref[:1]
    inverse = inverse_rms(middle)
    scaled = middle * inverse
    small_grad = mm_tn((scaled * gain).astype(BF16), grad_logits)
    fill_bias(bias, start_ref, rows * place.part)
    for copy in came:
        copy.wait_recv()
    total += jnp.concatenate([from_left[...], from_right[...]], axis=0).astype(F32)
    grad_gain = jnp.sum(total * scaled, axis=0, keepdims=True)
    lanes = lax.broadcasted_iota(jnp.int32, (width, 128), 1)
    small_grad += jnp.where(lanes == EXPERTS, as_column(grad_gain, 128), 0.0)
    small_grad_ref[...] = small_grad.astype(BF16)
    weighted = total * gain
    inner = jnp.mean(weighted * scaled, axis=-1, keepdims=True)
    d_out_fetch.wait()
    grad_middle = d_out_ref[...].astype(F32) + inverse * (weighted - scaled * inner)
    grad_middle_ref[...] = grad_middle
    stores.start(grad_middle_ref, grad_middle_out)
    grad_attn = grad_middle.astype(BF16)
    wo_load.wait()
    g_ref[...] = mm_nt(grad_attn, wo_ref[...].reshape(width, width)).astype(BF16)
    next(rest)
    next(expert)
    ctx_fetch.wait()
    tall = width // 4
    for i in range(4):
        got = mm_tn(ctx_ref[:, i * tall : (i + 1) * tall], grad_attn).astype(BF16)
        wo_ref[i] = got.reshape(wo_ref.shape[1:])
    next(dense)

    q_fetch.wait()
    kv_fetch.wait()
    when = {2: (dense,), 4: (rest,), 6: (dense, expert), 8: (dense,), 10: (dense, expert)}
    for group in range(KEY_VALUE_HEADS):
        keys = slice(2 * group * HEAD_SIZE, (2 * group + 1) * HEAD_SIZE)
        values = slice((2 * group + 1) * HEAD_SIZE, (2 * group + 2) * HEAD_SIZE)
        k_t[...] = kv_ref[:, keys].astype(F32).T.astype(BF16)
        gkv[...] = jnp.zeros_like(gkv)

        def one_head(i, carry, base):
            head = base + i
            query, grad = q_ref[:, head_columns(head)], g_ref[:, head_columns(head)]
            lse = lse_ref[head]
            inner = jnp.zeros_like(lse)
            for at in range(0, length, BLOCK):
                span = pl.ds(at, BLOCK)
                s = mm_nt(kv_ref[span, keys], query) + bias[span]
                p = jnp.exp2(s * (SCALE * LOG2E) - lse)
                gp = mm_nt(kv_ref[span, values], grad)
                inner += jnp.sum(p * gp, axis=0, keepdims=True)
                probs[span] = p
                grad_probs[span] = gp
                gkv[span, HEAD_SIZE:] += mm(p.astype(BF16), grad)
            gq = jnp.zeros((HEAD_SIZE, rows), F32)
            for at in range(0, length, BLOCK):
                span = pl.ds(at, BLOCK)
                gs = (probs[span] * (grad_probs[span] - inner)).astype(BF16)
                gkv[span, :HEAD_SIZE] += mm(gs, query)
                gq += mm(k_t[:, span], gs)
            turned = spin(gq.T * SCALE, cos_ref[...], -sin_ref[...])
            gq_ref[:, head_columns(head)] = turned.astype(BF16)
            return carry

        for base in range(group * GROUP, (group + 1) * GROUP, 2):
            lax.fori_loop(0, 2, lambda i, carry, base=base: one_head(i, carry, base), 0)
            for steps in when.get(base + 2, ()):
                next(steps)
        gkv_ref[:, keys] = (gkv[:, :HEAD_SIZE] * SCALE).astype(BF16)
        gkv_ref[:, values] = gkv[:, HEAD_SIZE:].astype(BF16)
    stores.start(gq_ref, gq_out)
    stores.start(gkv_ref, gkv_out)
    run_out(expert, dense, rest)
    for p, s in enumerate(strips):
        wo_out[:, columns(core, p)] = s.result[...]
        wo_out[:, columns(1 - core, p)] = s.near[3]
    for copy in stores.made:
        copy.wait()
    sends.finish()


def between(
    middle, gates, gg, sums, own, d_out, ctx, small, gain, start, query, kv, lse, cosine, sine,
    wo, w_grads, back_out, collective_id,
):
    rows, width = query.shape
    length = kv.shape[0]
    height, quarter = width // 16, width // 4
    high, cols = w_grads.shape[2], width // 2
    vmem = pltpu.VMEM
    return pl.pallas_call(
        middle_kernel,
        out_shape=[
            sds((rows, width), F32),
            sds((width, 128), BF16),
            sds((rows, width), BF16),
            sds(kv.shape, BF16),
            sds((height, width), BF16),
            sds((rows, width), F32),
            sds((2, 4, high, cols), BF16),
        ],
        in_specs=[VMEM] * 4 + [ANY] * 3 + [VMEM] * 3 + [ANY] * 2 + [VMEM] * 3 + [ANY] * 3,
        out_specs=[ANY, VMEM, ANY, ANY, VMEM, VMEM, VMEM],
        scratch_shapes=[
            vmem((rows, width), F32),
            *[vmem((rows, width), BF16)] * 3,
            vmem(kv.shape, BF16),
            vmem((rows, width), F32),
            vmem((rows, width), BF16),
            vmem(kv.shape, BF16),
            vmem((4, 4, height, width), BF16),
            vmem((rows, width), BF16),
            vmem((rows // 2, width), BF16),
            vmem((rows // 2, width), BF16),
            vmem((4, 4, high, cols), BF16),
            vmem((4, 4, high, cols), BF16),
            vmem((2, 2, 2, 2, high, cols), BF16),
            vmem((2, 2, 2, high, cols), BF16),
            vmem((length, rows), F32),
            vmem((HEAD_SIZE, length), BF16),
            vmem((length, 2 * HEAD_SIZE), F32),
            vmem((length, rows), F32),
            vmem((length, rows), F32),
            vmem((2, 2, 2, high, cols // 2), BF16),
            vmem((2, 2, high, cols // 2), BF16),
            *strip_buffers(height, quarter),
            *strip_buffers(height, quarter),
            *x_buffers(rows, width),
            pltpu.SemaphoreType.DMA,
            semaphores(5),
            semaphores(3),
            semaphores(8),
            semaphores(100),
            semaphores(100),
        ],
        compiler_params=remote_params(collective_id),
    )(
        middle, gates, gg, sums, own, d_out, ctx, small, gain, start, query, kv, lse, cosine, sine,
        wo, w_grads, back_out,
    )


def last_kernel(
    kv_terms, gq_ref, normed_ref, tokens_ref, gains_ref, cos_ref, sin_ref,
    small_ref, w_done, w_hbm,
    grad_inputs_ref, strips_out, small_out, w_sums,
    grads, small_total, w_ref, normed_t, kv_sum, *refs,
):
    place = Place()
    core = place.core
    neighbours = [place.partner, *place.x_to, *place.y_to, *place.z_to]
    greet(neighbours)
    bufs, x_bufs = refs[:30], refs[30:35]
    w_sem, local_sems, send_sems, recv_sems = refs[35:]
    load = pltpu.make_async_copy(w_hbm, w_ref, w_sem)
    load.start()
    await_greetings(neighbours)
    sends, keeps = Sends(send_sems, recv_sems), Keeps(local_sems)
    kv_steps = x_sum(place, sends, kv_terms, kv_sum, *x_bufs)
    next(kv_steps)

    def place_of(p, w, at, size):
        cols = pl.ds(p * w_done.shape[-1] + at, size)
        return w_sums.at[:, w, :, cols] if p else w_sums.at[w, :, :, cols]

    def spread(p, i):
        size = w_done.shape[-1] // GROUPS
        source = w_done.at[p, :, :, pl.ds(i * size, size)]
        return Spread(p == 0, source, lambda w: place_of(p, w, i * size, size), half_span)

    for p in range(2):
        keeps.start(w_done.at[p], place_of(p, place.ring(p == 0)[0], 0, w_done.shape[-1]))
    e0, e1, e2 = [
        ring_gather(place, sends, [spread(p, i) for p in range(2)]) for i in range(GROUPS)
    ]
    for steps in (e0, e0, e1):
        next(steps)
    strip = grads.shape[-1]
    wide = strip - HEAD_SIZE
    rows, width = normed_ref.shape
    height = grads.shape[3]

    def put(s, cols, right_side):
        got = mm(normed_t[...], right_side).astype(BF16)
        grads[s, :, :, :, cols] = got.reshape(4, 4, height, right_side.shape[1])

    def shared(at, size, bufs):
        cols = pl.ds(at, size)

        def theirs_of(p):
            s = 2 * (1 - core) + p
            if p == 0:
                return lambda w: grads.at[s, w, :, :, cols]
            return lambda w: grads.at[s, :, w, :, cols]

        return [
            Strip(
                p == 0, grads.at[2 * core + p, :, :, :, cols], bufs[6 * p : 6 * p + 6],
                None, theirs_of(p),
            )
            for p in range(2)
        ]

    wide_strips = shared(0, wide, bufs[:12])
    narrow_strips = shared(wide, HEAD_SIZE, bufs[12:24])
    wide_steps = dp_sum(place, sends, wide_strips, ())
    narrow_steps = dp_sum(place, sends, narrow_strips, ())
    normed_t[...] = normed_ref[...].astype(F32).T.astype(BF16)
    for s in range(4):
        put(s, pl.ds(0, wide), gq_ref[:, s * wide : (s + 1) * wide])
    next(wide_steps)
    next(kv_steps)
    next(e0)
    load.wait()
    grad_normed = None
    for s in range(4):
        at = s * strip
        term = mm_nt(gq_ref[:, s * wide : (s + 1) * wide], w_ref[:, at : at + wide])
        grad_normed = term if grad_normed is None else grad_normed + term
    next(wide_steps)
    next(kv_steps)
    run_out(kv_steps)
    cosine, sine = cos_ref[...], sin_ref[...]
    for s in range(4):
        got = kv_sum[:, s * HEAD_SIZE : (s + 1) * HEAD_SIZE]
        if s % 2 == 0:
            got = spin(got, cosine, -sine)
        got = got.astype(BF16)
        put(s, pl.ds(wide, HEAD_SIZE), got)
        grad_normed += mm_nt(got, w_ref[:, s * strip + wide : (s + 1) * strip])
    for steps in (narrow_steps, wide_steps, narrow_steps):
        next(steps)

    grad_inputs, grad_gain = rms_back(tokens_ref[...].astype(F32), gains_ref[1:2], grad_normed)
    grad_inputs_ref[...] = grad_inputs
    lanes = lax.broadcasted_iota(jnp.int32, (width, 128), 1)
    small = jnp.where(
        lanes == EXPERTS + 1, as_column(grad_gain, 128), small_ref[...].astype(F32)
    )
    small_total[...] = small.astype(BF16).reshape(small_total.shape)
    small_strip = Strip(True, small_total, bufs[24:])
    small_steps = dp_sum(place, sends, [small_strip], ())
    for steps in (
        small_steps, small_steps, wide_steps, narrow_steps, small_steps,
        wide_steps, narrow_steps, small_steps, wide_steps, e1, narrow_steps, e2, small_steps, e2,
        wide_steps, narrow_steps, e1,
    ):
        next(steps)
    run_out(wide_steps, narrow_steps, small_steps, e0, e1, e2)
    small_out[...] = small_strip.result[...].astype(F32) + small_strip.near[3].astype(F32)
    for p in range(2):
        for at, size, s in ((0, wide, wide_strips[p]), (wide, HEAD_SIZE, narrow_strips[p])):
            for c, got in ((core, s.result), (1 - core, s.near.at[3])):
                begin_at = pl.multiple_of((2 * c + p) * strip + at, 128)
                strips_out[:, pl.ds(begin_at, size)] = got[...]
    for copy in keeps.made:
        copy.wait()
    sends.finish()


def last(
    kv_terms, grad_query, normed, tokens, gain, cosine, sine, small, w_done, w, collective_id
):
    rows, width = normed.shape
    total = w.shape[1]
    height, strip = width // 16, total // 4
    kv_width = total - width
    vmem = pltpu.VMEM
    return pl.pallas_call(
        last_kernel,
        out_shape=[
            sds((rows, width), F32),
            sds((height, total), BF16),
            sds((height, 128), F32),
            sds((4, 4, w_done.shape[2], width), BF16),
        ],
        in_specs=[ANY] + [VMEM] * 8 + [ANY],
        out_specs=[VMEM] * 3 + [ANY],
        scratch_shapes=[
            vmem((4, 4, 4, height, strip), BF16),
            vmem((4, 4, height, 128), BF16),
            vmem((width, total), BF16),
            vmem((width, rows), BF16),
            vmem((rows, kv_width), F32),
            *strip_buffers(height, strip - HEAD_SIZE),
            *strip_buffers(height, strip - HEAD_SIZE),
            *strip_buffers(height, HEAD_SIZE),
            *strip_buffers(height, HEAD_SIZE),
            *strip_buffers(height, 128, shared=False),
            *x_buffers(rows, kv_width),
            pltpu.SemaphoreType.DMA,
            semaphores(2),
            semaphores(160),
            semaphores(160),
        ],
        compiler_params=remote_params(collective_id),
    )(kv_terms, grad_query, normed, tokens, gain, cosine, sine, small, w_done, w)


def finish_kernel(
    sums_ref, grad_middle_ref, grad_inputs_ref, middle_ref, combined_ref, strips_ref, wo_ref,
    small_ref, g_out, u_out, d_out, tokens_out, mixed_out, wq_out, wk_out, wv_out, wo_out,
    small_out,
):
    owners, high, width = sums_ref.shape
    ff = width // 2
    gu = high * 2 // 3
    g_out[...] = sums_ref[:, :gu, :ff].astype(F32).reshape(owners * gu, ff)
    u_out[...] = sums_ref[:, :gu, ff:].astype(F32).reshape(owners * gu, ff)
    d_out[...] = sums_ref[:, gu:].astype(F32).reshape(owners * (high - gu), width)
    tokens_out[...] = grad_middle_ref[...] + grad_inputs_ref[...]
    mixed_out[...] = (middle_ref[...] + combined_ref[...]).astype(BF16)

    @pl.when(pl.program_id(0) == 0)
    def _():
        strip = strips_ref.shape[1] // 4
        wide = strip - HEAD_SIZE
        for s in range(4):
            at = s * strip
            wq_out[:, s * wide : (s + 1) * wide] = strips_ref[:, at : at + wide].astype(F32)
            other = (wk_out, wv_out)[s % 2]
            begin_at = s // 2 * HEAD_SIZE
            got = strips_ref[:, at + wide : at + strip].astype(F32)
            other[:, begin_at : begin_at + HEAD_SIZE] = got
        wo_out[...] = wo_ref[...].astype(F32)
        small_out[...] = small_ref[...].T[: EXPERTS + 8]


def finish(sums, grad_middle, grad_inputs, middle, combined, strips, wo, small):
    owners, high, width = sums.shape
    rows = middle.shape[0]
    height, total = strips.shape
    kv_half = (total - width) // 2
    ff = width // 2
    gu, d = high * 2 // 3, high // 3
    steps = 8
    each, part = owners // steps, rows // steps
    by_step = lambda a, b: pl.BlockSpec((a, b), lambda i: (i, 0))
    whole = lambda a, b: pl.BlockSpec((a, b), lambda i: (0, 0))
    return pl.pallas_call(
        finish_kernel,
        grid=(steps,),
        out_shape=[
            sds((owners * gu, ff), F32),
            sds((owners * gu, ff), F32),
            sds((owners * d, width), F32),
            sds((rows, width), F32),
            sds((rows, width), BF16),
            sds((height, width), F32),
            sds((height, kv_half), F32),
            sds((height, kv_half), F32),
            sds((height, width), F32),
            sds((EXPERTS + 8, height), F32),
        ],
        in_specs=[pl.BlockSpec((each, high, width), lambda i: (i, 0, 0))]
        + [by_step(part, width)] * 4
        + [whole(height, total), whole(height, width), whole(height, 128)],
        out_specs=[
            by_step(each * gu, ff),
            by_step(each * gu, ff),
            by_step(each * d, width),
            by_step(part, width),
            by_step(part, width),
            whole(height, width),
            whole(height, kv_half),
            whole(height, kv_half),
            whole(height, width),
            whole(EXPERTS + 8, height),
        ],
        compiler_params=pltpu.CompilerParams(vmem_limit_bytes=63 * MIB),
        cost_estimate=pl.CostEstimate(flops=0, bytes_accessed=30 * MIB, transcendentals=0),
    )(sums, grad_middle, grad_inputs, middle, combined, strips, wo, small)


def on_device(
    tokens,
    d_out,
    gain_in,
    w_query,
    key_projection_weight,
    value_projection_weight,
    w_out,
    gain_mid,
    w_router,
    w_gate,
    w_up,
    w_down,
    routes,
    segments,
):
    rows, width = tokens.shape
    length = segments.shape[1]
    part = lax.axis_index("expert")
    seg_row = segments[0]
    offset = part * rows
    my_seg = lax.dynamic_slice_in_dim(seg_row, offset, rows, 0)
    start = jnp.sum((seg_row[None, :] < my_seg[:, None]).astype(jnp.int32), axis=1)
    angles = angles_for(offset + jnp.arange(rows, dtype=jnp.int32) - start)
    cosine, sine = jnp.cos(angles), jnp.sin(angles)
    cosine = jnp.concatenate([cosine, cosine], axis=1)
    sine = jnp.concatenate([-sine, sine], axis=1)
    start = start[None, :]

    rest = jnp.zeros((w_router.shape[0], 126 - EXPERTS), BF16)
    small = jnp.concatenate([w_router, gain_mid[:, None], gain_in[:, None], rest], axis=1)
    note = jnp.pad(routes.T, ((0, 8 - TOPK), (0, 0)))
    w_strips, small, wo_part, rows_near, notes, normed, query, kv_all, gains = begin(
        w_query, key_projection_weight, value_projection_weight, w_out, small, d_out, note,
        tokens, cosine, sine, 1,
    )
    w_strips = w_strips.reshape(width, -1)
    small = small.reshape(width, -1)
    kv_all = kv_all.reshape(length, -1)
    context, lse, wo, rows_far, rows_other = attend(
        start, query, kv_all, wo_part, d_out, rows_near, 2
    )

    middle, gates, gg, sums, own, back_out, w_grads = experts(
        context, tokens, small, gains, notes, (d_out, rows_near, rows_far, rows_other),
        wo.reshape(width, width), w_gate[0], w_up[0], w_down[0], 3,
    )
    grad_middle, small_grads, grad_query, kv_terms, wo_sum, combined, w_done = between(
        middle, gates, gg, sums, own, d_out, context, small, gains, start, query, kv_all,
        lse, cosine, sine, wo, w_grads, back_out, 4,
    )
    grad_inputs, strips_sum, small_sum, w_sums = last(
        kv_terms.reshape(8, rows, -1), grad_query, normed, tokens, gains, cosine, sine,
        small_grads, w_done, w_strips, 5,
    )
    g_wg, g_wu, g_wd, grad_tokens, mixed, g_wq, g_wk, g_wv, g_wo, g_small = finish(
        w_sums.reshape(16, -1, width), grad_middle, grad_inputs, middle, combined, strips_sum,
        wo_sum, small_sum,
    )
    return (
        mixed,
        grad_tokens,
        g_small[EXPERTS + 1],
        g_wq,
        g_wk,
        g_wv,
        g_wo,
        g_small[EXPERTS],
        g_small[:EXPERTS].T,
        g_wg[None],
        g_wu[None],
        g_wd[None],
    )


def solution(mesh):
    whole = P(("dp", "expert"), None)
    over_dp, by_dp, over_expert = P("dp"), P("dp", None), P("expert", None, None)
    return jax.shard_map(
        on_device,
        mesh=mesh,
        in_specs=(whole, whole, over_dp, by_dp, by_dp, by_dp, by_dp, over_dp, by_dp)
        + (over_expert,) * 3
        + (whole, by_dp),
        out_specs=(whole, whole, over_dp, by_dp, by_dp, by_dp, by_dp, over_dp, by_dp)
        + (over_expert,) * 3,
        check_vma=False,
    )
```
